32 devices in a mesh: fsdp: 2 (over x), rows: 16 (over z, y, core).
Axes of the slice: x: 2, y: 2, z: 4, core: 2. Of those that a mesh axis runs over, the one named last changes fastest.
Arguments:
- residual_target: float32 [2, 12, 128, 512], P('fsdp', None, 'rows'), may hold values from -40 to 40
- conditioning: float32 [2, 12, 128, 512], P('fsdp', None, 'rows'), may hold values from -20 to 20
- noise_sample: float32 [2, 12, 128, 512], P('fsdp', None, 'rows'), may hold values from -20 to 20
- noise_level: int32 [2], P('fsdp'), may hold values from 0 to 63
- input_kernel: float32 [9, 64, 24], P(None, 'fsdp'), may hold values from -0.4375 to 0.4375
- first_kernel: float32 [9, 64, 64], P(None, 'fsdp'), may hold values from -0.25 to 0.25
- second_kernel: float32 [9, 64, 64], P(None, 'fsdp'), may hold values from -0.25 to 0.25
- down_kernel: float32 [9, 128, 64], P(None, 'fsdp'), may hold values from -0.25 to 0.25
- coarse_kernel: float32 [9, 128, 128], P(None, 'fsdp'), may hold values from -0.1875 to 0.1875
- upward_kernel: float32 [9, 64, 128], P(None, 'fsdp'), may hold values from -0.1875 to 0.1875
- output_kernel: float32 [9, 12, 64], P(None, None, 'fsdp'), may hold values from -0.25 to 0.25
- embed_matrix: float32 [128, 64], P('fsdp'), may hold values from -0.5 to 0.5
Outputs:
- denoised: float32 [2, 12, 128, 512], P('fsdp', None, 'rows')
- loss_value: float32 [], replicated
- input_grad: float32 [9, 64, 24], P(None, 'fsdp')
- first_grad: float32 [9, 64, 64], P(None, 'fsdp')
- second_grad: float32 [9, 64, 64], P(None, 'fsdp')
- down_grad: float32 [9, 128, 64], P(None, 'fsdp')
- coarse_grad: float32 [9, 128, 128], P(None, 'fsdp')
- upward_grad: float32 [9, 64, 128], P(None, 'fsdp')
- output_grad: float32 [9, 12, 64], P(None, None, 'fsdp')
- embed_grad: float32 [128, 64], P('fsdp')
The draws below stay inside these ranges and needn't reach their ends.
All inputs are finite; a program needn't handle non-finite values.
Results may differ from the reference program's by a relative error of at most 0.03.
Values may be sent and summed in bfloat16 or wider, within the bound.
No kernel may reach another device: no remote copies, remote signals or barrier semaphores. Data moves between devices by JAX's collectives and lax.ppermute only.
A program may use at most 128 MiB of HBM per device.

```python
import jax
import jax.numpy as jnp
from jax import lax

FIELDS = 12
COND = 12
CIN = 24
C0 = 64
C1 = 128
GROUPS = 32
EMB = 128
STEPS = 64
WID = 512
R0 = 8
HEIGHT = 128
SAMPLES = 2


def band_gains(key, channels):
    exponents = jax.random.uniform(key, (SAMPLES, channels, HEIGHT // R0, 1), jnp.float32, -1.5, 1.5)
    return jnp.repeat(jnp.exp(exponents), R0, axis=2)


def band_offsets(key, channels, reach):
    offsets = jax.random.uniform(key, (SAMPLES, channels, HEIGHT // R0, 1), jnp.float32, -reach, reach)
    return jnp.repeat(offsets, R0, axis=2)


def draw_residual_target(key, part):
    key = jax.random.fold_in(key, 11)
    cell_key, gain_key, offset_key = jax.random.split(key, 3)
    shape = (SAMPLES, FIELDS, HEIGHT, WID)
    along = jnp.arange(HEIGHT, dtype=jnp.float32) / (HEIGHT - 1)
    cells = jnp.clip(jax.random.normal(cell_key, shape, jnp.float32), -6.0, 6.0)
    rising = 1.0 + along
    offset = 0.8
    gains = band_gains(gain_key, FIELDS)
    shifts = band_offsets(offset_key, FIELDS, 3.0)
    values = offset + shifts + rising[None, None, :, None] * gains * cells
    return jnp.clip(values, -40.0, 40.0)


def draw_conditioning(key, part):
    key = jax.random.fold_in(key, 23)
    cell_key, gain_key = jax.random.split(key)
    shape = (SAMPLES, COND, HEIGHT, WID)
    cells = jnp.clip(jax.random.normal(cell_key, shape, jnp.float32), -6.0, 6.0)
    return jnp.clip(band_gains(gain_key, COND) * cells, -20.0, 20.0)


def draw_noise_sample(key, part):
    key = jax.random.fold_in(key, 37)
    cell_key, gain_key = jax.random.split(key)
    shape = (SAMPLES, FIELDS, HEIGHT, WID)
    cells = jnp.clip(jax.random.normal(cell_key, shape, jnp.float32), -6.0, 6.0)
    return jnp.clip(band_gains(gain_key, FIELDS) * cells, -20.0, 20.0)


def block_levels(rng, dims, shards, least, top_value):
    def one(axis_at, blocks):
        heights = jax.random.uniform(jax.random.fold_in(jax.random.fold_in(rng, 6), axis_at), (blocks,), jnp.float32, least / len(shards), top_value / len(shards))
        return jnp.repeat(jnp.exp(heights), dims[axis_at] // blocks).reshape((-1,) + (1,) * (len(dims) - axis_at - 1))

    loudness = one(*shards[0])
    for cut in shards[1:]:
        loudness = loudness * one(*cut)
    return loudness


def scatter_about(key, extent, width, most, pieces=(), held_as=jnp.bfloat16):
    loudness = block_levels(key, extent, pieces, -0.22, 0.18) if pieces else 1.0
    values = jax.random.normal(key, extent, jnp.float32) * width * loudness
    return jnp.minimum(jnp.maximum(values, -most), most).astype(held_as)


def setup_inputs(seed: int = 0) -> dict:
    key_list = jax.random.split(jax.random.key(seed), 13)
    return {
        "residual_target": draw_residual_target(jax.random.fold_in(key_list[12], 71), 0),
        "conditioning": draw_conditioning(jax.random.fold_in(key_list[12], 71), 0),
        "noise_sample": draw_noise_sample(jax.random.fold_in(key_list[12], 71), 0),
        "noise_level": jax.random.randint(key_list[3], (SAMPLES,), 0, STEPS).astype(jnp.int32),
        "input_kernel": scatter_about(key_list[4], (9, C0, CIN), (9 * CIN) ** -0.5, 0.4375, ((1, 2),), jnp.float32),
        "first_kernel": scatter_about(key_list[5], (9, C0, C0), (9 * C0) ** -0.5, 0.25, ((1, 2),), jnp.float32),
        "second_kernel": scatter_about(key_list[6], (9, C0, C0), (9 * C0) ** -0.5, 0.25, ((1, 2),), jnp.float32),
        "down_kernel": scatter_about(key_list[7], (9, C1, C0), (9 * C0) ** -0.5, 0.25, ((1, 2),), jnp.float32),
        "coarse_kernel": scatter_about(key_list[8], (9, C1, C1), (9 * C1) ** -0.5, 0.1875, ((1, 2),), jnp.float32),
        "upward_kernel": scatter_about(key_list[9], (9, C0, C1), (9 * C1) ** -0.5, 0.1875, ((1, 2),), jnp.float32),
        "output_kernel": scatter_about(key_list[10], (9, FIELDS, C0), (9 * C0) ** -0.5, 0.25, ((2, 2),), jnp.float32),
        "embed_matrix": scatter_about(key_list[11], (EMB, C0), EMB ** -0.5, 0.5, ((0, 2),), jnp.float32),
    }


sigma_low = 0.002
sigma_high = 80.0
sigma_data = 0.5
rho_power = 7.0
eps_norm = 1e-05

def preconditions(level_index):
    ramp_value = level_index.astype(jnp.float32) / (STEPS - 1)
    top_root = sigma_high ** (1.0 / rho_power)
    bottom = sigma_low ** (1.0 / rho_power)
    sigma_level = (top_root + ramp_value * (bottom - top_root)) ** rho_power
    sigma_total = sigma_level * sigma_level + sigma_data * sigma_data
    skip_scale = sigma_data * sigma_data / sigma_total
    out_scale = sigma_level * sigma_data * lax.rsqrt(sigma_total)
    in_scale = lax.rsqrt(sigma_total)
    weight = sigma_total / (sigma_level * sigma_data) ** 2
    return (sigma_level, skip_scale, out_scale, in_scale, weight)

def embedding(sigma_level, features):
    half_count = features // 2
    ramp_steps = jnp.arange(half_count, dtype=jnp.float32) / half_count
    frequency = 64.0 * 0.01 ** ramp_steps
    phase_angle = 0.25 * jnp.log(sigma_level) * frequency
    return jnp.concatenate([jnp.cos(phase_angle), jnp.sin(phase_angle)]).astype(jnp.bfloat16)

def tap_products(padded, kernels, height, breadth):
    summed = jnp.zeros((kernels.shape[1], height, breadth), jnp.float32)
    for position in range(9):
        row_shift = position // 3
        col_shift = position % 3
        window = padded[:, row_shift:row_shift + height, col_shift:col_shift + breadth].astype(jnp.float32)
        summed = summed + jnp.einsum('oc,chw->ohw', kernels[position].astype(jnp.float32), window)
    return summed

def kernel_grad(padded, upstream):
    height, breadth = (upstream.shape[1], upstream.shape[2])
    upper = upstream.astype(jnp.float32)
    parts = []
    for position in range(9):
        row_shift = position // 3
        col_shift = position % 3
        window = padded[:, row_shift:row_shift + height, col_shift:col_shift + breadth].astype(jnp.float32)
        parts.append(jnp.einsum('ohw,chw->oc', upper, window))
    return jnp.stack(parts)

def convolve(source, kernels):
    padded = jnp.pad(source, ((0, 0), (1, 1), (1, 1)))
    return (tap_products(padded, kernels, source.shape[1], source.shape[2]), padded)

def transposed(kernels):
    return jnp.transpose(kernels[::-1], (0, 2, 1))

def norm_forward(values, groups):
    channels, height, breadth = values.shape
    grouped = values.reshape(groups, channels // groups, height, breadth)
    members = channels // groups * height * breadth
    group_mean = lax.optimization_barrier(jnp.sum(grouped, axis=(1, 2, 3))) / members
    squares = lax.optimization_barrier(jnp.sum(grouped * grouped, axis=(1, 2, 3))) / members
    inverse = lax.rsqrt(squares - group_mean * group_mean + eps_norm)
    normed = (grouped - group_mean[:, None, None, None]) * inverse[:, None, None, None]
    return (normed.reshape(values.shape), inverse)

def activate(normed):
    return jax.nn.silu(normed).astype(jnp.bfloat16)

def norm_backward(upstream, normed, inverse, groups):
    channels, height, breadth = normed.shape
    sigmoid = jax.nn.sigmoid(normed)
    grad_hat = (upstream * sigmoid * (1.0 + normed * (1.0 - sigmoid))).reshape(groups, channels // groups, height, breadth)
    hat_grouped = normed.reshape(groups, channels // groups, height, breadth)
    members = channels // groups * height * breadth
    grad_mean = lax.optimization_barrier(jnp.sum(grad_hat, axis=(1, 2, 3))) / members
    cross_mean = lax.optimization_barrier(jnp.sum(grad_hat * hat_grouped, axis=(1, 2, 3))) / members
    result = inverse[:, None, None, None] * (grad_hat - grad_mean[:, None, None, None] - hat_grouped * cross_mean[:, None, None, None])
    return result.reshape(normed.shape)

def pool_down(values):
    channels, height, breadth = values.shape
    return 0.25 * values.reshape(channels, height // 2, 2, breadth // 2, 2).sum(axis=(2, 4))

def lift_up(values):
    return jnp.repeat(jnp.repeat(values, 2, axis=1), 2, axis=2)

def lift_back(values):
    channels, height, breadth = values.shape
    return values.reshape(channels, height // 2, 2, breadth // 2, 2).sum(axis=(2, 4))

def reference(residual_target, conditioning, noise_sample, noise_level, input_kernel, first_kernel, second_kernel, down_kernel, coarse_kernel, upward_kernel, output_kernel, embed_matrix):
    input_taps = input_kernel.astype(jnp.bfloat16)
    first_taps = first_kernel.astype(jnp.bfloat16)
    second_taps = second_kernel.astype(jnp.bfloat16)
    down_taps = down_kernel.astype(jnp.bfloat16)
    coarse_taps = coarse_kernel.astype(jnp.bfloat16)
    upward_taps = upward_kernel.astype(jnp.bfloat16)
    output_taps = output_kernel.astype(jnp.bfloat16)
    embed_taps = embed_matrix.astype(jnp.bfloat16)
    members_all = residual_target.shape[0] * residual_target.shape[1] * residual_target.shape[2] * residual_target.shape[3]

    def one_patch(operands):
        target, condition, noise_cells, level_index = operands
        sigma_level, skip_scale, out_scale, in_scale, weight = preconditions(level_index)
        noisy = target + sigma_level * noise_cells
        stacked = jnp.concatenate([in_scale * noisy, condition], axis=0).astype(jnp.bfloat16)
        embedded = embedding(sigma_level, embed_taps.shape[0])
        level_shift = jnp.dot(embedded[None, :], embed_taps, preferred_element_type=jnp.float32)[0]
        act_a, pad_input = convolve(stacked, input_taps)
        hat_a, inv_a = norm_forward(act_a, GROUPS)
        raw_b, pad_first = convolve(activate(hat_a), first_taps)
        act_b = raw_b + level_shift[:, None, None]
        hat_b, inv_b = norm_forward(act_b, GROUPS)
        branch, pad_second = convolve(activate(hat_b), second_taps)
        fine_sum = act_a + branch
        pooled = pool_down(fine_sum).astype(jnp.bfloat16)
        act_c, pad_down = convolve(pooled, down_taps)
        hat_c, inv_c = norm_forward(act_c, GROUPS)
        coarse_branch, pad_coarse = convolve(activate(hat_c), coarse_taps)
        coarse = act_c + coarse_branch
        lifted = lift_up(coarse).astype(jnp.bfloat16)
        merged_raw, pad_upward = convolve(lifted, upward_taps)
        merged = merged_raw + fine_sum
        hat_d, inv_d = norm_forward(merged, GROUPS)
        fields, pad_output = convolve(activate(hat_d), output_taps)
        denoised = skip_scale * noisy + out_scale * fields
        mismatch = denoised - target
        loss_part = jnp.sum(weight * mismatch * mismatch)
        grad_fields = (2.0 * weight * out_scale / members_all * mismatch).astype(jnp.bfloat16)
        output_grad = kernel_grad(pad_output, grad_fields)
        back_d, unused = convolve(grad_fields, transposed(output_taps))
        grad_merged = norm_backward(back_d, hat_d, inv_d, GROUPS)
        merged_low = grad_merged.astype(jnp.bfloat16)
        upward_grad = kernel_grad(pad_upward, merged_low)
        back_lift, unused = convolve(merged_low, transposed(upward_taps))
        grad_coarse = lift_back(back_lift)
        coarse_low = grad_coarse.astype(jnp.bfloat16)
        coarse_grad = kernel_grad(pad_coarse, coarse_low)
        back_c, unused = convolve(coarse_low, transposed(coarse_taps))
        grad_act_c = grad_coarse + norm_backward(back_c, hat_c, inv_c, GROUPS)
        act_c_low = grad_act_c.astype(jnp.bfloat16)
        down_grad = kernel_grad(pad_down, act_c_low)
        back_pool, unused = convolve(act_c_low, transposed(down_taps))
        grad_fine = grad_merged + 0.25 * lift_up(back_pool)
        fine_low = grad_fine.astype(jnp.bfloat16)
        second_grad = kernel_grad(pad_second, fine_low)
        back_b, unused = convolve(fine_low, transposed(second_taps))
        grad_act_b = norm_backward(back_b, hat_b, inv_b, GROUPS)
        act_b_low = grad_act_b.astype(jnp.bfloat16)
        first_grad = kernel_grad(pad_first, act_b_low)
        embed_grad = embedded.astype(jnp.float32)[:, None] * lax.optimization_barrier(jnp.sum(grad_act_b, axis=(1, 2)))[None, :]
        back_a, unused = convolve(act_b_low, transposed(first_taps))
        grad_act_a = grad_fine + norm_backward(back_a, hat_a, inv_a, GROUPS)
        input_grad = kernel_grad(pad_input, grad_act_a.astype(jnp.bfloat16))
        return (denoised, loss_part, (input_grad, first_grad, second_grad, down_grad, coarse_grad, upward_grad, output_grad, embed_grad))
    denoised, loss_parts, gradients = lax.map(one_patch, (residual_target, conditioning, noise_sample, noise_level))
    loss_value = jnp.sum(loss_parts) / members_all
    summed = [lax.optimization_barrier(jnp.sum(item, axis=0)) for item in gradients]
    return (denoised, loss_value, summed[0], summed[1], summed[2], summed[3], summed[4], summed[5], summed[6], summed[7])
```

```python
import functools

import jax
import jax.numpy as jnp
from jax import lax
from jax.experimental import pallas as pl
from jax.experimental.pallas import tpu as pltpu
from jax.sharding import PartitionSpec as P

GROUPS = 32
STEPS = 64

sigma_low = 0.002
sigma_high = 80.0
sigma_data = 0.5
rho_power = 7.0
eps_norm = 1e-05

F32 = jnp.float32
BF16 = jnp.bfloat16

HALF = 256
ROWS = 8
CROWS = 4
FAR = 7


def preconditions(level_index):
    ramp_value = level_index.astype(jnp.float32) / (STEPS - 1)
    top_root = sigma_high ** (1.0 / rho_power)
    bottom = sigma_low ** (1.0 / rho_power)
    sigma_level = (top_root + ramp_value * (bottom - top_root)) ** rho_power
    sigma_total = sigma_level * sigma_level + sigma_data * sigma_data
    skip_scale = sigma_data * sigma_data / sigma_total
    out_scale = sigma_level * sigma_data * lax.rsqrt(sigma_total)
    in_scale = lax.rsqrt(sigma_total)
    weight = sigma_total / (sigma_level * sigma_data) ** 2
    return (sigma_level, skip_scale, out_scale, in_scale, weight)


def embedding(sigma_level, features):
    half_count = features // 2
    ramp_steps = jnp.arange(half_count, dtype=jnp.float32) / half_count
    frequency = 64.0 * 0.01**ramp_steps
    phase_angle = 0.25 * jnp.log(sigma_level) * frequency
    return jnp.concatenate([jnp.cos(phase_angle), jnp.sin(phase_angle)]).astype(jnp.bfloat16)


def row(ref, index):
    return ref[:, index * HALF : (index + 1) * HALF]


def put(ref, index, value):
    ref[:, index * HALF : (index + 1) * HALF] = value


def lane(shape):
    return lax.broadcasted_iota(jnp.int32, shape, 1)


def from_left(value):
    moved = pltpu.roll(value, 1, 1)
    return jnp.where(lane(value.shape) == 0, 0.0, moved)


def from_right(value):
    moved = pltpu.roll(value, value.shape[1] - 1, 1)
    return jnp.where(lane(value.shape) == value.shape[1] - 1, 0.0, moved)


def mm(left, right):
    return jnp.dot(left, right, preferred_element_type=F32)


def mm_nt(left, right):
    return lax.dot_general(left, right, (((1,), (1,)), ((), ())), preferred_element_type=F32)


def fine_taps(value):
    half = value.shape[0] // 2
    even, odd = value[:half], value[half:]
    return jnp.concatenate([from_left(odd), value, from_right(even)], axis=0).astype(BF16)


def coarse_taps(value):
    return jnp.concatenate([from_left(value), value, from_right(value)], axis=0).astype(BF16)


def fine_untap(taps):
    size = taps.shape[0] // 4
    even = taps[size : 2 * size] + from_left(taps[3 * size :])
    odd = taps[2 * size : 3 * size] + from_right(taps[:size])
    return jnp.concatenate([even, odd], axis=0)


def coarse_untap(taps):
    size = taps.shape[0] // 3
    return taps[size : 2 * size] + from_right(taps[:size]) + from_left(taps[2 * size :])


def spread(parts, first, last):
    out = {}
    for i in range(first, last + 1):
        size = parts[i - 1].shape[0] // 3
        out[i] = parts[i - 1][:size] + parts[i][size : 2 * size] + parts[i + 1][2 * size :]
    return out


def stack_rows(g, r):
    return jnp.concatenate([g[r + 1], g[r], g[r - 1]], axis=0)


def same_group(size, fine):
    left = lax.broadcasted_iota(jnp.int32, (size, size), 0)
    right = lax.broadcasted_iota(jnp.int32, (size, size), 1)
    if fine:
        half = size // 2
        left, right = left % half, right % half
        per = half // GROUPS
    else:
        per = size // GROUPS
    return left // per == right // per


def group_sums(stats_ref, fine):
    total = stats_ref[0]
    for index in range(1, stats_ref.shape[0]):
        total = total + stats_ref[index]
    member = same_group(128, fine)
    first = jnp.sum(jnp.where(member, total[0:1, :], 0.0), axis=1, keepdims=True)
    second = jnp.sum(jnp.where(member, total[1:2, :], 0.0), axis=1, keepdims=True)
    return first, second


def norm_columns(stats_ref, fine, members):
    first, second = group_sums(stats_ref, fine)
    mean = first / members
    inverse = lax.rsqrt(second / members - mean * mean + eps_norm)
    return mean, inverse


def back_columns(stats_ref, fine, members):
    first, second = group_sums(stats_ref, fine)
    return first / members, second / members


def to_row(column):
    size = column.shape[0]
    diagonal = lax.broadcasted_iota(jnp.int32, (size, size), 0) == lax.broadcasted_iota(
        jnp.int32, (size, size), 1
    )
    return jnp.sum(jnp.where(diagonal, column, 0.0), axis=0, keepdims=True)


def put_stats(ref, first, second):
    first = to_row(jnp.sum(first, axis=1, keepdims=True))
    second = to_row(jnp.sum(second, axis=1, keepdims=True))
    ref[...] = jnp.concatenate([first, second, jnp.zeros((6, 128), F32)], axis=0)


def silu(h):
    return h * (1.0 / (1.0 + jnp.exp(-h)))


def silu_slope(h):
    s = 1.0 / (1.0 + jnp.exp(-h))
    return s * (1.0 + h * (1.0 - s))


def masked(value, index, rows, scal):
    if index < 0:
        return value * scal[6]
    if index >= rows:
        return value * scal[7]
    return value


def pick(scal, when_odd, when_even):
    return jnp.where(scal[8] > 0.5, when_odd, when_even)


def spill(ref, value):
    for t in range(4):
        ref[t, : value.shape[0], :] = value[:, 128 * t : 128 * (t + 1)]


def strided(ref, index, size):
    return jnp.concatenate(
        [ref[t, pl.ds(index, size, stride=ROWS), :] for t in range(4)], axis=1
    )


def interleave(transposed):
    left = lax.broadcasted_iota(jnp.int32, (512, 512), 0)
    right = lax.broadcasted_iota(jnp.int32, (512, 512), 1)
    if transposed:
        left, right = right, left
    place = (left & 1) * HALF + (left >> 1)
    return jnp.where(place == right, 1.0, 0.0).astype(BF16)


def fine_grad(blocks, outs, ins):
    parts = []
    for a in range(3):
        even = blocks[(2 * a) * outs : (2 * a + 1) * outs]
        odd = blocks[(2 * a + 1) * outs : (2 * a + 2) * outs]
        parts.append(even[:, : 3 * ins] + odd[:, ins : 4 * ins])
    return jnp.concatenate(parts, axis=0).astype(BF16)


def place(width, target, offset):
    left = lax.broadcasted_iota(jnp.int32, (width, target), 0)
    right = lax.broadcasted_iota(jnp.int32, (width, target), 1)
    return jnp.where(left + offset == right, 1.0, 0.0).astype(BF16)


def flipped(value):
    size = value.shape[1]
    return mm_nt(place(size, size, 0), value).astype(BF16)


def fine_matrix(ref, outs, ins, slot):
    rows = []
    for a in range(3):
        total = None
        for b in range(3):
            tap = ref[(3 * a + b) * outs : (3 * a + b + 1) * outs, :ins]
            spot = jnp.concatenate(
                [place(ins, 4 * slot, b * slot), place(ins, 4 * slot, (b + 1) * slot)], axis=1
            )
            term = mm(tap, spot)
            total = term if total is None else total + term
        rows += [total[:, : 4 * slot], total[:, 4 * slot :]]
    return jnp.concatenate(rows, axis=0).astype(BF16)


def prepare_first(in_ref, first_ref, emb_ref, vec_ref, win, wfirst, wfirst_t, shift):
    win[...] = fine_matrix(in_ref, 64, 24, 32)
    first = fine_matrix(first_ref, 64, 64, 64)
    wfirst[...] = first
    wfirst_t[...] = flipped(first)
    line = mm(vec_ref[...], emb_ref[...])[0:1, :]
    both = jnp.concatenate([line, line], axis=1)
    diagonal = place(128, 128, 0).astype(F32)
    shift[...] = jnp.broadcast_to(
        jnp.sum(diagonal * both, axis=1, keepdims=True), (128, 128)
    )


def prepare_rest(
    second_ref, down_ref, coarse_ref, up_ref, out_ref,
    wsecond, wsecond_t, wdown, wdown_t, wcoarse, wcoarse_t, wup, wup_t, wout, wout_t,
):
    second = fine_matrix(second_ref, 64, 64, 64)
    wsecond[...] = second
    wsecond_t[...] = flipped(second)
    rows = []
    for a in range(3):
        total = None
        for b in range(3):
            tap = down_ref[(3 * a + b) * 128 : (3 * a + b + 1) * 128, :]
            term = mm(tap, place(64, 256, 64 * b))
            total = term if total is None else total + term
        rows.append(total)
    down = jnp.concatenate(rows, axis=0)[:, :192].astype(BF16)
    wdown[...] = down
    wdown_t[...] = flipped(down)
    rows = []
    for a in range(3):
        rows.append(
            jnp.concatenate(
                [coarse_ref[(3 * a + b) * 128 : (3 * a + b + 1) * 128, :] for b in range(3)], axis=1
            )
        )
    coarse = jnp.concatenate(rows, axis=0)
    wcoarse[...] = coarse
    wcoarse_t[...] = flipped(coarse)
    rows = []
    blank = jnp.zeros((64, 128), BF16)
    for a in range(3):
        taps = [up_ref[(3 * a + b) * 64 : (3 * a + b + 1) * 64, :] for b in range(3)]
        rows.append(jnp.concatenate(taps + [blank], axis=1))
        rows.append(jnp.concatenate([blank] + taps, axis=1))
    up = jnp.concatenate(rows, axis=0)
    wup[...] = up
    wup_t[...] = flipped(up)
    out = fine_matrix(out_ref, 16, 64, 64)
    wout[...] = out
    wout_t[...] = flipped(out)


def enter(scal, target, condition, noise, own, edge_a, edge_b, line_a, line_b, scratch):
    sigma, skip, in_scale = scal[0], scal[1], scal[3]
    noisy = target[...] + sigma * noise[...]
    q = skip * noisy - target[...]
    natural = jnp.concatenate([in_scale * noisy, condition[...]], axis=0).astype(BF16)
    spill(scratch, mm(natural, interleave(False)))
    blank = jnp.zeros((8, 512), F32)
    for i in range(ROWS):
        value = strided(scratch, i, 24)
        own[:, i * 512 : (i + 1) * 512] = jnp.concatenate([value, blank], axis=0).astype(BF16)
    top, low = own[:, : FAR * 512], own[:, (ROWS - FAR) * 512 :]
    edge_a[...] = pick(scal, top, low)
    edge_b[...] = pick(scal, low, top)
    spill(scratch, q)
    blank = jnp.zeros((4, 512), F32)
    top = jnp.concatenate([strided(scratch, 0, 12), blank], axis=0)
    low = jnp.concatenate([strided(scratch, ROWS - 1, 12), blank], axis=0)
    line_a[...] = pick(scal, top, low)
    line_b[...] = pick(scal, low, top)


def stage_a(scal, own, got_a, got_b, win, act, stats, kept, above, below):
    above[...] = pick(scal, got_a[...], got_b[...])
    below[...] = pick(scal, got_b[...], got_a[...])
    parts = {}
    total = jnp.zeros((128, HALF), F32)
    square = jnp.zeros((128, HALF), F32)
    for r in range(-FAR, ROWS + FAR):
        if r < 0:
            value = above[:, (r + FAR) * 512 : (r + FAR + 1) * 512]
        elif r < ROWS:
            value = own[:, r * 512 : (r + 1) * 512]
        else:
            value = below[:, (r - ROWS) * 512 : (r - ROWS + 1) * 512]
        value = value.astype(F32)
        z = fine_taps(jnp.concatenate([value[:, :HALF], value[:, HALF:]], axis=0))
        if -1 <= r <= ROWS:
            put(kept, r + 1, z)
        parts[r] = mm(win[...], z)
        i = r - 1
        if i > -FAR:
            value = spread(parts, i, i)[i]
            put(act, i + FAR - 1, value)
            del parts[i - 1]
            if 0 <= i < ROWS:
                total = total + value
                square = square + value * value
    put_stats(stats, total, square)


def stage_b(members, scal, act_a, stats_a, wfirst, shift, act_b, stats, kept):
    mean, inverse = norm_columns(stats_a, True, members)
    lift = shift[:, 0:1]
    parts = {}
    total = jnp.zeros((128, HALF), F32)
    square = jnp.zeros((128, HALF), F32)
    for r in range(-6, ROWS + 6):
        value = silu((row(act_a, r + 6) - mean) * inverse)
        z = fine_taps(masked(value, r, ROWS, scal))
        if 0 <= r < ROWS:
            put(kept, r, z)
        parts[r] = mm(wfirst[...], z)
        i = r - 1
        if i > -6:
            value = spread(parts, i, i)[i] + lift
            put(act_b, i + 5, value)
            del parts[i - 1]
            if 0 <= i < ROWS:
                total = total + value
                square = square + value * value
    put_stats(stats, total, square)


def stage_c(
    members, scal, act_a, act_b, stats_b, wsecond, wdown,
    fine, act_c, edge, stats, kept, kept_pool,
):
    mean, inverse = norm_columns(stats_b, True, members)
    parts = {}
    pooled = {}
    half = {}
    for r in range(-5, ROWS + 5):
        value = silu((row(act_b, r + 5) - mean) * inverse)
        z = fine_taps(masked(value, r, ROWS, scal))
        if 0 <= r < ROWS:
            put(kept, r, z)
        parts[r] = mm(wsecond[...], z)
        i = r - 1
        if i > -5:
            value = spread(parts, i, i)[i] + row(act_a, i + 6)
            put(fine, i + 4, value)
            del parts[i - 1]
            half[i] = value[:64] + value[64:]
            if i % 2:
                value = 0.25 * (half.pop(i - 1) + half.pop(i))
                value = masked(value, i // 2, CROWS, scal)
                pooled[i // 2] = value.astype(BF16).astype(F32)
    parts = {}
    total = jnp.zeros((128, HALF), F32)
    square = jnp.zeros((128, HALF), F32)
    for r in range(-2, CROWS + 2):
        z = coarse_taps(pooled[r])
        if 0 <= r < CROWS:
            put(kept_pool, r, z)
        parts[r] = mm(wdown[...], z)
        i = r - 1
        if i > -2:
            value = spread(parts, i, i)[i]
            put(act_c, i + 1, value)
            del parts[i - 1]
            if 0 <= i < CROWS:
                total = total + value
                square = square + value * value
            if i in (1, 2):
                put(edge, i - 1, value)
    put_stats(stats, total, square)


def stage_d(
    members, scal, act_c, got_a, got_b, stats_c, wcoarse, wup, fine,
    merged, wide_c, stats, kept_c, kept_up, ring,
):
    mean, inverse = norm_columns(stats_c, False, members)
    for j in range(2):
        put(ring, j, pick(scal, row(got_a, j), row(got_b, j)))
        put(ring, CROWS + 4 + j, pick(scal, row(got_b, j), row(got_a, j)))
    for j in range(CROWS + 2):
        put(ring, j + 2, row(act_c, j))
    parts = {}
    lifted = {}
    for r in range(-3, CROWS + 3):
        value = silu((row(ring, r + 3) - mean) * inverse)
        z = coarse_taps(masked(value, r, CROWS, scal))
        if 0 <= r < CROWS:
            put(kept_c, r, z)
        parts[r] = mm(wcoarse[...], z)
        i = r - 1
        if i > -3:
            value = spread(parts, i, i)[i] + row(ring, i + 3)
            put(wide_c, i + 2, row(ring, i + 3))
            del parts[i - 1]
            lifted[i] = masked(value, i, CROWS, scal).astype(BF16).astype(F32)
    parts = {}
    total = jnp.zeros((128, HALF), F32)
    square = jnp.zeros((128, HALF), F32)
    for r in range(-2, CROWS + 2):
        z = coarse_taps(lifted[r])
        if 0 <= r < CROWS:
            put(kept_up, r, z)
        four = jnp.concatenate([z[:128], z[128:256], z[128:256], z[256:]], axis=0)
        parts[2 * r] = parts[2 * r + 1] = mm(wup[...], four)
        for i in (2 * r - 1, 2 * r):
            if i >= -3:
                value = spread(parts, i, i)[i] + row(fine, i + 4)
                put(merged, i + 3, value)
                parts.pop(i - 1)
                if 0 <= i < ROWS:
                    total = total + value
                    square = square + value * value
    put_stats(stats, total, square)


def stage_out(
    members, scal, merged, stats_d, wout, wout_t, target, noise, line_a, line_b,
    denoised, loss, back, edge_a, edge_b, stats, grad, pairs, cells, gs, zs,
    goals, noisies, found,
):
    sigma, skip, out_scale, weight, coef = scal[0], scal[1], scal[2], scal[4], scal[5]
    mean, inverse = norm_columns(stats_d, True, members)
    parts = {}
    for r in range(-2, ROWS + 2):
        value = silu((row(merged, r + 3) - mean) * inverse)
        z = fine_taps(masked(value, r, ROWS, scal))
        if 0 <= r < ROWS:
            put(zs, r, z)
        parts[r] = mm(wout[...], z)
        i = r - 1
        if i > -2:
            value = spread(parts, i, i)[i]
            del parts[i - 1]
            pairs[16 * (i + 1) : 16 * (i + 2), :] = jnp.concatenate(
                [value[:16], value[16:]], axis=1
            )
    value = pairs[...]
    high = value.astype(BF16)
    low = (value - high.astype(F32)).astype(BF16)
    back_order = interleave(True)
    pairs[...] = mm(high, back_order) + mm(low, back_order)
    blank = jnp.zeros((4, 512), F32)
    loss_sum = jnp.zeros((12, 512), F32)
    top = pick(scal, line_a[...], line_b[...]) + out_scale * pairs[0:16, :]
    cells[0:16, :] = coef * scal[6] * top
    low = pick(scal, line_b[...], line_a[...]) + out_scale * pairs[16 * (ROWS + 1) :, :]
    cells[16 * (ROWS + 1) :, :] = coef * scal[7] * low
    spill(goals, target[...])
    spill(noisies, target[...] + sigma * noise[...])
    for i in range(ROWS):
        goal = strided(goals, i, 12)
        noisy = strided(noisies, i, 12)
        estimate = skip * noisy + out_scale * pairs[16 * (i + 1) : 16 * (i + 1) + 12, :]
        for t in range(4):
            found[t, pl.ds(i, 12, stride=ROWS), :] = estimate[:, 128 * t : 128 * (t + 1)]
        mismatch = estimate - goal
        loss_sum = loss_sum + weight * mismatch * mismatch
        cells[16 * (i + 1) : 16 * (i + 2), :] = jnp.concatenate([coef * mismatch, blank], axis=0)
    denoised[...] = jnp.concatenate([found[t] for t in range(4)], axis=1)
    loss[...] = jnp.broadcast_to(
        jnp.sum(jnp.sum(loss_sum, axis=1, keepdims=True), axis=0, keepdims=True), (8, 128)
    )
    pairs[...] = mm(cells[...].astype(BF16), interleave(False))
    g = {}
    for i in range(-1, ROWS + 1):
        value = pairs[16 * (i + 1) : 16 * (i + 2), :]
        g[i] = jnp.concatenate([value[:, :HALF], value[:, HALF:]], axis=0).astype(BF16)
    total = jnp.zeros((128, HALF), F32)
    cross = jnp.zeros((128, HALF), F32)
    for r in range(ROWS):
        rows = stack_rows(g, r)
        put(gs, r, rows)
        value = fine_untap(mm(wout_t[...], rows))
        put(back, r, value)
        hat = (row(merged, r + 3) - mean) * inverse
        e = value * silu_slope(hat)
        total = total + e
        cross = cross + e * hat
    put_stats(stats, total, cross)
    top, low = back[:, : 3 * HALF].astype(BF16), back[:, (ROWS - 3) * HALF :].astype(BF16)
    edge_a[...] = pick(scal, top, low)
    edge_b[...] = pick(scal, low, top)
    grad[...] = fine_grad(mm_nt(gs[...], zs[...]), 16, 64)


def stage_up(
    members, members_c, scal, merged, stats_d, stats_ed, back, got_a, got_b, kept_up, wup_t,
    act_c, stats_c, kept_c, wcoarse_t,
    grad_merged, back_c, grad_coarse, edge_a, edge_b, stats, grad_up, grad_c, gs, zs, gc,
):
    mean, inverse = norm_columns(stats_d, True, members)
    shift, slope = back_columns(stats_ed, True, members)
    g = {}
    for r in range(-3, ROWS + 3):
        hat = (row(merged, r + 3) - mean) * inverse
        if r < 0:
            u = pick(scal, row(got_a, r + 3), row(got_b, r + 3)).astype(F32)
        elif r < ROWS:
            u = row(back, r)
        else:
            u = pick(scal, row(got_b, r - ROWS), row(got_a, r - ROWS)).astype(F32)
        value = inverse * (u * silu_slope(hat) - shift - hat * slope)
        value = masked(value, r, ROWS, scal)
        if -2 <= r < ROWS + 2:
            put(grad_merged, r + 2, value)
        g[r] = value.astype(BF16)
    gk = {}
    half = {}
    for r in range(-2, ROWS + 2):
        rows = stack_rows(g, r)
        if 0 <= r < ROWS:
            put(gs, r, rows)
            put(zs, r, row(kept_up, r // 2))
        taps = mm(wup_t[...], rows)
        half[r] = taps[128:256] + taps[256:384] + from_right(taps[:128]) + from_left(taps[384:])
        if r % 2:
            value = masked(half.pop(r - 1) + half.pop(r), r // 2, CROWS, scal)
            put(grad_coarse, r // 2 + 1, value)
            gk[r // 2] = value.astype(BF16)
    blocks = mm_nt(gs[...], zs[...])
    parts = []
    for a in range(3):
        even = blocks[128 * a : 128 * a + 64]
        odd = blocks[128 * a + 64 : 128 * a + 128]
        parts.append(
            jnp.concatenate(
                [
                    even[:, :128] + odd[:, 128:256],
                    even[:, 128:256] + odd[:, 128:256],
                    even[:, 128:256] + odd[:, 256:],
                ],
                axis=1,
            )
        )
    grad_up[...] = jnp.concatenate(parts, axis=0).astype(BF16)
    mean, inverse = norm_columns(stats_c, False, members_c)
    total = jnp.zeros((128, HALF), F32)
    cross = jnp.zeros((128, HALF), F32)
    for r in range(CROWS):
        rows = stack_rows(gk, r)
        put(gc, r, rows)
        value = coarse_untap(mm(wcoarse_t[...], rows))
        put(back_c, r, value)
        hat = (row(act_c, r + 2) - mean) * inverse
        e = value * silu_slope(hat)
        total = total + e
        cross = cross + e * hat
    put_stats(stats, total, cross)
    grad_c[...] = mm_nt(gc[...], kept_c[...]).astype(BF16)
    top = [row(back_c, 0).astype(BF16), row(back_c, 1).astype(BF16), gk[1]]
    low = [row(back_c, 2).astype(BF16), row(back_c, 3).astype(BF16), gk[2]]
    for j in range(3):
        put(edge_a, j, pick(scal, top[j], low[j]))
        put(edge_b, j, pick(scal, low[j], top[j]))


def stage_down(
    members, members_c, scal, stats_c, stats_ec, act_c, back_c, grad_coarse, got_a, got_b,
    wdown_t, kept_pool, grad_merged, act_b, stats_b, kept_b, wsecond_t,
    grad_fine, back_b, stats, grad_down, grad_second, gs, gc,
):
    mean, inverse = norm_columns(stats_c, False, members_c)
    shift, slope = back_columns(stats_ec, False, members_c)
    g = {}
    for r in range(-2, CROWS + 2):
        hat = (row(act_c, r + 2) - mean) * inverse
        if r < 0:
            u = pick(scal, row(got_a, r + 2), row(got_b, r + 2)).astype(F32)
        elif r < CROWS:
            u = row(back_c, r)
        else:
            u = pick(scal, row(got_b, r - CROWS), row(got_a, r - CROWS)).astype(F32)
        if r == -2:
            through = pick(scal, row(got_a, 2), row(got_b, 2)).astype(F32)
        elif r == CROWS + 1:
            through = pick(scal, row(got_b, 2), row(got_a, 2)).astype(F32)
        else:
            through = row(grad_coarse, r + 1)
        value = through + inverse * (u * silu_slope(hat) - shift - hat * slope)
        g[r] = masked(value, r, CROWS, scal).astype(BF16)
    fine = {}
    for r in range(-1, CROWS + 1):
        rows = stack_rows(g, r)
        if 0 <= r < CROWS:
            put(gc, r, rows)
        value = 0.25 * coarse_untap(mm(wdown_t[...], rows))
        both = jnp.concatenate([value, value], axis=0)
        for i in (2 * r, 2 * r + 1):
            value = masked(row(grad_merged, i + 2) + both, i, ROWS, scal)
            if 0 <= i < ROWS:
                put(grad_fine, i, value)
            fine[i] = value.astype(BF16)
    grad_down[...] = mm_nt(gc[...], kept_pool[...]).astype(BF16)
    mean, inverse = norm_columns(stats_b, True, members)
    total = jnp.zeros((128, HALF), F32)
    cross = jnp.zeros((128, HALF), F32)
    for r in range(-1, ROWS + 1):
        rows = stack_rows(fine, r)
        value = fine_untap(mm(wsecond_t[...], rows))
        put(back_b, r + 1, value)
        if 0 <= r < ROWS:
            put(gs, r, rows)
            hat = (row(act_b, r + 5) - mean) * inverse
            e = value * silu_slope(hat)
            total = total + e
            cross = cross + e * hat
    put_stats(stats, total, cross)
    grad_second[...] = fine_grad(mm_nt(gs[...], kept_b[...]), 64, 64)


def stage_first(
    members, scal, stats_b, stats_eb, act_b, back_b, wfirst_t, act_a, stats_a, kept_a,
    back_a, stats, grad_first, cell_sums, gs,
):
    mean, inverse = norm_columns(stats_b, True, members)
    shift, slope = back_columns(stats_eb, True, members)
    g = {}
    sums = jnp.zeros((128, HALF), F32)
    for r in range(-1, ROWS + 1):
        hat = (row(act_b, r + 5) - mean) * inverse
        value = inverse * (row(back_b, r + 1) * silu_slope(hat) - shift - hat * slope)
        if 0 <= r < ROWS:
            sums = sums + value
        g[r] = masked(value, r, ROWS, scal).astype(BF16)
    line = to_row(jnp.sum(sums, axis=1, keepdims=True))
    cell_sums[...] = jnp.broadcast_to(line, (8, 128))
    mean, inverse = norm_columns(stats_a, True, members)
    total = jnp.zeros((128, HALF), F32)
    cross = jnp.zeros((128, HALF), F32)
    for r in range(ROWS):
        rows = stack_rows(g, r)
        put(gs, r, rows)
        value = fine_untap(mm(wfirst_t[...], rows))
        put(back_a, r, value)
        hat = (row(act_a, r + 6) - mean) * inverse
        e = value * silu_slope(hat)
        total = total + e
        cross = cross + e * hat
    put_stats(stats, total, cross)
    grad_first[...] = fine_grad(mm_nt(gs[...], kept_a[...]), 64, 64)


def stage_last(members, stats_a, stats_ea, act_a, back_a, grad_fine, kept_in, grad_in, gs):
    mean, inverse = norm_columns(stats_a, True, members)
    shift, slope = back_columns(stats_ea, True, members)
    for r in range(ROWS):
        hat = (row(act_a, r + 6) - mean) * inverse
        value = row(grad_fine, r) + inverse * (
            row(back_a, r) * silu_slope(hat) - shift - hat * slope
        )
        put(gs, r, value.astype(BF16))
    parts = []
    for a in range(3):
        blocks = mm_nt(gs[...], kept_in[:, a * HALF : (a + ROWS) * HALF])
        parts.append(blocks[:64, :96] + blocks[64:, 32:128])
    grad_in[...] = jnp.concatenate(parts, axis=0).astype(BF16)


def shape(rows, lanes, dtype=F32):
    return jax.ShapeDtypeStruct((rows, lanes), dtype)


def run(name, kernel, outs, scal, *operands, scratch=()):
    vmem = pl.BlockSpec(memory_space=pltpu.VMEM)
    specs = [vmem] * len(operands)
    if scal is not None:
        operands = (scal,) + operands
        specs = [pl.BlockSpec(memory_space=pltpu.SMEM)] + specs
    return pl.pallas_call(
        kernel,
        out_shape=tuple(outs),
        in_specs=specs,
        out_specs=tuple([vmem] * len(outs)),
        scratch_shapes=[pltpu.VMEM(dims, dtype) for dims, dtype in scratch],
        compiler_params=pltpu.CompilerParams(vmem_limit_bytes=56 * 1024 * 1024),
        name=name,
    )(*operands)


def sum_parts(stats):
    count = lax.axis_size("rows")
    return lax.all_to_all(jnp.broadcast_to(stats[None], (count,) + stats.shape), "rows", 0, 0)


def swap(value_a, value_b):
    count = lax.axis_size("rows")
    pairs = [(i, i ^ 1) for i in range(count)]
    across = []
    for i in range(1, count - 1, 2):
        across += [(i, i + 1), (i + 1, i)]
    return lax.ppermute(value_a, "rows", pairs), lax.ppermute(value_b, "rows", across)


def gather_kernels(shards, dims):
    count = lax.axis_size("fsdp")
    flat = jnp.concatenate([item.astype(BF16).reshape(-1) for item in shards])
    if count == 2:
        other = lax.ppermute(flat, "fsdp", [(0, 1), (1, 0)])
        low = lax.axis_index("fsdp") == 0
        pieces = [jnp.where(low, flat, other), jnp.where(low, other, flat)]
    else:
        whole = lax.all_gather(flat, "fsdp")
        pieces = [whole[i] for i in range(count)]
    outs = []
    start = 0
    for item, dim in zip(shards, dims):
        parts = [piece[start : start + item.size].reshape(item.shape) for piece in pieces]
        outs.append(jnp.concatenate(parts, axis=dim))
        start += item.size
    return outs


def reduce_gradients(grads):
    count, bands = lax.axis_size("fsdp"), lax.axis_size("rows")
    sizes = [item.shape[1] for item in grads]
    flat = jnp.concatenate(grads, axis=1)
    total = flat.shape[1]
    chunk = -(-total // (bands * 1024)) * 1024
    flat = jnp.pad(flat, ((0, 0), (0, chunk * bands - total)))
    flat = flat.reshape(count * bands, chunk // 128, 128)
    got = lax.all_to_all(flat, ("fsdp", "rows"), 0, 0)
    mine = jnp.sum(got.astype(F32), axis=0).astype(BF16)
    whole = lax.all_to_all(jnp.broadcast_to(mine[None], (bands,) + mine.shape), "rows", 0, 0)
    whole = whole.reshape(-1)
    outs = []
    start = 0
    for size in sizes:
        outs.append(whole[start : start + size])
        start += size
    return outs


def per_device(
    residual_target,
    conditioning,
    noise_sample,
    noise_level,
    input_kernel,
    first_kernel,
    second_kernel,
    down_kernel,
    coarse_kernel,
    upward_kernel,
    output_kernel,
    embed_matrix,
):
    bands, count = lax.axis_size("rows"), lax.axis_size("fsdp")
    members = 2 * ROWS * 2 * HALF * bands
    members_c = 4 * CROWS * HALF * bands
    members_all = count * residual_target.size * bands
    me = lax.axis_index("rows")
    sigma_level, skip_scale, out_scale, in_scale, weight = preconditions(noise_level[0])
    coef = 2.0 * weight * out_scale / members_all
    scal = jnp.stack(
        [
            sigma_level,
            skip_scale,
            out_scale,
            in_scale,
            weight,
            coef,
            (me > 0).astype(F32),
            (me < bands - 1).astype(F32),
            (me % 2).astype(F32),
        ]
    )
    embedded = embedding(sigma_level, embed_matrix.shape[0] * count)
    target = residual_target.reshape(12 * ROWS, 512)
    condition = conditioning.reshape(12 * ROWS, 512)
    noise = noise_sample.reshape(12 * ROWS, 512)

    far = shape(32, FAR * 512, BF16)
    own, edge_a, edge_b, line_a, line_b = run(
        "enter",
        enter,
        [shape(32, ROWS * 512, BF16), far, far, shape(16, 512), shape(16, 512)],
        scal,
        target,
        condition,
        noise,
        scratch=[((4, 192, 128), F32)],
    )
    got_a, got_b = swap(edge_a, edge_b)
    line_a, line_b = swap(line_a, line_b)

    win_k, first_k, emb_k = gather_kernels([input_kernel, first_kernel, embed_matrix], (1, 1, 0))
    second_k, down_k, coarse_k, up_k, out_k = gather_kernels(
        [second_kernel, down_kernel, coarse_kernel, upward_kernel, output_kernel], (1, 1, 1, 1, 2)
    )
    out_k = jnp.pad(out_k, ((0, 0), (0, 4), (0, 0)))

    def flat(item):
        return item.reshape(-1, item.shape[-1])

    vector = jnp.broadcast_to(embedded[None, :], (16, embedded.shape[0]))
    win, wfirst, wfirst_t, shift = run(
        "prepare_first",
        prepare_first,
        [shape(384, 128, BF16), shape(384, 256, BF16), shape(256, 384, BF16), shape(128, 128)],
        None,
        flat(win_k),
        flat(first_k),
        emb_k,
        vector,
    )
    (
        wsecond, wsecond_t, wdown, wdown_t, wcoarse, wcoarse_t, wup, wup_t, wout, wout_t
    ) = run(
        "prepare_rest",
        prepare_rest,
        [
            shape(384, 256, BF16), shape(256, 384, BF16),
            shape(384, 192, BF16), shape(192, 384, BF16),
            shape(384, 384, BF16), shape(384, 384, BF16),
            shape(384, 512, BF16), shape(512, 384, BF16),
            shape(96, 256, BF16), shape(256, 96, BF16),
        ],
        None,
        flat(second_k), flat(down_k), flat(coarse_k), flat(up_k), flat(out_k),
    )

    stat = shape(8, 128)
    act_a, stats_a, kept_in = run(
        "stage_a",
        stage_a,
        [shape(128, 20 * HALF), stat, shape(128, 10 * HALF, BF16)],
        scal,
        own, got_a, got_b, win,
        scratch=[((32, FAR * 512), BF16), ((32, FAR * 512), BF16)],
    )
    stats_a = sum_parts(stats_a)
    act_b, stats_b, kept_a = run(
        "stage_b",
        functools.partial(stage_b, members),
        [shape(128, 18 * HALF), stat, shape(256, 8 * HALF, BF16)],
        scal,
        act_a, stats_a, wfirst, shift,
    )
    stats_b = sum_parts(stats_b)
    fine, act_c, edge, stats_c, kept_b, kept_pool = run(
        "stage_c",
        functools.partial(stage_c, members),
        [
            shape(128, 16 * HALF), shape(128, 6 * HALF), shape(128, 2 * HALF), stat,
            shape(256, 8 * HALF, BF16), shape(192, 4 * HALF, BF16),
        ],
        scal,
        act_a, act_b, stats_b, wsecond, wdown,
    )
    got_a, got_b = swap(edge, edge)
    stats_c = sum_parts(stats_c)
    merged, wide_c, stats_d, kept_c, kept_up = run(
        "stage_d",
        functools.partial(stage_d, members_c),
        [
            shape(128, 14 * HALF), shape(128, 8 * HALF), stat,
            shape(384, 4 * HALF, BF16), shape(384, 4 * HALF, BF16),
        ],
        scal,
        act_c, got_a, got_b, stats_c, wcoarse, wup, fine,
        scratch=[((128, 10 * HALF), F32)],
    )
    stats_d = sum_parts(stats_d)
    denoised, loss, back_d, edge_a, edge_b, stats_ed, grad_out = run(
        "stage_out",
        functools.partial(stage_out, members),
        [
            shape(96, 512), stat, shape(128, 8 * HALF),
            shape(128, 3 * HALF, BF16), shape(128, 3 * HALF, BF16), stat,
            shape(48, 192, BF16),
        ],
        scal,
        merged, stats_d, wout, wout_t, target, noise, line_a, line_b,
        scratch=[
            ((160, 512), F32), ((160, 512), F32), ((96, 8 * HALF), BF16), ((256, 8 * HALF), BF16),
            ((4, 96, 128), F32), ((4, 96, 128), F32), ((4, 96, 128), F32),
        ],
    )
    got_a, got_b = swap(edge_a, edge_b)
    stats_ed = sum_parts(stats_ed)
    grad_merged, back_c, grad_coarse, edge_a, edge_b, stats_ec, grad_up, grad_c = run(
        "stage_up",
        functools.partial(stage_up, members, members_c),
        [
            shape(128, 12 * HALF), shape(128, 4 * HALF), shape(128, 6 * HALF),
            shape(128, 3 * HALF, BF16), shape(128, 3 * HALF, BF16), stat,
            shape(192, 384, BF16), shape(384, 384, BF16),
        ],
        scal,
        merged, stats_d, stats_ed, back_d, got_a, got_b, kept_up, wup_t,
        wide_c, stats_c, kept_c, wcoarse_t,
        scratch=[
            ((384, 8 * HALF), BF16), ((384, 8 * HALF), BF16), ((384, 4 * HALF), BF16)
        ],
    )
    got_a, got_b = swap(edge_a, edge_b)
    stats_ec = sum_parts(stats_ec)
    grad_fine, back_b, stats_eb, grad_down, grad_second = run(
        "stage_down",
        functools.partial(stage_down, members, members_c),
        [
            shape(128, 8 * HALF), shape(128, 10 * HALF), stat,
            shape(384, 192, BF16), shape(192, 192, BF16),
        ],
        scal,
        stats_c, stats_ec, wide_c, back_c, grad_coarse, got_a, got_b,
        wdown_t, kept_pool, grad_merged, act_b, stats_b, kept_b, wsecond_t,
        scratch=[((384, 8 * HALF), BF16), ((384, 4 * HALF), BF16)],
    )
    stats_eb = sum_parts(stats_eb)
    back_a, stats_ea, grad_first, cell_sums = run(
        "stage_first",
        functools.partial(stage_first, members),
        [shape(128, 8 * HALF), stat, shape(192, 192, BF16), stat],
        scal,
        stats_b, stats_eb, act_b, back_b, wfirst_t, act_a, stats_a, kept_a,
        scratch=[((384, 8 * HALF), BF16)],
    )
    stats_ea = sum_parts(stats_ea)
    (grad_in,) = run(
        "stage_last",
        functools.partial(stage_last, members),
        [shape(192, 96, BF16)],
        None,
        stats_a, stats_ea, act_a, back_a, grad_fine, kept_in,
        scratch=[((128, 8 * HALF), BF16)],
    )

    loss_value = lax.psum(loss[0, 0], ("fsdp", "rows")) / members_all
    sums = cell_sums[0, :64] + cell_sums[0, 64:]
    embed_grad = (embedded.astype(F32)[:, None] * sums[None, :]).astype(BF16)

    def split(item, outs, ins, dim):
        width = item.shape[1] // 3
        taps = item.reshape(3, item.shape[0] // 3, 3, width)[:, :outs, :, :ins]
        taps = jnp.transpose(taps, (0, 2, 1, 3)).reshape(9, outs, ins)
        if dim == 1:
            parts = taps.reshape(9, count, outs // count, ins)
            return jnp.moveaxis(parts, 1, 0).reshape(count, -1)
        parts = taps.reshape(9, outs, count, ins // count)
        return jnp.moveaxis(parts, 2, 0).reshape(count, -1)

    done = reduce_gradients(
        [
            split(grad_in, 64, 24, 1),
            split(grad_first, 64, 64, 1),
            split(grad_second, 64, 64, 1),
            split(grad_down, 128, 64, 1),
            split(grad_c, 128, 128, 1),
            split(grad_up, 64, 128, 1),
            split(grad_out, 12, 64, 2),
            embed_grad.reshape(count, -1),
        ]
    )
    kernels = (
        input_kernel, first_kernel, second_kernel, down_kernel,
        coarse_kernel, upward_kernel, output_kernel, embed_matrix,
    )
    shards = [item.astype(F32).reshape(like.shape) for item, like in zip(done, kernels)]
    return (denoised.reshape(residual_target.shape), loss_value, *shards)


def solution(mesh):
    in_specs = (
        P("fsdp", None, "rows", None),
        P("fsdp", None, "rows", None),
        P("fsdp", None, "rows", None),
        P("fsdp"),
        P(None, "fsdp", None),
        P(None, "fsdp", None),
        P(None, "fsdp", None),
        P(None, "fsdp", None),
        P(None, "fsdp", None),
        P(None, "fsdp", None),
        P(None, None, "fsdp"),
        P("fsdp", None),
    )
    out_specs = (
        P("fsdp", None, "rows", None),
        P(),
        P(None, "fsdp", None),
        P(None, "fsdp", None),
        P(None, "fsdp", None),
        P(None, "fsdp", None),
        P(None, "fsdp", None),
        P(None, "fsdp", None),
        P(None, None, "fsdp"),
        P("fsdp", None),
    )
    return jax.shard_map(
        per_device, mesh=mesh, in_specs=in_specs, out_specs=out_specs, check_vma=False
    )
```

```python
import functools

import jax
import jax.numpy as jnp
from jax import lax
from jax.experimental import pallas as pl
from jax.experimental.pallas import tpu as pltpu
from jax.sharding import PartitionSpec as P

GROUPS = 32
STEPS = 64

sigma_low = 0.002
sigma_high = 80.0
sigma_data = 0.5
rho_power = 7.0
eps_norm = 1e-05

F32 = jnp.float32
BF16 = jnp.bfloat16

HALF = 256
ROWS = 8
CROWS = 4
FAR = 7


def preconditions(level_index):
    ramp_value = level_index.astype(jnp.float32) / (STEPS - 1)
    top_root = sigma_high ** (1.0 / rho_power)
    bottom = sigma_low ** (1.0 / rho_power)
    sigma_level = (top_root + ramp_value * (bottom - top_root)) ** rho_power
    sigma_total = sigma_level * sigma_level + sigma_data * sigma_data
    skip_scale = sigma_data * sigma_data / sigma_total
    out_scale = sigma_level * sigma_data * lax.rsqrt(sigma_total)
    in_scale = lax.rsqrt(sigma_total)
    weight = sigma_total / (sigma_level * sigma_data) ** 2
    return (sigma_level, skip_scale, out_scale, in_scale, weight)


def embedding(sigma_level, features):
    half_count = features // 2
    ramp_steps = jnp.arange(half_count, dtype=jnp.float32) / half_count
    frequency = 64.0 * 0.01**ramp_steps
    phase_angle = 0.25 * jnp.log(sigma_level) * frequency
    return jnp.concatenate([jnp.cos(phase_angle), jnp.sin(phase_angle)]).astype(jnp.bfloat16)


class Source:
    def __init__(self, array, spot, sems, flat):
        self.shape = array.shape
        self.spot = spot
        self.copies = []
        if len(sems) == 1:
            self.copies.append(pltpu.make_async_copy(array, spot, sems[0]))
        else:
            for r, sem in enumerate(sems):
                width = array.shape[2]
                part = spot.at[:, r * width : (r + 1) * width] if flat else spot.at[r]
                self.copies.append(pltpu.make_async_copy(array.at[r], part, sem))
        self.waited = [False] * len(sems)
        for copy in self.copies:
            copy.start()

    def wait(self, index):
        if not self.waited[index]:
            self.waited[index] = True
            self.copies[index].wait()

    def __getitem__(self, index):
        for copy in range(len(self.copies)):
            self.wait(copy)
        return self.spot[index]

    def row(self, index):
        self.wait(index)
        return self.spot[index]


class Sink:
    def __init__(self, array, spot, sems):
        self.array, self.spot, self.sems = array, spot, sems
        self.copies = []

    def send(self, source, target, sem):
        copy = pltpu.make_async_copy(source, target, sem)
        copy.start()
        self.copies.append(copy)

    def __setitem__(self, index, value):
        self.spot[index] = value

    def __getitem__(self, index):
        return self.spot[index]

    def row(self, index):
        return self.spot[index]

    def put(self, index, value):
        self.spot[index] = value
        self.send(self.spot.at[index], self.array.at[index], self.sems[index])

    def finish(self):
        if not self.copies:
            self.send(self.spot, self.array, self.sems[0])

    def wait(self):
        for copy in self.copies:
            copy.wait()


def row(ref, index):
    if isinstance(ref, (Source, Sink)) and len(ref.spot.shape) == 3:
        return ref.row(index)
    return ref[:, index * HALF : (index + 1) * HALF]


def put(ref, index, value):
    if isinstance(ref, Sink) and len(ref.spot.shape) == 3:
        ref.put(index, value)
    else:
        ref[:, index * HALF : (index + 1) * HALF] = value


def lane(shape):
    return lax.broadcasted_iota(jnp.int32, shape, 1)


def from_left(value):
    moved = pltpu.roll(value, 1, 1)
    return jnp.where(lane(value.shape) == 0, 0.0, moved)


def from_right(value):
    moved = pltpu.roll(value, value.shape[1] - 1, 1)
    return jnp.where(lane(value.shape) == value.shape[1] - 1, 0.0, moved)


def mm(left, right):
    return jnp.dot(left, right, preferred_element_type=F32)


def mm_nt(left, right):
    return lax.dot_general(left, right, (((1,), (1,)), ((), ())), preferred_element_type=F32)


def fine_taps(value):
    half = value.shape[0] // 2
    even, odd = value[:half], value[half:]
    return jnp.concatenate([from_left(odd), value, from_right(even)], axis=0).astype(BF16)


def coarse_taps(value):
    return jnp.concatenate([from_left(value), value, from_right(value)], axis=0).astype(BF16)


def fine_untap(taps):
    size = taps.shape[0] // 4
    even = taps[size : 2 * size] + from_left(taps[3 * size :])
    odd = taps[2 * size : 3 * size] + from_right(taps[:size])
    return jnp.concatenate([even, odd], axis=0)


def coarse_untap(taps):
    size = taps.shape[0] // 3
    return taps[size : 2 * size] + from_right(taps[:size]) + from_left(taps[2 * size :])


def spread(parts, first, last):
    out = {}
    for i in range(first, last + 1):
        size = parts[i - 1].shape[0] // 3
        out[i] = parts[i - 1][:size] + parts[i][size : 2 * size] + parts[i + 1][2 * size :]
    return out


def stack_rows(g, r):
    return jnp.concatenate([g[r + 1], g[r], g[r - 1]], axis=0)


def same_group(size, fine):
    left = lax.broadcasted_iota(jnp.int32, (size, size), 0)
    right = lax.broadcasted_iota(jnp.int32, (size, size), 1)
    if fine:
        half = size // 2
        left, right = left % half, right % half
        per = half // GROUPS
    else:
        per = size // GROUPS
    return left // per == right // per


def group_sums(stats_ref, fine):
    total = stats_ref[0]
    for index in range(1, stats_ref.shape[0]):
        total = total + stats_ref[index]
    member = same_group(128, fine)
    first = jnp.sum(jnp.where(member, total[0:1, :], 0.0), axis=1, keepdims=True)
    second = jnp.sum(jnp.where(member, total[1:2, :], 0.0), axis=1, keepdims=True)
    return first, second


def norm_columns(stats_ref, fine, members):
    first, second = group_sums(stats_ref, fine)
    mean = first / members
    inverse = lax.rsqrt(second / members - mean * mean + eps_norm)
    return mean, inverse


def back_columns(stats_ref, fine, members):
    first, second = group_sums(stats_ref, fine)
    return first / members, second / members


def to_row(column):
    size = column.shape[0]
    diagonal = lax.broadcasted_iota(jnp.int32, (size, size), 0) == lax.broadcasted_iota(
        jnp.int32, (size, size), 1
    )
    return jnp.sum(jnp.where(diagonal, column, 0.0), axis=0, keepdims=True)


def put_stats(ref, first, second, third=None):
    first = to_row(jnp.sum(first, axis=1, keepdims=True))
    second = to_row(jnp.sum(second, axis=1, keepdims=True))
    if third is None:
        third = jnp.zeros((1, 128), F32)
    block = jnp.concatenate([first, second, third, jnp.zeros((5, 128), F32)], axis=0)
    for index in range(ref.spot.shape[0]):
        ref.spot[index] = block
    ref.finish()


def silu(h):
    return h * (1.0 / (1.0 + jnp.exp(-h)))


def silu_slope(h):
    s = 1.0 / (1.0 + jnp.exp(-h))
    return s * (1.0 + h * (1.0 - s))


def masked(value, index, rows, scal):
    if index < 0:
        return value * scal[6]
    if index >= rows:
        return value * scal[7]
    return value


def pick(scal, when_odd, when_even):
    return jnp.where(scal[8] > 0.5, when_odd, when_even)


def spill(ref, value):
    for t in range(4):
        ref[t, : value.shape[0], :] = value[:, 128 * t : 128 * (t + 1)]


def strided(ref, index, size):
    return jnp.concatenate(
        [ref[t, pl.ds(index, size, stride=ROWS), :] for t in range(4)], axis=1
    )


def interleave(transposed):
    left = lax.broadcasted_iota(jnp.int32, (512, 512), 0)
    right = lax.broadcasted_iota(jnp.int32, (512, 512), 1)
    if transposed:
        left, right = right, left
    place = (left & 1) * HALF + (left >> 1)
    return jnp.where(place == right, 1.0, 0.0).astype(BF16)


def fine_grad(blocks, outs, ins):
    parts = []
    for a in range(3):
        even = blocks[(2 * a) * outs : (2 * a + 1) * outs]
        odd = blocks[(2 * a + 1) * outs : (2 * a + 2) * outs]
        parts.append(even[:, : 3 * ins] + odd[:, ins : 4 * ins])
    return jnp.concatenate(parts, axis=0).astype(BF16)


def place(width, target, offset):
    left = lax.broadcasted_iota(jnp.int32, (width, target), 0)
    right = lax.broadcasted_iota(jnp.int32, (width, target), 1)
    return jnp.where(left + offset == right, 1.0, 0.0).astype(BF16)


def flipped(value):
    size = value.shape[1]
    return mm_nt(place(size, size, 0), value).astype(BF16)


def tap_of(pieces, offset, index, size):
    each = size // len(pieces)
    start = offset + index * each
    return jnp.concatenate([piece[start : start + each, :] for piece in pieces], axis=0).astype(
        BF16
    )


def in_order(scal, pieces):
    if len(pieces) == 2:
        mine, other = pieces[0][...], pieces[1][...]
        low = scal[9] > 0.5
        return [jnp.where(low, mine, other), jnp.where(low, other, mine)]
    return [piece[...] for piece in pieces]


def fine_matrix(taps, slot):
    rows = []
    for a in range(3):
        total = None
        for b in range(3):
            spot = jnp.concatenate(
                [place(slot, 4 * slot, b * slot), place(slot, 4 * slot, (b + 1) * slot)], axis=1
            )
            term = mm(taps[3 * a + b][:, :slot], spot)
            total = term if total is None else total + term
        rows += [total[:, : 4 * slot], total[:, 4 * slot :]]
    return jnp.concatenate(rows, axis=0).astype(BF16)


def pack(widths, *refs):
    shards, (out, scratch) = refs[: len(widths)], refs[len(widths) :]
    scratch[...] = jnp.zeros(scratch.shape, F32)
    start = 0
    for shard, (taps, rows) in zip(shards, widths):
        if taps == 1:
            scratch[start : start + rows, : shard.shape[1]] = shard[...]
            start += rows
        else:
            for t in range(taps):
                value = shard[t]
                scratch[start : start + value.shape[0], : value.shape[1]] = value
                start += rows
    out[...] = scratch[...].astype(BF16)
    out.finish()


def prepare_first(embed_size, scal, vec, *refs):
    pieces, (win, wfirst, wfirst_t, shift) = refs[:-4], refs[-4:]
    count = len(pieces)
    pieces = in_order(scal, pieces)
    each = 9 * (64 // count)
    win[...] = fine_matrix([tap_of(pieces, 0, t, 64) for t in range(9)], 32)
    win.finish()
    first = fine_matrix([tap_of(pieces, each, t, 64) for t in range(9)], 64)
    wfirst[...] = first
    wfirst.finish()
    wfirst_t[...] = flipped(first)
    wfirst_t.finish()
    line = mm(vec[...], tap_of(pieces, 2 * each, 0, embed_size))[0:1, :64]
    both = jnp.concatenate([line, line], axis=1)
    diagonal = place(128, 128, 0).astype(F32)
    shift[...] = jnp.broadcast_to(
        jnp.sum(diagonal * both, axis=1, keepdims=True), (128, 128)
    )


def prepare_rest(scal, *refs):
    pieces = refs[:-10]
    wsecond, wsecond_t, wdown, wdown_t, wcoarse, wcoarse_t, wup, wup_t, wout, wout_t = refs[-10:]
    count = len(pieces)
    pieces = in_order(scal, pieces)
    start = 0

    def taps_of(size):
        nonlocal start
        taps = [tap_of(pieces, start, t, size) for t in range(9)]
        start += 9 * (size // count)
        return taps

    def give(value, forward, backward):
        forward[...] = value
        forward.finish()
        backward[...] = flipped(value)
        backward.finish()

    give(fine_matrix(taps_of(64), 64), wsecond, wsecond_t)
    taps = taps_of(128)
    rows = []
    for a in range(3):
        total = None
        for b in range(3):
            term = mm(taps[3 * a + b][:, :64], place(64, 256, 64 * b))
            total = term if total is None else total + term
        rows.append(total)
    give(jnp.concatenate(rows, axis=0)[:, :192].astype(BF16), wdown, wdown_t)
    taps = taps_of(128)
    rows = [jnp.concatenate(taps[3 * a : 3 * a + 3], axis=1) for a in range(3)]
    give(jnp.concatenate(rows, axis=0), wcoarse, wcoarse_t)
    taps = taps_of(64)
    rows = []
    blank = jnp.zeros((64, 128), BF16)
    for a in range(3):
        rows.append(jnp.concatenate(taps[3 * a : 3 * a + 3] + [blank], axis=1))
        rows.append(jnp.concatenate([blank] + taps[3 * a : 3 * a + 3], axis=1))
    give(jnp.concatenate(rows, axis=0), wup, wup_t)
    taps = []
    width = 64 // count
    for t in range(9):
        total = None
        for s in range(count):
            tap = pieces[s][start + 16 * t : start + 16 * (t + 1), :].astype(BF16)
            term = mm(tap[:, :width], place(width, 128, s * width))
            total = term if total is None else total + term
        taps.append(total.astype(BF16))
    give(fine_matrix(taps, 64), wout, wout_t)


def enter(scal, target, condition, noise, own, edge_a, edge_b, line_a, line_b, scratch):
    sigma, skip, in_scale = scal[0], scal[1], scal[3]
    noisy = target[...] + sigma * noise[...]
    q = skip * noisy - target[...]
    natural = jnp.concatenate([in_scale * noisy, condition[...]], axis=0).astype(BF16)
    spill(scratch, mm(natural, interleave(False)))
    blank = jnp.zeros((8, 512), F32)
    for i in range(ROWS):
        value = strided(scratch, i, 24)
        own[:, i * 512 : (i + 1) * 512] = jnp.concatenate([value, blank], axis=0).astype(BF16)
    top, low = own[:, : FAR * 512], own[:, (ROWS - FAR) * 512 :]
    edge_a[...] = pick(scal, top, low)
    edge_b[...] = pick(scal, low, top)
    spill(scratch, q)
    blank = jnp.zeros((4, 512), F32)
    top = jnp.concatenate([strided(scratch, 0, 12), blank], axis=0)
    low = jnp.concatenate([strided(scratch, ROWS - 1, 12), blank], axis=0)
    line_a[...] = pick(scal, top, low)
    line_b[...] = pick(scal, low, top)


def stage_a(scal, win, got_a, got_b, own, act, stats, kept, above, below):
    above[...] = pick(scal, got_a[...], got_b[...])
    below[...] = pick(scal, got_b[...], got_a[...])
    parts = {}
    total = jnp.zeros((128, HALF), F32)
    square = jnp.zeros((128, HALF), F32)
    for r in range(-FAR, ROWS + FAR):
        if r < 0:
            value = above[:, (r + FAR) * 512 : (r + FAR + 1) * 512]
        elif r < ROWS:
            value = own[:, r * 512 : (r + 1) * 512]
        else:
            value = below[:, (r - ROWS) * 512 : (r - ROWS + 1) * 512]
        value = value.astype(F32)
        z = fine_taps(jnp.concatenate([value[:, :HALF], value[:, HALF:]], axis=0))
        if -1 <= r <= ROWS:
            put(kept, r + 1, z)
        parts[r] = mm(win[...], z)
        i = r - 1
        if i > -FAR:
            value = spread(parts, i, i)[i]
            put(act, i + FAR - 1, value)
            del parts[i - 1]
            if 0 <= i < ROWS:
                total = total + value
                square = square + value * value
    put_stats(stats, total, square)


def stage_b(members, scal, stats_a, shift, wfirst, act_a, act_b, stats, kept):
    mean, inverse = norm_columns(stats_a, True, members)
    lift = shift[:, 0:1]
    parts = {}
    total = jnp.zeros((128, HALF), F32)
    square = jnp.zeros((128, HALF), F32)
    for r in range(-6, ROWS + 6):
        value = silu((row(act_a, r + 6) - mean) * inverse)
        z = fine_taps(masked(value, r, ROWS, scal))
        if 0 <= r < ROWS:
            put(kept, r, z)
        parts[r] = mm(wfirst[...], z)
        i = r - 1
        if i > -6:
            value = spread(parts, i, i)[i] + lift
            put(act_b, i + 5, value)
            del parts[i - 1]
            if 0 <= i < ROWS:
                total = total + value
                square = square + value * value
    put_stats(stats, total, square)


def stage_c(
    members, scal, stats_b, wsecond, act_b, act_a, wdown,
    fine, act_c, edge, stats, kept, kept_pool,
):
    mean, inverse = norm_columns(stats_b, True, members)
    parts = {}
    pooled = {}
    half = {}
    for r in range(-5, ROWS + 5):
        value = silu((row(act_b, r + 5) - mean) * inverse)
        z = fine_taps(masked(value, r, ROWS, scal))
        if 0 <= r < ROWS:
            put(kept, r, z)
        parts[r] = mm(wsecond[...], z)
        i = r - 1
        if i > -5:
            value = spread(parts, i, i)[i] + row(act_a, i + 6)
            put(fine, i + 4, value)
            del parts[i - 1]
            half[i] = value[:64] + value[64:]
            if i % 2:
                value = 0.25 * (half.pop(i - 1) + half.pop(i))
                value = masked(value, i // 2, CROWS, scal)
                pooled[i // 2] = value.astype(BF16).astype(F32)
    parts = {}
    total = jnp.zeros((128, HALF), F32)
    square = jnp.zeros((128, HALF), F32)
    for r in range(-2, CROWS + 2):
        z = coarse_taps(pooled[r])
        if 0 <= r < CROWS:
            put(kept_pool, r, z)
        parts[r] = mm(wdown[...], z)
        i = r - 1
        if i > -2:
            value = spread(parts, i, i)[i]
            put(act_c, i + 1, value)
            del parts[i - 1]
            if 0 <= i < CROWS:
                total = total + value
                square = square + value * value
            if i in (1, 2):
                put(edge, i - 1, value)
    put_stats(stats, total, square)


def stage_d(
    members, scal, stats_c, wcoarse, got_a, got_b, act_c, wup, fine,
    merged, wide_c, stats, kept_c, kept_up, ring,
):
    mean, inverse = norm_columns(stats_c, False, members)
    for j in range(2):
        put(ring, j, pick(scal, row(got_a, j), row(got_b, j)))
        put(ring, CROWS + 4 + j, pick(scal, row(got_b, j), row(got_a, j)))
    for j in range(CROWS + 2):
        put(ring, j + 2, row(act_c, j))
    parts = {}
    lifted = {}
    for r in range(-3, CROWS + 3):
        value = silu((row(ring, r + 3) - mean) * inverse)
        z = coarse_taps(masked(value, r, CROWS, scal))
        if 0 <= r < CROWS:
            put(kept_c, r, z)
        parts[r] = mm(wcoarse[...], z)
        i = r - 1
        if i > -3:
            value = spread(parts, i, i)[i] + row(ring, i + 3)
            put(wide_c, i + 2, row(ring, i + 3))
            del parts[i - 1]
            lifted[i] = masked(value, i, CROWS, scal).astype(BF16).astype(F32)
    parts = {}
    total = jnp.zeros((128, HALF), F32)
    square = jnp.zeros((128, HALF), F32)
    for r in range(-2, CROWS + 2):
        z = coarse_taps(lifted[r])
        if 0 <= r < CROWS:
            put(kept_up, r, z)
        four = jnp.concatenate([z[:128], z[128:256], z[128:256], z[256:]], axis=0)
        parts[2 * r] = parts[2 * r + 1] = mm(wup[...], four)
        for i in (2 * r - 1, 2 * r):
            if i >= -3:
                value = spread(parts, i, i)[i] + row(fine, i + 4)
                put(merged, i + 3, value)
                parts.pop(i - 1)
                if 0 <= i < ROWS:
                    total = total + value
                    square = square + value * value
    put_stats(stats, total, square)


def stage_out(
    members, scal, stats_d, wout, merged, line_a, line_b, target, noise, wout_t,
    denoised, back, edge_a, edge_b, stats, grad, pairs, cells, gs, zs,
    goals, noisies, found,
):
    sigma, skip, out_scale, weight, coef = scal[0], scal[1], scal[2], scal[4], scal[5]
    mean, inverse = norm_columns(stats_d, True, members)
    parts = {}
    for r in range(-2, ROWS + 2):
        value = silu((row(merged, r + 3) - mean) * inverse)
        z = fine_taps(masked(value, r, ROWS, scal))
        if 0 <= r < ROWS:
            put(zs, r, z)
        parts[r] = mm(wout[...], z)
        i = r - 1
        if i > -2:
            value = spread(parts, i, i)[i]
            del parts[i - 1]
            pairs[16 * (i + 1) : 16 * (i + 2), :] = jnp.concatenate(
                [value[:16], value[16:]], axis=1
            )
    value = pairs[...]
    high = value.astype(BF16)
    low = (value - high.astype(F32)).astype(BF16)
    back_order = interleave(True)
    pairs[...] = mm(high, back_order) + mm(low, back_order)
    blank = jnp.zeros((4, 512), F32)
    loss_sum = jnp.zeros((12, 512), F32)
    top = pick(scal, line_a[...], line_b[...]) + out_scale * pairs[0:16, :]
    cells[0:16, :] = coef * scal[6] * top
    low = pick(scal, line_b[...], line_a[...]) + out_scale * pairs[16 * (ROWS + 1) :, :]
    cells[16 * (ROWS + 1) :, :] = coef * scal[7] * low
    spill(goals, target[...])
    spill(noisies, target[...] + sigma * noise[...])
    for i in range(ROWS):
        goal = strided(goals, i, 12)
        noisy = strided(noisies, i, 12)
        estimate = skip * noisy + out_scale * pairs[16 * (i + 1) : 16 * (i + 1) + 12, :]
        for t in range(4):
            found[t, pl.ds(i, 12, stride=ROWS), :] = estimate[:, 128 * t : 128 * (t + 1)]
        mismatch = estimate - goal
        loss_sum = loss_sum + weight * mismatch * mismatch
        cells[16 * (i + 1) : 16 * (i + 2), :] = jnp.concatenate([coef * mismatch, blank], axis=0)
    denoised[...] = jnp.concatenate([found[t] for t in range(4)], axis=1)
    denoised.finish()
    loss_sum = jnp.broadcast_to(
        jnp.sum(jnp.sum(loss_sum, axis=1, keepdims=True), axis=0, keepdims=True), (1, 128)
    )
    pairs[...] = mm(cells[...].astype(BF16), interleave(False))
    g = {}
    for i in range(-1, ROWS + 1):
        value = pairs[16 * (i + 1) : 16 * (i + 2), :]
        g[i] = jnp.concatenate([value[:, :HALF], value[:, HALF:]], axis=0).astype(BF16)
    total = jnp.zeros((128, HALF), F32)
    cross = jnp.zeros((128, HALF), F32)
    for r in range(ROWS):
        rows = stack_rows(g, r)
        put(gs, r, rows)
        value = fine_untap(mm(wout_t[...], rows))
        put(back, r, value)
        hat = (row(merged, r + 3) - mean) * inverse
        e = value * silu_slope(hat)
        total = total + e
        cross = cross + e * hat
    put_stats(stats, total, cross, loss_sum)
    for j in range(3):
        top, low = row(back, j).astype(BF16), row(back, ROWS - 3 + j).astype(BF16)
        put(edge_a, j, pick(scal, top, low))
        put(edge_b, j, pick(scal, low, top))
    grad[...] = fine_grad(mm_nt(gs[...], zs[...]), 16, 64)


def stage_up(
    members, members_c, scal, stats_d, stats_ed, got_a, got_b, merged, back, wup_t, kept_up,
    stats_c, act_c, wcoarse_t, kept_c,
    grad_merged, back_c, grad_coarse, edge_a, edge_b, stats, grad_up, grad_c, loss, gs, zs, gc,
):
    total = stats_ed[0]
    for index in range(1, stats_ed.shape[0]):
        total = total + stats_ed[index]
    loss[...] = jnp.broadcast_to(total[2:3, :], (8, 128))
    loss.finish()
    mean, inverse = norm_columns(stats_d, True, members)
    shift, slope = back_columns(stats_ed, True, members)
    g = {}
    for r in range(-3, ROWS + 3):
        hat = (row(merged, r + 3) - mean) * inverse
        if r < 0:
            u = pick(scal, row(got_a, r + 3), row(got_b, r + 3)).astype(F32)
        elif r < ROWS:
            u = row(back, r)
        else:
            u = pick(scal, row(got_b, r - ROWS), row(got_a, r - ROWS)).astype(F32)
        value = inverse * (u * silu_slope(hat) - shift - hat * slope)
        value = masked(value, r, ROWS, scal)
        if -2 <= r < ROWS + 2:
            put(grad_merged, r + 2, value)
        g[r] = value.astype(BF16)
    gk = {}
    half = {}
    for r in range(-2, ROWS + 2):
        rows = stack_rows(g, r)
        if 0 <= r < ROWS:
            put(gs, r, rows)
            put(zs, r, row(kept_up, r // 2))
        taps = mm(wup_t[...], rows)
        half[r] = taps[128:256] + taps[256:384] + from_right(taps[:128]) + from_left(taps[384:])
        if r % 2:
            value = masked(half.pop(r - 1) + half.pop(r), r // 2, CROWS, scal)
            put(grad_coarse, r // 2 + 1, value)
            gk[r // 2] = value.astype(BF16)
    blocks = mm_nt(gs[...], zs[...])
    parts = []
    for a in range(3):
        even = blocks[128 * a : 128 * a + 64]
        odd = blocks[128 * a + 64 : 128 * a + 128]
        parts.append(
            jnp.concatenate(
                [
                    even[:, :128] + odd[:, 128:256],
                    even[:, 128:256] + odd[:, 128:256],
                    even[:, 128:256] + odd[:, 256:],
                ],
                axis=1,
            )
        )
    grad_up[...] = jnp.concatenate(parts, axis=0).astype(BF16)
    mean, inverse = norm_columns(stats_c, False, members_c)
    total = jnp.zeros((128, HALF), F32)
    cross = jnp.zeros((128, HALF), F32)
    for r in range(CROWS):
        rows = stack_rows(gk, r)
        put(gc, r, rows)
        value = coarse_untap(mm(wcoarse_t[...], rows))
        put(back_c, r, value)
        hat = (row(act_c, r + 2) - mean) * inverse
        e = value * silu_slope(hat)
        total = total + e
        cross = cross + e * hat
    put_stats(stats, total, cross)
    grad_c[...] = mm_nt(gc[...], kept_c[...]).astype(BF16)
    top = [row(back_c, 0).astype(BF16), row(back_c, 1).astype(BF16), gk[1]]
    low = [row(back_c, 2).astype(BF16), row(back_c, 3).astype(BF16), gk[2]]
    for j in range(3):
        put(edge_a, j, pick(scal, top[j], low[j]))
        put(edge_b, j, pick(scal, low[j], top[j]))


def stage_down(
    members, members_c, scal, stats_c, stats_ec, got_a, got_b, act_c, back_c, grad_coarse,
    wdown_t, grad_merged, kept_pool, stats_b, wsecond_t, act_b, kept_b,
    grad_fine, back_b, stats, grad_down, grad_second, gs, gc,
):
    mean, inverse = norm_columns(stats_c, False, members_c)
    shift, slope = back_columns(stats_ec, False, members_c)
    g = {}
    for r in range(-2, CROWS + 2):
        hat = (row(act_c, r + 2) - mean) * inverse
        if r < 0:
            u = pick(scal, row(got_a, r + 2), row(got_b, r + 2)).astype(F32)
        elif r < CROWS:
            u = row(back_c, r)
        else:
            u = pick(scal, row(got_b, r - CROWS), row(got_a, r - CROWS)).astype(F32)
        if r == -2:
            through = pick(scal, row(got_a, 2), row(got_b, 2)).astype(F32)
        elif r == CROWS + 1:
            through = pick(scal, row(got_b, 2), row(got_a, 2)).astype(F32)
        else:
            through = row(grad_coarse, r + 1)
        value = through + inverse * (u * silu_slope(hat) - shift - hat * slope)
        g[r] = masked(value, r, CROWS, scal).astype(BF16)
    fine = {}
    for r in range(-1, CROWS + 1):
        rows = stack_rows(g, r)
        if 0 <= r < CROWS:
            put(gc, r, rows)
        value = 0.25 * coarse_untap(mm(wdown_t[...], rows))
        both = jnp.concatenate([value, value], axis=0)
        for i in (2 * r, 2 * r + 1):
            value = masked(row(grad_merged, i + 2) + both, i, ROWS, scal)
            if 0 <= i < ROWS:
                put(grad_fine, i, value)
            fine[i] = value.astype(BF16)
    grad_down[...] = mm_nt(gc[...], kept_pool[...]).astype(BF16)
    mean, inverse = norm_columns(stats_b, True, members)
    total = jnp.zeros((128, HALF), F32)
    cross = jnp.zeros((128, HALF), F32)
    for r in range(-1, ROWS + 1):
        rows = stack_rows(fine, r)
        value = fine_untap(mm(wsecond_t[...], rows))
        put(back_b, r + 1, value)
        if 0 <= r < ROWS:
            put(gs, r, rows)
            hat = (row(act_b, r + 5) - mean) * inverse
            e = value * silu_slope(hat)
            total = total + e
            cross = cross + e * hat
    put_stats(stats, total, cross)
    grad_second[...] = fine_grad(mm_nt(gs[...], kept_b[...]), 64, 64)


def stage_first(
    members, scal, stats_b, stats_eb, act_b, back_b, wfirst_t, stats_a, act_a, kept_a,
    back_a, stats, grad_first, cell_sums, gs,
):
    mean, inverse = norm_columns(stats_b, True, members)
    shift, slope = back_columns(stats_eb, True, members)
    g = {}
    sums = jnp.zeros((128, HALF), F32)
    for r in range(-1, ROWS + 1):
        hat = (row(act_b, r + 5) - mean) * inverse
        value = inverse * (row(back_b, r + 1) * silu_slope(hat) - shift - hat * slope)
        if 0 <= r < ROWS:
            sums = sums + value
        g[r] = masked(value, r, ROWS, scal).astype(BF16)
    line = to_row(jnp.sum(sums, axis=1, keepdims=True))
    cell_sums[...] = jnp.broadcast_to(line, (8, 128))
    mean, inverse = norm_columns(stats_a, True, members)
    total = jnp.zeros((128, HALF), F32)
    cross = jnp.zeros((128, HALF), F32)
    for r in range(ROWS):
        rows = stack_rows(g, r)
        put(gs, r, rows)
        value = fine_untap(mm(wfirst_t[...], rows))
        put(back_a, r, value)
        hat = (row(act_a, r + 6) - mean) * inverse
        e = value * silu_slope(hat)
        total = total + e
        cross = cross + e * hat
    put_stats(stats, total, cross)
    grad_first[...] = fine_grad(mm_nt(gs[...], kept_a[...]), 64, 64)


def stage_last(members, scal, stats_a, stats_ea, act_a, back_a, grad_fine, kept_in, grad_in, gs):
    mean, inverse = norm_columns(stats_a, True, members)
    shift, slope = back_columns(stats_ea, True, members)
    for r in range(ROWS):
        hat = (row(act_a, r + 6) - mean) * inverse
        value = row(grad_fine, r) + inverse * (
            row(back_a, r) * silu_slope(hat) - shift - hat * slope
        )
        put(gs, r, value.astype(BF16))
    parts = []
    for a in range(3):
        blocks = mm_nt(gs[...], kept_in[:, a * HALF : (a + ROWS) * HALF])
        parts.append(blocks[:64, :96] + blocks[64:, 32:128])
    grad_in[...] = jnp.concatenate(parts, axis=0).astype(BF16)


def shape(*dims, dtype=F32):
    return jax.ShapeDtypeStruct(dims, dtype)


def run(name, kernel, outs, scal, *operands, scratch=(), flat=()):
    vmem = []
    counts = []

    def by_row(item):
        return len(item.shape) == 3 and item.shape[1] >= 128

    for place_at, item in enumerate(list(operands) + list(outs)):
        dims = item.shape
        if place_at in flat:
            dims = (dims[1], dims[0] * dims[2])
        vmem.append(pltpu.VMEM(dims, item.dtype))
        counts.append(item.shape[0] if by_row(item) else 1)
    ins = len(operands)

    def body(*refs):
        numbers, refs = refs[0], refs[1:]
        arrays, refs = refs[: len(vmem)], refs[len(vmem) :]
        spots, refs = refs[: len(vmem)], refs[len(vmem) :]
        sems, extra = refs[0], refs[1:]
        wrapped = []
        start = 0
        for place_at, (array, spot) in enumerate(zip(arrays, spots)):
            mine = [sems.at[start + i] for i in range(counts[place_at])]
            start += counts[place_at]
            if place_at < ins:
                wrapped.append(Source(array, spot, mine, place_at in flat))
            else:
                wrapped.append(Sink(array, spot, mine))
        kernel(numbers, *wrapped, *extra)
        for item in wrapped[:ins]:
            for index in range(len(item.copies)):
                item.wait(index)
        for item in wrapped[ins:]:
            item.finish()
        for item in wrapped[ins:]:
            item.wait()

    anywhere = pl.BlockSpec(memory_space=pltpu.HBM)
    return pl.pallas_call(
        body,
        out_shape=tuple(outs),
        in_specs=[pl.BlockSpec(memory_space=pltpu.SMEM)] + [anywhere] * ins,
        out_specs=tuple([anywhere] * len(outs)),
        scratch_shapes=vmem
        + [pltpu.SemaphoreType.DMA((sum(counts),))]
        + [pltpu.VMEM(dims, dtype) for dims, dtype in scratch],
        compiler_params=pltpu.CompilerParams(vmem_limit_bytes=48 * 1024 * 1024),
        name=name,
    )(scal, *operands)


def sum_parts(stats):
    return lax.all_to_all(stats, "rows", 0, 0)


def swap(value_a, value_b):
    count = lax.axis_size("rows")
    pairs = [(i, i ^ 1) for i in range(count)]
    across = []
    for i in range(1, count - 1, 2):
        across += [(i, i + 1), (i + 1, i)]
    return lax.ppermute(value_a, "rows", pairs), lax.ppermute(value_b, "rows", across)


def gather_packed(packed):
    if lax.axis_size("fsdp") == 2:
        return [packed, lax.ppermute(packed, "fsdp", [(0, 1), (1, 0)])]
    whole = lax.all_gather(packed, "fsdp").astype(F32)
    return [whole[i] for i in range(whole.shape[0])]


def reduce_gradients(grads):
    count, bands = lax.axis_size("fsdp"), lax.axis_size("rows")
    sizes = [item.shape[1] for item in grads]
    flat = jnp.concatenate(grads, axis=1)
    total = flat.shape[1]
    chunk = -(-total // (bands * 1024)) * 1024
    flat = jnp.pad(flat, ((0, 0), (0, chunk * bands - total)))
    flat = flat.reshape(count * bands, chunk // 128, 128)
    got = lax.all_to_all(flat, ("fsdp", "rows"), 0, 0)
    mine = jnp.sum(got.astype(F32), axis=0).astype(BF16)
    whole = lax.all_to_all(jnp.broadcast_to(mine[None], (bands,) + mine.shape), "rows", 0, 0)
    whole = whole.reshape(-1)
    outs = []
    start = 0
    for size in sizes:
        outs.append(whole[start : start + size])
        start += size
    return outs


def per_device(
    residual_target,
    conditioning,
    noise_sample,
    noise_level,
    input_kernel,
    first_kernel,
    second_kernel,
    down_kernel,
    coarse_kernel,
    upward_kernel,
    output_kernel,
    embed_matrix,
):
    bands, count = lax.axis_size("rows"), lax.axis_size("fsdp")
    members = 2 * ROWS * 2 * HALF * bands
    members_c = 4 * CROWS * HALF * bands
    members_all = count * residual_target.size * bands
    me = lax.axis_index("rows")
    sigma_level, skip_scale, out_scale, in_scale, weight = preconditions(noise_level[0])
    coef = 2.0 * weight * out_scale / members_all
    scal = jnp.stack(
        [
            sigma_level,
            skip_scale,
            out_scale,
            in_scale,
            weight,
            coef,
            (me > 0).astype(F32),
            (me < bands - 1).astype(F32),
            (me % 2).astype(F32),
            (lax.axis_index("fsdp") == 0).astype(F32),
        ]
    )
    embedded = embedding(sigma_level, embed_matrix.shape[0] * count)
    target = residual_target.reshape(12 * ROWS, 512)
    condition = conditioning.reshape(12 * ROWS, 512)
    noise = noise_sample.reshape(12 * ROWS, 512)

    def pack_all(name, shards, rows):
        widths = tuple((9 if item.ndim == 3 else 1, size) for item, size in zip(shards, rows))
        total = sum(taps * size for taps, size in widths)
        (packed,) = run(
            name,
            functools.partial(lambda scal, *refs: pack(widths, *refs)),
            [shape(total, 128, dtype=BF16)],
            scal,
            *shards,
            scratch=[((total, 128), F32)],
        )
        return gather_packed(packed)

    fine_o, coarse_o = input_kernel.shape[1], down_kernel.shape[1]
    early = pack_all(
        "pack_first",
        [input_kernel, first_kernel, embed_matrix],
        [fine_o, fine_o, embed_matrix.shape[0]],
    )
    far = shape(32, FAR * 512, dtype=BF16)
    own, edge_a, edge_b, line_a, line_b = run(
        "enter",
        enter,
        [shape(32, ROWS * 512, dtype=BF16), far, far, shape(16, 512), shape(16, 512)],
        scal,
        target,
        condition,
        noise,
        scratch=[((4, 192, 128), F32)],
    )
    got_a, got_b = swap(edge_a, edge_b)
    line_a, line_b = swap(line_a, line_b)
    late = pack_all(
        "pack_rest",
        [second_kernel, down_kernel, coarse_kernel, upward_kernel, output_kernel],
        [fine_o, coarse_o, coarse_o, fine_o, 16],
    )
    vector = jnp.broadcast_to(embedded[None, :], (16, embedded.shape[0]))
    win, wfirst, wfirst_t, shift = run(
        "prepare_first",
        functools.partial(prepare_first, embedded.shape[0]),
        [
            shape(384, 128, dtype=BF16), shape(384, 256, dtype=BF16),
            shape(256, 384, dtype=BF16), shape(128, 128),
        ],
        scal,
        vector, *early,
    )
    (
        wsecond, wsecond_t, wdown, wdown_t, wcoarse, wcoarse_t, wup, wup_t, wout, wout_t
    ) = run(
        "prepare_rest",
        prepare_rest,
        [
            shape(384, 256, dtype=BF16), shape(256, 384, dtype=BF16),
            shape(384, 192, dtype=BF16), shape(192, 384, dtype=BF16),
            shape(384, 384, dtype=BF16), shape(384, 384, dtype=BF16),
            shape(384, 512, dtype=BF16), shape(512, 384, dtype=BF16),
            shape(96, 256, dtype=BF16), shape(256, 96, dtype=BF16),
        ],
        scal,
        *late,
    )

    def rows_of(number, channels=128, dtype=F32):
        return shape(number, channels, HALF, dtype=dtype)

    stat = shape(bands, 8, 128)
    act_a, stats_a, kept_in = run(
        "stage_a",
        stage_a,
        [rows_of(20), stat, rows_of(10, dtype=BF16)],
        scal,
        win, got_a, got_b, own,
        scratch=[((32, FAR * 512), BF16), ((32, FAR * 512), BF16)],
    )
    stats_a = sum_parts(stats_a)
    act_b, stats_b, kept_a = run(
        "stage_b",
        functools.partial(stage_b, members),
        [rows_of(18), stat, rows_of(8, 256, BF16)],
        scal,
        stats_a, shift, wfirst, act_a,
    )
    stats_b = sum_parts(stats_b)
    fine, act_c, edge, stats_c, kept_b, kept_pool = run(
        "stage_c",
        functools.partial(stage_c, members),
        [
            rows_of(16), rows_of(6), shape(128, 2 * HALF), stat,
            rows_of(8, 256, BF16), rows_of(4, 192, BF16),
        ],
        scal,
        stats_b, wsecond, act_b, act_a, wdown,
    )
    got_a, got_b = swap(edge, edge)
    stats_c = sum_parts(stats_c)
    merged, wide_c, stats_d, kept_c, kept_up = run(
        "stage_d",
        functools.partial(stage_d, members_c),
        [rows_of(14), rows_of(8), stat, rows_of(4, 384, BF16), rows_of(4, 384, BF16)],
        scal,
        stats_c, wcoarse, got_a, got_b, act_c, wup, fine,
        scratch=[((128, 10 * HALF), F32)],
    )
    stats_d = sum_parts(stats_d)
    denoised, back_d, edge_a, edge_b, stats_ed, grad_out = run(
        "stage_out",
        functools.partial(stage_out, members),
        [
            shape(96, 512), rows_of(8),
            shape(128, 3 * HALF, dtype=BF16), shape(128, 3 * HALF, dtype=BF16), stat,
            shape(48, 192, dtype=BF16),
        ],
        scal,
        stats_d, wout, merged, line_a, line_b, target, noise, wout_t,
        scratch=[
            ((160, 512), F32), ((160, 512), F32), ((96, 8 * HALF), BF16), ((256, 8 * HALF), BF16),
            ((4, 96, 128), F32), ((4, 96, 128), F32), ((4, 96, 128), F32),
        ],
    )
    got_a, got_b = swap(edge_a, edge_b)
    stats_ed = sum_parts(stats_ed)
    grad_merged, back_c, grad_coarse, edge_a, edge_b, stats_ec, grad_up, grad_c, loss = run(
        "stage_up",
        functools.partial(stage_up, members, members_c),
        [
            rows_of(12), rows_of(4), rows_of(6),
            shape(128, 3 * HALF, dtype=BF16), shape(128, 3 * HALF, dtype=BF16), stat,
            shape(192, 384, dtype=BF16), shape(384, 384, dtype=BF16), shape(8, 128),
        ],
        scal,
        stats_d, stats_ed, got_a, got_b, merged, back_d, wup_t, kept_up,
        stats_c, wide_c, wcoarse_t, kept_c,
        scratch=[
            ((384, 8 * HALF), BF16), ((384, 8 * HALF), BF16), ((384, 4 * HALF), BF16)
        ],
        flat=(11,),
    )
    got_a, got_b = swap(edge_a, edge_b)
    stats_ec = sum_parts(stats_ec)
    if count == 2:
        loss = loss + lax.ppermute(loss, "fsdp", [(0, 1), (1, 0)])
    else:
        loss = lax.psum(loss, "fsdp")
    grad_fine, back_b, stats_eb, grad_down, grad_second = run(
        "stage_down",
        functools.partial(stage_down, members, members_c),
        [
            rows_of(8), rows_of(10), stat,
            shape(384, 192, dtype=BF16), shape(192, 192, dtype=BF16),
        ],
        scal,
        stats_c, stats_ec, got_a, got_b, wide_c, back_c, grad_coarse,
        wdown_t, grad_merged, kept_pool, stats_b, wsecond_t, act_b, kept_b,
        scratch=[((384, 8 * HALF), BF16), ((384, 4 * HALF), BF16)],
        flat=(9, 13),
    )
    stats_eb = sum_parts(stats_eb)
    back_a, stats_ea, grad_first, cell_sums = run(
        "stage_first",
        functools.partial(stage_first, members),
        [rows_of(8), stat, shape(192, 192, dtype=BF16), shape(8, 128)],
        scal,
        stats_b, stats_eb, act_b, back_b, wfirst_t, stats_a, act_a, kept_a,
        scratch=[((384, 8 * HALF), BF16)],
        flat=(7,),
    )
    stats_ea = sum_parts(stats_ea)
    (grad_in,) = run(
        "stage_last",
        functools.partial(stage_last, members),
        [shape(192, 96, dtype=BF16)],
        scal,
        stats_a, stats_ea, act_a, back_a, grad_fine, kept_in,
        scratch=[((128, 8 * HALF), BF16)],
        flat=(5,),
    )

    loss_value = loss[0, 0] / members_all
    sums = cell_sums[0, :64] + cell_sums[0, 64:]
    embed_grad = (embedded.astype(F32)[:, None] * sums[None, :]).astype(BF16)

    def split(item, outs, ins, dim):
        width = item.shape[1] // 3
        taps = item.reshape(3, item.shape[0] // 3, 3, width)[:, :outs, :, :ins]
        taps = jnp.transpose(taps, (0, 2, 1, 3)).reshape(9, outs, ins)
        if dim == 1:
            parts = taps.reshape(9, count, outs // count, ins)
            return jnp.moveaxis(parts, 1, 0).reshape(count, -1)
        parts = taps.reshape(9, outs, count, ins // count)
        return jnp.moveaxis(parts, 2, 0).reshape(count, -1)

    done = reduce_gradients(
        [
            split(grad_in, 64, 24, 1),
            split(grad_first, 64, 64, 1),
            split(grad_second, 64, 64, 1),
            split(grad_down, 128, 64, 1),
            split(grad_c, 128, 128, 1),
            split(grad_up, 64, 128, 1),
            split(grad_out, 12, 64, 2),
            embed_grad.reshape(count, -1),
        ]
    )
    kernels = (
        input_kernel, first_kernel, second_kernel, down_kernel,
        coarse_kernel, upward_kernel, output_kernel, embed_matrix,
    )
    shards = [item.astype(F32).reshape(like.shape) for item, like in zip(done, kernels)]
    return (denoised.reshape(residual_target.shape), loss_value, *shards)


def solution(mesh):
    in_specs = (
        P("fsdp", None, "rows", None),
        P("fsdp", None, "rows", None),
        P("fsdp", None, "rows", None),
        P("fsdp"),
        P(None, "fsdp", None),
        P(None, "fsdp", None),
        P(None, "fsdp", None),
        P(None, "fsdp", None),
        P(None, "fsdp", None),
        P(None, "fsdp", None),
        P(None, None, "fsdp"),
        P("fsdp", None),
    )
    out_specs = (
        P("fsdp", None, "rows", None),
        P(),
        P(None, "fsdp", None),
        P(None, "fsdp", None),
        P(None, "fsdp", None),
        P(None, "fsdp", None),
        P(None, "fsdp", None),
        P(None, "fsdp", None),
        P(None, None, "fsdp"),
        P("fsdp", None),
    )
    return jax.shard_map(
        per_device, mesh=mesh, in_specs=in_specs, out_specs=out_specs, check_vma=False
    )
```

```python
import functools

import jax
import jax.numpy as jnp
from jax import lax
from jax.experimental import pallas as pl
from jax.experimental.pallas import tpu as pltpu
from jax.sharding import PartitionSpec as P

GROUPS = 32
STEPS = 64

sigma_low = 0.002
sigma_high = 80.0
sigma_data = 0.5
rho_power = 7.0
eps_norm = 1e-05

F32 = jnp.float32
BF16 = jnp.bfloat16

HALF = 256
ROWS = 8
CROWS = 4
FAR = 7
LIMIT = 24 * 1024 * 1024


def preconditions(level_index):
    ramp_value = level_index.astype(jnp.float32) / (STEPS - 1)
    top_root = sigma_high ** (1.0 / rho_power)
    bottom = sigma_low ** (1.0 / rho_power)
    sigma_level = (top_root + ramp_value * (bottom - top_root)) ** rho_power
    sigma_total = sigma_level * sigma_level + sigma_data * sigma_data
    skip_scale = sigma_data * sigma_data / sigma_total
    out_scale = sigma_level * sigma_data * lax.rsqrt(sigma_total)
    in_scale = lax.rsqrt(sigma_total)
    weight = sigma_total / (sigma_level * sigma_data) ** 2
    return (sigma_level, skip_scale, out_scale, in_scale, weight)


def embedding(sigma_level, features):
    half_count = features // 2
    ramp_steps = jnp.arange(half_count, dtype=jnp.float32) / half_count
    frequency = 64.0 * 0.01**ramp_steps
    phase_angle = 0.25 * jnp.log(sigma_level) * frequency
    return jnp.concatenate([jnp.cos(phase_angle), jnp.sin(phase_angle)]).astype(jnp.bfloat16)


class Source:
    def __init__(self, spot, copies, first):
        self.spot, self.copies, self.first = spot, copies, first
        self.shape = spot.shape
        for _, copy in copies:
            copy.start()

    def wait(self, stage):
        for when, copy in self.copies:
            if when == stage:
                copy.wait()


class Sink:
    def __init__(self, spot, copies, first):
        self.spot, self.copies, self.first = spot, copies, first
        self.shape = spot.shape
        self.started = []

    def done(self, index):
        for last, copy in self.copies:
            if last == index:
                copy.start()
                self.started.append(copy)

    def finish(self):
        for _, copy in self.copies:
            if not any(copy is other for other in self.started):
                copy.start()
                self.started.append(copy)


def spot(ref, index):
    if len(ref.shape) == 3:
        return (index - getattr(ref, "first", 0),)
    start = index - getattr(ref, "first", 0)
    return (slice(None), slice(start * HALF, (start + 1) * HALF))


def row(ref, index):
    return getattr(ref, "spot", ref)[spot(ref, index)]


def put(ref, index, value):
    getattr(ref, "spot", ref)[spot(ref, index)] = value
    if isinstance(ref, Sink):
        ref.done(index)


def whole(ref):
    return ref.spot[...]


def give(ref, value):
    ref.spot[...] = value
    ref.finish()


def lane(shape):
    return lax.broadcasted_iota(jnp.int32, shape, 1)


def from_left(value):
    moved = pltpu.roll(value, 1, 1)
    return jnp.where(lane(value.shape) == 0, 0.0, moved)


def from_right(value):
    moved = pltpu.roll(value, value.shape[1] - 1, 1)
    return jnp.where(lane(value.shape) == value.shape[1] - 1, 0.0, moved)


def mm(left, right):
    return jnp.dot(left, right, preferred_element_type=F32)


def mm_nt(left, right):
    return lax.dot_general(left, right, (((1,), (1,)), ((), ())), preferred_element_type=F32)


def fine_taps(value):
    half = value.shape[0] // 2
    even, odd = value[:half], value[half:]
    return jnp.concatenate([from_left(odd), value, from_right(even)], axis=0).astype(BF16)


def coarse_taps(value):
    return jnp.concatenate([from_left(value), value, from_right(value)], axis=0).astype(BF16)


def fine_untap(taps):
    size = taps.shape[0] // 4
    even = taps[size : 2 * size] + from_left(taps[3 * size :])
    odd = taps[2 * size : 3 * size] + from_right(taps[:size])
    return jnp.concatenate([even, odd], axis=0)


def coarse_untap(taps):
    size = taps.shape[0] // 3
    return taps[size : 2 * size] + from_right(taps[:size]) + from_left(taps[2 * size :])


def spread(parts, first, last):
    out = {}
    for i in range(first, last + 1):
        size = parts[i - 1].shape[0] // 3
        out[i] = parts[i - 1][:size] + parts[i][size : 2 * size] + parts[i + 1][2 * size :]
    return out


def stack_rows(g, r):
    return jnp.concatenate([g[r + 1], g[r], g[r - 1]], axis=0)


def same_group(size, fine):
    left = lax.broadcasted_iota(jnp.int32, (size, size), 0)
    right = lax.broadcasted_iota(jnp.int32, (size, size), 1)
    if fine:
        half = size // 2
        left, right = left % half, right % half
        per = half // GROUPS
    else:
        per = size // GROUPS
    return left // per == right // per


def total_stats(stats):
    total = stats.spot[0]
    for index in range(1, stats.shape[0]):
        total = total + stats.spot[index]
    return total


def group_sums(stats, fine):
    total = total_stats(stats)
    member = same_group(128, fine)
    first = jnp.sum(jnp.where(member, total[0:1, :], 0.0), axis=1, keepdims=True)
    second = jnp.sum(jnp.where(member, total[1:2, :], 0.0), axis=1, keepdims=True)
    return first, second


def norm_columns(stats_ref, fine, members):
    first, second = group_sums(stats_ref, fine)
    mean = first / members
    inverse = lax.rsqrt(second / members - mean * mean + eps_norm)
    return mean, inverse


def back_columns(stats_ref, fine, members):
    first, second = group_sums(stats_ref, fine)
    return first / members, second / members


def to_row(column):
    size = column.shape[0]
    diagonal = lax.broadcasted_iota(jnp.int32, (size, size), 0) == lax.broadcasted_iota(
        jnp.int32, (size, size), 1
    )
    return jnp.sum(jnp.where(diagonal, column, 0.0), axis=0, keepdims=True)


def put_stats(ref, first, second, third=None):
    first = to_row(jnp.sum(first, axis=1, keepdims=True))
    second = to_row(jnp.sum(second, axis=1, keepdims=True))
    if third is None:
        third = jnp.zeros((1, 128), F32)
    block = jnp.concatenate([first, second, third, jnp.zeros((5, 128), F32)], axis=0)
    for index in range(ref.shape[0]):
        ref.spot[index] = block
    ref.finish()


def silu(h):
    return h * (1.0 / (1.0 + jnp.exp(-h)))


def silu_slope(h):
    s = 1.0 / (1.0 + jnp.exp(-h))
    return s * (1.0 + h * (1.0 - s))


def masked(value, index, rows, scal):
    if index < 0:
        return value * scal[6]
    if index >= rows:
        return value * scal[7]
    return value


def pick(scal, when_odd, when_even):
    return jnp.where(scal[8] > 0.5, when_odd, when_even)


def spill(ref, value):
    for t in range(4):
        ref[t, : value.shape[0], :] = value[:, 128 * t : 128 * (t + 1)]


def strided(ref, index, size):
    return jnp.concatenate(
        [ref[t, pl.ds(index, size, stride=ROWS), :] for t in range(4)], axis=1
    )


def interleave(transposed):
    left = lax.broadcasted_iota(jnp.int32, (512, 512), 0)
    right = lax.broadcasted_iota(jnp.int32, (512, 512), 1)
    if transposed:
        left, right = right, left
    place = (left & 1) * HALF + (left >> 1)
    return jnp.where(place == right, 1.0, 0.0).astype(BF16)


def fine_grad(blocks, outs, ins):
    parts = []
    for a in range(3):
        even = blocks[(2 * a) * outs : (2 * a + 1) * outs]
        odd = blocks[(2 * a + 1) * outs : (2 * a + 2) * outs]
        parts.append(even[:, : 3 * ins] + odd[:, ins : 4 * ins])
    return parts


def grad_blocks(parts, ins):
    if ins == 128:
        return [part[:, 128 * b : 128 * (b + 1)] for part in parts for b in range(3)]
    if ins == 64:
        blank = jnp.zeros(parts[0][:, :64].shape, F32)
        blocks = [part[:, :128] for part in parts]
        blocks.append(jnp.concatenate([parts[0][:, 128:192], parts[1][:, 128:192]], axis=1))
        blocks.append(jnp.concatenate([parts[2][:, 128:192], blank], axis=1))
        return blocks
    return parts


def put_grad(ref, start, blocks, split=True):
    count = ref.shape[0]
    size = blocks[0].shape[0] // count if split else blocks[0].shape[0]
    for block in blocks:
        for f in range(count):
            piece = block[f * size : (f + 1) * size] if split else block
            ref.spot[f, start : start + size, :] = piece.astype(BF16)
        start += size
    return start


def clear_rest(ref, start):
    count, size, _ = ref.shape
    if start < size:
        for f in range(count):
            ref.spot[f, start:, :] = jnp.zeros((size - start, 128), BF16)


def place(width, target, offset):
    left = lax.broadcasted_iota(jnp.int32, (width, target), 0)
    right = lax.broadcasted_iota(jnp.int32, (width, target), 1)
    return jnp.where(left + offset == right, 1.0, 0.0).astype(BF16)


def flipped(value):
    size = value.shape[1]
    return mm_nt(place(size, size, 0), value).astype(BF16)


def tap_of(pieces, offset, index, size):
    each = size // len(pieces)
    start = offset + index * each
    return jnp.concatenate([piece[start : start + each, :] for piece in pieces], axis=0).astype(
        BF16
    )


def in_order(scal, pieces):
    if len(pieces) == 2:
        mine, other = whole(pieces[0]), whole(pieces[1])
        low = scal[9] > 0.5
        return [jnp.where(low, mine, other), jnp.where(low, other, mine)]
    return [whole(piece) for piece in pieces]


def fine_matrix(taps, slot):
    rows = []
    for a in range(3):
        total = None
        for b in range(3):
            spread_out = jnp.concatenate(
                [place(slot, 4 * slot, b * slot), place(slot, 4 * slot, (b + 1) * slot)], axis=1
            )
            term = mm(taps[3 * a + b][:, :slot], spread_out)
            total = term if total is None else total + term
        rows += [total[:, : 4 * slot], total[:, 4 * slot :]]
    return jnp.concatenate(rows, axis=0).astype(BF16)


def pack(widths, scal, *refs):
    shards, (out, scratch) = refs[: len(widths)], refs[-2:]
    scratch[...] = jnp.zeros(scratch.shape, F32)
    start = 0
    for shard, (taps, rows) in zip(shards, widths):
        if taps == 1:
            scratch[start : start + rows, : shard.shape[1]] = whole(shard)
            start += rows
        else:
            for t in range(taps):
                value = shard.spot[t]
                scratch[start : start + value.shape[0], : value.shape[1]] = value
                start += rows
    give(out, scratch[...].astype(BF16))


def prepare_first(embed_size, scal, vec, *refs):
    pieces, (win, wfirst, wfirst_t, shift) = refs[:-4], refs[-4:]
    count = len(pieces)
    pieces = in_order(scal, pieces)
    each = 9 * (64 // count)
    give(win, fine_matrix([tap_of(pieces, 0, t, 64) for t in range(9)], 32))
    first = fine_matrix([tap_of(pieces, each, t, 64) for t in range(9)], 64)
    give(wfirst, first)
    give(wfirst_t, flipped(first))
    line = mm(whole(vec), tap_of(pieces, 2 * each, 0, embed_size))[0:1, :64]
    both = jnp.concatenate([line, line], axis=1)
    diagonal = place(128, 128, 0).astype(F32)
    column = jnp.sum(diagonal * both, axis=1, keepdims=True)
    give(shift, jnp.broadcast_to(column, (128, 128)))


def prepare_rest(scal, *refs):
    pieces = refs[:-10]
    wsecond, wsecond_t, wdown, wdown_t, wcoarse, wcoarse_t, wup, wup_t, wout, wout_t = refs[-10:]
    count = len(pieces)
    pieces = in_order(scal, pieces)
    start = 0

    def taps_of(size):
        nonlocal start
        taps = [tap_of(pieces, start, t, size) for t in range(9)]
        start += 9 * (size // count)
        return taps

    def both(value, forward, backward):
        give(forward, value)
        give(backward, flipped(value))

    both(fine_matrix(taps_of(64), 64), wsecond, wsecond_t)
    taps = taps_of(128)
    rows = []
    for a in range(3):
        total = None
        for b in range(3):
            term = mm(taps[3 * a + b][:, :64], place(64, 256, 64 * b))
            total = term if total is None else total + term
        rows.append(total)
    both(jnp.concatenate(rows, axis=0)[:, :192].astype(BF16), wdown, wdown_t)
    taps = taps_of(128)
    rows = [jnp.concatenate(taps[3 * a : 3 * a + 3], axis=1) for a in range(3)]
    both(jnp.concatenate(rows, axis=0), wcoarse, wcoarse_t)
    taps = taps_of(64)
    rows = []
    blank = jnp.zeros((64, 128), BF16)
    for a in range(3):
        rows.append(jnp.concatenate(taps[3 * a : 3 * a + 3] + [blank], axis=1))
        rows.append(jnp.concatenate([blank] + taps[3 * a : 3 * a + 3], axis=1))
    both(jnp.concatenate(rows, axis=0), wup, wup_t)
    taps = []
    width = 64 // count
    for t in range(9):
        total = None
        for s in range(count):
            tap = pieces[s][start + 16 * t : start + 16 * (t + 1), :].astype(BF16)
            term = mm(tap[:, :width], place(width, 128, s * width))
            total = term if total is None else total + term
        taps.append(total.astype(BF16))
    both(fine_matrix(taps, 64), wout, wout_t)


def enter(scal, target, condition, noise, own, edge_a, edge_b, line_a, line_b, scratch):
    sigma, skip, in_scale = scal[0], scal[1], scal[3]
    goal = whole(target)
    noisy = goal + sigma * whole(noise)
    q = skip * noisy - goal
    natural = jnp.concatenate([in_scale * noisy, whole(condition)], axis=0).astype(BF16)
    spill(scratch, mm(natural, interleave(False)))
    blank = jnp.zeros((8, 512), F32)
    for i in range(ROWS):
        value = strided(scratch, i, 24)
        own.spot[:, i * 512 : (i + 1) * 512] = jnp.concatenate([value, blank], axis=0).astype(BF16)
    top, low = own.spot[:, : FAR * 512], own.spot[:, (ROWS - FAR) * 512 :]
    give(edge_a, pick(scal, top, low))
    give(edge_b, pick(scal, low, top))
    own.finish()
    spill(scratch, q)
    blank = jnp.zeros((4, 512), F32)
    top = jnp.concatenate([strided(scratch, 0, 12), blank], axis=0)
    low = jnp.concatenate([strided(scratch, ROWS - 1, 12), blank], axis=0)
    give(line_a, pick(scal, top, low))
    give(line_b, pick(scal, low, top))


def stage_a(scal, win, got_a, got_b, own, act, stats, kept, above, below):
    above[...] = pick(scal, whole(got_a), whole(got_b))
    below[...] = pick(scal, whole(got_b), whole(got_a))
    weights = whole(win)
    parts = {}
    total = jnp.zeros((128, HALF), F32)
    square = jnp.zeros((128, HALF), F32)
    for r in range(-FAR, ROWS + FAR):
        if r < 0:
            value = above[:, (r + FAR) * 512 : (r + FAR + 1) * 512]
        elif r < ROWS:
            value = own.spot[:, r * 512 : (r + 1) * 512]
        else:
            value = below[:, (r - ROWS) * 512 : (r - ROWS + 1) * 512]
        value = value.astype(F32)
        z = fine_taps(jnp.concatenate([value[:, :HALF], value[:, HALF:]], axis=0))
        if -1 <= r <= ROWS:
            put(kept, r, z)
        parts[r] = mm(weights, z)
        i = r - 1
        if i > -FAR:
            value = spread(parts, i, i)[i]
            put(act, i, value)
            del parts[i - 1]
            if 0 <= i < ROWS:
                total = total + value
                square = square + value * value
    put_stats(stats, total, square)


def stage_b(members, scal, stats_a, shift, wfirst, act_a, act_b, stats, kept, hats, passed, sem):
    passing = pltpu.make_async_copy(act_a.spot.at[pl.ds(2, 16)], passed.spot, sem)
    passing.start()
    mean, inverse = norm_columns(stats_a, True, members)
    lift = shift.spot[:, 0:1]
    weights = whole(wfirst)
    parts = {}
    total = jnp.zeros((128, HALF), F32)
    square = jnp.zeros((128, HALF), F32)
    for r in range(-6, ROWS + 6):
        hat = (row(act_a, r) - mean) * inverse
        z = fine_taps(masked(silu(hat), r, ROWS, scal))
        if 0 <= r < ROWS:
            put(kept, r, z)
            put(hats, r, hat.astype(BF16))
        parts[r] = mm(weights, z)
        i = r - 1
        if i > -6:
            value = spread(parts, i, i)[i] + lift
            put(act_b, i, value)
            del parts[i - 1]
            if 0 <= i < ROWS:
                total = total + value
                square = square + value * value
    put_stats(stats, total, square)
    passing.wait()


def stage_c(
    members, scal, stats_b, wsecond, act_b, act_a, wdown,
    fine, act_c, edge, stats, kept, kept_pool, hats,
):
    mean, inverse = norm_columns(stats_b, True, members)
    weights = whole(wsecond)
    parts = {}
    pooled = {}
    half = {}
    for r in range(-5, ROWS + 5):
        hat = (row(act_b, r) - mean) * inverse
        z = fine_taps(masked(silu(hat), r, ROWS, scal))
        if 0 <= r < ROWS:
            put(kept, r, z)
        if -1 <= r <= ROWS:
            put(hats, r, hat.astype(BF16))
        parts[r] = mm(weights, z)
        i = r - 1
        if i > -5:
            value = spread(parts, i, i)[i] + row(act_a, i)
            if -3 <= i < ROWS + 3:
                put(fine, i, value)
            del parts[i - 1]
            half[i] = value[:64] + value[64:]
            if i % 2:
                value = 0.25 * (half.pop(i - 1) + half.pop(i))
                value = masked(value, i // 2, CROWS, scal)
                pooled[i // 2] = value.astype(BF16).astype(F32)
    weights = whole(wdown)
    parts = {}
    total = jnp.zeros((128, HALF), F32)
    square = jnp.zeros((128, HALF), F32)
    for r in range(-2, CROWS + 2):
        z = coarse_taps(pooled[r])
        if 0 <= r < CROWS:
            put(kept_pool, r, z)
        parts[r] = mm(weights, z)
        i = r - 1
        if i > -2:
            value = spread(parts, i, i)[i]
            put(act_c, i, value)
            del parts[i - 1]
            if 0 <= i < CROWS:
                total = total + value
                square = square + value * value
            if i in (1, 2):
                put(edge, i, value)
    put_stats(stats, total, square)


def stage_d(
    members, scal, stats_c, wcoarse, got_a, got_b, act_c, wup, fine,
    merged, hats, stats, kept_c, kept_up,
):
    mean, inverse = norm_columns(stats_c, False, members)
    ring = {}
    for j in range(2):
        ring[j - 3] = pick(scal, row(got_a, j), row(got_b, j))
        ring[CROWS + 1 + j] = pick(scal, row(got_b, j), row(got_a, j))
    for j in range(-1, CROWS + 1):
        ring[j] = row(act_c, j)
    weights = whole(wcoarse)
    parts = {}
    lifted = {}
    for r in range(-3, CROWS + 3):
        hat = (ring[r] - mean) * inverse
        z = coarse_taps(masked(silu(hat), r, CROWS, scal))
        if 0 <= r < CROWS:
            put(kept_c, r, z)
        if -2 <= r < CROWS + 2:
            put(hats, r, hat.astype(BF16))
        parts[r] = mm(weights, z)
        i = r - 1
        if i > -3:
            value = spread(parts, i, i)[i] + ring[i]
            del parts[i - 1]
            lifted[i] = masked(value, i, CROWS, scal).astype(BF16).astype(F32)
    weights = whole(wup)
    parts = {}
    total = jnp.zeros((128, HALF), F32)
    square = jnp.zeros((128, HALF), F32)
    for r in range(-2, CROWS + 2):
        z = coarse_taps(lifted[r])
        if 0 <= r < CROWS:
            put(kept_up, r, z)
        four = jnp.concatenate([z[:128], z[128:256], z[128:256], z[256:]], axis=0)
        parts[2 * r] = parts[2 * r + 1] = mm(weights, four)
        for i in (2 * r - 1, 2 * r):
            if i >= -3:
                value = spread(parts, i, i)[i] + row(fine, i)
                put(merged, i, value)
                parts.pop(i - 1)
                if 0 <= i < ROWS:
                    total = total + value
                    square = square + value * value
    put_stats(stats, total, square)


def stage_out(
    members, scal, stats_d, wout, merged, line_a, line_b, target, noise, wout_t,
    denoised, back, edge_a, edge_b, stats, grad, hats, pairs, cells, gs, zs,
    goals, noisies, found,
):
    sigma, skip, out_scale, weight, coef = scal[0], scal[1], scal[2], scal[4], scal[5]
    mean, inverse = norm_columns(stats_d, True, members)
    weights = whole(wout)
    parts = {}
    hat_of = {}
    for r in range(-3, ROWS + 3):
        hat = (row(merged, r) - mean) * inverse
        put(hats, r, hat.astype(BF16))
        if r == -3 or r == ROWS + 2:
            continue
        z = fine_taps(masked(silu(hat), r, ROWS, scal))
        if 0 <= r < ROWS:
            put(zs, r, z)
        parts[r] = mm(weights, z)
        i = r - 1
        if i > -2:
            value = spread(parts, i, i)[i]
            del parts[i - 1]
            pairs[16 * (i + 1) : 16 * (i + 2), :] = jnp.concatenate(
                [value[:16], value[16:]], axis=1
            )
    value = pairs[...]
    high = value.astype(BF16)
    low = (value - high.astype(F32)).astype(BF16)
    back_order = interleave(True)
    pairs[...] = mm(high, back_order) + mm(low, back_order)
    blank = jnp.zeros((4, 512), F32)
    loss_sum = jnp.zeros((12, 512), F32)
    top = pick(scal, whole(line_a), whole(line_b)) + out_scale * pairs[0:16, :]
    cells[0:16, :] = coef * scal[6] * top
    low = pick(scal, whole(line_b), whole(line_a)) + out_scale * pairs[16 * (ROWS + 1) :, :]
    cells[16 * (ROWS + 1) :, :] = coef * scal[7] * low
    spill(goals, whole(target))
    spill(noisies, whole(target) + sigma * whole(noise))
    for i in range(ROWS):
        goal = strided(goals, i, 12)
        noisy = strided(noisies, i, 12)
        estimate = skip * noisy + out_scale * pairs[16 * (i + 1) : 16 * (i + 1) + 12, :]
        for t in range(4):
            found[t, pl.ds(i, 12, stride=ROWS), :] = estimate[:, 128 * t : 128 * (t + 1)]
        mismatch = estimate - goal
        loss_sum = loss_sum + weight * mismatch * mismatch
        cells[16 * (i + 1) : 16 * (i + 2), :] = jnp.concatenate([coef * mismatch, blank], axis=0)
    give(denoised, jnp.concatenate([found[t] for t in range(4)], axis=1))
    loss_sum = jnp.broadcast_to(
        jnp.sum(jnp.sum(loss_sum, axis=1, keepdims=True), axis=0, keepdims=True), (1, 128)
    )
    pairs[...] = mm(cells[...].astype(BF16), interleave(False))
    g = {}
    for i in range(-1, ROWS + 1):
        value = pairs[16 * (i + 1) : 16 * (i + 2), :]
        g[i] = jnp.concatenate([value[:, :HALF], value[:, HALF:]], axis=0).astype(BF16)
    weights = whole(wout_t)
    total = jnp.zeros((128, HALF), F32)
    cross = jnp.zeros((128, HALF), F32)
    for r in range(ROWS):
        rows = stack_rows(g, r)
        put(gs, r, rows)
        value = fine_untap(mm(weights, rows))
        put(back, r, value.astype(BF16))
        hat = row(hats, r).astype(F32)
        e = value * silu_slope(hat)
        total = total + e
        cross = cross + e * hat
    for j in range(3):
        top, low = row(back, j), row(back, ROWS - 3 + j)
        put(edge_a, j, pick(scal, top, low))
        put(edge_b, j, pick(scal, low, top))
    put_stats(stats, total, cross, loss_sum)
    parts = fine_grad(mm_nt(gs[...], zs[...]), 16, 64)
    put_grad(grad, 0, grad_blocks(parts, 64), split=False)


def stage_up(
    members, members_c, scal, stats_d, stats_ed, got_a, got_b, hats, back, wup_t, stats_c, hats_c,
    wcoarse_t, kept_up, kept_c, grad_out,
    grad_merged, back_c, grad_coarse, edge_a, edge_b, stats, loss, grads, gs, zs, gc,
):
    give(loss, jnp.broadcast_to(total_stats(stats_ed)[2:3, :], (8, 128)))
    mean, inverse = norm_columns(stats_d, True, members)
    shift, slope = back_columns(stats_ed, True, members)
    g = {}
    for r in range(-3, ROWS + 3):
        hat = row(hats, r).astype(F32)
        if r < 0:
            u = pick(scal, row(got_a, r + 3), row(got_b, r + 3)).astype(F32)
        elif r < ROWS:
            u = row(back, r).astype(F32)
        else:
            u = pick(scal, row(got_b, r - ROWS), row(got_a, r - ROWS)).astype(F32)
        value = inverse * (u * silu_slope(hat) - shift - hat * slope)
        g[r] = masked(value, r, ROWS, scal).astype(BF16)
        if -2 <= r < ROWS + 2:
            put(grad_merged, r, g[r])
    weights = whole(wup_t)
    gk = {}
    half = {}
    for r in range(-2, ROWS + 2):
        rows = stack_rows(g, r)
        if 0 <= r < ROWS:
            put(gs, r, rows)
        taps = mm(weights, rows)
        half[r] = taps[128:256] + taps[256:384] + from_right(taps[:128]) + from_left(taps[384:])
        if r % 2:
            value = masked(half.pop(r - 1) + half.pop(r), r // 2, CROWS, scal)
            gk[r // 2] = value.astype(BF16)
            put(grad_coarse, r // 2, gk[r // 2])
    weights = whole(wcoarse_t)
    mean, inverse = norm_columns(stats_c, False, members_c)
    total = jnp.zeros((128, HALF), F32)
    cross = jnp.zeros((128, HALF), F32)
    for r in range(CROWS):
        rows = stack_rows(gk, r)
        put(gc, r, rows)
        value = coarse_untap(mm(weights, rows))
        put(back_c, r, value.astype(BF16))
        hat = row(hats_c, r).astype(F32)
        e = value * silu_slope(hat)
        total = total + e
        cross = cross + e * hat
    top = [row(back_c, 0), row(back_c, 1), gk[1]]
    low = [row(back_c, 2), row(back_c, 3), gk[2]]
    for j in range(3):
        put(edge_a, j, pick(scal, top[j], low[j]))
        put(edge_b, j, pick(scal, low[j], top[j]))
    put_stats(stats, total, cross)
    kept_up.wait(1)
    kept_c.wait(1)
    grad_out.wait(1)
    for r in range(ROWS):
        put(zs, r, row(kept_up, r // 2))
    blocks = mm_nt(gs[...], zs[...])
    parts = []
    for a in range(3):
        even = blocks[128 * a : 128 * a + 64]
        odd = blocks[128 * a + 64 : 128 * a + 128]
        parts.append(
            jnp.concatenate(
                [
                    even[:, :128] + odd[:, 128:256],
                    even[:, 128:256] + odd[:, 128:256],
                    even[:, 128:256] + odd[:, 256:],
                ],
                axis=1,
            )
        )
    start = put_grad(grads, 0, grad_blocks(parts, 128))
    blocks = mm_nt(gc[...], whole(kept_c))
    parts = [blocks[128 * a : 128 * (a + 1)] for a in range(3)]
    start = put_grad(grads, start, grad_blocks(parts, 128))
    for f in range(grads.shape[0]):
        grads.spot[f, start : start + 80, :] = grad_out.spot[f]
    clear_rest(grads, start + 80)


def stage_down(
    members, members_c, scal, stats_c, stats_ec, got_a, got_b, hats_c, back_c, grad_coarse,
    wdown_t, grad_merged, stats_b, wsecond_t, hats, kept_pool, kept_b,
    grad_fine, back_b, stats, grads, gs, gc,
):
    mean, inverse = norm_columns(stats_c, False, members_c)
    shift, slope = back_columns(stats_ec, False, members_c)
    g = {}
    for r in range(-2, CROWS + 2):
        hat = row(hats_c, r).astype(F32)
        if r < 0:
            u = pick(scal, row(got_a, r + 2), row(got_b, r + 2)).astype(F32)
        elif r < CROWS:
            u = row(back_c, r).astype(F32)
        else:
            u = pick(scal, row(got_b, r - CROWS), row(got_a, r - CROWS)).astype(F32)
        if r == -2:
            through = pick(scal, row(got_a, 2), row(got_b, 2)).astype(F32)
        elif r == CROWS + 1:
            through = pick(scal, row(got_b, 2), row(got_a, 2)).astype(F32)
        else:
            through = row(grad_coarse, r).astype(F32)
        value = through + inverse * (u * silu_slope(hat) - shift - hat * slope)
        g[r] = masked(value, r, CROWS, scal).astype(BF16)
    weights = whole(wdown_t)
    fine = {}
    for r in range(-1, CROWS + 1):
        rows = stack_rows(g, r)
        if 0 <= r < CROWS:
            put(gc, r, rows)
        value = 0.25 * coarse_untap(mm(weights, rows))
        both = jnp.concatenate([value, value], axis=0)
        for i in (2 * r, 2 * r + 1):
            value = masked(row(grad_merged, i).astype(F32) + both, i, ROWS, scal)
            fine[i] = value.astype(BF16)
            if 0 <= i < ROWS:
                put(grad_fine, i, fine[i])
    weights = whole(wsecond_t)
    mean, inverse = norm_columns(stats_b, True, members)
    total = jnp.zeros((128, HALF), F32)
    cross = jnp.zeros((128, HALF), F32)
    for r in range(-1, ROWS + 1):
        rows = stack_rows(fine, r)
        value = fine_untap(mm(weights, rows))
        put(back_b, r, value.astype(BF16))
        if 0 <= r < ROWS:
            put(gs, r, rows)
            hat = row(hats, r).astype(F32)
            e = value * silu_slope(hat)
            total = total + e
            cross = cross + e * hat
    put_stats(stats, total, cross)
    kept_pool.wait(1)
    kept_b.wait(1)
    blocks = mm_nt(gc[...], whole(kept_pool))
    parts = [blocks[128 * a : 128 * (a + 1)] for a in range(3)]
    start = put_grad(grads, 0, grad_blocks(parts, 64))
    parts = fine_grad(mm_nt(gs[...], whole(kept_b)), 64, 64)
    clear_rest(grads, put_grad(grads, start, grad_blocks(parts, 64)))


def stage_first(
    members, scal, stats_b, stats_eb, hats_b, back_b, wfirst_t, stats_a, hats, vec, kept_a,
    back_a, stats, grads, gs,
):
    mean, inverse = norm_columns(stats_b, True, members)
    shift, slope = back_columns(stats_eb, True, members)
    g = {}
    sums = jnp.zeros((128, HALF), F32)
    for r in range(-1, ROWS + 1):
        hat = row(hats_b, r).astype(F32)
        u = row(back_b, r).astype(F32)
        value = inverse * (u * silu_slope(hat) - shift - hat * slope)
        if 0 <= r < ROWS:
            sums = sums + value
        g[r] = masked(value, r, ROWS, scal).astype(BF16)
    weights = whole(wfirst_t)
    total = jnp.zeros((128, HALF), F32)
    cross = jnp.zeros((128, HALF), F32)
    for r in range(ROWS):
        rows = stack_rows(g, r)
        put(gs, r, rows)
        value = fine_untap(mm(weights, rows))
        put(back_a, r, value.astype(BF16))
        hat = row(hats, r).astype(F32)
        e = value * silu_slope(hat)
        total = total + e
        cross = cross + e * hat
    put_stats(stats, total, cross)
    kept_a.wait(1)
    parts = fine_grad(mm_nt(gs[...], whole(kept_a)), 64, 64)
    start = put_grad(grads, 0, grad_blocks(parts, 64))
    line = to_row(jnp.sum(sums, axis=1, keepdims=True))
    line = line + pltpu.roll(line, 64, 1)
    column = jnp.sum(place(128, 128, 0).astype(F32) * vec.spot[0:1, :].astype(F32), axis=1, keepdims=True)
    outer = (column * line).astype(BF16)
    size = 128 // grads.shape[0]
    for f in range(grads.shape[0]):
        grads.spot[f, start : start + size, :] = outer[f * size : (f + 1) * size]


def stage_last(
    members, scal, stats_a, stats_ea, hats, back_a, grad_fine, kept_in, early, middle, first,
    loss, loss_other, grads, loss_sum, gs, sems,
):
    copies, start = [], 0
    for index, ref in enumerate((early, middle)):
        rows = pl.ds(start, ref.shape[1])
        copies.append(
            pltpu.make_async_copy(ref.spot, grads.spot.at[:, rows, :], sems.at[index])
        )
        copies[index].start()
        start += ref.shape[1]
    give(loss_sum, whole(loss) + whole(loss_other))
    mean, inverse = norm_columns(stats_a, True, members)
    shift, slope = back_columns(stats_ea, True, members)
    for r in range(ROWS):
        hat = row(hats, r).astype(F32)
        u = row(back_a, r).astype(F32)
        value = row(grad_fine, r).astype(F32) + inverse * (
            u * silu_slope(hat) - shift - hat * slope
        )
        put(gs, r, value.astype(BF16))
    parts = []
    for a in range(3):
        blocks = mm_nt(gs[...], kept_in.spot[:, a * HALF : (a + ROWS) * HALF])
        parts.append(
            jnp.concatenate(
                [blocks[:64, :96] + blocks[64:, 32:128], jnp.zeros((64, 32), F32)], axis=1
            )
        )
    size = first.shape[1]
    for f in range(grads.shape[0]):
        grads.spot[f, start : start + size, :] = first.spot[f]
    clear_rest(grads, put_grad(grads, start + size, parts))
    for copy in copies:
        copy.wait()


def add_up(scal, got, out):
    total = got.spot[0].astype(F32)
    for index in range(1, got.shape[0]):
        total = total + got.spot[index].astype(F32)
    total = total.astype(BF16)
    for index in range(out.shape[0]):
        out.spot[index] = total


def unpack(starts, scal, got, *refs):
    first, down, second, coarse, up, out, embed, inputs, flat = refs
    size = got.shape[1]
    for index in range(got.shape[0]):
        flat[index * size : (index + 1) * size, :] = got.spot[index].astype(F32)

    def take(ref, start, out, size, ins):
        for t in range(9):
            a, b = t // 3, t % 3
            if ins == 128:
                at, lanes = t, 0
            elif ins == 64:
                at, lanes = (a, b) if b < 2 else (3 + a // 2, a % 2)
            else:
                at, lanes = a, b
            step = 32 if ins == 24 else ins
            value = ref[start + at * size : start + (at + 1) * size, :]
            rows = out.shape[1]
            out.spot[t] = value[:rows, lanes * step : lanes * step + ins]
        return start + (9 if ins == 128 else 5 if ins == 64 else 3) * size

    start = take(flat, 0, up, up.shape[1], 128)
    start = take(flat, start, coarse, coarse.shape[1], 128)
    take(flat, start, out, 16, 64)
    start = take(flat, starts[0], down, down.shape[1], 64)
    take(flat, start, second, second.shape[1], 64)
    start = take(flat, starts[1], first, first.shape[1], 64)
    size = embed.shape[0]
    give(embed, flat[start : start + size, :64])
    take(flat, start + size, inputs, inputs.shape[1], 24)


class Field:
    def __init__(self, array, first):
        self.array, self.first = array, first


class Saved:
    def __init__(self, item, low=None, high=None, when=0):
        self.item, self.low, self.high, self.when = item, low, high, when


def shape(*dims, dtype=F32):
    return jax.ShapeDtypeStruct(dims, dtype)


def rows_of(first, number, dtype=F32):
    return Field(shape(number, 128, HALF, dtype=dtype), first)


def flat_rows(first, number, channels):
    return Field(shape(channels, number * HALF, dtype=BF16), first)


def opened(item):
    saved = item if isinstance(item, Saved) else None
    item = saved.item if saved else item
    if isinstance(item, Field):
        return saved, item.array, item.first
    return saved, item, 0


def run(name, kernel, outs, scal, *operands, scratch=()):
    vmem, hbm = pl.BlockSpec(memory_space=pltpu.VMEM), pl.BlockSpec(memory_space=pltpu.HBM)
    in_specs, arrays, plans, spots = [pl.BlockSpec(memory_space=pltpu.SMEM)], [scal], [], []
    for item in operands:
        saved, item, first = opened(item)
        if saved is None:
            in_specs.append(vmem)
            arrays.append(item)
            plans.append((first, None, None))
            continue
        part = None
        dims = item.shape
        if saved.low is not None:
            part = pl.ds(saved.low - first, saved.high - saved.low)
            dims = (saved.high - saved.low,) + dims[1:]
            first = saved.low
        in_specs.append(hbm)
        arrays.append(pltpu.with_memory_space_constraint(item, pltpu.HBM))
        if saved.when is None:
            plans.append((first, None, None))
            continue
        plans.append((first, (saved.when, part), len(spots)))
        spots.append(pltpu.VMEM(dims, item.dtype))
    ins = len(operands)
    out_specs, out_shapes = [], []
    for item in outs:
        saved, item, first = opened(item)
        if saved is None:
            out_specs.append(vmem)
            out_shapes.append(item)
            plans.append((first, None, None))
            continue
        out_specs.append(hbm)
        out_shapes.append(pltpu.HBM(item.shape, item.dtype))
        last = None
        if isinstance(saved.item, Field):
            count = item.shape[0] if len(item.shape) == 3 else item.shape[1] // HALF
            last = first + count - 1
        if saved.when is None:
            plans.append((first, None, None))
            continue
        plans.append((first, (last, None), len(spots)))
        spots.append(pltpu.VMEM(item.shape, item.dtype))

    def body(numbers, *refs):
        given, refs = refs[: len(plans)], refs[len(plans) :]
        held, refs = refs[: len(spots)], refs[len(spots) :]
        sems, extra = refs[0], refs[1:]
        wrapped = []
        for index, (ref, (first, plan, place_at)) in enumerate(zip(given, plans)):
            copies = []
            if plan is not None:
                where = held[place_at]
                when, part = plan
                if index < ins:
                    source = ref if part is None else ref.at[part]
                    copies.append((when, pltpu.make_async_copy(source, where, sems.at[place_at])))
                else:
                    copies.append((when, pltpu.make_async_copy(where, ref, sems.at[place_at])))
                ref = where
            wrapped.append((Source if index < ins else Sink)(ref, copies, first))
        for item in wrapped[:ins]:
            item.wait(0)
        kernel(numbers, *wrapped, *extra)
        for item in wrapped[ins:]:
            item.finish()
        for item in wrapped[ins:]:
            for copy in item.started:
                copy.wait()

    made = pl.pallas_call(
        body,
        out_shape=tuple(out_shapes),
        in_specs=in_specs,
        out_specs=tuple(out_specs),
        scratch_shapes=spots
        + [pltpu.SemaphoreType.DMA((max(len(spots), 1),))]
        + [pltpu.VMEM(*item) if isinstance(item, tuple) else item for item in scratch],
        compiler_params=pltpu.CompilerParams(vmem_limit_bytes=LIMIT),
        name=name,
    )(*arrays)
    results = []
    for array, item in zip(made, outs):
        item = item.item if isinstance(item, Saved) else item
        results.append(Field(array, item.first) if isinstance(item, Field) else array)
    return results


def sum_parts(stats):
    return lax.all_to_all(stats, "rows", 0, 0)


def swap(value_a, value_b):
    count = lax.axis_size("rows")
    pairs = [(i, i ^ 1) for i in range(count)]
    across = []
    for i in range(1, count - 1, 2):
        across += [(i, i + 1), (i + 1, i)]
    return lax.ppermute(value_a, "rows", pairs), lax.ppermute(value_b, "rows", across)


def gather_packed(packed):
    if lax.axis_size("fsdp") == 2:
        return [packed, lax.ppermute(packed, "fsdp", [(0, 1), (1, 0)])]
    whole = lax.all_gather(packed, "fsdp").astype(F32)
    return [whole[i] for i in range(whole.shape[0])]


def group_shape(rows, count):
    return shape(count, -(-rows // 16) * 16, 128, dtype=BF16)


def per_device(
    residual_target,
    conditioning,
    noise_sample,
    noise_level,
    input_kernel,
    first_kernel,
    second_kernel,
    down_kernel,
    coarse_kernel,
    upward_kernel,
    output_kernel,
    embed_matrix,
):
    bands, count = lax.axis_size("rows"), lax.axis_size("fsdp")
    members = 2 * ROWS * 2 * HALF * bands
    members_c = 4 * CROWS * HALF * bands
    members_all = count * residual_target.size * bands
    me = lax.axis_index("rows")
    sigma_level, skip_scale, out_scale, in_scale, weight = preconditions(noise_level[0])
    coef = 2.0 * weight * out_scale / members_all
    scal = jnp.stack(
        [
            sigma_level,
            skip_scale,
            out_scale,
            in_scale,
            weight,
            coef,
            (me > 0).astype(F32),
            (me < bands - 1).astype(F32),
            (me % 2).astype(F32),
            (lax.axis_index("fsdp") == 0).astype(F32),
        ]
    )
    embedded = embedding(sigma_level, embed_matrix.shape[0] * count)
    target = residual_target.reshape(12 * ROWS, 512)
    condition = conditioning.reshape(12 * ROWS, 512)
    noise = noise_sample.reshape(12 * ROWS, 512)

    def pack_all(name, shards, rows, *after):
        widths = tuple((9 if item.ndim == 3 else 1, size) for item, size in zip(shards, rows))
        total = sum(taps * size for taps, size in widths)
        (packed,) = run(
            name,
            functools.partial(pack, widths),
            [shape(total, 128, dtype=BF16)],
            scal,
            *[Saved(item) for item in shards],
            *after,
            scratch=[((total, 128), F32)],
        )
        return gather_packed(packed)

    fine_o, coarse_o = input_kernel.shape[1], down_kernel.shape[1]
    early = pack_all(
        "pack_first",
        [input_kernel, first_kernel, embed_matrix],
        [fine_o, fine_o, embed_matrix.shape[0]],
    )
    far = shape(32, FAR * 512, dtype=BF16)
    own, edge_a, edge_b, line_a, line_b = run(
        "enter",
        enter,
        [shape(32, ROWS * 512, dtype=BF16), far, far, shape(16, 512), shape(16, 512)],
        scal,
        Saved(target),
        Saved(condition),
        Saved(noise),
        scratch=[((4, 192, 128), F32)],
    )
    got_a, got_b = swap(edge_a, edge_b)
    line_a, line_b = swap(line_a, line_b)
    vector = jnp.broadcast_to(embedded[None, :], (16, embedded.shape[0]))
    win, wfirst, wfirst_t, shift = run(
        "prepare_first",
        functools.partial(prepare_first, embedded.shape[0]),
        [
            shape(384, 128, dtype=BF16), Saved(shape(384, 256, dtype=BF16)),
            Saved(shape(256, 384, dtype=BF16)), shape(128, 128),
        ],
        scal,
        vector, *early,
    )
    stat = shape(bands, 8, 128)
    act_a, stats_a, kept_in = run(
        "stage_a",
        stage_a,
        [rows_of(-6, 20), stat, Saved(flat_rows(-1, 10, 128))],
        scal,
        win, got_a, got_b, own,
        scratch=[((32, FAR * 512), BF16), ((32, FAR * 512), BF16)],
    )
    rest = pack_all(
        "pack_rest",
        [second_kernel, down_kernel, coarse_kernel, upward_kernel, output_kernel],
        [fine_o, coarse_o, coarse_o, fine_o, 16],
        stats_a,
    )
    (
        wsecond, wsecond_t, wdown, wdown_t, wcoarse, wcoarse_t, wup, wup_t, wout, wout_t
    ) = run(
        "prepare_rest",
        prepare_rest,
        [
            Saved(shape(384, 256, dtype=BF16)), Saved(shape(256, 384, dtype=BF16)),
            Saved(shape(384, 192, dtype=BF16)), Saved(shape(192, 384, dtype=BF16)),
            Saved(shape(384, 384, dtype=BF16)), Saved(shape(384, 384, dtype=BF16)),
            Saved(shape(384, 512, dtype=BF16)), Saved(shape(512, 384, dtype=BF16)),
            Saved(shape(96, 256, dtype=BF16)), Saved(shape(256, 96, dtype=BF16)),
        ],
        scal,
        *rest,
    )

    stats_a = sum_parts(stats_a)
    act_b, stats_b, kept_a, hats_a, act_a = run(
        "stage_b",
        functools.partial(stage_b, members),
        [
            rows_of(-5, 18), stat, Saved(flat_rows(0, 8, 256)), Saved(rows_of(0, 8, BF16)),
            Saved(rows_of(-4, 16), when=None),
        ],
        scal,
        stats_a, shift, Saved(wfirst), act_a,
        scratch=[pltpu.SemaphoreType.DMA(())],
    )
    stats_b = sum_parts(stats_b)
    fine, act_c, edge, stats_c, kept_b, kept_pool, hats_b = run(
        "stage_c",
        functools.partial(stage_c, members),
        [
            rows_of(-3, 14), rows_of(-1, 6), Field(shape(128, 2 * HALF), 1), stat,
            Saved(flat_rows(0, 8, 256)), Saved(flat_rows(0, 4, 192)), Saved(rows_of(-1, 10, BF16)),
        ],
        scal,
        stats_b, Saved(wsecond), act_b, Saved(act_a), Saved(wdown),
    )
    got_a, got_b = swap(edge.array, edge.array)
    stats_c = sum_parts(stats_c)
    merged, hats_c, stats_d, kept_c, kept_up = run(
        "stage_d",
        functools.partial(stage_d, members_c),
        [
            rows_of(-3, 14), Saved(rows_of(-2, 8, BF16)), stat,
            Saved(flat_rows(0, 4, 384)), Saved(flat_rows(0, 4, 384)),
        ],
        scal,
        stats_c, Saved(wcoarse), got_a, got_b, act_c, Saved(wup), fine,
    )
    stats_d = sum_parts(stats_d)
    edge = Field(shape(128, 3 * HALF, dtype=BF16), 0)
    denoised, back_d, edge_a, edge_b, stats_ed, grad_out, hats_d = run(
        "stage_out",
        functools.partial(stage_out, members),
        [
            Saved(shape(96, 512)), rows_of(0, 8, BF16), edge, edge, stat,
            Saved(shape(count, 80, 128, dtype=BF16)), rows_of(-3, 14, BF16),
        ],
        scal,
        stats_d, Saved(wout), merged, Saved(line_a), Saved(line_b), Saved(target), Saved(noise),
        Saved(wout_t),
        scratch=[
            ((160, 512), F32), ((160, 512), F32), ((96, 8 * HALF), BF16), ((256, 8 * HALF), BF16),
            ((4, 96, 128), F32), ((4, 96, 128), F32), ((4, 96, 128), F32),
        ],
    )
    got_a, got_b = swap(edge_a.array, edge_b.array)
    stats_ed = sum_parts(stats_ed)
    grad_merged, back_c, grad_coarse, edge_a, edge_b, stats_ec, loss, early = run(
        "stage_up",
        functools.partial(stage_up, members, members_c),
        [
            rows_of(-2, 12, BF16), rows_of(0, 4, BF16), rows_of(-1, 6, BF16), edge, edge, stat,
            shape(8, 128), Saved(group_shape(9 * (fine_o + coarse_o) + 80, count)),
        ],
        scal,
        stats_d, stats_ed, got_a, got_b, hats_d, back_d, Saved(wup_t), stats_c, Saved(hats_c),
        Saved(wcoarse_t), Saved(kept_up, when=1), Saved(kept_c, when=1), Saved(grad_out, when=1),
        scratch=[
            ((384, 8 * HALF), BF16), ((384, 8 * HALF), BF16), ((384, 4 * HALF), BF16)
        ],
    )
    got_a, got_b = swap(edge_a.array, edge_b.array)
    stats_ec = sum_parts(stats_ec)
    if count == 2:
        loss_other = lax.ppermute(loss, "fsdp", [(0, 1), (1, 0)])
    else:
        loss_other = lax.psum(loss, "fsdp") - loss
    grad_fine, back_b, stats_eb, middle = run(
        "stage_down",
        functools.partial(stage_down, members, members_c),
        [
            Saved(rows_of(0, 8, BF16)), rows_of(-1, 10, BF16), stat,
            Saved(group_shape(5 * (fine_o + coarse_o), count)),
        ],
        scal,
        stats_c, stats_ec, got_a, got_b, Saved(hats_c), back_c, grad_coarse,
        Saved(wdown_t), grad_merged, stats_b, Saved(wsecond_t), Saved(hats_b, 0, 8),
        Saved(kept_pool, when=1), Saved(kept_b, when=1),
        scratch=[((384, 8 * HALF), BF16), ((384, 4 * HALF), BF16)],
    )
    stats_eb = sum_parts(stats_eb)
    back_a, stats_ea, grad_first = run(
        "stage_first",
        functools.partial(stage_first, members),
        [
            rows_of(0, 8, BF16), stat,
            Saved(shape(count, 5 * fine_o + embed_matrix.shape[0], 128, dtype=BF16)),
        ],
        scal,
        stats_b, stats_eb, Saved(hats_b), back_b, Saved(wfirst_t), stats_a, Saved(hats_a), vector,
        Saved(kept_a, when=1),
        scratch=[((384, 8 * HALF), BF16)],
    )
    stats_ea = sum_parts(stats_ea)
    late = group_shape(8 * fine_o + embed_matrix.shape[0], count)
    starts = [early.shape[1], early.shape[1] + middle.shape[1]]
    total = starts[1] + late.shape[1]
    chunk = -(-total // (16 * bands)) * 16
    grads, loss = run(
        "stage_last",
        functools.partial(stage_last, members),
        [shape(count, chunk * bands, 128, dtype=BF16), shape(8, 128)],
        scal,
        stats_a, stats_ea, Saved(hats_a), back_a, Saved(grad_fine), Saved(kept_in),
        Saved(early, when=None), Saved(middle, when=None), Saved(grad_first), loss, loss_other,
        scratch=[((128, 8 * HALF), BF16), pltpu.SemaphoreType.DMA((2,))],
    )
    loss_value = loss[0, 0] / members_all
    got = lax.all_to_all(grads.reshape(count * bands, chunk, 128), ("fsdp", "rows"), 0, 0)
    (mine,) = run("add_up", add_up, [shape(bands, chunk, 128, dtype=BF16)], scal, got)
    got = lax.all_to_all(mine, "rows", 0, 0)
    first_g, down_g, second_g, coarse_g, up_g, out_g, embed_g, in_g = run(
        "unpack",
        functools.partial(unpack, starts),
        [
            shape(*first_kernel.shape),
            shape(*down_kernel.shape),
            shape(*second_kernel.shape),
            shape(*coarse_kernel.shape),
            shape(*upward_kernel.shape),
            shape(9, 12, 64),
            shape(*embed_matrix.shape),
            shape(*input_kernel.shape),
        ],
        scal,
        got,
        scratch=[((chunk * bands, 128), F32)],
    )
    width = output_kernel.shape[2]
    out_g = lax.dynamic_slice_in_dim(out_g, lax.axis_index("fsdp") * width, width, axis=2)
    return (
        denoised.reshape(residual_target.shape),
        loss_value,
        in_g,
        first_g,
        second_g,
        down_g,
        coarse_g,
        up_g,
        out_g,
        embed_g,
    )


def solution(mesh):
    in_specs = (
        P("fsdp", None, "rows", None),
        P("fsdp", None, "rows", None),
        P("fsdp", None, "rows", None),
        P("fsdp"),
        P(None, "fsdp", None),
        P(None, "fsdp", None),
        P(None, "fsdp", None),
        P(None, "fsdp", None),
        P(None, "fsdp", None),
        P(None, "fsdp", None),
        P(None, None, "fsdp"),
        P("fsdp", None),
    )
    out_specs = (
        P("fsdp", None, "rows", None),
        P(),
        P(None, "fsdp", None),
        P(None, "fsdp", None),
        P(None, "fsdp", None),
        P(None, "fsdp", None),
        P(None, "fsdp", None),
        P(None, "fsdp", None),
        P(None, None, "fsdp"),
        P("fsdp", None),
    )
    return jax.shard_map(
        per_device, mesh=mesh, in_specs=in_specs, out_specs=out_specs, check_vma=False
    )
```

```python
import functools

import jax
import jax.numpy as jnp
from jax import lax
from jax.experimental import pallas as pl
from jax.experimental.pallas import tpu as pltpu
from jax.sharding import PartitionSpec as P

GROUPS = 32
STEPS = 64

sigma_low = 0.002
sigma_high = 80.0
sigma_data = 0.5
rho_power = 7.0
eps_norm = 1e-05

F32 = jnp.float32
BF16 = jnp.bfloat16

HALF = 256
ROWS = 8
CROWS = 4
FAR = 7
LIMIT = 24 * 1024 * 1024


def preconditions(level_index):
    ramp_value = level_index.astype(jnp.float32) / (STEPS - 1)
    top_root = sigma_high ** (1.0 / rho_power)
    bottom = sigma_low ** (1.0 / rho_power)
    sigma_level = (top_root + ramp_value * (bottom - top_root)) ** rho_power
    sigma_total = sigma_level * sigma_level + sigma_data * sigma_data
    skip_scale = sigma_data * sigma_data / sigma_total
    out_scale = sigma_level * sigma_data * lax.rsqrt(sigma_total)
    in_scale = lax.rsqrt(sigma_total)
    weight = sigma_total / (sigma_level * sigma_data) ** 2
    return (sigma_level, skip_scale, out_scale, in_scale, weight)


def embedding(sigma_level, features):
    half_count = features // 2
    ramp_steps = jnp.arange(half_count, dtype=jnp.float32) / half_count
    frequency = 64.0 * 0.01**ramp_steps
    phase_angle = 0.25 * jnp.log(sigma_level) * frequency
    return jnp.concatenate([jnp.cos(phase_angle), jnp.sin(phase_angle)]).astype(jnp.bfloat16)


class Source:
    def __init__(self, spot, copies, first):
        self.spot, self.copies, self.first = spot, copies, first
        self.shape = spot.shape
        for _, copy in copies:
            copy.start()

    def wait(self, stage):
        for when, copy in self.copies:
            if when == stage:
                copy.wait()


class Sink:
    def __init__(self, spot, copies, first):
        self.spot, self.copies, self.first = spot, copies, first
        self.shape = spot.shape
        self.started = []

    def done(self, index):
        for last, copy in self.copies:
            if last == index:
                copy.start()
                self.started.append(copy)

    def finish(self):
        for _, copy in self.copies:
            if not any(copy is other for other in self.started):
                copy.start()
                self.started.append(copy)


def spot(ref, index):
    if len(ref.shape) == 3:
        return (index - getattr(ref, "first", 0),)
    start = index - getattr(ref, "first", 0)
    return (slice(None), slice(start * HALF, (start + 1) * HALF))


def row(ref, index):
    return getattr(ref, "spot", ref)[spot(ref, index)]


def put(ref, index, value):
    getattr(ref, "spot", ref)[spot(ref, index)] = value
    if isinstance(ref, Sink):
        ref.done(index)


def whole(ref):
    return ref.spot[...]


def give(ref, value):
    ref.spot[...] = value
    ref.finish()


def lane(shape):
    return lax.broadcasted_iota(jnp.int32, shape, 1)


def from_left(value):
    moved = pltpu.roll(value, 1, 1)
    return jnp.where(lane(value.shape) == 0, 0.0, moved)


def from_right(value):
    moved = pltpu.roll(value, value.shape[1] - 1, 1)
    return jnp.where(lane(value.shape) == value.shape[1] - 1, 0.0, moved)


def mm(left, right):
    return jnp.dot(left, right, preferred_element_type=F32)


def mm_nt(left, right):
    return lax.dot_general(left, right, (((1,), (1,)), ((), ())), preferred_element_type=F32)


def fine_taps(value):
    half = value.shape[0] // 2
    even, odd = value[:half], value[half:]
    return jnp.concatenate([from_left(odd), value, from_right(even)], axis=0).astype(BF16)


def coarse_taps(value):
    return jnp.concatenate([from_left(value), value, from_right(value)], axis=0).astype(BF16)


def fine_untap(taps):
    size = taps.shape[0] // 4
    even = taps[size : 2 * size] + from_left(taps[3 * size :])
    odd = taps[2 * size : 3 * size] + from_right(taps[:size])
    return jnp.concatenate([even, odd], axis=0)


def coarse_untap(taps):
    size = taps.shape[0] // 3
    return taps[size : 2 * size] + from_right(taps[:size]) + from_left(taps[2 * size :])


def spread(parts, first, last):
    out = {}
    for i in range(first, last + 1):
        size = parts[i - 1].shape[0] // 3
        out[i] = parts[i - 1][:size] + parts[i][size : 2 * size] + parts[i + 1][2 * size :]
    return out


def stack_rows(g, r):
    return jnp.concatenate([g[r + 1], g[r], g[r - 1]], axis=0)


def same_group(size, fine):
    left = lax.broadcasted_iota(jnp.int32, (size, size), 0)
    right = lax.broadcasted_iota(jnp.int32, (size, size), 1)
    if fine:
        half = size // 2
        left, right = left % half, right % half
        per = half // GROUPS
    else:
        per = size // GROUPS
    return left // per == right // per


def total_stats(stats):
    total = stats.spot[0]
    for index in range(1, stats.shape[0]):
        total = total + stats.spot[index]
    return total


def group_sums(stats, fine):
    total = total_stats(stats)
    member = same_group(128, fine)
    first = jnp.sum(jnp.where(member, total[0:1, :], 0.0), axis=1, keepdims=True)
    second = jnp.sum(jnp.where(member, total[1:2, :], 0.0), axis=1, keepdims=True)
    return first, second


def norm_columns(stats_ref, fine, members):
    first, second = group_sums(stats_ref, fine)
    mean = first / members
    inverse = lax.rsqrt(second / members - mean * mean + eps_norm)
    return mean, inverse


def back_columns(stats_ref, fine, members):
    first, second = group_sums(stats_ref, fine)
    return first / members, second / members


def to_row(column):
    size = column.shape[0]
    diagonal = lax.broadcasted_iota(jnp.int32, (size, size), 0) == lax.broadcasted_iota(
        jnp.int32, (size, size), 1
    )
    return jnp.sum(jnp.where(diagonal, column, 0.0), axis=0, keepdims=True)


def put_stats(ref, first, second, third=None):
    first = to_row(jnp.sum(first, axis=1, keepdims=True))
    second = to_row(jnp.sum(second, axis=1, keepdims=True))
    if third is None:
        third = jnp.zeros((1, 128), F32)
    block = jnp.concatenate([first, second, third, jnp.zeros((5, 128), F32)], axis=0)
    for index in range(ref.shape[0]):
        ref.spot[index] = block
    ref.finish()


def silu(h):
    t = 0.5 * h
    return t + t * jnp.tanh(t)


def silu_slope(h):
    s = 0.5 + 0.5 * jnp.tanh(0.5 * h)
    return s * (1.0 + h * (1.0 - s))


def masked(value, index, rows, scal):
    if index < 0:
        return value * scal[6]
    if index >= rows:
        return value * scal[7]
    return value


def pick(scal, when_odd, when_even):
    return jnp.where(scal[8] > 0.5, when_odd, when_even)


def spill(ref, value):
    for t in range(4):
        ref[t, : value.shape[0], :] = value[:, 128 * t : 128 * (t + 1)]


def strided(ref, index, size):
    return jnp.concatenate(
        [ref[t, pl.ds(index, size, stride=ROWS), :] for t in range(4)], axis=1
    )


def interleave(transposed):
    left = lax.broadcasted_iota(jnp.int32, (512, 512), 0)
    right = lax.broadcasted_iota(jnp.int32, (512, 512), 1)
    if transposed:
        left, right = right, left
    place = (left & 1) * HALF + (left >> 1)
    return jnp.where(place == right, 1.0, 0.0).astype(BF16)


def fine_grad(blocks, outs, ins):
    parts = []
    for a in range(3):
        even = blocks[(2 * a) * outs : (2 * a + 1) * outs]
        odd = blocks[(2 * a + 1) * outs : (2 * a + 2) * outs]
        parts.append(even[:, : 3 * ins] + odd[:, ins : 4 * ins])
    return parts


def grad_blocks(parts, ins):
    if ins == 128:
        return [part[:, 128 * b : 128 * (b + 1)] for part in parts for b in range(3)]
    if ins == 64:
        blank = jnp.zeros(parts[0][:, :64].shape, F32)
        blocks = [part[:, :128] for part in parts]
        blocks.append(jnp.concatenate([parts[0][:, 128:192], parts[1][:, 128:192]], axis=1))
        blocks.append(jnp.concatenate([parts[2][:, 128:192], blank], axis=1))
        return blocks
    return parts


def put_grad(ref, start, blocks, split=True):
    count = ref.shape[0]
    size = blocks[0].shape[0] // count if split else blocks[0].shape[0]
    for block in blocks:
        for f in range(count):
            piece = block[f * size : (f + 1) * size] if split else block
            ref.spot[f, start : start + size, :] = piece.astype(BF16)
        start += size
    return start


def clear_rest(ref, start):
    count, size, _ = ref.shape
    if start < size:
        for f in range(count):
            ref.spot[f, start:, :] = jnp.zeros((size - start, 128), BF16)


def place(width, target, offset):
    left = lax.broadcasted_iota(jnp.int32, (width, target), 0)
    right = lax.broadcasted_iota(jnp.int32, (width, target), 1)
    return jnp.where(left + offset == right, 1.0, 0.0).astype(BF16)


def flipped(value):
    size = value.shape[1]
    return mm_nt(place(size, size, 0), value).astype(BF16)


def tap_of(pieces, offset, index, size):
    each = size // len(pieces)
    start = offset + index * each
    return jnp.concatenate([piece[start : start + each, :] for piece in pieces], axis=0).astype(
        BF16
    )


def in_order(scal, pieces):
    if len(pieces) == 2:
        mine, other = whole(pieces[0]), whole(pieces[1])
        low = scal[9] > 0.5
        return [jnp.where(low, mine, other), jnp.where(low, other, mine)]
    return [whole(piece) for piece in pieces]


def fine_matrix(taps, slot):
    rows = []
    for a in range(3):
        total = None
        for b in range(3):
            spread_out = jnp.concatenate(
                [place(slot, 4 * slot, b * slot), place(slot, 4 * slot, (b + 1) * slot)], axis=1
            )
            term = mm(taps[3 * a + b][:, :slot], spread_out)
            total = term if total is None else total + term
        rows += [total[:, : 4 * slot], total[:, 4 * slot :]]
    return jnp.concatenate(rows, axis=0).astype(BF16)


def pack(widths, scal, *refs):
    shards, (out, scratch) = refs[: len(widths)], refs[-2:]
    scratch[...] = jnp.zeros(scratch.shape, F32)
    start = 0
    for shard, (taps, rows, swapped) in zip(shards, widths):
        if taps == 1:
            scratch[start : start + rows, : shard.shape[1]] = whole(shard)
            start += rows
        else:
            for t in range(taps):
                value = shard.spot[t]
                if swapped:
                    value = mm_nt(place(value.shape[1], value.shape[1], 0), value.astype(BF16))
                scratch[start : start + value.shape[0], : value.shape[1]] = value
                start += rows
    give(out, scratch[...].astype(BF16))


def prepare_first(embed_size, scal, vec, *refs):
    pieces, (win, wfirst, wfirst_t, shift) = refs[:-4], refs[-4:]
    count = len(pieces)
    pieces = in_order(scal, pieces)
    each = 9 * (64 // count)
    give(win, fine_matrix([tap_of(pieces, 0, t, 64) for t in range(9)], 32))
    first = fine_matrix([tap_of(pieces, each, t, 64) for t in range(9)], 64)
    give(wfirst, first)
    give(wfirst_t, flipped(first))
    line = mm(whole(vec), tap_of(pieces, 2 * each, 0, embed_size))[0:1, :64]
    both = jnp.concatenate([line, line], axis=1)
    diagonal = place(128, 128, 0).astype(F32)
    column = jnp.sum(diagonal * both, axis=1, keepdims=True)
    give(shift, jnp.broadcast_to(column, (128, 128)))


def prepare_rest(scal, *refs):
    pieces = refs[:-10]
    wsecond, wsecond_t, wdown, wdown_t, wcoarse, wcoarse_t, wup, wup_t, wout, wout_t = refs[-10:]
    count = len(pieces)
    pieces = in_order(scal, pieces)
    start = 0

    def taps_of(size):
        nonlocal start
        taps = [tap_of(pieces, start, t, size) for t in range(9)]
        start += 9 * (size // count)
        return taps

    def both(value, forward, backward):
        give(forward, value)
        give(backward, flipped(value))

    both(fine_matrix(taps_of(64), 64), wsecond, wsecond_t)
    taps = taps_of(128)
    rows = []
    for a in range(3):
        total = None
        for b in range(3):
            term = mm(taps[3 * a + b][:, :64], place(64, 256, 64 * b))
            total = term if total is None else total + term
        rows.append(total)
    both(jnp.concatenate(rows, axis=0)[:, :192].astype(BF16), wdown, wdown_t)
    taps = taps_of(128)
    rows = [jnp.concatenate(taps[3 * a : 3 * a + 3], axis=1) for a in range(3)]
    both(jnp.concatenate(rows, axis=0), wcoarse, wcoarse_t)
    taps = taps_of(64)
    rows = []
    blank = jnp.zeros((64, 128), BF16)
    for a in range(3):
        rows.append(jnp.concatenate(taps[3 * a : 3 * a + 3] + [blank], axis=1))
        rows.append(jnp.concatenate([blank] + taps[3 * a : 3 * a + 3], axis=1))
    both(jnp.concatenate(rows, axis=0), wup, wup_t)
    taps = []
    width = 64 // count
    for t in range(9):
        total = None
        for s in range(count):
            tap = pieces[s][start + 16 * t : start + 16 * (t + 1), :].astype(BF16)
            term = mm(tap[:, :width], place(width, 128, s * width))
            total = term if total is None else total + term
        taps.append(total.astype(BF16))
    both(fine_matrix(taps, 64), wout, wout_t)


def enter(scal, target, condition, noise, done, own, edge_a, edge_b, scratch, marks):
    sigma, skip, in_scale = scal[0], scal[1], scal[3]
    goal = whole(target)
    noisy = goal + sigma * whole(noise)
    q = skip * noisy - goal
    natural = jnp.concatenate([in_scale * noisy, whole(condition)], axis=0).astype(BF16)
    spill(scratch, mm(natural, interleave(False)))
    blank = jnp.zeros((8, 512), F32)
    for i in range(ROWS):
        value = strided(scratch, i, 24)
        own.spot[:, i * 512 : (i + 1) * 512] = jnp.concatenate([value, blank], axis=0).astype(BF16)
    spill(scratch, q)
    blank = jnp.zeros((4, 512), F32)
    for j, i in enumerate((0, ROWS - 1)):
        rest = jnp.concatenate([strided(scratch, i, 12), blank], axis=0)
        marks[j] = jnp.zeros(marks.shape[1:], BF16)
        for part in range(3):
            piece = rest.astype(BF16)
            rest = rest - piece.astype(F32)
            for k in range(2):
                lanes = slice((2 * part + k) * 512, (2 * part + k + 1) * 512)
                marks[j, 8:, lanes] = piece[8 * k : 8 * k + 8]
    for j, edge in enumerate((edge_a, edge_b)):
        odd = scal[8] > 0.5 if j == 0 else scal[8] < 0.5
        low = (ROWS - FAR) * 512
        edge.spot[:16, :] = jnp.where(odd, own.spot[:16, : FAR * 512], own.spot[:16, low:])
        edge.spot[16:, :] = jnp.where(odd, own.spot[16:, : FAR * 512], own.spot[16:, low:]) + (
            jnp.where(odd, marks[0], marks[1])
        )


def marked(scal, got):
    halves = []
    for k in range(2):
        total = None
        for part in range(3):
            lanes = slice((2 * part + k) * 512, (2 * part + k + 1) * 512)
            piece = got.spot[16:32, lanes].astype(F32)[8:]
            total = piece if total is None else total + piece
        halves.append(total)
    return jnp.concatenate(halves, axis=0)


def stage_a(scal, win, got_a, got_b, own, done, act, stats, kept, line_a, line_b, above, below):
    give(line_a, marked(scal, got_a))
    give(line_b, marked(scal, got_b))
    above[...] = pick(scal, whole(got_a), whole(got_b))
    below[...] = pick(scal, whole(got_b), whole(got_a))
    clear = jnp.zeros((16, FAR * 512), BF16)
    keep = lax.broadcasted_iota(jnp.int32, (16, FAR * 512), 0) < 8
    for ref in (above, below):
        ref[16:, :] = jnp.where(keep, ref[16:, :], clear)
    weights = whole(win)
    parts = {}
    total = jnp.zeros((128, HALF), F32)
    square = jnp.zeros((128, HALF), F32)
    for r in range(-FAR, ROWS + FAR):
        if r < 0:
            value = above[:, (r + FAR) * 512 : (r + FAR + 1) * 512]
        elif r < ROWS:
            value = own.spot[:, r * 512 : (r + 1) * 512]
        else:
            value = below[:, (r - ROWS) * 512 : (r - ROWS + 1) * 512]
        value = value.astype(F32)
        z = fine_taps(jnp.concatenate([value[:, :HALF], value[:, HALF:]], axis=0))
        if -1 <= r <= ROWS:
            put(kept, r, z)
        parts[r] = mm(weights, z)
        i = r - 1
        if i > -FAR:
            value = spread(parts, i, i)[i]
            put(act, i, value)
            del parts[i - 1]
            if 0 <= i < ROWS:
                total = total + value
                square = square + value * value
    put_stats(stats, total, square)


def stage_b(members, scal, stats_a, shift, wfirst, act_a, act_b, stats, kept, hats, passed, totals, sem):
    give(totals, total_stats(stats_a)[None])
    passing = pltpu.make_async_copy(act_a.spot.at[pl.ds(2, 16)], passed.spot, sem)
    passing.start()
    mean, inverse = norm_columns(stats_a, True, members)
    lift = shift.spot[:, 0:1]
    parts = {}
    total = jnp.zeros((128, HALF), F32)
    square = jnp.zeros((128, HALF), F32)
    for r in range(-6, ROWS + 6):
        hat = (row(act_a, r) - mean) * inverse
        z = fine_taps(masked(silu(hat), r, ROWS, scal))
        if 0 <= r < ROWS:
            put(kept, r, z)
            put(hats, r, hat.astype(BF16))
        if r == -6:
            wfirst.wait(1)
        parts[r] = mm(whole(wfirst), z)
        i = r - 1
        if i > -6:
            value = spread(parts, i, i)[i] + lift
            put(act_b, i, value)
            del parts[i - 1]
            if 0 <= i < ROWS:
                total = total + value
                square = square + value * value
    put_stats(stats, total, square)
    passing.wait()


def stage_c(
    members, scal, stats_b, wsecond, act_b, act_a, wdown,
    fine, act_c, edge, stats, kept, kept_pool, hats, totals,
):
    give(totals, total_stats(stats_b)[None])
    mean, inverse = norm_columns(stats_b, True, members)
    parts = {}
    pooled = {}
    half = {}
    for r in range(-5, ROWS + 5):
        hat = (row(act_b, r) - mean) * inverse
        z = fine_taps(masked(silu(hat), r, ROWS, scal))
        if 0 <= r < ROWS:
            put(kept, r, z)
        if -1 <= r <= ROWS:
            put(hats, r, hat.astype(BF16))
        if r == -5:
            wsecond.wait(1)
        if r == -3:
            act_a.wait(1)
        parts[r] = mm(whole(wsecond), z)
        i = r - 1
        if i > -5:
            value = spread(parts, i, i)[i] + row(act_a, i)
            if -3 <= i < ROWS + 3:
                put(fine, i, value)
            del parts[i - 1]
            half[i] = value[:64] + value[64:]
            if i % 2:
                value = 0.25 * (half.pop(i - 1) + half.pop(i))
                value = masked(value, i // 2, CROWS, scal)
                pooled[i // 2] = value.astype(BF16).astype(F32)
    wdown.wait(1)
    weights = whole(wdown)
    parts = {}
    total = jnp.zeros((128, HALF), F32)
    square = jnp.zeros((128, HALF), F32)
    for r in range(-2, CROWS + 2):
        z = coarse_taps(pooled[r])
        if 0 <= r < CROWS:
            put(kept_pool, r, z)
        parts[r] = mm(weights, z)
        i = r - 1
        if i > -2:
            value = spread(parts, i, i)[i]
            put(act_c, i, value)
            del parts[i - 1]
            if 0 <= i < CROWS:
                total = total + value
                square = square + value * value
            if i in (1, 2):
                put(edge, i, value)
    put_stats(stats, total, square)


def stage_d(
    members, scal, stats_c, wcoarse, got_a, got_b, act_c, wup, fine,
    merged, hats, stats, kept_c, kept_up, totals,
):
    give(totals, total_stats(stats_c)[None])
    mean, inverse = norm_columns(stats_c, False, members)
    ring = {}
    for j in range(2):
        ring[j - 3] = pick(scal, row(got_a, j), row(got_b, j))
        ring[CROWS + 1 + j] = pick(scal, row(got_b, j), row(got_a, j))
    for j in range(-1, CROWS + 1):
        ring[j] = row(act_c, j)
    parts = {}
    lifted = {}
    for r in range(-3, CROWS + 3):
        hat = (ring[r] - mean) * inverse
        z = coarse_taps(masked(silu(hat), r, CROWS, scal))
        if 0 <= r < CROWS:
            put(kept_c, r, z)
        if -2 <= r < CROWS + 2:
            put(hats, r, hat.astype(BF16))
        if r == -3:
            wcoarse.wait(1)
        parts[r] = mm(whole(wcoarse), z)
        i = r - 1
        if i > -3:
            value = spread(parts, i, i)[i] + ring[i]
            del parts[i - 1]
            lifted[i] = masked(value, i, CROWS, scal).astype(BF16).astype(F32)
    wup.wait(1)
    weights = whole(wup)
    parts = {}
    total = jnp.zeros((128, HALF), F32)
    square = jnp.zeros((128, HALF), F32)
    for r in range(-2, CROWS + 2):
        z = coarse_taps(lifted[r])
        if 0 <= r < CROWS:
            put(kept_up, r, z)
        four = jnp.concatenate([z[:128], z[128:256], z[128:256], z[256:]], axis=0)
        parts[2 * r] = parts[2 * r + 1] = mm(weights, four)
        for i in (2 * r - 1, 2 * r):
            if i >= -3:
                value = spread(parts, i, i)[i] + row(fine, i)
                put(merged, i, value)
                parts.pop(i - 1)
                if 0 <= i < ROWS:
                    total = total + value
                    square = square + value * value
    put_stats(stats, total, square)


def stage_out(
    members, scal, stats_d, wout, merged, line_a, line_b, target, noise, wout_t,
    denoised, back, edge_a, edge_b, stats, hats, cotangents, zs, totals, pairs, cells,
    goals, noisies, found,
):
    give(totals, total_stats(stats_d)[None])
    sigma, skip, out_scale, weight, coef = scal[0], scal[1], scal[2], scal[4], scal[5]
    mean, inverse = norm_columns(stats_d, True, members)
    parts = {}
    for r in range(-3, ROWS + 3):
        hat = (row(merged, r) - mean) * inverse
        put(hats, r, hat.astype(BF16))
        if r == -3 or r == ROWS + 2:
            continue
        z = fine_taps(masked(silu(hat), r, ROWS, scal))
        if 0 <= r < ROWS:
            put(zs, r, z)
        if r == -2:
            wout.wait(1)
        parts[r] = mm(whole(wout), z)
        i = r - 1
        if i > -2:
            value = spread(parts, i, i)[i]
            del parts[i - 1]
            pairs[16 * (i + 1) : 16 * (i + 2), :] = jnp.concatenate(
                [value[:16], value[16:]], axis=1
            )
    value = pairs[...]
    high = value.astype(BF16)
    low = (value - high.astype(F32)).astype(BF16)
    back_order = interleave(True)
    for item in (line_a, line_b, target, noise, wout_t):
        item.wait(1)
    pairs[...] = mm(high, back_order) + mm(low, back_order)
    blank = jnp.zeros((4, 512), F32)
    loss_sum = jnp.zeros((12, 512), F32)
    top = pick(scal, whole(line_a), whole(line_b)) + out_scale * pairs[0:16, :]
    cells[0:16, :] = coef * scal[6] * top
    low = pick(scal, whole(line_b), whole(line_a)) + out_scale * pairs[16 * (ROWS + 1) :, :]
    cells[16 * (ROWS + 1) :, :] = coef * scal[7] * low
    spill(goals, whole(target))
    spill(noisies, whole(target) + sigma * whole(noise))
    for i in range(ROWS):
        goal = strided(goals, i, 12)
        noisy = strided(noisies, i, 12)
        estimate = skip * noisy + out_scale * pairs[16 * (i + 1) : 16 * (i + 1) + 12, :]
        for t in range(4):
            found[t, pl.ds(i, 12, stride=ROWS), :] = estimate[:, 128 * t : 128 * (t + 1)]
        mismatch = estimate - goal
        loss_sum = loss_sum + weight * mismatch * mismatch
        cells[16 * (i + 1) : 16 * (i + 2), :] = jnp.concatenate([coef * mismatch, blank], axis=0)
    give(denoised, jnp.concatenate([found[t] for t in range(4)], axis=1))
    loss_sum = jnp.broadcast_to(
        jnp.sum(jnp.sum(loss_sum, axis=1, keepdims=True), axis=0, keepdims=True), (1, 128)
    )
    pairs[...] = mm(cells[...].astype(BF16), interleave(False))
    g = {}
    for i in range(-1, ROWS + 1):
        value = pairs[16 * (i + 1) : 16 * (i + 2), :]
        g[i] = jnp.concatenate([value[:, :HALF], value[:, HALF:]], axis=0).astype(BF16)
        put(cotangents, i, g[i])
    weights = whole(wout_t)
    total = jnp.zeros((128, HALF), F32)
    cross = jnp.zeros((128, HALF), F32)
    for r in range(ROWS):
        value = fine_untap(mm(weights, stack_rows(g, r)))
        put(back, r, value.astype(BF16))
        hat = row(hats, r).astype(F32)
        e = value * silu_slope(hat)
        total = total + e
        cross = cross + e * hat
    for j in range(3):
        top, low = row(back, j), row(back, ROWS - 3 + j)
        put(edge_a, j, pick(scal, top, low))
        put(edge_b, j, pick(scal, low, top))
    put_stats(stats, total, cross, loss_sum)


def grads_out(scal, cotangents, zs, grad, gs):
    g = {r: row(cotangents, r) for r in range(-1, ROWS + 1)}
    for r in range(ROWS):
        put(gs, r, stack_rows(g, r))
    parts = fine_grad(mm_nt(gs[...], whole(zs)), 16, 64)
    put_grad(grad, 0, grad_blocks(parts, 64), split=False)


def grads_up(scal, grad_merged, grad_coarse, kept_up, kept_c, grad_out, grads, gs, zs, gc):
    g = {r: row(grad_merged, r) for r in range(-1, ROWS + 1)}
    for r in range(ROWS):
        put(gs, r, stack_rows(g, r))
        put(zs, r, row(kept_up, r // 2))
    g = {r: row(grad_coarse, r) for r in range(-1, CROWS + 1)}
    for r in range(CROWS):
        put(gc, r, stack_rows(g, r))
    blocks = mm_nt(gs[...], zs[...])
    parts = []
    for a in range(3):
        even = blocks[128 * a : 128 * a + 64]
        odd = blocks[128 * a + 64 : 128 * a + 128]
        parts.append(
            jnp.concatenate(
                [
                    even[:, :128] + odd[:, 128:256],
                    even[:, 128:256] + odd[:, 128:256],
                    even[:, 128:256] + odd[:, 256:],
                ],
                axis=1,
            )
        )
    start = put_grad(grads, 0, grad_blocks(parts, 128))
    blocks = mm_nt(gc[...], whole(kept_c))
    parts = [blocks[128 * a : 128 * (a + 1)] for a in range(3)]
    start = put_grad(grads, start, grad_blocks(parts, 128))
    for f in range(grads.shape[0]):
        grads.spot[f, start : start + 80, :] = grad_out.spot[f]
    clear_rest(grads, start + 80)


def grads_down(scal, grad_fine, grad_c, kept_pool, kept_b, grads, gs, gc):
    g = {r: row(grad_fine, r) for r in range(-1, ROWS + 1)}
    for r in range(ROWS):
        put(gs, r, stack_rows(g, r))
    g = {r: row(grad_c, r) for r in range(-1, CROWS + 1)}
    for r in range(CROWS):
        put(gc, r, stack_rows(g, r))
    blocks = mm_nt(gc[...], whole(kept_pool))
    parts = [blocks[128 * a : 128 * (a + 1)] for a in range(3)]
    start = put_grad(grads, 0, grad_blocks(parts, 64))
    parts = fine_grad(mm_nt(gs[...], whole(kept_b)), 64, 64)
    clear_rest(grads, put_grad(grads, start, grad_blocks(parts, 64)))


def grads_first(scal, grad_b, line, vec, kept_a, grads, gs):
    g = {r: row(grad_b, r) for r in range(-1, ROWS + 1)}
    for r in range(ROWS):
        put(gs, r, stack_rows(g, r))
    parts = fine_grad(mm_nt(gs[...], whole(kept_a)), 64, 64)
    start = put_grad(grads, 0, grad_blocks(parts, 64))
    line = line.spot[0:1, :]
    line = line + pltpu.roll(line, 64, 1)
    column = jnp.sum(
        place(128, 128, 0).astype(F32) * vec.spot[0:1, :].astype(F32), axis=1, keepdims=True
    )
    outer = (column * line).astype(BF16)
    size = 128 // grads.shape[0]
    for f in range(grads.shape[0]):
        grads.spot[f, start : start + size, :] = outer[f * size : (f + 1) * size]


def stage_up(
    members, members_c, scal, stats_d, stats_ed, got_a, got_b, hats, back, wup_t, stats_c, hats_c,
    wcoarse_t, done,
    grad_merged, back_c, grad_coarse, edge_a, edge_b, stats, loss,
):
    give(loss, jnp.broadcast_to(total_stats(stats_ed)[2:3, :], (8, 128)))
    mean, inverse = norm_columns(stats_d, True, members)
    shift, slope = back_columns(stats_ed, True, members)
    g = {}
    for r in range(-3, ROWS + 3):
        hat = row(hats, r).astype(F32)
        if r < 0:
            u = pick(scal, row(got_a, r + 3), row(got_b, r + 3)).astype(F32)
        elif r < ROWS:
            u = row(back, r).astype(F32)
        else:
            u = pick(scal, row(got_b, r - ROWS), row(got_a, r - ROWS)).astype(F32)
        value = inverse * (u * silu_slope(hat) - shift - hat * slope)
        g[r] = masked(value, r, ROWS, scal).astype(BF16)
        if -2 <= r < ROWS + 2:
            put(grad_merged, r, g[r])
    wup_t.wait(1)
    weights = whole(wup_t)
    gk = {}
    half = {}
    for r in range(-2, ROWS + 2):
        taps = mm(weights, stack_rows(g, r))
        half[r] = taps[128:256] + taps[256:384] + from_right(taps[:128]) + from_left(taps[384:])
        if r % 2:
            value = masked(half.pop(r - 1) + half.pop(r), r // 2, CROWS, scal)
            gk[r // 2] = value.astype(BF16)
            put(grad_coarse, r // 2, gk[r // 2])
    wcoarse_t.wait(1)
    hats_c.wait(1)
    stats_c.wait(1)
    weights = whole(wcoarse_t)
    mean, inverse = norm_columns(stats_c, False, members_c)
    total = jnp.zeros((128, HALF), F32)
    cross = jnp.zeros((128, HALF), F32)
    for r in range(CROWS):
        value = coarse_untap(mm(weights, stack_rows(gk, r)))
        put(back_c, r, value.astype(BF16))
        hat = row(hats_c, r).astype(F32)
        e = value * silu_slope(hat)
        total = total + e
        cross = cross + e * hat
    top = [row(back_c, 0), row(back_c, 1), gk[1]]
    low = [row(back_c, 2), row(back_c, 3), gk[2]]
    for j in range(3):
        put(edge_a, j, pick(scal, top[j], low[j]))
        put(edge_b, j, pick(scal, low[j], top[j]))
    put_stats(stats, total, cross)


def stage_down(
    members, members_c, scal, stats_c, stats_ec, got_a, got_b, hats_c, back_c, grad_coarse,
    wdown_t, grad_merged, stats_b, wsecond_t, hats, done,
    grad_fine, back_b, stats, grad_c,
):
    mean, inverse = norm_columns(stats_c, False, members_c)
    shift, slope = back_columns(stats_ec, False, members_c)
    g = {}
    for r in range(-2, CROWS + 2):
        hat = row(hats_c, r).astype(F32)
        if r < 0:
            u = pick(scal, row(got_a, r + 2), row(got_b, r + 2)).astype(F32)
        elif r < CROWS:
            u = row(back_c, r).astype(F32)
        else:
            u = pick(scal, row(got_b, r - CROWS), row(got_a, r - CROWS)).astype(F32)
        if r == -2:
            through = pick(scal, row(got_a, 2), row(got_b, 2)).astype(F32)
        elif r == CROWS + 1:
            through = pick(scal, row(got_b, 2), row(got_a, 2)).astype(F32)
        else:
            through = row(grad_coarse, r).astype(F32)
        value = through + inverse * (u * silu_slope(hat) - shift - hat * slope)
        g[r] = masked(value, r, CROWS, scal).astype(BF16)
        if -1 <= r <= CROWS:
            put(grad_c, r, g[r])
    wdown_t.wait(1)
    weights = whole(wdown_t)
    fine = {}
    for r in range(-1, CROWS + 1):
        value = 0.25 * coarse_untap(mm(weights, stack_rows(g, r)))
        both = jnp.concatenate([value, value], axis=0)
        for i in (2 * r, 2 * r + 1):
            value = masked(row(grad_merged, i).astype(F32) + both, i, ROWS, scal)
            fine[i] = value.astype(BF16)
            if -1 <= i <= ROWS:
                put(grad_fine, i, fine[i])
    wsecond_t.wait(1)
    hats.wait(1)
    weights = whole(wsecond_t)
    mean, inverse = norm_columns(stats_b, True, members)
    total = jnp.zeros((128, HALF), F32)
    cross = jnp.zeros((128, HALF), F32)
    for r in range(-1, ROWS + 1):
        value = fine_untap(mm(weights, stack_rows(fine, r)))
        put(back_b, r, value.astype(BF16))
        if 0 <= r < ROWS:
            hat = row(hats, r).astype(F32)
            e = value * silu_slope(hat)
            total = total + e
            cross = cross + e * hat
    put_stats(stats, total, cross)


def stage_first(
    members, scal, stats_b, stats_eb, hats_b, back_b, wfirst_t, stats_a, hats, done,
    back_a, stats, grad_b, line,
):
    mean, inverse = norm_columns(stats_b, True, members)
    shift, slope = back_columns(stats_eb, True, members)
    g = {}
    sums = jnp.zeros((128, HALF), F32)
    for r in range(-1, ROWS + 1):
        hat = row(hats_b, r).astype(F32)
        u = row(back_b, r).astype(F32)
        value = inverse * (u * silu_slope(hat) - shift - hat * slope)
        if 0 <= r < ROWS:
            sums = sums + value
        g[r] = masked(value, r, ROWS, scal).astype(BF16)
        put(grad_b, r, g[r])
    wfirst_t.wait(1)
    hats.wait(1)
    weights = whole(wfirst_t)
    total = jnp.zeros((128, HALF), F32)
    cross = jnp.zeros((128, HALF), F32)
    for r in range(ROWS):
        value = fine_untap(mm(weights, stack_rows(g, r)))
        put(back_a, r, value.astype(BF16))
        hat = row(hats, r).astype(F32)
        e = value * silu_slope(hat)
        total = total + e
        cross = cross + e * hat
    put_stats(stats, total, cross)
    sums = to_row(jnp.sum(sums, axis=1, keepdims=True))
    give(line, jnp.broadcast_to(sums, (8, 128)))


def stage_last(
    members, scal, stats_a, stats_ea, hats, back_a, grad_fine, kept_in, early, middle, first,
    loss, loss_other, keep, send, loss_sum, gs, held, sems,
):
    grads = Source(held, [], 0)
    copies, start = [], 0
    for index, ref in enumerate((early, middle)):
        rows = pl.ds(start, ref.shape[1])
        copies.append(
            pltpu.make_async_copy(ref.spot, grads.spot.at[:, rows, :], sems.at[index])
        )
        copies[index].start()
        start += ref.shape[1]
    give(loss_sum, whole(loss) + whole(loss_other))
    mean, inverse = norm_columns(stats_a, True, members)
    shift, slope = back_columns(stats_ea, True, members)
    for r in range(ROWS):
        hat = row(hats, r).astype(F32)
        u = row(back_a, r).astype(F32)
        value = row(grad_fine, r).astype(F32) + inverse * (
            u * silu_slope(hat) - shift - hat * slope
        )
        put(gs, r, value.astype(BF16))
    kept_in.wait(1)
    first.wait(1)
    parts = []
    for a in range(3):
        blocks = mm_nt(gs[...], kept_in.spot[:, a * HALF : (a + ROWS) * HALF])
        parts.append(
            jnp.concatenate(
                [blocks[:64, :96] + blocks[64:, 32:128], jnp.zeros((64, 32), F32)], axis=1
            )
        )
    size = first.shape[1]
    for f in range(grads.shape[0]):
        grads.spot[f, start : start + size, :] = first.spot[f]
    clear_rest(grads, put_grad(grads, start + size, parts))
    for copy in copies:
        copy.wait()
    half = keep.shape[1]
    odd = scal[8] > 0.5
    for f in range(keep.shape[0]):
        low, high = held[f, :half, :], held[f, half:, :]
        keep.spot[f] = jnp.where(odd, high, low)
        send.spot[f] = jnp.where(odd, low, high)


def join(scal, kept, got, out):
    give(out, (whole(kept).astype(F32) + whole(got).astype(F32)).astype(BF16))


def add_up(scal, got, out):
    total = got.spot[0].astype(F32)
    for index in range(1, got.shape[0]):
        total = total + got.spot[index].astype(F32)
    total = total.astype(BF16)
    for index in range(out.shape[0]):
        out.spot[index] = total


def unpack(starts, scal, mine, other, *refs):
    first, down, second, coarse, up, out, embed, inputs, flat = refs
    half = mine.shape[0]
    odd = scal[8] > 0.5
    flat[:half, :] = jnp.where(odd, whole(other), whole(mine)).astype(F32)
    flat[half:, :] = jnp.where(odd, whole(mine), whole(other)).astype(F32)

    def take(ref, start, out, size, ins, trim=False):
        for t in range(9):
            a, b = t // 3, t % 3
            if ins == 128:
                at, lanes = t, 0
            elif ins == 64:
                at, lanes = (a, b) if b < 2 else (3 + a // 2, a % 2)
            else:
                at, lanes = a, b
            value = ref[start + at * size : start + (at + 1) * size, :]
            if ins == 24:
                out.spot[t] = mm_nt(place(24, 128, 32 * lanes), value.astype(BF16))
                continue
            value = value[:, lanes * ins : (lanes + 1) * ins]
            if trim:
                value = value[:12]
                if out.shape[2] == 32:
                    value = jnp.where(scal[9] > 0.5, value[:, :32], value[:, 32:])
            out.spot[t] = value
        return start + (9 if ins == 128 else 5 if ins == 64 else 3) * size

    start = take(flat, 0, up, up.shape[1], 128)
    start = take(flat, start, coarse, coarse.shape[1], 128)
    take(flat, start, out, 16, 64, trim=True)
    start = take(flat, starts[0], down, down.shape[1], 64)
    take(flat, start, second, second.shape[1], 64)
    start = take(flat, starts[1], first, first.shape[1], 64)
    size = embed.shape[0]
    give(embed, flat[start : start + size, :64])
    take(flat, start + size, inputs, inputs.shape[2], 24)


class Field:
    def __init__(self, array, first):
        self.array, self.first = array, first


class Saved:
    def __init__(self, item, low=None, high=None, when=0):
        self.item, self.low, self.high, self.when = item, low, high, when


def shape(*dims, dtype=F32):
    return jax.ShapeDtypeStruct(dims, dtype)


def rows_of(first, number, dtype=F32):
    return Field(shape(number, 128, HALF, dtype=dtype), first)


def flat_rows(first, number, channels):
    return Field(shape(channels, number * HALF, dtype=BF16), first)


def opened(item):
    saved = item if isinstance(item, Saved) else None
    item = saved.item if saved else item
    if isinstance(item, Field):
        return saved, item.array, item.first
    return saved, item, 0


def run(name, kernel, outs, scal, *operands, scratch=()):
    vmem, hbm = pl.BlockSpec(memory_space=pltpu.VMEM), pl.BlockSpec(memory_space=pltpu.HBM)
    in_specs, arrays, plans, spots = [pl.BlockSpec(memory_space=pltpu.SMEM)], [scal], [], []
    for item in operands:
        saved, item, first = opened(item)
        if saved is None:
            in_specs.append(vmem)
            arrays.append(item)
            plans.append((first, None, None))
            continue
        part = None
        dims = item.shape
        if saved.low is not None:
            part = pl.ds(saved.low - first, saved.high - saved.low)
            dims = (saved.high - saved.low,) + dims[1:]
            first = saved.low
        in_specs.append(hbm)
        arrays.append(pltpu.with_memory_space_constraint(item, pltpu.HBM))
        if saved.when is None:
            plans.append((first, None, None))
            continue
        plans.append((first, (saved.when, part), len(spots)))
        spots.append(pltpu.VMEM(dims, item.dtype))
    ins = len(operands)
    out_specs, out_shapes = [], []
    for item in outs:
        saved, item, first = opened(item)
        if saved is None:
            out_specs.append(vmem)
            out_shapes.append(item)
            plans.append((first, None, None))
            continue
        out_specs.append(hbm)
        out_shapes.append(pltpu.HBM(item.shape, item.dtype))
        last = None
        if isinstance(saved.item, Field):
            count = item.shape[0] if len(item.shape) == 3 else item.shape[1] // HALF
            last = first + count - 1
        if saved.when is None:
            plans.append((first, None, None))
            continue
        plans.append((first, (last, None), len(spots)))
        spots.append(pltpu.VMEM(item.shape, item.dtype))

    def body(numbers, *refs):
        given, refs = refs[: len(plans)], refs[len(plans) :]
        held, refs = refs[: len(spots)], refs[len(spots) :]
        sems, extra = refs[0], refs[1:]
        wrapped = []
        for index, (ref, (first, plan, place_at)) in enumerate(zip(given, plans)):
            copies = []
            if plan is not None:
                where = held[place_at]
                when, part = plan
                if index < ins:
                    source = ref if part is None else ref.at[part]
                    copies.append((when, pltpu.make_async_copy(source, where, sems.at[place_at])))
                else:
                    copies.append((when, pltpu.make_async_copy(where, ref, sems.at[place_at])))
                ref = where
            wrapped.append((Source if index < ins else Sink)(ref, copies, first))
        for item in wrapped[:ins]:
            item.wait(0)
        kernel(numbers, *wrapped, *extra)
        for item in wrapped[ins:]:
            item.finish()
        for item in wrapped[ins:]:
            for copy in item.started:
                copy.wait()

    made = pl.pallas_call(
        body,
        out_shape=tuple(out_shapes),
        in_specs=in_specs,
        out_specs=tuple(out_specs),
        scratch_shapes=spots
        + [pltpu.SemaphoreType.DMA((max(len(spots), 1),))]
        + [pltpu.VMEM(*item) if isinstance(item, tuple) else item for item in scratch],
        compiler_params=pltpu.CompilerParams(vmem_limit_bytes=LIMIT),
        name=name,
    )(*arrays)
    results = []
    for array, item in zip(made, outs):
        item = item.item if isinstance(item, Saved) else item
        results.append(Field(array, item.first) if isinstance(item, Field) else array)
    return results


def sum_parts(stats):
    return lax.all_to_all(stats, "rows", 0, 0)


def swap(value_a, value_b):
    count = lax.axis_size("rows")
    pairs = [(i, i ^ 1) for i in range(count)]
    across = []
    for i in range(1, count - 1, 2):
        across += [(i, i + 1), (i + 1, i)]
    return lax.ppermute(value_a, "rows", pairs), lax.ppermute(value_b, "rows", across)


def gather_packed(packed):
    if lax.axis_size("fsdp") == 2:
        return [packed, lax.ppermute(packed, "fsdp", [(0, 1), (1, 0)])]
    whole = lax.all_gather(packed, "fsdp").astype(F32)
    return [whole[i] for i in range(whole.shape[0])]


def group_shape(rows, count):
    return shape(count, -(-rows // 16) * 16, 128, dtype=BF16)


def per_device(
    residual_target,
    conditioning,
    noise_sample,
    noise_level,
    input_kernel,
    first_kernel,
    second_kernel,
    down_kernel,
    coarse_kernel,
    upward_kernel,
    output_kernel,
    embed_matrix,
):
    bands, count = lax.axis_size("rows"), lax.axis_size("fsdp")
    members = 2 * ROWS * 2 * HALF * bands
    members_c = 4 * CROWS * HALF * bands
    members_all = count * residual_target.size * bands
    me = lax.axis_index("rows")
    sigma_level, skip_scale, out_scale, in_scale, weight = preconditions(noise_level[0])
    coef = 2.0 * weight * out_scale / members_all
    scal = jnp.stack(
        [
            sigma_level,
            skip_scale,
            out_scale,
            in_scale,
            weight,
            coef,
            (me > 0).astype(F32),
            (me < bands - 1).astype(F32),
            (me % 2).astype(F32),
            (lax.axis_index("fsdp") == 0).astype(F32),
        ]
    )
    embedded = embedding(sigma_level, embed_matrix.shape[0] * count)
    target = residual_target.reshape(12 * ROWS, 512)
    condition = conditioning.reshape(12 * ROWS, 512)
    noise = noise_sample.reshape(12 * ROWS, 512)

    def pack_all(name, shards, rows, *after):
        widths = tuple(
            (9 if item.ndim == 3 else 1, size, item.ndim == 3 and item.shape[1] == 24)
            for item, size in zip(shards, rows)
        )
        total = sum(taps * size for taps, size, _ in widths)
        (packed,) = run(
            name,
            functools.partial(pack, widths),
            [shape(total, 128, dtype=BF16)],
            scal,
            *[Saved(item) for item in shards],
            *after,
            scratch=[((total, 128), F32)],
        )
        return packed

    fine_o, coarse_o = input_kernel.shape[1], down_kernel.shape[1]
    inputs_t = jnp.swapaxes(input_kernel, 1, 2)
    early_packed = pack_all(
        "pack_first",
        [inputs_t, first_kernel, embed_matrix],
        [fine_o, fine_o, embed_matrix.shape[0]],
    )
    early = gather_packed(early_packed)
    far = shape(32, FAR * 512, dtype=BF16)
    own, edge_a, edge_b = run(
        "enter",
        enter,
        [shape(32, ROWS * 512, dtype=BF16), far, far],
        scal,
        Saved(target),
        Saved(condition),
        Saved(noise),
        early[0],
        scratch=[((4, 192, 128), F32), ((2, 16, FAR * 512), BF16)],
    )
    got_a, got_b = swap(edge_a, edge_b)
    rest = pack_all(
        "pack_rest",
        [second_kernel, down_kernel, coarse_kernel, upward_kernel, output_kernel],
        [fine_o, coarse_o, coarse_o, fine_o, 16],
        own,
    )
    vector = jnp.broadcast_to(embedded[None, :], (16, embedded.shape[0]))
    win, wfirst, wfirst_t, shift = run(
        "prepare_first",
        functools.partial(prepare_first, embedded.shape[0]),
        [
            shape(384, 128, dtype=BF16), Saved(shape(384, 256, dtype=BF16)),
            Saved(shape(256, 384, dtype=BF16)), shape(128, 128),
        ],
        scal,
        vector, *early,
    )
    stat = shape(bands, 8, 128)
    total = Saved(shape(1, 8, 128))
    act_a, stats_a, kept_in, line_a, line_b = run(
        "stage_a",
        stage_a,
        [
            rows_of(-6, 20), stat, Saved(flat_rows(-1, 10, 128)),
            Saved(shape(16, 512)), Saved(shape(16, 512)),
        ],
        scal,
        win, got_a, got_b, own, rest,
        scratch=[((32, FAR * 512), BF16), ((32, FAR * 512), BF16)],
    )
    stats_a = sum_parts(stats_a)
    rest, stats_a = lax.optimization_barrier((rest, stats_a))
    (
        wsecond, wsecond_t, wdown, wdown_t, wcoarse, wcoarse_t, wup, wup_t, wout, wout_t
    ) = run(
        "prepare_rest",
        prepare_rest,
        [
            Saved(shape(384, 256, dtype=BF16)), Saved(shape(256, 384, dtype=BF16)),
            Saved(shape(384, 192, dtype=BF16)), Saved(shape(192, 384, dtype=BF16)),
            Saved(shape(384, 384, dtype=BF16)), Saved(shape(384, 384, dtype=BF16)),
            Saved(shape(384, 512, dtype=BF16)), Saved(shape(512, 384, dtype=BF16)),
            Saved(shape(96, 256, dtype=BF16)), Saved(shape(256, 96, dtype=BF16)),
        ],
        scal,
        *gather_packed(rest),
    )

    act_b, stats_b, kept_a, hats_a, act_a, total_a = run(
        "stage_b",
        functools.partial(stage_b, members),
        [
            rows_of(-5, 18), stat, Saved(flat_rows(0, 8, 256)), Saved(rows_of(0, 8, BF16)),
            Saved(rows_of(-4, 16), when=None), total,
        ],
        scal,
        stats_a, shift, Saved(wfirst, when=1), act_a,
        scratch=[pltpu.SemaphoreType.DMA(())],
    )
    stats_b = sum_parts(stats_b)
    fine, act_c, edge, stats_c, kept_b, kept_pool, hats_b, total_b = run(
        "stage_c",
        functools.partial(stage_c, members),
        [
            rows_of(-3, 14), rows_of(-1, 6), Field(shape(128, 2 * HALF), 1), stat,
            Saved(flat_rows(0, 8, 256)), Saved(flat_rows(0, 4, 192)), Saved(rows_of(-1, 10, BF16)),
            total,
        ],
        scal,
        stats_b, Saved(wsecond, when=1), act_b, Saved(act_a, when=1), Saved(wdown, when=1),
    )
    got_a, got_b = swap(edge.array, edge.array)
    stats_c = sum_parts(stats_c)
    merged, hats_c, stats_d, kept_c, kept_up, total_c = run(
        "stage_d",
        functools.partial(stage_d, members_c),
        [
            rows_of(-3, 14), Saved(rows_of(-2, 8, BF16)), stat,
            Saved(flat_rows(0, 4, 384)), Saved(flat_rows(0, 4, 384)), total,
        ],
        scal,
        stats_c, Saved(wcoarse), Saved(got_a), Saved(got_b), act_c, Saved(wup), fine,
    )
    stats_d = sum_parts(stats_d)
    edge = Field(shape(128, 3 * HALF, dtype=BF16), 0)
    denoised, back_d, edge_a, edge_b, stats_ed, hats_d, cotangents, kept_d, total_d = run(
        "stage_out",
        functools.partial(stage_out, members),
        [
            Saved(shape(96, 512)), rows_of(0, 8, BF16), edge, edge, stat,
            Saved(rows_of(-3, 14, BF16)),
            Field(shape(10, 32, HALF, dtype=BF16), -1), Saved(flat_rows(0, 8, 256)), total,
        ],
        scal,
        stats_d, Saved(wout, when=1), merged, Saved(line_a, when=1), Saved(line_b, when=1),
        Saved(target, when=1), Saved(noise, when=1), Saved(wout_t, when=1),
        scratch=[
            ((160, 512), F32), ((160, 512), F32),
            ((4, 96, 128), F32), ((4, 96, 128), F32), ((4, 96, 128), F32),
        ],
    )
    got_a, got_b = swap(edge_a.array, edge_b.array)
    (grad_out,) = run(
        "grads_out",
        grads_out,
        [Saved(shape(count, 80, 128, dtype=BF16))],
        scal,
        cotangents, Saved(kept_d),
        scratch=[((96, 8 * HALF), BF16)],
    )
    stats_ed = sum_parts(stats_ed)
    grad_merged, back_c, grad_coarse, edge_a, edge_b, stats_ec, loss = run(
        "stage_up",
        functools.partial(stage_up, members, members_c),
        [
            rows_of(-2, 12, BF16), rows_of(0, 4, BF16), rows_of(-1, 6, BF16), edge, edge, stat,
            shape(8, 128),
        ],
        scal,
        Saved(total_d), stats_ed, Saved(got_a), Saved(got_b), Saved(hats_d), back_d, Saved(wup_t, when=1),
        Saved(total_c, when=1),
        Saved(hats_c, when=1), Saved(wcoarse_t, when=1), Saved(grad_out, when=None),
    )
    got_a, got_b = swap(edge_a.array, edge_b.array)
    (early,) = run(
        "grads_up",
        grads_up,
        [Saved(group_shape(9 * (fine_o + coarse_o) + 80, count))],
        scal,
        grad_merged, grad_coarse, Saved(kept_up), Saved(kept_c), Saved(grad_out),
        scratch=[
            ((384, 8 * HALF), BF16), ((384, 8 * HALF), BF16), ((384, 4 * HALF), BF16)
        ],
    )
    stats_ec = sum_parts(stats_ec)
    if count == 2:
        loss_other = lax.ppermute(loss, "fsdp", [(0, 1), (1, 0)])
    else:
        loss_other = lax.psum(loss, "fsdp") - loss
    grad_fine, back_b, stats_eb, grad_c = run(
        "stage_down",
        functools.partial(stage_down, members, members_c),
        [rows_of(-1, 10, BF16), rows_of(-1, 10, BF16), stat, rows_of(-1, 6, BF16)],
        scal,
        Saved(total_c), stats_ec, Saved(got_a), Saved(got_b), Saved(hats_c), back_c, grad_coarse,
        Saved(wdown_t, when=1), grad_merged, Saved(total_b), Saved(wsecond_t, when=1),
        Saved(hats_b, 0, 8, when=1), Saved(early, when=None),
    )
    (middle,) = run(
        "grads_down",
        grads_down,
        [Saved(group_shape(5 * (fine_o + coarse_o), count))],
        scal,
        grad_fine, grad_c, Saved(kept_pool), Saved(kept_b),
        scratch=[((384, 8 * HALF), BF16), ((384, 4 * HALF), BF16)],
    )
    stats_eb = sum_parts(stats_eb)
    back_a, stats_ea, grad_b, line = run(
        "stage_first",
        functools.partial(stage_first, members),
        [rows_of(0, 8, BF16), stat, rows_of(-1, 10, BF16), shape(8, 128)],
        scal,
        Saved(total_b), stats_eb, Saved(hats_b), back_b, Saved(wfirst_t, when=1), Saved(total_a),
        Saved(hats_a, when=1), Saved(middle, when=None),
    )
    (grad_first,) = run(
        "grads_first",
        grads_first,
        [Saved(shape(count, 5 * fine_o + embed_matrix.shape[0], 128, dtype=BF16))],
        scal,
        grad_b, line, vector, Saved(kept_a),
        scratch=[((384, 8 * HALF), BF16)],
    )
    stats_ea = sum_parts(stats_ea)
    late = group_shape(8 * fine_o + embed_matrix.shape[0], count)
    starts = [early.shape[1], early.shape[1] + middle.shape[1]]
    total = starts[1] + late.shape[1]
    chunk = -(-total // (16 * bands)) * 16
    chips = bands // 2
    half = shape(count, chunk * chips, 128, dtype=BF16)
    keep, send, loss = run(
        "stage_last",
        functools.partial(stage_last, members),
        [half, half, shape(8, 128)],
        scal,
        Saved(total_a), stats_ea, Saved(hats_a), back_a, grad_fine, Saved(kept_in, when=1),
        Saved(early, when=None), Saved(middle, when=None), Saved(grad_first, when=1), loss, loss_other,
        scratch=[
            ((128, 8 * HALF), BF16), ((count, chunk * bands, 128), BF16),
            pltpu.SemaphoreType.DMA((2,)),
        ],
    )
    loss_value = loss[0, 0] / members_all
    pairs = [(i, i ^ 1) for i in range(bands)]
    got = lax.ppermute(send, "rows", pairs)
    (both,) = run("join", join, [half], scal, keep, got)
    both = both.reshape(count * chips, chunk, 128)
    cores = [[f * bands + r for f in range(count) for r in range(c, bands, 2)] for c in range(2)]
    got = lax.all_to_all(both, ("fsdp", "rows"), 0, 0, axis_index_groups=cores)
    (mine,) = run("add_up", add_up, [shape(chips, chunk, 128, dtype=BF16)], scal, got)
    cores = [[r for r in range(c, bands, 2)] for c in range(2)]
    mine = lax.all_to_all(mine, "rows", 0, 0, axis_index_groups=cores)
    mine = mine.reshape(chips * chunk, 128)
    other = lax.ppermute(mine, "rows", pairs)
    first_g, down_g, second_g, coarse_g, up_g, out_g, embed_g, in_g = run(
        "unpack",
        functools.partial(unpack, starts),
        [
            shape(*first_kernel.shape),
            shape(*down_kernel.shape),
            shape(*second_kernel.shape),
            shape(*coarse_kernel.shape),
            shape(*upward_kernel.shape),
            shape(9, 12, output_kernel.shape[2] if count == 2 else 64),
            shape(*embed_matrix.shape),
            shape(*inputs_t.shape),
        ],
        scal,
        mine, other,
        scratch=[((chunk * bands, 128), F32)],
    )
    width = output_kernel.shape[2]
    if count != 2:
        out_g = lax.dynamic_slice_in_dim(out_g, lax.axis_index("fsdp") * width, width, axis=2)
    return (
        denoised.reshape(residual_target.shape),
        loss_value,
        jnp.swapaxes(in_g, 1, 2),
        first_g,
        second_g,
        down_g,
        coarse_g,
        up_g,
        out_g,
        embed_g,
    )


def solution(mesh):
    in_specs = (
        P("fsdp", None, "rows", None),
        P("fsdp", None, "rows", None),
        P("fsdp", None, "rows", None),
        P("fsdp"),
        P(None, "fsdp", None),
        P(None, "fsdp", None),
        P(None, "fsdp", None),
        P(None, "fsdp", None),
        P(None, "fsdp", None),
        P(None, "fsdp", None),
        P(None, None, "fsdp"),
        P("fsdp", None),
    )
    out_specs = (
        P("fsdp", None, "rows", None),
        P(),
        P(None, "fsdp", None),
        P(None, "fsdp", None),
        P(None, "fsdp", None),
        P(None, "fsdp", None),
        P(None, "fsdp", None),
        P(None, "fsdp", None),
        P(None, None, "fsdp"),
        P("fsdp", None),
    )
    return jax.shard_map(
        per_device, mesh=mesh, in_specs=in_specs, out_specs=out_specs, check_vma=False
    )
```

```python
import functools

import jax
import jax.numpy as jnp
from jax import lax
from jax.experimental import pallas as pl
from jax.experimental.pallas import tpu as pltpu
from jax.sharding import PartitionSpec as P

GROUPS = 32
STEPS = 64

sigma_low = 0.002
sigma_high = 80.0
sigma_data = 0.5
rho_power = 7.0
eps_norm = 1e-05

F32 = jnp.float32
BF16 = jnp.bfloat16

HALF = 256
ROWS = 8
CROWS = 4
FAR = 7
LIMIT = 24 * 1024 * 1024


def preconditions(level_index):
    ramp_value = level_index.astype(jnp.float32) / (STEPS - 1)
    top_root = sigma_high ** (1.0 / rho_power)
    bottom = sigma_low ** (1.0 / rho_power)
    sigma_level = (top_root + ramp_value * (bottom - top_root)) ** rho_power
    sigma_total = sigma_level * sigma_level + sigma_data * sigma_data
    skip_scale = sigma_data * sigma_data / sigma_total
    out_scale = sigma_level * sigma_data * lax.rsqrt(sigma_total)
    in_scale = lax.rsqrt(sigma_total)
    weight = sigma_total / (sigma_level * sigma_data) ** 2
    return (sigma_level, skip_scale, out_scale, in_scale, weight)


def embedding(sigma_level, features):
    half_count = features // 2
    ramp_steps = jnp.arange(half_count, dtype=jnp.float32) / half_count
    frequency = 64.0 * 0.01**ramp_steps
    phase_angle = 0.25 * jnp.log(sigma_level) * frequency
    return jnp.concatenate([jnp.cos(phase_angle), jnp.sin(phase_angle)]).astype(jnp.bfloat16)


class Source:
    def __init__(self, spot, copies, first):
        self.spot, self.copies, self.first = spot, copies, first
        self.shape = spot.shape
        for _, copy in copies:
            copy.start()

    def wait(self, stage):
        for when, copy in self.copies:
            if when == stage:
                copy.wait()


class Sink:
    def __init__(self, spot, copies, first):
        self.spot, self.copies, self.first = spot, copies, first
        self.shape = spot.shape
        self.started = []

    def done(self, index):
        for last, copy in self.copies:
            if last == index:
                copy.start()
                self.started.append(copy)

    def send(self, source, sem):
        copy = pltpu.make_async_copy(source, self.spot, sem)
        copy.start()
        self.started.append(copy)

    def finish(self):
        for _, copy in self.copies:
            if not any(copy is other for other in self.started):
                copy.start()
                self.started.append(copy)


def spot(ref, index):
    if len(ref.shape) == 3:
        return (index - getattr(ref, "first", 0),)
    start = index - getattr(ref, "first", 0)
    return (slice(None), slice(start * HALF, (start + 1) * HALF))


def row(ref, index):
    return getattr(ref, "spot", ref)[spot(ref, index)]


def put(ref, index, value):
    getattr(ref, "spot", ref)[spot(ref, index)] = value
    if isinstance(ref, Sink):
        ref.done(index)


def whole(ref):
    return ref.spot[...]


def give(ref, value):
    ref.spot[...] = value
    ref.finish()


def lane(shape):
    return lax.broadcasted_iota(jnp.int32, shape, 1)


def from_left(value):
    moved = pltpu.roll(value, 1, 1)
    return jnp.where(lane(value.shape) == 0, 0.0, moved)


def from_right(value):
    moved = pltpu.roll(value, value.shape[1] - 1, 1)
    return jnp.where(lane(value.shape) == value.shape[1] - 1, 0.0, moved)


def mm(left, right):
    return jnp.dot(left, right, preferred_element_type=F32)


def mm_nt(left, right):
    return lax.dot_general(left, right, (((1,), (1,)), ((), ())), preferred_element_type=F32)


def fine_taps(value):
    half = value.shape[0] // 2
    even, odd = value[:half], value[half:]
    return jnp.concatenate([from_left(odd), value, from_right(even)], axis=0).astype(BF16)


def coarse_taps(value):
    return jnp.concatenate([from_left(value), value, from_right(value)], axis=0).astype(BF16)


def fine_untap(taps):
    size = taps.shape[0] // 4
    even = taps[size : 2 * size] + from_left(taps[3 * size :])
    odd = taps[2 * size : 3 * size] + from_right(taps[:size])
    return jnp.concatenate([even, odd], axis=0)


def coarse_untap(taps):
    size = taps.shape[0] // 3
    return taps[size : 2 * size] + from_right(taps[:size]) + from_left(taps[2 * size :])


def spread(parts, first, last):
    out = {}
    for i in range(first, last + 1):
        size = parts[i - 1].shape[0] // 3
        out[i] = parts[i - 1][:size] + parts[i][size : 2 * size] + parts[i + 1][2 * size :]
    return out


def stack_rows(g, r):
    return jnp.concatenate([g[r + 1], g[r], g[r - 1]], axis=0)


def same_group(size, fine):
    left = lax.broadcasted_iota(jnp.int32, (size, size), 0)
    right = lax.broadcasted_iota(jnp.int32, (size, size), 1)
    if fine:
        half = size // 2
        left, right = left % half, right % half
        per = half // GROUPS
    else:
        per = size // GROUPS
    return left // per == right // per


def total_stats(stats):
    total = stats.spot[0]
    for index in range(1, stats.shape[0]):
        total = total + stats.spot[index]
    return total


def group_sums(stats, fine):
    total = total_stats(stats)
    member = same_group(128, fine)
    first = jnp.sum(jnp.where(member, total[0:1, :], 0.0), axis=1, keepdims=True)
    second = jnp.sum(jnp.where(member, total[1:2, :], 0.0), axis=1, keepdims=True)
    return first, second


def norm_columns(stats_ref, fine, members):
    first, second = group_sums(stats_ref, fine)
    mean = first / members
    inverse = lax.rsqrt(second / members - mean * mean + eps_norm)
    return mean, inverse


def back_columns(stats_ref, fine, members):
    first, second = group_sums(stats_ref, fine)
    return first / members, second / members


def to_row(column):
    size = column.shape[0]
    diagonal = lax.broadcasted_iota(jnp.int32, (size, size), 0) == lax.broadcasted_iota(
        jnp.int32, (size, size), 1
    )
    return jnp.sum(jnp.where(diagonal, column, 0.0), axis=0, keepdims=True)


def put_stats(ref, first, second, third=None):
    first = to_row(jnp.sum(first, axis=1, keepdims=True))
    second = to_row(jnp.sum(second, axis=1, keepdims=True))
    if third is None:
        third = jnp.zeros((1, 128), F32)
    block = jnp.concatenate([first, second, third, jnp.zeros((1, 128), F32)], axis=0)
    for index in range(ref.shape[0]):
        ref.spot[index] = block
    ref.finish()


def silu(h):
    t = 0.5 * h
    return t + t * jnp.tanh(t)


def silu_slope(h):
    s = 0.5 + 0.5 * jnp.tanh(0.5 * h)
    return s * (1.0 + h * (1.0 - s))


def masked(value, index, rows, scal):
    if index < 0:
        return value * scal[6]
    if index >= rows:
        return value * scal[7]
    return value


def pick(scal, when_odd, when_even):
    return jnp.where(scal[8] > 0.5, when_odd, when_even)


def spill(ref, value):
    for t in range(4):
        ref[t, : value.shape[0], :] = value[:, 128 * t : 128 * (t + 1)]


def strided(ref, index, size):
    return jnp.concatenate(
        [ref[t, pl.ds(index, size, stride=ROWS), :] for t in range(4)], axis=1
    )


def interleave(transposed):
    left = lax.broadcasted_iota(jnp.int32, (512, 512), 0)
    right = lax.broadcasted_iota(jnp.int32, (512, 512), 1)
    if transposed:
        left, right = right, left
    place = (left & 1) * HALF + (left >> 1)
    return jnp.where(place == right, 1.0, 0.0).astype(BF16)


def fine_grad(blocks, outs, ins):
    parts = []
    for a in range(3):
        even = blocks[(2 * a) * outs : (2 * a + 1) * outs]
        odd = blocks[(2 * a + 1) * outs : (2 * a + 2) * outs]
        parts.append(even[:, : 3 * ins] + odd[:, ins : 4 * ins])
    return parts


def grad_blocks(parts, ins):
    if ins == 128:
        return [part[:, 128 * b : 128 * (b + 1)] for part in parts for b in range(3)]
    if ins == 64:
        blank = jnp.zeros(parts[0][:, :64].shape, F32)
        blocks = [part[:, :128] for part in parts]
        blocks.append(jnp.concatenate([parts[0][:, 128:192], parts[1][:, 128:192]], axis=1))
        blocks.append(jnp.concatenate([parts[2][:, 128:192], blank], axis=1))
        return blocks
    return parts


def put_grad(ref, start, blocks, split=True):
    count = ref.shape[0]
    size = blocks[0].shape[0] // count if split else blocks[0].shape[0]
    for block in blocks:
        for f in range(count):
            piece = block[f * size : (f + 1) * size] if split else block
            ref.spot[f, start : start + size, :] = piece.astype(BF16)
        start += size
    return start


def clear_rest(ref, start):
    count, size, _ = ref.shape
    if start < size:
        for f in range(count):
            ref.spot[f, start:, :] = jnp.zeros((size - start, 128), BF16)


def place(width, target, offset):
    left = lax.broadcasted_iota(jnp.int32, (width, target), 0)
    right = lax.broadcasted_iota(jnp.int32, (width, target), 1)
    return jnp.where(left + offset == right, 1.0, 0.0).astype(BF16)


def flipped(value):
    size = value.shape[1]
    return mm_nt(place(size, size, 0), value).astype(BF16)


def tap_of(pieces, offset, index, size):
    each = size // len(pieces)
    start = offset + index * each
    return jnp.concatenate([piece[start : start + each, :] for piece in pieces], axis=0).astype(
        BF16
    )


def in_order(scal, pieces):
    if len(pieces) == 2:
        mine, other = whole(pieces[0]), whole(pieces[1])
        low = scal[9] > 0.5
        return [jnp.where(low, mine, other), jnp.where(low, other, mine)]
    return [whole(piece) for piece in pieces]


def fine_matrix(taps, slot):
    rows = []
    for a in range(3):
        total = None
        for b in range(3):
            spread_out = jnp.concatenate(
                [place(slot, 4 * slot, b * slot), place(slot, 4 * slot, (b + 1) * slot)], axis=1
            )
            term = mm(taps[3 * a + b][:, :slot], spread_out)
            total = term if total is None else total + term
        rows += [total[:, : 4 * slot], total[:, 4 * slot :]]
    return jnp.concatenate(rows, axis=0).astype(BF16)


def pack(widths, scal, *refs):
    shards, (out, scratch) = refs[: len(widths)], refs[-2:]
    scratch[...] = jnp.zeros(scratch.shape, F32)
    start = 0
    for shard, (taps, rows, swapped) in zip(shards, widths):
        if taps == 1:
            scratch[start : start + rows, : shard.shape[1]] = whole(shard)
            start += rows
        else:
            for t in range(taps):
                value = shard.spot[t]
                if swapped:
                    value = mm_nt(place(value.shape[1], value.shape[1], 0), value.astype(BF16))
                scratch[start : start + value.shape[0], : value.shape[1]] = value
                start += rows
    give(out, scratch[...].astype(BF16))


def prepare_first(embed_size, scal, vec, *refs):
    pieces, (win, wfirst, wfirst_t, shift) = refs[:-4], refs[-4:]
    count = len(pieces)
    pieces = in_order(scal, pieces)
    each = 9 * (64 // count)
    give(win, fine_matrix([tap_of(pieces, 0, t, 64) for t in range(9)], 32))
    first = fine_matrix([tap_of(pieces, each, t, 64) for t in range(9)], 64)
    give(wfirst, first)
    give(wfirst_t, flipped(first))
    line = mm(whole(vec), tap_of(pieces, 2 * each, 0, embed_size))[0:1, :64]
    both = jnp.concatenate([line, line], axis=1)
    diagonal = place(128, 128, 0).astype(F32)
    column = jnp.sum(diagonal * both, axis=1, keepdims=True)
    give(shift, jnp.broadcast_to(column, (128, 128)))


def prepare_rest(scal, *refs):
    pieces = refs[:-10]
    wsecond, wsecond_t, wdown, wdown_t, wcoarse, wcoarse_t, wup, wup_t, wout, wout_t = refs[-10:]
    count = len(pieces)
    pieces = in_order(scal, pieces)
    start = 0

    def taps_of(size):
        nonlocal start
        taps = [tap_of(pieces, start, t, size) for t in range(9)]
        start += 9 * (size // count)
        return taps

    def both(value, forward, backward):
        give(forward, value)
        give(backward, flipped(value))

    both(fine_matrix(taps_of(64), 64), wsecond, wsecond_t)
    taps = taps_of(128)
    rows = []
    for a in range(3):
        total = None
        for b in range(3):
            term = mm(taps[3 * a + b][:, :64], place(64, 256, 64 * b))
            total = term if total is None else total + term
        rows.append(total)
    both(jnp.concatenate(rows, axis=0)[:, :192].astype(BF16), wdown, wdown_t)
    taps = taps_of(128)
    rows = [jnp.concatenate(taps[3 * a : 3 * a + 3], axis=1) for a in range(3)]
    both(jnp.concatenate(rows, axis=0), wcoarse, wcoarse_t)
    taps = taps_of(64)
    rows = []
    blank = jnp.zeros((64, 128), BF16)
    for a in range(3):
        rows.append(jnp.concatenate(taps[3 * a : 3 * a + 3] + [blank], axis=1))
        rows.append(jnp.concatenate([blank] + taps[3 * a : 3 * a + 3], axis=1))
    both(jnp.concatenate(rows, axis=0), wup, wup_t)
    taps = []
    width = 64 // count
    for t in range(9):
        total = None
        for s in range(count):
            tap = pieces[s][start + 16 * t : start + 16 * (t + 1), :].astype(BF16)
            term = mm(tap[:, :width], place(width, 128, s * width))
            total = term if total is None else total + term
        taps.append(total.astype(BF16))
    both(fine_matrix(taps, 64), wout, wout_t)


def enter(scal, target, condition, noise, done, own, edge_a, edge_b, figures, scratch, marks):
    values = [jnp.full((1, 128), scal[k], F32) for k in range(6)]
    give(figures, jnp.concatenate(values + [jnp.zeros((2, 128), F32)], axis=0))
    sigma, skip, in_scale = scal[0], scal[1], scal[3]
    goal = whole(target)
    noisy = goal + sigma * whole(noise)
    q = skip * noisy - goal
    natural = jnp.concatenate([in_scale * noisy, whole(condition)], axis=0).astype(BF16)
    spill(scratch, mm(natural, interleave(False)))
    blank = jnp.zeros((8, 512), F32)
    for i in range(ROWS):
        value = strided(scratch, i, 24)
        own.spot[:, i * 512 : (i + 1) * 512] = jnp.concatenate([value, blank], axis=0).astype(BF16)
    spill(scratch, q)
    blank = jnp.zeros((4, 512), F32)
    for j, i in enumerate((0, ROWS - 1)):
        rest = jnp.concatenate([strided(scratch, i, 12), blank], axis=0)
        marks[j] = jnp.zeros(marks.shape[1:], BF16)
        for part in range(3):
            piece = rest.astype(BF16)
            rest = rest - piece.astype(F32)
            for k in range(2):
                lanes = slice((2 * part + k) * 512, (2 * part + k + 1) * 512)
                marks[j, 8:, lanes] = piece[8 * k : 8 * k + 8]
    for j, edge in enumerate((edge_a, edge_b)):
        odd = scal[8] > 0.5 if j == 0 else scal[8] < 0.5
        low = (ROWS - FAR) * 512
        edge.spot[:16, :] = jnp.where(odd, own.spot[:16, : FAR * 512], own.spot[:16, low:])
        edge.spot[16:, :] = jnp.where(odd, own.spot[16:, : FAR * 512], own.spot[16:, low:]) + (
            jnp.where(odd, marks[0], marks[1])
        )


def marked(scal, got):
    halves = []
    for k in range(2):
        total = None
        for part in range(3):
            lanes = slice((2 * part + k) * 512, (2 * part + k + 1) * 512)
            piece = got.spot[16:32, lanes].astype(F32)[8:]
            total = piece if total is None else total + piece
        halves.append(total)
    return jnp.concatenate(halves, axis=0)


def stage_a(scal, win, got_a, got_b, own, done, act, stats, kept, line_a, line_b, above, below):
    give(line_a, marked(scal, got_a))
    give(line_b, marked(scal, got_b))
    above[...] = pick(scal, whole(got_a), whole(got_b))
    below[...] = pick(scal, whole(got_b), whole(got_a))
    clear = jnp.zeros((16, FAR * 512), BF16)
    keep = lax.broadcasted_iota(jnp.int32, (16, FAR * 512), 0) < 8
    for ref in (above, below):
        ref[16:, :] = jnp.where(keep, ref[16:, :], clear)
    weights = whole(win)
    parts = {}
    total = jnp.zeros((128, HALF), F32)
    square = jnp.zeros((128, HALF), F32)
    for r in range(-FAR, ROWS + FAR):
        if r < 0:
            value = above[:, (r + FAR) * 512 : (r + FAR + 1) * 512]
        elif r < ROWS:
            value = own.spot[:, r * 512 : (r + 1) * 512]
        else:
            value = below[:, (r - ROWS) * 512 : (r - ROWS + 1) * 512]
        value = value.astype(F32)
        z = fine_taps(jnp.concatenate([value[:, :HALF], value[:, HALF:]], axis=0))
        if -1 <= r <= ROWS:
            put(kept, r, z)
        parts[r] = mm(weights, z)
        i = r - 1
        if i > -FAR:
            value = spread(parts, i, i)[i]
            put(act, i, value)
            del parts[i - 1]
            if 0 <= i < ROWS:
                total = total + value
                square = square + value * value
    put_stats(stats, total, square)


def slot(ref, index):
    return ref[:, index * HALF : (index + 1) * HALF]


def fill(ref, index, value):
    ref[:, index * HALF : (index + 1) * HALF] = value


def stage_b(
    members, scal, stats_a, shift, wfirst, act_a,
    act_b, stats, kept, hats, passed, totals, zs, sems,
):
    passed.send(act_a.spot.at[pl.ds(2, 16)], sems.at[0])
    give(totals, total_stats(stats_a)[None])
    mean, inverse = norm_columns(stats_a, True, members)
    lift = shift.spot[:, 0:1]
    for r in range(-6, ROWS + 6):
        hat = (row(act_a, r) - mean) * inverse
        fill(zs, r + 6, fine_taps(masked(silu(hat), r, ROWS, scal)))
        if 0 <= r < ROWS:
            hats.spot[r] = hat.astype(BF16)
    hats.finish()
    kept.send(zs.at[:, pl.ds(6 * HALF, 8 * HALF)], sems.at[1])
    wfirst.wait(1)
    parts = {}
    total = jnp.zeros((128, HALF), F32)
    square = jnp.zeros((128, HALF), F32)
    for r in range(-6, ROWS + 6):
        parts[r] = mm(whole(wfirst), slot(zs, r + 6))
        i = r - 1
        if i > -6:
            value = spread(parts, i, i)[i] + lift
            put(act_b, i, value)
            del parts[i - 1]
            if 0 <= i < ROWS:
                total = total + value
                square = square + value * value
    put_stats(stats, total, square)


def stage_c(
    members, scal, stats_b, wsecond, act_b, act_a, wdown,
    fine, act_c, edge, stats, kept, kept_pool, hats, totals, zs, sems,
):
    give(totals, total_stats(stats_b)[None])
    mean, inverse = norm_columns(stats_b, True, members)
    for r in range(-5, ROWS + 5):
        hat = (row(act_b, r) - mean) * inverse
        fill(zs, r + 5, fine_taps(masked(silu(hat), r, ROWS, scal)))
        if -1 <= r <= ROWS:
            hats.spot[r + 1] = hat.astype(BF16)
    hats.finish()
    kept.send(zs.at[:, pl.ds(5 * HALF, 8 * HALF)], sems.at[0])
    for item in (wsecond, act_a, wdown):
        item.wait(1)
    parts = {}
    pooled = {}
    half = {}
    for r in range(-5, ROWS + 5):
        parts[r] = mm(whole(wsecond), slot(zs, r + 5))
        i = r - 1
        if i > -5:
            value = spread(parts, i, i)[i] + row(act_a, i)
            if -3 <= i < ROWS + 3:
                put(fine, i, value)
            del parts[i - 1]
            half[i] = value[:64] + value[64:]
            if i % 2:
                value = 0.25 * (half.pop(i - 1) + half.pop(i))
                value = masked(value, i // 2, CROWS, scal)
                pooled[i // 2] = value.astype(BF16).astype(F32)
    weights = whole(wdown)
    parts = {}
    total = jnp.zeros((128, HALF), F32)
    square = jnp.zeros((128, HALF), F32)
    for r in range(-2, CROWS + 2):
        z = coarse_taps(pooled[r])
        if 0 <= r < CROWS:
            put(kept_pool, r, z)
        parts[r] = mm(weights, z)
        i = r - 1
        if i > -2:
            value = spread(parts, i, i)[i]
            put(act_c, i, value)
            del parts[i - 1]
            if 0 <= i < CROWS:
                total = total + value
                square = square + value * value
            if i in (1, 2):
                put(edge, i, value)
    put_stats(stats, total, square)


def stage_d(
    members, scal, stats_c, wcoarse, got_a, got_b, act_c, wup, fine,
    merged, hats, stats, kept_c, kept_up, totals, zs, sems,
):
    give(totals, total_stats(stats_c)[None])
    mean, inverse = norm_columns(stats_c, False, members)
    ring = {}
    for j in range(2):
        ring[j - 3] = pick(scal, row(got_a, j), row(got_b, j))
        ring[CROWS + 1 + j] = pick(scal, row(got_b, j), row(got_a, j))
    for j in range(-1, CROWS + 1):
        ring[j] = row(act_c, j)
    for r in range(-3, CROWS + 3):
        hat = (ring[r] - mean) * inverse
        fill(zs, r + 3, coarse_taps(masked(silu(hat), r, CROWS, scal)))
        if -2 <= r < CROWS + 2:
            hats.spot[r + 2] = hat.astype(BF16)
    hats.finish()
    kept_c.send(zs.at[:, pl.ds(3 * HALF, 4 * HALF)], sems.at[0])
    wcoarse.wait(1)
    wup.wait(1)
    parts = {}
    lifted = {}
    for r in range(-3, CROWS + 3):
        parts[r] = mm(whole(wcoarse), slot(zs, r + 3))
        i = r - 1
        if i > -3:
            value = spread(parts, i, i)[i] + ring[i]
            del parts[i - 1]
            lifted[i] = masked(value, i, CROWS, scal).astype(BF16).astype(F32)
    weights = whole(wup)
    parts = {}
    total = jnp.zeros((128, HALF), F32)
    square = jnp.zeros((128, HALF), F32)
    for r in range(-2, CROWS + 2):
        z = coarse_taps(lifted[r])
        if 0 <= r < CROWS:
            put(kept_up, r, z)
        four = jnp.concatenate([z[:128], z[128:256], z[128:256], z[256:]], axis=0)
        parts[2 * r] = parts[2 * r + 1] = mm(weights, four)
        for i in (2 * r - 1, 2 * r):
            if i >= -3:
                value = spread(parts, i, i)[i] + row(fine, i)
                put(merged, i, value)
                parts.pop(i - 1)
                if 0 <= i < ROWS:
                    total = total + value
                    square = square + value * value
    put_stats(stats, total, square)


def stage_out(
    members, scal, stats_d, wout, merged, line_a, line_b, target, noise, wout_t, figures,
    denoised, back, edge_a, edge_b, stats, hats, cotangents, kept, totals, pairs, cells,
    goals, noisies, found, zs, sems,
):
    give(totals, total_stats(stats_d)[None])
    mean, inverse = norm_columns(stats_d, True, members)
    for r in range(-3, ROWS + 3):
        hat = (row(merged, r) - mean) * inverse
        hats.spot[r + 3] = hat.astype(BF16)
        if -3 < r < ROWS + 2:
            fill(zs, r + 2, fine_taps(masked(silu(hat), r, ROWS, scal)))
    hats.finish()
    kept.send(zs.at[:, pl.ds(2 * HALF, 8 * HALF)], sems.at[0])
    for item in (wout, line_a, line_b, target, noise, wout_t, figures):
        item.wait(1)
    parts = {}
    for r in range(-2, ROWS + 2):
        parts[r] = mm(whole(wout), slot(zs, r + 2))
        i = r - 1
        if i > -2:
            value = spread(parts, i, i)[i]
            del parts[i - 1]
            pairs[16 * (i + 1) : 16 * (i + 2), :] = jnp.concatenate(
                [value[:16], value[16:]], axis=1
            )
    value = pairs[...]
    high = value.astype(BF16)
    low = (value - high.astype(F32)).astype(BF16)
    back_order = interleave(True)
    sigma, skip, out_scale, weight, coef = [
        figures.spot[k : k + 1, 0:1] for k in (0, 1, 2, 4, 5)
    ]
    pairs[...] = mm(high, back_order) + mm(low, back_order)
    blank = jnp.zeros((4, 512), F32)
    loss_sum = jnp.zeros((12, 512), F32)
    top = pick(scal, whole(line_a), whole(line_b)) + out_scale * pairs[0:16, :]
    cells[0:16, :] = coef * scal[6] * top
    low = pick(scal, whole(line_b), whole(line_a)) + out_scale * pairs[16 * (ROWS + 1) :, :]
    cells[16 * (ROWS + 1) :, :] = coef * scal[7] * low
    spill(goals, whole(target))
    spill(noisies, whole(target) + sigma * whole(noise))
    for i in range(ROWS):
        goal = strided(goals, i, 12)
        noisy = strided(noisies, i, 12)
        estimate = skip * noisy + out_scale * pairs[16 * (i + 1) : 16 * (i + 1) + 12, :]
        for t in range(4):
            found[t, pl.ds(i, 12, stride=ROWS), :] = estimate[:, 128 * t : 128 * (t + 1)]
        mismatch = estimate - goal
        loss_sum = loss_sum + weight * mismatch * mismatch
        cells[16 * (i + 1) : 16 * (i + 2), :] = jnp.concatenate([coef * mismatch, blank], axis=0)
    give(denoised, jnp.concatenate([found[t] for t in range(4)], axis=1))
    loss_sum = jnp.broadcast_to(
        jnp.sum(jnp.sum(loss_sum, axis=1, keepdims=True), axis=0, keepdims=True), (1, 128)
    )
    pairs[...] = mm(cells[...].astype(BF16), interleave(False))
    g = {}
    for i in range(-1, ROWS + 1):
        value = pairs[16 * (i + 1) : 16 * (i + 2), :]
        g[i] = jnp.concatenate([value[:, :HALF], value[:, HALF:]], axis=0).astype(BF16)
        put(cotangents, i, g[i])
    weights = whole(wout_t)
    total = jnp.zeros((128, HALF), F32)
    cross = jnp.zeros((128, HALF), F32)
    for r in range(ROWS):
        value = fine_untap(mm(weights, stack_rows(g, r)))
        put(back, r, value.astype(BF16))
        hat = row(hats, r).astype(F32)
        e = value * silu_slope(hat)
        total = total + e
        cross = cross + e * hat
    for j in range(3):
        top, low = row(back, j), row(back, ROWS - 3 + j)
        put(edge_a, j, pick(scal, top, low))
        put(edge_b, j, pick(scal, low, top))
    put_stats(stats, total, cross, loss_sum)


def grads_out(scal, cotangents, zs, grad, gs):
    g = {r: row(cotangents, r) for r in range(-1, ROWS + 1)}
    for r in range(ROWS):
        put(gs, r, stack_rows(g, r))
    parts = fine_grad(mm_nt(gs[...], whole(zs)), 16, 64)
    put_grad(grad, 0, grad_blocks(parts, 64), split=False)


def grads_up(scal, grad_merged, grad_coarse, kept_up, kept_c, grad_out, grads, gs, zs, gc):
    g = {r: row(grad_merged, r) for r in range(-1, ROWS + 1)}
    for r in range(ROWS):
        put(gs, r, stack_rows(g, r))
        put(zs, r, row(kept_up, r // 2))
    g = {r: row(grad_coarse, r) for r in range(-1, CROWS + 1)}
    for r in range(CROWS):
        put(gc, r, stack_rows(g, r))
    blocks = mm_nt(gs[...], zs[...])
    parts = []
    for a in range(3):
        even = blocks[128 * a : 128 * a + 64]
        odd = blocks[128 * a + 64 : 128 * a + 128]
        parts.append(
            jnp.concatenate(
                [
                    even[:, :128] + odd[:, 128:256],
                    even[:, 128:256] + odd[:, 128:256],
                    even[:, 128:256] + odd[:, 256:],
                ],
                axis=1,
            )
        )
    start = put_grad(grads, 0, grad_blocks(parts, 128))
    blocks = mm_nt(gc[...], whole(kept_c))
    parts = [blocks[128 * a : 128 * (a + 1)] for a in range(3)]
    start = put_grad(grads, start, grad_blocks(parts, 128))
    for f in range(grads.shape[0]):
        grads.spot[f, start : start + 80, :] = grad_out.spot[f]
    clear_rest(grads, start + 80)


def grads_down(scal, grad_fine, grad_c, kept_pool, kept_b, grads, gs, gc):
    g = {r: row(grad_fine, r) for r in range(-1, ROWS + 1)}
    for r in range(ROWS):
        put(gs, r, stack_rows(g, r))
    g = {r: row(grad_c, r) for r in range(-1, CROWS + 1)}
    for r in range(CROWS):
        put(gc, r, stack_rows(g, r))
    blocks = mm_nt(gc[...], whole(kept_pool))
    parts = [blocks[128 * a : 128 * (a + 1)] for a in range(3)]
    start = put_grad(grads, 0, grad_blocks(parts, 64))
    parts = fine_grad(mm_nt(gs[...], whole(kept_b)), 64, 64)
    clear_rest(grads, put_grad(grads, start, grad_blocks(parts, 64)))


def grads_first(scal, grad_b, line, vec, kept_a, grads, gs):
    g = {r: row(grad_b, r) for r in range(-1, ROWS + 1)}
    for r in range(ROWS):
        put(gs, r, stack_rows(g, r))
    parts = fine_grad(mm_nt(gs[...], whole(kept_a)), 64, 64)
    start = put_grad(grads, 0, grad_blocks(parts, 64))
    line = line.spot[0:1, :]
    line = line + pltpu.roll(line, 64, 1)
    column = jnp.sum(
        place(128, 128, 0).astype(F32) * vec.spot[0:1, :].astype(F32), axis=1, keepdims=True
    )
    outer = (column * line).astype(BF16)
    size = 128 // grads.shape[0]
    for f in range(grads.shape[0]):
        grads.spot[f, start : start + size, :] = outer[f * size : (f + 1) * size]


def stage_up(
    members, members_c, scal, stats_d, stats_ed, got_a, got_b, hats, back, wup_t, stats_c, hats_c,
    wcoarse_t, done,
    grad_merged, back_c, grad_coarse, edge_a, edge_b, stats, loss, total_next,
):
    give(loss, jnp.broadcast_to(total_stats(stats_ed)[2:3, :], (8, 128)))
    mean, inverse = norm_columns(stats_d, True, members)
    shift, slope = back_columns(stats_ed, True, members)
    g = {}
    for r in range(-3, ROWS + 3):
        hat = row(hats, r).astype(F32)
        if r < 0:
            u = pick(scal, row(got_a, r + 3), row(got_b, r + 3)).astype(F32)
        elif r < ROWS:
            u = row(back, r).astype(F32)
        else:
            u = pick(scal, row(got_b, r - ROWS), row(got_a, r - ROWS)).astype(F32)
        value = inverse * (u * silu_slope(hat) - shift - hat * slope)
        g[r] = masked(value, r, ROWS, scal).astype(BF16)
        if -2 <= r < ROWS + 2:
            put(grad_merged, r, g[r])
    wup_t.wait(1)
    weights = whole(wup_t)
    gk = {}
    half = {}
    for r in range(-2, ROWS + 2):
        taps = mm(weights, stack_rows(g, r))
        half[r] = taps[128:256] + taps[256:384] + from_right(taps[:128]) + from_left(taps[384:])
        if r % 2:
            value = masked(half.pop(r - 1) + half.pop(r), r // 2, CROWS, scal)
            gk[r // 2] = value.astype(BF16)
            put(grad_coarse, r // 2, gk[r // 2])
    wcoarse_t.wait(1)
    hats_c.wait(1)
    stats_c.wait(1)
    weights = whole(wcoarse_t)
    mean, inverse = norm_columns(stats_c, False, members_c)
    total = jnp.zeros((128, HALF), F32)
    cross = jnp.zeros((128, HALF), F32)
    for r in range(CROWS):
        value = coarse_untap(mm(weights, stack_rows(gk, r)))
        put(back_c, r, value.astype(BF16))
        hat = row(hats_c, r).astype(F32)
        e = value * silu_slope(hat)
        total = total + e
        cross = cross + e * hat
    top = [row(back_c, 0), row(back_c, 1), gk[1]]
    low = [row(back_c, 2), row(back_c, 3), gk[2]]
    for j in range(3):
        put(edge_a, j, pick(scal, top[j], low[j]))
        put(edge_b, j, pick(scal, low[j], top[j]))
    put_stats(stats, total, cross)
    give(total_next, whole(stats_c))


def stage_down(
    members, members_c, scal, stats_c, stats_ec, got_a, got_b, hats_c, back_c, grad_coarse,
    wdown_t, grad_merged, stats_b, wsecond_t, hats, done,
    grad_fine, back_b, stats, grad_c, total_next,
):
    mean, inverse = norm_columns(stats_c, False, members_c)
    shift, slope = back_columns(stats_ec, False, members_c)
    g = {}
    for r in range(-2, CROWS + 2):
        hat = row(hats_c, r).astype(F32)
        if r < 0:
            u = pick(scal, row(got_a, r + 2), row(got_b, r + 2)).astype(F32)
        elif r < CROWS:
            u = row(back_c, r).astype(F32)
        else:
            u = pick(scal, row(got_b, r - CROWS), row(got_a, r - CROWS)).astype(F32)
        if r == -2:
            through = pick(scal, row(got_a, 2), row(got_b, 2)).astype(F32)
        elif r == CROWS + 1:
            through = pick(scal, row(got_b, 2), row(got_a, 2)).astype(F32)
        else:
            through = row(grad_coarse, r).astype(F32)
        value = through + inverse * (u * silu_slope(hat) - shift - hat * slope)
        g[r] = masked(value, r, CROWS, scal).astype(BF16)
        if -1 <= r <= CROWS:
            put(grad_c, r, g[r])
    wdown_t.wait(1)
    weights = whole(wdown_t)
    fine = {}
    for r in range(-1, CROWS + 1):
        value = 0.25 * coarse_untap(mm(weights, stack_rows(g, r)))
        both = jnp.concatenate([value, value], axis=0)
        for i in (2 * r, 2 * r + 1):
            value = masked(row(grad_merged, i).astype(F32) + both, i, ROWS, scal)
            fine[i] = value.astype(BF16)
            if -1 <= i <= ROWS:
                put(grad_fine, i, fine[i])
    wsecond_t.wait(1)
    hats.wait(1)
    stats_b.wait(1)
    weights = whole(wsecond_t)
    mean, inverse = norm_columns(stats_b, True, members)
    total = jnp.zeros((128, HALF), F32)
    cross = jnp.zeros((128, HALF), F32)
    for r in range(-1, ROWS + 1):
        value = fine_untap(mm(weights, stack_rows(fine, r)))
        put(back_b, r, value.astype(BF16))
        if 0 <= r < ROWS:
            hat = row(hats, r).astype(F32)
            e = value * silu_slope(hat)
            total = total + e
            cross = cross + e * hat
    put_stats(stats, total, cross)
    give(total_next, whole(stats_b))


def stage_first(
    members, scal, stats_b, stats_eb, hats_b, back_b, wfirst_t, stats_a, hats, done,
    back_a, stats, grad_b, line, total_next,
):
    mean, inverse = norm_columns(stats_b, True, members)
    shift, slope = back_columns(stats_eb, True, members)
    g = {}
    sums = jnp.zeros((128, HALF), F32)
    for r in range(-1, ROWS + 1):
        hat = row(hats_b, r).astype(F32)
        u = row(back_b, r).astype(F32)
        value = inverse * (u * silu_slope(hat) - shift - hat * slope)
        if 0 <= r < ROWS:
            sums = sums + value
        g[r] = masked(value, r, ROWS, scal).astype(BF16)
        put(grad_b, r, g[r])
    wfirst_t.wait(1)
    hats.wait(1)
    stats_a.wait(1)
    weights = whole(wfirst_t)
    total = jnp.zeros((128, HALF), F32)
    cross = jnp.zeros((128, HALF), F32)
    for r in range(ROWS):
        value = fine_untap(mm(weights, stack_rows(g, r)))
        put(back_a, r, value.astype(BF16))
        hat = row(hats, r).astype(F32)
        e = value * silu_slope(hat)
        total = total + e
        cross = cross + e * hat
    put_stats(stats, total, cross)
    sums = to_row(jnp.sum(sums, axis=1, keepdims=True))
    give(line, jnp.broadcast_to(sums, (8, 128)))
    give(total_next, whole(stats_a))


def stage_last(
    members, scal, stats_a, stats_ea, hats, back_a, grad_fine, kept_in, early, middle, first,
    loss, loss_other, keep, send, loss_sum, gs, held, sems,
):
    grads = Source(held, [], 0)
    copies, start = [], 0
    for index, ref in enumerate((early, middle)):
        rows = pl.ds(start, ref.shape[1])
        copies.append(
            pltpu.make_async_copy(ref.spot, grads.spot.at[:, rows, :], sems.at[index])
        )
        copies[index].start()
        start += ref.shape[1]
    give(loss_sum, whole(loss) + whole(loss_other))
    mean, inverse = norm_columns(stats_a, True, members)
    shift, slope = back_columns(stats_ea, True, members)
    for r in range(ROWS):
        hat = row(hats, r).astype(F32)
        u = row(back_a, r).astype(F32)
        value = row(grad_fine, r).astype(F32) + inverse * (
            u * silu_slope(hat) - shift - hat * slope
        )
        put(gs, r, value.astype(BF16))
    kept_in.wait(1)
    first.wait(1)
    parts = []
    for a in range(3):
        blocks = mm_nt(gs[...], kept_in.spot[:, a * HALF : (a + ROWS) * HALF])
        parts.append(
            jnp.concatenate(
                [blocks[:64, :96] + blocks[64:, 32:128], jnp.zeros((64, 32), F32)], axis=1
            )
        )
    size = first.shape[1]
    for f in range(grads.shape[0]):
        grads.spot[f, start : start + size, :] = first.spot[f]
    clear_rest(grads, put_grad(grads, start + size, parts))
    for copy in copies:
        copy.wait()
    half = keep.shape[1]
    odd = scal[8] > 0.5
    for f in range(keep.shape[0]):
        low, high = held[f, :half, :], held[f, half:, :]
        keep.spot[f] = jnp.where(odd, high, low)
        send.spot[f] = jnp.where(odd, low, high)


def join(scal, kept, got, out):
    give(out, (whole(kept).astype(F32) + whole(got).astype(F32)).astype(BF16))


def add_up(scal, got, out):
    total = got.spot[0].astype(F32)
    for index in range(1, got.shape[0]):
        total = total + got.spot[index].astype(F32)
    total = total.astype(BF16)
    for index in range(out.shape[0]):
        out.spot[index] = total


def unpack(starts, scal, mine, other, *refs):
    first, down, second, coarse, up, out, embed, inputs, flat = refs
    half = mine.shape[0]
    odd = scal[8] > 0.5
    flat[:half, :] = jnp.where(odd, whole(other), whole(mine)).astype(F32)
    flat[half:, :] = jnp.where(odd, whole(mine), whole(other)).astype(F32)

    def take(ref, start, out, size, ins, trim=False):
        for t in range(9):
            a, b = t // 3, t % 3
            if ins == 128:
                at, lanes = t, 0
            elif ins == 64:
                at, lanes = (a, b) if b < 2 else (3 + a // 2, a % 2)
            else:
                at, lanes = a, b
            value = ref[start + at * size : start + (at + 1) * size, :]
            if ins == 24:
                out.spot[t] = mm_nt(place(24, 128, 32 * lanes), value.astype(BF16))
                continue
            value = value[:, lanes * ins : (lanes + 1) * ins]
            if trim:
                value = value[:12]
                if out.shape[2] == 32:
                    value = jnp.where(scal[9] > 0.5, value[:, :32], value[:, 32:])
            out.spot[t] = value
        return start + (9 if ins == 128 else 5 if ins == 64 else 3) * size

    start = take(flat, 0, up, up.shape[1], 128)
    start = take(flat, start, coarse, coarse.shape[1], 128)
    take(flat, start, out, 16, 64, trim=True)
    start = take(flat, starts[0], down, down.shape[1], 64)
    take(flat, start, second, second.shape[1], 64)
    start = take(flat, starts[1], first, first.shape[1], 64)
    size = embed.shape[0]
    give(embed, flat[start : start + size, :64])
    take(flat, start + size, inputs, inputs.shape[2], 24)


class Field:
    def __init__(self, array, first):
        self.array, self.first = array, first


class Saved:
    def __init__(self, item, low=None, high=None, when=0):
        self.item, self.low, self.high, self.when = item, low, high, when


def shape(*dims, dtype=F32):
    return jax.ShapeDtypeStruct(dims, dtype)


def rows_of(first, number, dtype=F32):
    return Field(shape(number, 128, HALF, dtype=dtype), first)


def flat_rows(first, number, channels):
    return Field(shape(channels, number * HALF, dtype=BF16), first)


def opened(item):
    saved = item if isinstance(item, Saved) else None
    item = saved.item if saved else item
    if isinstance(item, Field):
        return saved, item.array, item.first
    return saved, item, 0


def position():
    me, bands = lax.axis_index("rows"), lax.axis_size("rows")
    return {
        6: jnp.where(me > 0, 1.0, 0.0),
        7: jnp.where(me < bands - 1, 1.0, 0.0),
        8: jnp.where(me % 2 == 1, 1.0, 0.0),
        9: jnp.where(lax.axis_index("fsdp") == 0, 1.0, 0.0),
    }


def run(name, kernel, outs, scal, *operands, scratch=()):
    vmem, hbm = pl.BlockSpec(memory_space=pltpu.VMEM), pl.BlockSpec(memory_space=pltpu.HBM)
    in_specs, arrays, plans, spots = [], [], [], []
    if scal is not None:
        in_specs, arrays = [pl.BlockSpec(memory_space=pltpu.SMEM)], [scal]
    for item in operands:
        saved, item, first = opened(item)
        if saved is None:
            in_specs.append(vmem)
            arrays.append(item)
            plans.append((first, None, None))
            continue
        part = None
        dims = item.shape
        if saved.low is not None:
            part = pl.ds(saved.low - first, saved.high - saved.low)
            dims = (saved.high - saved.low,) + dims[1:]
            first = saved.low
        in_specs.append(hbm)
        arrays.append(pltpu.with_memory_space_constraint(item, pltpu.HBM))
        if saved.when is None:
            plans.append((first, None, None))
            continue
        plans.append((first, (saved.when, part), len(spots)))
        spots.append(pltpu.VMEM(dims, item.dtype))
    ins = len(operands)
    out_specs, out_shapes = [], []
    for item in outs:
        saved, item, first = opened(item)
        if saved is None:
            out_specs.append(vmem)
            out_shapes.append(item)
            plans.append((first, None, None))
            continue
        out_specs.append(hbm)
        out_shapes.append(pltpu.HBM(item.shape, item.dtype))
        last = None
        if isinstance(saved.item, Field):
            count = item.shape[0] if len(item.shape) == 3 else item.shape[1] // HALF
            last = first + count - 1
        if saved.when is None:
            plans.append((first, None, None))
            continue
        plans.append((first, (last, None), len(spots)))
        spots.append(pltpu.VMEM(item.shape, item.dtype))

    def body(*refs):
        numbers = position()
        if scal is not None:
            numbers.update({index: refs[0][index] for index in range(6)})
            refs = refs[1:]
        given, refs = refs[: len(plans)], refs[len(plans) :]
        held, refs = refs[: len(spots)], refs[len(spots) :]
        sems, extra = refs[0], refs[1:]
        wrapped = []
        for index, (ref, (first, plan, place_at)) in enumerate(zip(given, plans)):
            copies = []
            if plan is not None:
                where = held[place_at]
                when, part = plan
                if index < ins:
                    source = ref if part is None else ref.at[part]
                    copies.append((when, pltpu.make_async_copy(source, where, sems.at[place_at])))
                else:
                    copies.append((when, pltpu.make_async_copy(where, ref, sems.at[place_at])))
                ref = where
            wrapped.append((Source if index < ins else Sink)(ref, copies, first))
        for item in wrapped[:ins]:
            item.wait(0)
        kernel(numbers, *wrapped, *extra)
        for item in wrapped[ins:]:
            item.finish()
        for item in wrapped[ins:]:
            for copy in item.started:
                copy.wait()

    made = pl.pallas_call(
        body,
        out_shape=tuple(out_shapes),
        in_specs=in_specs,
        out_specs=tuple(out_specs),
        scratch_shapes=spots
        + [pltpu.SemaphoreType.DMA((max(len(spots), 1),))]
        + [pltpu.VMEM(*item) if isinstance(item, tuple) else item for item in scratch],
        compiler_params=pltpu.CompilerParams(vmem_limit_bytes=LIMIT),
        name=name,
    )(*arrays)
    results = []
    for array, item in zip(made, outs):
        item = item.item if isinstance(item, Saved) else item
        results.append(Field(array, item.first) if isinstance(item, Field) else array)
    return results


def sum_parts(stats):
    return lax.all_to_all(stats, "rows", 0, 0)


def swap(value_a, value_b):
    count = lax.axis_size("rows")
    pairs = [(i, i ^ 1) for i in range(count)]
    across = []
    for i in range(1, count - 1, 2):
        across += [(i, i + 1), (i + 1, i)]
    return lax.ppermute(value_a, "rows", pairs), lax.ppermute(value_b, "rows", across)


def gather_packed(packed):
    if lax.axis_size("fsdp") == 2:
        return [packed, lax.ppermute(packed, "fsdp", [(0, 1), (1, 0)])]
    whole = lax.all_gather(packed, "fsdp").astype(F32)
    return [whole[i] for i in range(whole.shape[0])]


def group_shape(rows, count):
    return shape(count, -(-rows // 16) * 16, 128, dtype=BF16)


def per_device(
    residual_target,
    conditioning,
    noise_sample,
    noise_level,
    input_kernel,
    first_kernel,
    second_kernel,
    down_kernel,
    coarse_kernel,
    upward_kernel,
    output_kernel,
    embed_matrix,
):
    bands, count = lax.axis_size("rows"), lax.axis_size("fsdp")
    members = 2 * ROWS * 2 * HALF * bands
    members_c = 4 * CROWS * HALF * bands
    members_all = count * residual_target.size * bands
    sigma_level, skip_scale, out_scale, in_scale, weight = preconditions(noise_level[0])
    coef = 2.0 * weight * out_scale / members_all
    scal = jnp.stack([sigma_level, skip_scale, out_scale, in_scale, weight, coef])
    embedded = embedding(sigma_level, embed_matrix.shape[0] * count)
    target = residual_target.reshape(12 * ROWS, 512)
    condition = conditioning.reshape(12 * ROWS, 512)
    noise = noise_sample.reshape(12 * ROWS, 512)

    def pack_all(name, shards, rows, *after):
        widths = tuple(
            (9 if item.ndim == 3 else 1, size, item.ndim == 3 and item.shape[1] == 24)
            for item, size in zip(shards, rows)
        )
        total = sum(taps * size for taps, size, _ in widths)
        (packed,) = run(
            name,
            functools.partial(pack, widths),
            [shape(total, 128, dtype=BF16)],
            None,
            *[Saved(item) for item in shards],
            *after,
            scratch=[((total, 128), F32)],
        )
        return packed

    fine_o, coarse_o = input_kernel.shape[1], down_kernel.shape[1]
    inputs_t = jnp.swapaxes(input_kernel, 1, 2)
    early_packed = pack_all(
        "pack_first",
        [inputs_t, first_kernel, embed_matrix],
        [fine_o, fine_o, embed_matrix.shape[0]],
    )
    early = gather_packed(early_packed)
    far = shape(32, FAR * 512, dtype=BF16)
    own, edge_a, edge_b, figures = run(
        "enter",
        enter,
        [shape(32, ROWS * 512, dtype=BF16), far, far, Saved(shape(8, 128))],
        scal,
        Saved(target),
        Saved(condition),
        Saved(noise),
        early[0],
        scratch=[((4, 192, 128), F32), ((2, 16, FAR * 512), BF16)],
    )
    got_a, got_b = swap(edge_a, edge_b)
    rest = pack_all(
        "pack_rest",
        [second_kernel, down_kernel, coarse_kernel, upward_kernel, output_kernel],
        [fine_o, coarse_o, coarse_o, fine_o, 16],
        own,
    )
    vector = jnp.broadcast_to(embedded[None, :], (16, embedded.shape[0]))
    win, wfirst, wfirst_t, shift = run(
        "prepare_first",
        functools.partial(prepare_first, embedded.shape[0]),
        [
            shape(384, 128, dtype=BF16), Saved(shape(384, 256, dtype=BF16)),
            Saved(shape(256, 384, dtype=BF16)), shape(128, 128),
        ],
        None,
        vector, *early,
    )
    stat = shape(bands, 4, 128)
    total = Saved(shape(1, 4, 128))
    act_a, stats_a, kept_in, line_a, line_b = run(
        "stage_a",
        stage_a,
        [
            rows_of(-6, 20), stat, Saved(flat_rows(-1, 10, 128)),
            Saved(shape(16, 512)), Saved(shape(16, 512)),
        ],
        None,
        win, got_a, got_b, own, rest,
        scratch=[((32, FAR * 512), BF16), ((32, FAR * 512), BF16)],
    )
    stats_a = sum_parts(stats_a)
    rest, stats_a = lax.optimization_barrier((rest, stats_a))
    (
        wsecond, wsecond_t, wdown, wdown_t, wcoarse, wcoarse_t, wup, wup_t, wout, wout_t
    ) = run(
        "prepare_rest",
        prepare_rest,
        [
            Saved(shape(384, 256, dtype=BF16)), Saved(shape(256, 384, dtype=BF16)),
            Saved(shape(384, 192, dtype=BF16)), Saved(shape(192, 384, dtype=BF16)),
            Saved(shape(384, 384, dtype=BF16)), Saved(shape(384, 384, dtype=BF16)),
            Saved(shape(384, 512, dtype=BF16)), Saved(shape(512, 384, dtype=BF16)),
            Saved(shape(96, 256, dtype=BF16)), Saved(shape(256, 96, dtype=BF16)),
        ],
        None,
        *gather_packed(rest),
    )

    act_b, stats_b, kept_a, hats_a, act_a, total_a = run(
        "stage_b",
        functools.partial(stage_b, members),
        [
            rows_of(-5, 18), stat, Saved(flat_rows(0, 8, 256), when=None),
            Saved(rows_of(0, 8, BF16)),
            Saved(rows_of(-4, 16), when=None), total,
        ],
        None,
        stats_a, shift, Saved(wfirst, when=1), act_a,
        scratch=[((256, 20 * HALF), BF16), pltpu.SemaphoreType.DMA((2,))],
    )
    stats_b = sum_parts(stats_b)
    fine, act_c, edge, stats_c, kept_b, kept_pool, hats_b, total_b = run(
        "stage_c",
        functools.partial(stage_c, members),
        [
            rows_of(-3, 14), rows_of(-1, 6), Field(shape(128, 2 * HALF), 1), stat,
            Saved(flat_rows(0, 8, 256), when=None), Saved(flat_rows(0, 4, 192)),
            Saved(rows_of(-1, 10, BF16)), total,
        ],
        None,
        stats_b, Saved(wsecond, when=1), act_b, Saved(act_a, when=1), Saved(wdown, when=1),
        scratch=[((256, 18 * HALF), BF16), pltpu.SemaphoreType.DMA((1,))],
    )
    got_a, got_b = swap(edge.array, edge.array)
    stats_c = sum_parts(stats_c)
    merged, hats_c, stats_d, kept_c, kept_up, total_c = run(
        "stage_d",
        functools.partial(stage_d, members_c),
        [
            rows_of(-3, 14), Saved(rows_of(-2, 8, BF16)), stat,
            Saved(flat_rows(0, 4, 384), when=None), Saved(flat_rows(0, 4, 384)), total,
        ],
        None,
        stats_c, Saved(wcoarse, when=1), got_a, got_b, act_c, Saved(wup, when=1), fine,
        scratch=[((384, 10 * HALF), BF16), pltpu.SemaphoreType.DMA((1,))],
    )
    stats_d = sum_parts(stats_d)
    edge = Field(shape(128, 3 * HALF, dtype=BF16), 0)
    denoised, back_d, edge_a, edge_b, stats_ed, hats_d, cotangents, kept_d, total_d = run(
        "stage_out",
        functools.partial(stage_out, members),
        [
            Saved(shape(96, 512)), rows_of(0, 8, BF16), edge, edge, stat,
            Saved(rows_of(-3, 14, BF16)),
            Field(shape(10, 32, HALF, dtype=BF16), -1),
            Saved(flat_rows(0, 8, 256), when=None), shape(1, 4, 128),
        ],
        None,
        stats_d, Saved(wout, when=1), merged, Saved(line_a, when=1), Saved(line_b, when=1),
        Saved(target, when=1), Saved(noise, when=1), Saved(wout_t, when=1),
        Saved(figures, when=1),
        scratch=[
            ((160, 512), F32), ((160, 512), F32),
            ((4, 96, 128), F32), ((4, 96, 128), F32), ((4, 96, 128), F32),
            ((256, 12 * HALF), BF16), pltpu.SemaphoreType.DMA((1,)),
        ],
    )
    got_a, got_b = swap(edge_a.array, edge_b.array)
    (grad_out,) = run(
        "grads_out",
        grads_out,
        [Saved(shape(count, 80, 128, dtype=BF16))],
        None,
        cotangents, Saved(kept_d),
        scratch=[((96, 8 * HALF), BF16)],
    )
    stats_ed = sum_parts(stats_ed)
    grad_merged, back_c, grad_coarse, edge_a, edge_b, stats_ec, loss, total_c = run(
        "stage_up",
        functools.partial(stage_up, members, members_c),
        [
            rows_of(-2, 12, BF16), rows_of(0, 4, BF16), rows_of(-1, 6, BF16), edge, edge, stat,
            shape(8, 128), shape(1, 4, 128),
        ],
        None,
        total_d, stats_ed, got_a, got_b, Saved(hats_d), back_d, Saved(wup_t, when=1),
        Saved(total_c, when=1),
        Saved(hats_c, when=1), Saved(wcoarse_t, when=1), Saved(grad_out, when=None),
    )
    got_a, got_b = swap(edge_a.array, edge_b.array)
    (early,) = run(
        "grads_up",
        grads_up,
        [Saved(group_shape(9 * (fine_o + coarse_o) + 80, count))],
        None,
        grad_merged, grad_coarse, Saved(kept_up), Saved(kept_c), Saved(grad_out),
        scratch=[
            ((384, 8 * HALF), BF16), ((384, 8 * HALF), BF16), ((384, 4 * HALF), BF16)
        ],
    )
    stats_ec = sum_parts(stats_ec)
    if count == 2:
        loss_other = lax.ppermute(loss, "fsdp", [(0, 1), (1, 0)])
    else:
        loss_other = lax.psum(loss, "fsdp") - loss
    grad_fine, back_b, stats_eb, grad_c, total_b = run(
        "stage_down",
        functools.partial(stage_down, members, members_c),
        [
            rows_of(-1, 10, BF16), rows_of(-1, 10, BF16), stat, rows_of(-1, 6, BF16),
            shape(1, 4, 128),
        ],
        None,
        total_c, stats_ec, got_a, got_b, Saved(hats_c), back_c, grad_coarse,
        Saved(wdown_t, when=1), grad_merged, Saved(total_b, when=1), Saved(wsecond_t, when=1),
        Saved(hats_b, 0, 8, when=1), Saved(early, when=None),
    )
    (middle,) = run(
        "grads_down",
        grads_down,
        [Saved(group_shape(5 * (fine_o + coarse_o), count))],
        None,
        grad_fine, grad_c, Saved(kept_pool), Saved(kept_b),
        scratch=[((384, 8 * HALF), BF16), ((384, 4 * HALF), BF16)],
    )
    stats_eb = sum_parts(stats_eb)
    back_a, stats_ea, grad_b, line, total_a = run(
        "stage_first",
        functools.partial(stage_first, members),
        [
            rows_of(0, 8, BF16), stat, rows_of(-1, 10, BF16), shape(8, 128),
            shape(1, 4, 128),
        ],
        None,
        total_b, stats_eb, Saved(hats_b), back_b, Saved(wfirst_t, when=1), Saved(total_a, when=1),
        Saved(hats_a, when=1), Saved(middle, when=None),
    )
    (grad_first,) = run(
        "grads_first",
        grads_first,
        [Saved(shape(count, 5 * fine_o + embed_matrix.shape[0], 128, dtype=BF16))],
        None,
        grad_b, line, vector, Saved(kept_a),
        scratch=[((384, 8 * HALF), BF16)],
    )
    stats_ea = sum_parts(stats_ea)
    late = group_shape(8 * fine_o + embed_matrix.shape[0], count)
    starts = [early.shape[1], early.shape[1] + middle.shape[1]]
    total = starts[1] + late.shape[1]
    chunk = -(-total // (16 * bands)) * 16
    chips = bands // 2
    half = shape(count, chunk * chips, 128, dtype=BF16)
    keep, send, loss = run(
        "stage_last",
        functools.partial(stage_last, members),
        [half, half, shape(8, 128)],
        None,
        total_a, stats_ea, Saved(hats_a), back_a, grad_fine, Saved(kept_in, when=1),
        Saved(early, when=None), Saved(middle, when=None), Saved(grad_first, when=1), loss, loss_other,
        scratch=[
            ((128, 8 * HALF), BF16), ((count, chunk * bands, 128), BF16),
            pltpu.SemaphoreType.DMA((2,)),
        ],
    )
    loss_value = loss[0, 0] / members_all
    pairs = [(i, i ^ 1) for i in range(bands)]
    got = lax.ppermute(send, "rows", pairs)
    (both,) = run("join", join, [half], None, keep, got)
    both = both.reshape(count * chips, chunk, 128)
    cores = [[f * bands + r for f in range(count) for r in range(c, bands, 2)] for c in range(2)]
    got = lax.all_to_all(both, ("fsdp", "rows"), 0, 0, axis_index_groups=cores)
    (mine,) = run("add_up", add_up, [shape(chips, chunk, 128, dtype=BF16)], None, got)
    cores = [[r for r in range(c, bands, 2)] for c in range(2)]
    mine = lax.all_to_all(mine, "rows", 0, 0, axis_index_groups=cores)
    mine = mine.reshape(chips * chunk, 128)
    other = lax.ppermute(mine, "rows", pairs)
    first_g, down_g, second_g, coarse_g, up_g, out_g, embed_g, in_g = run(
        "unpack",
        functools.partial(unpack, starts),
        [
            shape(*first_kernel.shape),
            shape(*down_kernel.shape),
            shape(*second_kernel.shape),
            shape(*coarse_kernel.shape),
            shape(*upward_kernel.shape),
            shape(9, 12, output_kernel.shape[2] if count == 2 else 64),
            shape(*embed_matrix.shape),
            shape(*inputs_t.shape),
        ],
        None,
        mine, other,
        scratch=[((chunk * bands, 128), F32)],
    )
    width = output_kernel.shape[2]
    if count != 2:
        out_g = lax.dynamic_slice_in_dim(out_g, lax.axis_index("fsdp") * width, width, axis=2)
    return (
        denoised.reshape(residual_target.shape),
        loss_value,
        jnp.swapaxes(in_g, 1, 2),
        first_g,
        second_g,
        down_g,
        coarse_g,
        up_g,
        out_g,
        embed_g,
    )


def solution(mesh):
    in_specs = (
        P("fsdp", None, "rows", None),
        P("fsdp", None, "rows", None),
        P("fsdp", None, "rows", None),
        P("fsdp"),
        P(None, "fsdp", None),
        P(None, "fsdp", None),
        P(None, "fsdp", None),
        P(None, "fsdp", None),
        P(None, "fsdp", None),
        P(None, "fsdp", None),
        P(None, None, "fsdp"),
        P("fsdp", None),
    )
    out_specs = (
        P("fsdp", None, "rows", None),
        P(),
        P(None, "fsdp", None),
        P(None, "fsdp", None),
        P(None, "fsdp", None),
        P(None, "fsdp", None),
        P(None, "fsdp", None),
        P(None, "fsdp", None),
        P(None, None, "fsdp"),
        P("fsdp", None),
    )
    return jax.shard_map(
        per_device, mesh=mesh, in_specs=in_specs, out_specs=out_specs, check_vma=False
    )
```

```python
import functools

import jax
import jax.numpy as jnp
from jax import lax
from jax.experimental import pallas as pl
from jax.experimental.pallas import tpu as pltpu
from jax.sharding import PartitionSpec as P

GROUPS = 32
STEPS = 64

sigma_low = 0.002
sigma_high = 80.0
sigma_data = 0.5
rho_power = 7.0
eps_norm = 1e-05

F32 = jnp.float32
BF16 = jnp.bfloat16

HALF = 256
ROWS = 8
CROWS = 4
FAR = 7
LIMIT = 24 * 1024 * 1024


def preconditions(level_index):
    ramp_value = level_index.astype(jnp.float32) / (STEPS - 1)
    top_root = sigma_high ** (1.0 / rho_power)
    bottom = sigma_low ** (1.0 / rho_power)
    sigma_level = (top_root + ramp_value * (bottom - top_root)) ** rho_power
    sigma_total = sigma_level * sigma_level + sigma_data * sigma_data
    skip_scale = sigma_data * sigma_data / sigma_total
    out_scale = sigma_level * sigma_data * lax.rsqrt(sigma_total)
    in_scale = lax.rsqrt(sigma_total)
    weight = sigma_total / (sigma_level * sigma_data) ** 2
    return (sigma_level, skip_scale, out_scale, in_scale, weight)


def embedding(sigma_level, features):
    half_count = features // 2
    ramp_steps = jnp.arange(half_count, dtype=jnp.float32) / half_count
    frequency = 64.0 * 0.01**ramp_steps
    phase_angle = 0.25 * jnp.log(sigma_level) * frequency
    return jnp.concatenate([jnp.cos(phase_angle), jnp.sin(phase_angle)]).astype(jnp.bfloat16)


class Source:
    def __init__(self, spot, copies, first):
        self.spot, self.copies, self.first = spot, copies, first
        self.shape = spot.shape
        for _, copy in copies:
            copy.start()

    def wait(self, stage):
        for when, copy in self.copies:
            if when == stage:
                copy.wait()


class Sink:
    def __init__(self, spot, copies, first):
        self.spot, self.copies, self.first = spot, copies, first
        self.shape = spot.shape
        self.started = []

    def done(self, index):
        for last, copy in self.copies:
            if last == index:
                copy.start()
                self.started.append(copy)

    def send(self, source, sem):
        copy = pltpu.make_async_copy(source, self.spot, sem)
        copy.start()
        self.started.append(copy)

    def finish(self):
        for _, copy in self.copies:
            if not any(copy is other for other in self.started):
                copy.start()
                self.started.append(copy)


def spot(ref, index):
    if len(ref.shape) == 3:
        return (index - getattr(ref, "first", 0),)
    start = index - getattr(ref, "first", 0)
    return (slice(None), slice(start * HALF, (start + 1) * HALF))


def row(ref, index):
    return getattr(ref, "spot", ref)[spot(ref, index)]


def put(ref, index, value):
    getattr(ref, "spot", ref)[spot(ref, index)] = value
    if isinstance(ref, Sink):
        ref.done(index)


def whole(ref):
    return ref.spot[...]


def give(ref, value):
    ref.spot[...] = value
    ref.finish()


def lane(shape):
    return lax.broadcasted_iota(jnp.int32, shape, 1)


def from_left(value):
    moved = pltpu.roll(value, 1, 1)
    return jnp.where(lane(value.shape) == 0, 0.0, moved)


def from_right(value):
    moved = pltpu.roll(value, value.shape[1] - 1, 1)
    return jnp.where(lane(value.shape) == value.shape[1] - 1, 0.0, moved)


def mm(left, right):
    return jnp.dot(left, right, preferred_element_type=F32)


def mm_nt(left, right):
    return lax.dot_general(left, right, (((1,), (1,)), ((), ())), preferred_element_type=F32)


def fine_taps(value):
    half = value.shape[0] // 2
    even, odd = value[:half], value[half:]
    return jnp.concatenate([from_left(odd), value, from_right(even)], axis=0).astype(BF16)


def coarse_taps(value):
    return jnp.concatenate([from_left(value), value, from_right(value)], axis=0).astype(BF16)


def fine_untap(taps):
    size = taps.shape[0] // 4
    even = taps[size : 2 * size] + from_left(taps[3 * size :])
    odd = taps[2 * size : 3 * size] + from_right(taps[:size])
    return jnp.concatenate([even, odd], axis=0)


def coarse_untap(taps):
    size = taps.shape[0] // 3
    return taps[size : 2 * size] + from_right(taps[:size]) + from_left(taps[2 * size :])


def spread(parts, first, last):
    out = {}
    for i in range(first, last + 1):
        size = parts[i - 1].shape[0] // 3
        out[i] = parts[i - 1][:size] + parts[i][size : 2 * size] + parts[i + 1][2 * size :]
    return out


def stack_rows(g, r):
    return jnp.concatenate([g[r + 1], g[r], g[r - 1]], axis=0)


def same_group(size, fine):
    left = lax.broadcasted_iota(jnp.int32, (size, size), 0)
    right = lax.broadcasted_iota(jnp.int32, (size, size), 1)
    if fine:
        half = size // 2
        left, right = left % half, right % half
        per = half // GROUPS
    else:
        per = size // GROUPS
    return left // per == right // per


def total_stats(stats):
    total = stats.spot[0]
    for index in range(1, stats.shape[0]):
        total = total + stats.spot[index]
    return total


def group_sums(stats, fine):
    total = total_stats(stats)
    member = same_group(128, fine)
    first = jnp.sum(jnp.where(member, total[0:1, :], 0.0), axis=1, keepdims=True)
    second = jnp.sum(jnp.where(member, total[1:2, :], 0.0), axis=1, keepdims=True)
    return first, second


def norm_columns(stats_ref, fine, members):
    first, second = group_sums(stats_ref, fine)
    mean = first / members
    inverse = lax.rsqrt(second / members - mean * mean + eps_norm)
    return mean, inverse


def back_columns(stats_ref, fine, members):
    first, second = group_sums(stats_ref, fine)
    return first / members, second / members


def to_row(column):
    size = column.shape[0]
    diagonal = lax.broadcasted_iota(jnp.int32, (size, size), 0) == lax.broadcasted_iota(
        jnp.int32, (size, size), 1
    )
    return jnp.sum(jnp.where(diagonal, column, 0.0), axis=0, keepdims=True)


def put_stats(ref, first, second, third=None):
    first = to_row(jnp.sum(first, axis=1, keepdims=True))
    second = to_row(jnp.sum(second, axis=1, keepdims=True))
    if third is None:
        third = jnp.zeros((1, 128), F32)
    block = jnp.concatenate([first, second, third, jnp.zeros((1, 128), F32)], axis=0)
    for index in range(ref.shape[0]):
        ref.spot[index] = block
    ref.finish()


def silu(h):
    t = 0.5 * h
    return t + t * jnp.tanh(t)


def silu_slope(h):
    s = 0.5 + 0.5 * jnp.tanh(0.5 * h)
    return s * (1.0 + h * (1.0 - s))


def masked(value, index, rows, scal):
    if index < 0:
        return value * scal[6]
    if index >= rows:
        return value * scal[7]
    return value


def pick(scal, when_odd, when_even):
    return jnp.where(scal[8] > 0.5, when_odd, when_even)


def spill(ref, value):
    for t in range(4):
        ref[t, : value.shape[0], :] = value[:, 128 * t : 128 * (t + 1)]


def strided(ref, index, size):
    return jnp.concatenate(
        [ref[t, pl.ds(index, size, stride=ROWS), :] for t in range(4)], axis=1
    )


def interleave(transposed):
    left = lax.broadcasted_iota(jnp.int32, (512, 512), 0)
    right = lax.broadcasted_iota(jnp.int32, (512, 512), 1)
    if transposed:
        left, right = right, left
    place = (left & 1) * HALF + (left >> 1)
    return jnp.where(place == right, 1.0, 0.0).astype(BF16)


def fine_grad(blocks, outs, ins):
    parts = []
    for a in range(3):
        even = blocks[(2 * a) * outs : (2 * a + 1) * outs]
        odd = blocks[(2 * a + 1) * outs : (2 * a + 2) * outs]
        parts.append(even[:, : 3 * ins] + odd[:, ins : 4 * ins])
    return parts


def grad_blocks(parts, ins):
    if ins == 128:
        return [part[:, 128 * b : 128 * (b + 1)] for part in parts for b in range(3)]
    if ins == 64:
        blank = jnp.zeros(parts[0][:, :64].shape, F32)
        blocks = [part[:, :128] for part in parts]
        blocks.append(jnp.concatenate([parts[0][:, 128:192], parts[1][:, 128:192]], axis=1))
        blocks.append(jnp.concatenate([parts[2][:, 128:192], blank], axis=1))
        return blocks
    return parts


def put_grad(ref, start, blocks, split=True):
    count = ref.shape[0]
    size = blocks[0].shape[0] // count if split else blocks[0].shape[0]
    for block in blocks:
        for f in range(count):
            piece = block[f * size : (f + 1) * size] if split else block
            ref.spot[f, start : start + size, :] = piece.astype(BF16)
        start += size
    return start


def clear_rest(ref, start):
    count, size, _ = ref.shape
    if start < size:
        for f in range(count):
            ref.spot[f, start:, :] = jnp.zeros((size - start, 128), BF16)


def place(width, target, offset):
    left = lax.broadcasted_iota(jnp.int32, (width, target), 0)
    right = lax.broadcasted_iota(jnp.int32, (width, target), 1)
    return jnp.where(left + offset == right, 1.0, 0.0).astype(BF16)


def flipped(value):
    size = value.shape[1]
    return mm_nt(place(size, size, 0), value).astype(BF16)


def tap_of(pieces, offset, index, size, paired=False):
    each = size // len(pieces)
    start = offset + (index // 2 if paired else index) * each
    tap = jnp.concatenate([piece[start : start + each, :] for piece in pieces], axis=0)
    if paired:
        tap = tap[:, 64 * (index % 2) : 64 * (index % 2) + 64]
    return tap.astype(BF16)


def in_order(scal, pieces):
    if len(pieces) == 2:
        mine, other = whole(pieces[0]), whole(pieces[1])
        low = scal[9] > 0.5
        return [jnp.where(low, mine, other), jnp.where(low, other, mine)]
    return [whole(piece) for piece in pieces]


def fine_matrix(taps, slot):
    rows = []
    for a in range(3):
        total = None
        for b in range(3):
            spread_out = jnp.concatenate(
                [place(slot, 4 * slot, b * slot), place(slot, 4 * slot, (b + 1) * slot)], axis=1
            )
            term = mm(taps[3 * a + b][:, :slot], spread_out)
            total = term if total is None else total + term
        rows += [total[:, : 4 * slot], total[:, 4 * slot :]]
    return jnp.concatenate(rows, axis=0).astype(BF16)


def pack(widths, scal, *refs):
    shards, (out, scratch) = refs[: len(widths)], refs[-2:]
    scratch[...] = jnp.zeros(scratch.shape, F32)
    start = 0
    for shard, (taps, rows, swapped) in zip(shards, widths):
        if taps == 1:
            scratch[start : start + rows, : shard.shape[1]] = whole(shard)
            start += rows
        else:
            for t in range(taps):
                value = shard.spot[t]
                if swapped:
                    value = mm_nt(place(value.shape[1], value.shape[1], 0), value.astype(BF16))
                if value.shape[1] == 64:
                    lanes = slice(64 * (t % 2), 64 * (t % 2) + 64)
                    scratch[start : start + value.shape[0], lanes] = value
                    start += rows if t % 2 or t == taps - 1 else 0
                else:
                    scratch[start : start + value.shape[0], : value.shape[1]] = value
                    start += rows
    give(out, scratch[...].astype(BF16))


def prepare_rest(scal, *refs):
    pieces = refs[:-10]
    wsecond, wsecond_t, wdown, wdown_t, wcoarse, wcoarse_t, wup, wup_t, wout, wout_t = refs[-10:]
    count = len(pieces)
    pieces = in_order(scal, pieces)
    start = 0

    def taps_of(size, paired=False):
        nonlocal start
        taps = [tap_of(pieces, start, t, size, paired) for t in range(9)]
        start += (5 if paired else 9) * (size // count)
        return taps

    def both(value, forward, backward):
        give(forward, value)
        give(backward, flipped(value))

    both(fine_matrix(taps_of(64, True), 64), wsecond, wsecond_t)
    taps = taps_of(128, True)
    rows = []
    for a in range(3):
        total = None
        for b in range(3):
            term = mm(taps[3 * a + b][:, :64], place(64, 256, 64 * b))
            total = term if total is None else total + term
        rows.append(total)
    both(jnp.concatenate(rows, axis=0)[:, :192].astype(BF16), wdown, wdown_t)
    taps = taps_of(128)
    rows = [jnp.concatenate(taps[3 * a : 3 * a + 3], axis=1) for a in range(3)]
    both(jnp.concatenate(rows, axis=0), wcoarse, wcoarse_t)
    taps = taps_of(64)
    rows = []
    blank = jnp.zeros((64, 128), BF16)
    for a in range(3):
        rows.append(jnp.concatenate(taps[3 * a : 3 * a + 3] + [blank], axis=1))
        rows.append(jnp.concatenate([blank] + taps[3 * a : 3 * a + 3], axis=1))
    both(jnp.concatenate(rows, axis=0), wup, wup_t)
    taps = []
    width = 64 // count
    for t in range(9):
        total = None
        for s in range(count):
            tap = pieces[s][start + 16 * t : start + 16 * (t + 1), :].astype(BF16)
            term = mm(tap[:, :width], place(width, 128, s * width))
            total = term if total is None else total + term
        taps.append(total.astype(BF16))
    both(fine_matrix(taps, 64), wout, wout_t)


def enter(
    widths, scal, target, condition, noise, *refs
):
    *shards, packed, own, edge_a, edge_b, figures, taps, scratch, marks = refs
    for item in shards:
        item.wait(1)
    pack(widths, scal, *shards, packed, taps)
    for item in (target, condition, noise):
        item.wait(2)
    values = [jnp.full((1, 128), scal[k], F32) for k in range(6)]
    give(figures, jnp.concatenate(values + [jnp.zeros((2, 128), F32)], axis=0))
    sigma, skip, in_scale = scal[0], scal[1], scal[3]
    goal = whole(target)
    noisy = goal + sigma * whole(noise)
    q = skip * noisy - goal
    natural = jnp.concatenate([in_scale * noisy, whole(condition)], axis=0).astype(BF16)
    spill(scratch, mm(natural, interleave(False)))
    blank = jnp.zeros((8, 512), F32)
    for i in range(ROWS):
        value = strided(scratch, i, 24)
        own.spot[:, i * 512 : (i + 1) * 512] = jnp.concatenate([value, blank], axis=0).astype(BF16)
    spill(scratch, q)
    blank = jnp.zeros((4, 512), F32)
    for j, i in enumerate((0, ROWS - 1)):
        rest = jnp.concatenate([strided(scratch, i, 12), blank], axis=0)
        marks[j] = jnp.zeros(marks.shape[1:], BF16)
        for part in range(3):
            piece = rest.astype(BF16)
            rest = rest - piece.astype(F32)
            for k in range(2):
                lanes = slice((2 * part + k) * 512, (2 * part + k + 1) * 512)
                marks[j, 8:, lanes] = piece[8 * k : 8 * k + 8]
    for j, edge in enumerate((edge_a, edge_b)):
        odd = scal[8] > 0.5 if j == 0 else scal[8] < 0.5
        low = (ROWS - FAR) * 512
        edge.spot[:16, :] = jnp.where(odd, own.spot[:16, : FAR * 512], own.spot[:16, low:])
        edge.spot[16:, :] = jnp.where(odd, own.spot[16:, : FAR * 512], own.spot[16:, low:]) + (
            jnp.where(odd, marks[0], marks[1])
        )


def marked(scal, got):
    halves = []
    for k in range(2):
        total = None
        for part in range(3):
            lanes = slice((2 * part + k) * 512, (2 * part + k + 1) * 512)
            piece = got.spot[16:32, lanes].astype(F32)[8:]
            total = piece if total is None else total + piece
        halves.append(total)
    return jnp.concatenate(halves, axis=0)


def stage_a(scal, got_a, got_b, own, done, *refs):
    *pieces, act, stats, kept, line_a, line_b, above, below = refs
    pieces = in_order(scal, pieces)
    weights = fine_matrix([tap_of(pieces, 0, t, 64) for t in range(9)], 32)
    give(line_a, marked(scal, got_a))
    give(line_b, marked(scal, got_b))
    above[...] = pick(scal, whole(got_a), whole(got_b))
    below[...] = pick(scal, whole(got_b), whole(got_a))
    clear = jnp.zeros((16, FAR * 512), BF16)
    keep = lax.broadcasted_iota(jnp.int32, (16, FAR * 512), 0) < 8
    for ref in (above, below):
        ref[16:, :] = jnp.where(keep, ref[16:, :], clear)
    parts = {}
    total = jnp.zeros((128, HALF), F32)
    square = jnp.zeros((128, HALF), F32)
    for r in range(-FAR, ROWS + FAR):
        if r < 0:
            value = above[:, (r + FAR) * 512 : (r + FAR + 1) * 512]
        elif r < ROWS:
            value = own.spot[:, r * 512 : (r + 1) * 512]
        else:
            value = below[:, (r - ROWS) * 512 : (r - ROWS + 1) * 512]
        value = value.astype(F32)
        z = fine_taps(jnp.concatenate([value[:, :HALF], value[:, HALF:]], axis=0))
        if -1 <= r <= ROWS:
            put(kept, r, z)
        parts[r] = mm(weights, z)
        i = r - 1
        if i > -FAR:
            value = spread(parts, i, i)[i]
            put(act, i, value)
            del parts[i - 1]
            if 0 <= i < ROWS:
                total = total + value
                square = square + value * value
    put_stats(stats, total, square)


def slot(ref, index):
    return ref[:, index * HALF : (index + 1) * HALF]


def fill(ref, index, value):
    ref[:, index * HALF : (index + 1) * HALF] = value


def stage_b(members, embed_size, scal, stats_a, act_a, vec, *refs):
    *pieces, act_b, stats, kept, hats, passed, totals, wfirst_t, wfirst, zs, sems = refs
    passed.send(act_a.spot.at[pl.ds(2, 16)], sems.at[0])
    give(totals, total_stats(stats_a)[None])
    count = len(pieces)
    pieces = in_order(scal, pieces)
    start = 9 * (64 // count)
    first = fine_matrix([tap_of(pieces, start, t, 64, True) for t in range(9)], 64)
    start += 5 * (64 // count)
    wfirst[...] = first
    give(wfirst_t, flipped(first))
    line = mm(whole(vec), tap_of(pieces, start, 0, embed_size))[0:1, :64]
    both = jnp.concatenate([line, line], axis=1)
    lift = jnp.sum(place(128, 128, 0).astype(F32) * both, axis=1, keepdims=True)
    mean, inverse = norm_columns(stats_a, True, members)
    for r in range(-6, ROWS + 6):
        hat = (row(act_a, r) - mean) * inverse
        fill(zs, r + 6, fine_taps(masked(silu(hat), r, ROWS, scal)))
        if 0 <= r < ROWS:
            hats.spot[r] = hat.astype(BF16)
    hats.finish()
    kept.send(zs.at[:, pl.ds(6 * HALF, 8 * HALF)], sems.at[1])
    parts = {}
    total = jnp.zeros((128, HALF), F32)
    square = jnp.zeros((128, HALF), F32)
    for r in range(-6, ROWS + 6):
        parts[r] = mm(wfirst[...], slot(zs, r + 6))
        i = r - 1
        if i > -6:
            value = spread(parts, i, i)[i] + lift
            put(act_b, i, value)
            del parts[i - 1]
            if 0 <= i < ROWS:
                total = total + value
                square = square + value * value
    put_stats(stats, total, square)


def stage_c(
    members, scal, stats_b, wsecond, act_b, act_a, wdown,
    fine, act_c, edge, stats, kept, kept_pool, hats, totals, zs, convolved, sems,
):
    give(totals, total_stats(stats_b)[None])
    mean, inverse = norm_columns(stats_b, True, members)
    for r in range(-5, ROWS + 5):
        hat = (row(act_b, r) - mean) * inverse
        fill(zs, r + 5, fine_taps(masked(silu(hat), r, ROWS, scal)))
        if -1 <= r <= ROWS:
            hats.spot[r + 1] = hat.astype(BF16)
    hats.finish()
    kept.send(zs.at[:, pl.ds(5 * HALF, 8 * HALF)], sems.at[0])
    wsecond.wait(1)
    parts = {}
    for r in range(-5, ROWS + 5):
        parts[r] = mm(whole(wsecond), slot(zs, r + 5))
        i = r - 1
        if i > -5:
            convolved[i + 4] = spread(parts, i, i)[i]
            del parts[i - 1]
    act_a.wait(1)
    wdown.wait(1)
    pooled = {}
    half = {}
    for i in range(-4, ROWS + 4):
        value = convolved[i + 4] + row(act_a, i)
        if -3 <= i < ROWS + 3:
            put(fine, i, value)
        half[i] = value[:64] + value[64:]
        if i % 2:
            value = 0.25 * (half.pop(i - 1) + half.pop(i))
            value = masked(value, i // 2, CROWS, scal)
            pooled[i // 2] = value.astype(BF16).astype(F32)
    weights = whole(wdown)
    parts = {}
    total = jnp.zeros((128, HALF), F32)
    square = jnp.zeros((128, HALF), F32)
    for r in range(-2, CROWS + 2):
        z = coarse_taps(pooled[r])
        if 0 <= r < CROWS:
            put(kept_pool, r, z)
        parts[r] = mm(weights, z)
        i = r - 1
        if i > -2:
            value = spread(parts, i, i)[i]
            put(act_c, i, value)
            del parts[i - 1]
            if 0 <= i < CROWS:
                total = total + value
                square = square + value * value
            if i in (1, 2):
                put(edge, i, value)
    put_stats(stats, total, square)


def stage_d(
    members, scal, stats_c, wcoarse, got_a, got_b, act_c, wup, fine,
    merged, hats, stats, kept_c, kept_up, totals, zs, sems,
):
    give(totals, total_stats(stats_c)[None])
    mean, inverse = norm_columns(stats_c, False, members)
    ring = {}
    for j in range(2):
        ring[j - 3] = pick(scal, row(got_a, j), row(got_b, j))
        ring[CROWS + 1 + j] = pick(scal, row(got_b, j), row(got_a, j))
    for j in range(-1, CROWS + 1):
        ring[j] = row(act_c, j)
    for r in range(-3, CROWS + 3):
        hat = (ring[r] - mean) * inverse
        fill(zs, r + 3, coarse_taps(masked(silu(hat), r, CROWS, scal)))
        if -2 <= r < CROWS + 2:
            hats.spot[r + 2] = hat.astype(BF16)
    hats.finish()
    kept_c.send(zs.at[:, pl.ds(3 * HALF, 4 * HALF)], sems.at[0])
    wcoarse.wait(1)
    wup.wait(1)
    parts = {}
    lifted = {}
    for r in range(-3, CROWS + 3):
        parts[r] = mm(whole(wcoarse), slot(zs, r + 3))
        i = r - 1
        if i > -3:
            value = spread(parts, i, i)[i] + ring[i]
            del parts[i - 1]
            lifted[i] = masked(value, i, CROWS, scal).astype(BF16).astype(F32)
    weights = whole(wup)
    parts = {}
    total = jnp.zeros((128, HALF), F32)
    square = jnp.zeros((128, HALF), F32)
    for r in range(-2, CROWS + 2):
        z = coarse_taps(lifted[r])
        if 0 <= r < CROWS:
            put(kept_up, r, z)
        four = jnp.concatenate([z[:128], z[128:256], z[128:256], z[256:]], axis=0)
        parts[2 * r] = parts[2 * r + 1] = mm(weights, four)
        for i in (2 * r - 1, 2 * r):
            if i >= -3:
                value = spread(parts, i, i)[i] + row(fine, i)
                put(merged, i, value)
                parts.pop(i - 1)
                if 0 <= i < ROWS:
                    total = total + value
                    square = square + value * value
    put_stats(stats, total, square)


def stage_out(
    members, scal, stats_d, wout, merged, line_a, line_b, target, noise, wout_t, figures,
    denoised, back, edge_a, edge_b, stats, hats, cotangents, kept, totals, pairs, cells,
    goals, noisies, found, zs, sems,
):
    give(totals, total_stats(stats_d)[None])
    mean, inverse = norm_columns(stats_d, True, members)
    for r in range(-3, ROWS + 3):
        hat = (row(merged, r) - mean) * inverse
        hats.spot[r + 3] = hat.astype(BF16)
        if -3 < r < ROWS + 2:
            fill(zs, r + 2, fine_taps(masked(silu(hat), r, ROWS, scal)))
    hats.finish()
    kept.send(zs.at[:, pl.ds(2 * HALF, 8 * HALF)], sems.at[0])
    for item in (wout, line_a, line_b, target, noise, wout_t, figures):
        item.wait(1)
    parts = {}
    for r in range(-2, ROWS + 2):
        parts[r] = mm(whole(wout), slot(zs, r + 2))
        i = r - 1
        if i > -2:
            value = spread(parts, i, i)[i]
            del parts[i - 1]
            pairs[16 * (i + 1) : 16 * (i + 2), :] = jnp.concatenate(
                [value[:16], value[16:]], axis=1
            )
    value = pairs[...]
    high = value.astype(BF16)
    low = (value - high.astype(F32)).astype(BF16)
    back_order = interleave(True)
    sigma, skip, out_scale, weight, coef = [
        figures.spot[k : k + 1, 0:1] for k in (0, 1, 2, 4, 5)
    ]
    pairs[...] = mm(high, back_order) + mm(low, back_order)
    blank = jnp.zeros((4, 512), F32)
    loss_sum = jnp.zeros((12, 512), F32)
    top = pick(scal, whole(line_a), whole(line_b)) + out_scale * pairs[0:16, :]
    cells[0:16, :] = coef * scal[6] * top
    low = pick(scal, whole(line_b), whole(line_a)) + out_scale * pairs[16 * (ROWS + 1) :, :]
    cells[16 * (ROWS + 1) :, :] = coef * scal[7] * low
    spill(goals, whole(target))
    spill(noisies, whole(target) + sigma * whole(noise))
    for i in range(ROWS):
        goal = strided(goals, i, 12)
        noisy = strided(noisies, i, 12)
        estimate = skip * noisy + out_scale * pairs[16 * (i + 1) : 16 * (i + 1) + 12, :]
        for t in range(4):
            found[t, pl.ds(i, 12, stride=ROWS), :] = estimate[:, 128 * t : 128 * (t + 1)]
        mismatch = estimate - goal
        loss_sum = loss_sum + weight * mismatch * mismatch
        cells[16 * (i + 1) : 16 * (i + 2), :] = jnp.concatenate([coef * mismatch, blank], axis=0)
    give(denoised, jnp.concatenate([found[t] for t in range(4)], axis=1))
    loss_sum = jnp.broadcast_to(
        jnp.sum(jnp.sum(loss_sum, axis=1, keepdims=True), axis=0, keepdims=True), (1, 128)
    )
    pairs[...] = mm(cells[...].astype(BF16), interleave(False))
    g = {}
    for i in range(-1, ROWS + 1):
        value = pairs[16 * (i + 1) : 16 * (i + 2), :]
        g[i] = jnp.concatenate([value[:, :HALF], value[:, HALF:]], axis=0).astype(BF16)
        put(cotangents, i, g[i])
    weights = whole(wout_t)
    total = jnp.zeros((128, HALF), F32)
    cross = jnp.zeros((128, HALF), F32)
    for r in range(ROWS):
        value = fine_untap(mm(weights, stack_rows(g, r)))
        put(back, r, value.astype(BF16))
        hat = row(hats, r).astype(F32)
        e = value * silu_slope(hat)
        total = total + e
        cross = cross + e * hat
    for j in range(3):
        top, low = row(back, j), row(back, ROWS - 3 + j)
        put(edge_a, j, pick(scal, top, low))
        put(edge_b, j, pick(scal, low, top))
    put_stats(stats, total, cross, loss_sum)


def grads_out(scal, cotangents, zs, grad, gs):
    g = {r: row(cotangents, r) for r in range(-1, ROWS + 1)}
    for r in range(ROWS):
        put(gs, r, stack_rows(g, r))
    parts = fine_grad(mm_nt(gs[...], whole(zs)), 16, 64)
    put_grad(grad, 0, grad_blocks(parts, 64), split=False)


def grads_up(scal, grad_merged, grad_coarse, kept_up, kept_c, grad_out, grads, gs, zs, gc):
    g = {r: row(grad_merged, r) for r in range(-1, ROWS + 1)}
    for r in range(ROWS):
        put(gs, r, stack_rows(g, r))
        put(zs, r, row(kept_up, r // 2))
    g = {r: row(grad_coarse, r) for r in range(-1, CROWS + 1)}
    for r in range(CROWS):
        put(gc, r, stack_rows(g, r))
    blocks = mm_nt(gs[...], zs[...])
    parts = []
    for a in range(3):
        even = blocks[128 * a : 128 * a + 64]
        odd = blocks[128 * a + 64 : 128 * a + 128]
        parts.append(
            jnp.concatenate(
                [
                    even[:, :128] + odd[:, 128:256],
                    even[:, 128:256] + odd[:, 128:256],
                    even[:, 128:256] + odd[:, 256:],
                ],
                axis=1,
            )
        )
    start = put_grad(grads, 0, grad_blocks(parts, 128))
    blocks = mm_nt(gc[...], whole(kept_c))
    parts = [blocks[128 * a : 128 * (a + 1)] for a in range(3)]
    start = put_grad(grads, start, grad_blocks(parts, 128))
    for f in range(grads.shape[0]):
        grads.spot[f, start : start + 80, :] = grad_out.spot[f]
    clear_rest(grads, start + 80)


def grads_down(scal, grad_fine, grad_c, kept_pool, kept_b, grads, gs, gc):
    g = {r: row(grad_fine, r) for r in range(-1, ROWS + 1)}
    for r in range(ROWS):
        put(gs, r, stack_rows(g, r))
    g = {r: row(grad_c, r) for r in range(-1, CROWS + 1)}
    for r in range(CROWS):
        put(gc, r, stack_rows(g, r))
    blocks = mm_nt(gc[...], whole(kept_pool))
    parts = [blocks[128 * a : 128 * (a + 1)] for a in range(3)]
    start = put_grad(grads, 0, grad_blocks(parts, 64))
    parts = fine_grad(mm_nt(gs[...], whole(kept_b)), 64, 64)
    clear_rest(grads, put_grad(grads, start, grad_blocks(parts, 64)))


def grads_first(scal, grad_b, line, vec, kept_a, grads, gs):
    g = {r: row(grad_b, r) for r in range(-1, ROWS + 1)}
    for r in range(ROWS):
        put(gs, r, stack_rows(g, r))
    parts = fine_grad(mm_nt(gs[...], whole(kept_a)), 64, 64)
    start = put_grad(grads, 0, grad_blocks(parts, 64))
    line = line.spot[0:1, :]
    line = line + pltpu.roll(line, 64, 1)
    column = jnp.sum(
        place(128, 128, 0).astype(F32) * vec.spot[0:1, :].astype(F32), axis=1, keepdims=True
    )
    outer = (column * line).astype(BF16)
    size = 128 // grads.shape[0]
    for f in range(grads.shape[0]):
        grads.spot[f, start : start + size, :] = outer[f * size : (f + 1) * size]


def stage_up(
    members, members_c, scal, stats_d, stats_ed, got_a, got_b, hats, back, wup_t, stats_c, hats_c,
    wcoarse_t, done,
    grad_merged, back_c, grad_coarse, edge_a, edge_b, stats, loss, total_next,
):
    give(loss, jnp.broadcast_to(total_stats(stats_ed)[2:3, :], (8, 128)))
    mean, inverse = norm_columns(stats_d, True, members)
    shift, slope = back_columns(stats_ed, True, members)
    hats.wait(1)
    g = {}
    for r in range(-3, ROWS + 3):
        hat = row(hats, r).astype(F32)
        if r < 0:
            u = pick(scal, row(got_a, r + 3), row(got_b, r + 3)).astype(F32)
        elif r < ROWS:
            u = row(back, r).astype(F32)
        else:
            u = pick(scal, row(got_b, r - ROWS), row(got_a, r - ROWS)).astype(F32)
        value = inverse * (u * silu_slope(hat) - shift - hat * slope)
        g[r] = masked(value, r, ROWS, scal).astype(BF16)
        if -2 <= r < ROWS + 2:
            put(grad_merged, r, g[r])
    wup_t.wait(1)
    weights = whole(wup_t)
    gk = {}
    half = {}
    for r in range(-2, ROWS + 2):
        taps = mm(weights, stack_rows(g, r))
        half[r] = taps[128:256] + taps[256:384] + from_right(taps[:128]) + from_left(taps[384:])
        if r % 2:
            value = masked(half.pop(r - 1) + half.pop(r), r // 2, CROWS, scal)
            gk[r // 2] = value.astype(BF16)
            put(grad_coarse, r // 2, gk[r // 2])
    wcoarse_t.wait(1)
    hats_c.wait(1)
    stats_c.wait(1)
    weights = whole(wcoarse_t)
    mean, inverse = norm_columns(stats_c, False, members_c)
    total = jnp.zeros((128, HALF), F32)
    cross = jnp.zeros((128, HALF), F32)
    for r in range(CROWS):
        value = coarse_untap(mm(weights, stack_rows(gk, r)))
        put(back_c, r, value.astype(BF16))
        hat = row(hats_c, r).astype(F32)
        e = value * silu_slope(hat)
        total = total + e
        cross = cross + e * hat
    top = [row(back_c, 0), row(back_c, 1), gk[1]]
    low = [row(back_c, 2), row(back_c, 3), gk[2]]
    for j in range(3):
        put(edge_a, j, pick(scal, top[j], low[j]))
        put(edge_b, j, pick(scal, low[j], top[j]))
    put_stats(stats, total, cross)
    give(total_next, whole(stats_c))


def stage_down(
    members, members_c, scal, stats_c, stats_ec, got_a, got_b, hats_c, back_c, grad_coarse,
    wdown_t, grad_merged, stats_b, wsecond_t, hats, done,
    grad_fine, back_b, stats, grad_c, total_next,
):
    mean, inverse = norm_columns(stats_c, False, members_c)
    shift, slope = back_columns(stats_ec, False, members_c)
    hats_c.wait(1)
    g = {}
    for r in range(-2, CROWS + 2):
        hat = row(hats_c, r).astype(F32)
        if r < 0:
            u = pick(scal, row(got_a, r + 2), row(got_b, r + 2)).astype(F32)
        elif r < CROWS:
            u = row(back_c, r).astype(F32)
        else:
            u = pick(scal, row(got_b, r - CROWS), row(got_a, r - CROWS)).astype(F32)
        if r == -2:
            through = pick(scal, row(got_a, 2), row(got_b, 2)).astype(F32)
        elif r == CROWS + 1:
            through = pick(scal, row(got_b, 2), row(got_a, 2)).astype(F32)
        else:
            through = row(grad_coarse, r).astype(F32)
        value = through + inverse * (u * silu_slope(hat) - shift - hat * slope)
        g[r] = masked(value, r, CROWS, scal).astype(BF16)
        if -1 <= r <= CROWS:
            put(grad_c, r, g[r])
    wdown_t.wait(1)
    weights = whole(wdown_t)
    fine = {}
    for r in range(-1, CROWS + 1):
        value = 0.25 * coarse_untap(mm(weights, stack_rows(g, r)))
        both = jnp.concatenate([value, value], axis=0)
        for i in (2 * r, 2 * r + 1):
            value = masked(row(grad_merged, i).astype(F32) + both, i, ROWS, scal)
            fine[i] = value.astype(BF16)
            if -1 <= i <= ROWS:
                put(grad_fine, i, fine[i])
    wsecond_t.wait(1)
    hats.wait(1)
    stats_b.wait(1)
    weights = whole(wsecond_t)
    mean, inverse = norm_columns(stats_b, True, members)
    total = jnp.zeros((128, HALF), F32)
    cross = jnp.zeros((128, HALF), F32)
    for r in range(-1, ROWS + 1):
        value = fine_untap(mm(weights, stack_rows(fine, r)))
        put(back_b, r, value.astype(BF16))
        if 0 <= r < ROWS:
            hat = row(hats, r).astype(F32)
            e = value * silu_slope(hat)
            total = total + e
            cross = cross + e * hat
    put_stats(stats, total, cross)
    give(total_next, whole(stats_b))


def stage_first(
    members, scal, stats_b, stats_eb, hats_b, back_b, wfirst_t, stats_a, hats, done,
    back_a, stats, grad_b, line, total_next,
):
    mean, inverse = norm_columns(stats_b, True, members)
    shift, slope = back_columns(stats_eb, True, members)
    hats_b.wait(1)
    g = {}
    sums = jnp.zeros((128, HALF), F32)
    for r in range(-1, ROWS + 1):
        hat = row(hats_b, r).astype(F32)
        u = row(back_b, r).astype(F32)
        value = inverse * (u * silu_slope(hat) - shift - hat * slope)
        if 0 <= r < ROWS:
            sums = sums + value
        g[r] = masked(value, r, ROWS, scal).astype(BF16)
        put(grad_b, r, g[r])
    wfirst_t.wait(1)
    hats.wait(1)
    stats_a.wait(1)
    weights = whole(wfirst_t)
    total = jnp.zeros((128, HALF), F32)
    cross = jnp.zeros((128, HALF), F32)
    for r in range(ROWS):
        value = fine_untap(mm(weights, stack_rows(g, r)))
        put(back_a, r, value.astype(BF16))
        hat = row(hats, r).astype(F32)
        e = value * silu_slope(hat)
        total = total + e
        cross = cross + e * hat
    put_stats(stats, total, cross)
    sums = to_row(jnp.sum(sums, axis=1, keepdims=True))
    give(line, jnp.broadcast_to(sums, (8, 128)))
    give(total_next, whole(stats_a))


def stage_last(
    members, members_all, scal, stats_a, stats_ea, hats, back_a, grad_fine, kept_in, early, middle, first,
    loss, loss_other, keep, send, loss_sum, gs, held, sems,
):
    grads = Source(held, [], 0)
    copies, start = [], 0
    for index, ref in enumerate((early, middle)):
        rows = pl.ds(start, ref.shape[1])
        copies.append(
            pltpu.make_async_copy(ref.spot, grads.spot.at[:, rows, :], sems.at[index])
        )
        copies[index].start()
        start += ref.shape[1]
    give(loss_sum, (loss.spot[0:1, 0:1] + loss_other.spot[0:1, 0:1]) * (1.0 / members_all))
    mean, inverse = norm_columns(stats_a, True, members)
    shift, slope = back_columns(stats_ea, True, members)
    for r in range(ROWS):
        hat = row(hats, r).astype(F32)
        u = row(back_a, r).astype(F32)
        value = row(grad_fine, r).astype(F32) + inverse * (
            u * silu_slope(hat) - shift - hat * slope
        )
        put(gs, r, value.astype(BF16))
    kept_in.wait(1)
    first.wait(1)
    parts = []
    for a in range(3):
        blocks = mm_nt(gs[...], kept_in.spot[:, a * HALF : (a + ROWS) * HALF])
        parts.append(
            jnp.concatenate(
                [blocks[:64, :96] + blocks[64:, 32:128], jnp.zeros((64, 32), F32)], axis=1
            )
        )
    size = first.shape[1]
    for f in range(grads.shape[0]):
        grads.spot[f, start : start + size, :] = first.spot[f]
    clear_rest(grads, put_grad(grads, start + size, parts))
    for copy in copies:
        copy.wait()
    half = keep.shape[1]
    odd = scal[8] > 0.5
    for f in range(keep.shape[0]):
        low, high = held[f, :half, :], held[f, half:, :]
        keep.spot[f] = jnp.where(odd, high, low)
        send.spot[f] = jnp.where(odd, low, high)


def join(scal, kept, got, out):
    give(out, (whole(kept).astype(F32) + whole(got).astype(F32)).astype(BF16))


def add_up(scal, got, out):
    total = got.spot[0].astype(F32)
    for index in range(1, got.shape[0]):
        total = total + got.spot[index].astype(F32)
    total = total.astype(BF16)
    for index in range(out.shape[0]):
        out.spot[index] = total


def unpack(starts, scal, mine, other, *refs):
    first, down, second, coarse, up, out, embed, inputs, flat = refs
    half = mine.shape[0]
    odd = scal[8] > 0.5
    flat[:half, :] = jnp.where(odd, whole(other), whole(mine)).astype(F32)
    flat[half:, :] = jnp.where(odd, whole(mine), whole(other)).astype(F32)

    def take(ref, start, out, size, ins, trim=False):
        for t in range(9):
            a, b = t // 3, t % 3
            if ins == 128:
                at, lanes = t, 0
            elif ins == 64:
                at, lanes = (a, b) if b < 2 else (3 + a // 2, a % 2)
            else:
                at, lanes = a, b
            value = ref[start + at * size : start + (at + 1) * size, :]
            if ins == 24:
                out.spot[t] = mm_nt(place(24, 128, 32 * lanes), value.astype(BF16))
                continue
            value = value[:, lanes * ins : (lanes + 1) * ins]
            if trim:
                value = value[:12]
                if out.shape[2] == 32:
                    value = jnp.where(scal[9] > 0.5, value[:, :32], value[:, 32:])
            out.spot[t] = value
        return start + (9 if ins == 128 else 5 if ins == 64 else 3) * size

    start = take(flat, 0, up, up.shape[1], 128)
    start = take(flat, start, coarse, coarse.shape[1], 128)
    take(flat, start, out, 16, 64, trim=True)
    start = take(flat, starts[0], down, down.shape[1], 64)
    take(flat, start, second, second.shape[1], 64)
    start = take(flat, starts[1], first, first.shape[1], 64)
    size = embed.shape[0]
    give(embed, flat[start : start + size, :64])
    take(flat, start + size, inputs, inputs.shape[2], 24)


class Field:
    def __init__(self, array, first):
        self.array, self.first = array, first


class Saved:
    def __init__(self, item, low=None, high=None, when=0):
        self.item, self.low, self.high, self.when = item, low, high, when


def shape(*dims, dtype=F32):
    return jax.ShapeDtypeStruct(dims, dtype)


def rows_of(first, number, dtype=F32):
    return Field(shape(number, 128, HALF, dtype=dtype), first)


def flat_rows(first, number, channels):
    return Field(shape(channels, number * HALF, dtype=BF16), first)


def opened(item):
    saved = item if isinstance(item, Saved) else None
    item = saved.item if saved else item
    if isinstance(item, Field):
        return saved, item.array, item.first
    return saved, item, 0


def position():
    me, bands = lax.axis_index("rows"), lax.axis_size("rows")
    return {
        6: jnp.where(me > 0, 1.0, 0.0),
        7: jnp.where(me < bands - 1, 1.0, 0.0),
        8: jnp.where(me % 2 == 1, 1.0, 0.0),
        9: jnp.where(lax.axis_index("fsdp") == 0, 1.0, 0.0),
    }


def run(name, kernel, outs, scal, *operands, scratch=()):
    vmem, hbm = pl.BlockSpec(memory_space=pltpu.VMEM), pl.BlockSpec(memory_space=pltpu.HBM)
    in_specs, arrays, plans, spots = [], [], [], []
    if scal is not None:
        in_specs, arrays = [pl.BlockSpec(memory_space=pltpu.SMEM)], [scal]
    for item in operands:
        saved, item, first = opened(item)
        if saved is None:
            in_specs.append(vmem)
            arrays.append(item)
            plans.append((first, None, None))
            continue
        part = None
        dims = item.shape
        if saved.low is not None:
            part = pl.ds(saved.low - first, saved.high - saved.low)
            dims = (saved.high - saved.low,) + dims[1:]
            first = saved.low
        in_specs.append(hbm)
        arrays.append(pltpu.with_memory_space_constraint(item, pltpu.HBM))
        if saved.when is None:
            plans.append((first, None, None))
            continue
        plans.append((first, (saved.when, part), len(spots)))
        spots.append(pltpu.VMEM(dims, item.dtype))
    ins = len(operands)
    out_specs, out_shapes = [], []
    for item in outs:
        saved, item, first = opened(item)
        if saved is None:
            out_specs.append(vmem)
            out_shapes.append(item)
            plans.append((first, None, None))
            continue
        out_specs.append(hbm)
        out_shapes.append(pltpu.HBM(item.shape, item.dtype))
        last = None
        if isinstance(saved.item, Field):
            count = item.shape[0] if len(item.shape) == 3 else item.shape[1] // HALF
            last = first + count - 1
        if saved.when is None:
            plans.append((first, None, None))
            continue
        plans.append((first, (last, None), len(spots)))
        spots.append(pltpu.VMEM(item.shape, item.dtype))

    def body(*refs):
        numbers = position()
        if scal is not None:
            numbers.update({index: refs[0][index] for index in range(6)})
            refs = refs[1:]
        given, refs = refs[: len(plans)], refs[len(plans) :]
        held, refs = refs[: len(spots)], refs[len(spots) :]
        sems, extra = refs[0], refs[1:]
        wrapped = []
        for index, (ref, (first, plan, place_at)) in enumerate(zip(given, plans)):
            copies = []
            if plan is not None:
                where = held[place_at]
                when, part = plan
                if index < ins:
                    source = ref if part is None else ref.at[part]
                    copies.append((when, pltpu.make_async_copy(source, where, sems.at[place_at])))
                else:
                    copies.append((when, pltpu.make_async_copy(where, ref, sems.at[place_at])))
                ref = where
            wrapped.append((Source if index < ins else Sink)(ref, copies, first))
        for item in wrapped[:ins]:
            item.wait(0)
        kernel(numbers, *wrapped, *extra)
        for item in wrapped[ins:]:
            item.finish()
        for item in wrapped[ins:]:
            for copy in item.started:
                copy.wait()

    made = pl.pallas_call(
        body,
        out_shape=tuple(out_shapes),
        in_specs=in_specs,
        out_specs=tuple(out_specs),
        scratch_shapes=spots
        + [pltpu.SemaphoreType.DMA((max(len(spots), 1),))]
        + [pltpu.VMEM(*item) if isinstance(item, tuple) else item for item in scratch],
        compiler_params=pltpu.CompilerParams(vmem_limit_bytes=LIMIT),
        name=name,
    )(*arrays)
    results = []
    for array, item in zip(made, outs):
        item = item.item if isinstance(item, Saved) else item
        results.append(Field(array, item.first) if isinstance(item, Field) else array)
    return results


def sum_parts(stats):
    return lax.all_to_all(stats, "rows", 0, 0)


def swap(value_a, value_b):
    count = lax.axis_size("rows")
    pairs = [(i, i ^ 1) for i in range(count)]
    across = []
    for i in range(1, count - 1, 2):
        across += [(i, i + 1), (i + 1, i)]
    return lax.ppermute(value_a, "rows", pairs), lax.ppermute(value_b, "rows", across)


def gather_packed(packed):
    if lax.axis_size("fsdp") == 2:
        return [packed, lax.ppermute(packed, "fsdp", [(0, 1), (1, 0)])]
    whole = lax.all_gather(packed, "fsdp").astype(F32)
    return [whole[i] for i in range(whole.shape[0])]


def group_shape(rows, count):
    return shape(count, -(-rows // 16) * 16, 128, dtype=BF16)


def per_device(
    residual_target,
    conditioning,
    noise_sample,
    noise_level,
    input_kernel,
    first_kernel,
    second_kernel,
    down_kernel,
    coarse_kernel,
    upward_kernel,
    output_kernel,
    embed_matrix,
):
    bands, count = lax.axis_size("rows"), lax.axis_size("fsdp")
    members = 2 * ROWS * 2 * HALF * bands
    members_c = 4 * CROWS * HALF * bands
    members_all = count * residual_target.size * bands
    sigma_level, skip_scale, out_scale, in_scale, weight = preconditions(noise_level[0])
    coef = 2.0 * weight * out_scale / members_all
    scal = jnp.stack([sigma_level, skip_scale, out_scale, in_scale, weight, coef])
    embedded = embedding(sigma_level, embed_matrix.shape[0] * count)
    target = residual_target.reshape(12 * ROWS, 512)
    condition = conditioning.reshape(12 * ROWS, 512)
    noise = noise_sample.reshape(12 * ROWS, 512)

    def widths_of(shards, rows):
        widths = tuple(
            (9 if item.ndim == 3 else 1, size, item.ndim == 3 and item.shape[1] == 24)
            for item, size in zip(shards, rows)
        )
        total = 0
        for item, (taps, size, swapped) in zip(shards, widths):
            paired = taps == 9 and item.shape[2] == 64
            total += (5 if paired else taps) * size
        return widths, total

    fine_o, coarse_o = input_kernel.shape[1], down_kernel.shape[1]
    inputs_t = jnp.swapaxes(input_kernel, 1, 2)
    shards = [inputs_t, first_kernel, embed_matrix]
    widths, packed_rows = widths_of(shards, [fine_o, fine_o, embed_matrix.shape[0]])
    far = shape(32, FAR * 512, dtype=BF16)
    early, own, edge_a, edge_b, figures = run(
        "enter",
        functools.partial(enter, widths),
        [
            shape(packed_rows, 128, dtype=BF16), shape(32, ROWS * 512, dtype=BF16), far, far,
            Saved(shape(8, 128)),
        ],
        scal,
        Saved(target, when=2),
        Saved(condition, when=2),
        Saved(noise, when=2),
        *[Saved(item, when=1) for item in shards],
        scratch=[
            ((packed_rows, 128), F32), ((4, 192, 128), F32), ((2, 16, FAR * 512), BF16)
        ],
    )
    got_a, got_b = swap(edge_a, edge_b)
    early = gather_packed(early)
    shards = [second_kernel, down_kernel, coarse_kernel, upward_kernel, output_kernel]
    widths, packed_rows = widths_of(shards, [fine_o, coarse_o, coarse_o, fine_o, 16])
    (rest,) = run(
        "pack_rest",
        functools.partial(pack, widths),
        [shape(packed_rows, 128, dtype=BF16)],
        None,
        *[Saved(item) for item in shards],
        own,
        scratch=[((packed_rows, 128), F32)],
    )
    vector = jnp.broadcast_to(embedded[None, :], (16, embedded.shape[0]))
    stat = shape(bands, 4, 128)
    total = Saved(shape(1, 4, 128))
    act_a, stats_a, kept_in, line_a, line_b = run(
        "stage_a",
        stage_a,
        [
            rows_of(-6, 20), stat, Saved(flat_rows(-1, 10, 128)),
            Saved(shape(16, 512)), Saved(shape(16, 512)),
        ],
        None,
        got_a, got_b, own, rest, *early,
        scratch=[((32, FAR * 512), BF16), ((32, FAR * 512), BF16)],
    )
    stats_a = sum_parts(stats_a)
    rest, stats_a = lax.optimization_barrier((rest, stats_a))
    (
        wsecond, wsecond_t, wdown, wdown_t, wcoarse, wcoarse_t, wup, wup_t, wout, wout_t
    ) = run(
        "prepare_rest",
        prepare_rest,
        [
            Saved(shape(384, 256, dtype=BF16)), Saved(shape(256, 384, dtype=BF16)),
            Saved(shape(384, 192, dtype=BF16)), Saved(shape(192, 384, dtype=BF16)),
            Saved(shape(384, 384, dtype=BF16)), Saved(shape(384, 384, dtype=BF16)),
            Saved(shape(384, 512, dtype=BF16)), Saved(shape(512, 384, dtype=BF16)),
            Saved(shape(96, 256, dtype=BF16)), Saved(shape(256, 96, dtype=BF16)),
        ],
        None,
        *gather_packed(rest),
    )

    act_b, stats_b, kept_a, hats_a, act_a, total_a, wfirst_t = run(
        "stage_b",
        functools.partial(stage_b, members, embedded.shape[0]),
        [
            rows_of(-5, 18), stat, Saved(flat_rows(0, 8, 256), when=None),
            Saved(rows_of(0, 8, BF16)),
            Saved(rows_of(-4, 16), when=None), total, Saved(shape(256, 384, dtype=BF16)),
        ],
        None,
        stats_a, act_a, vector, *early,
        scratch=[((384, 256), BF16), ((256, 20 * HALF), BF16), pltpu.SemaphoreType.DMA((2,))],
    )
    stats_b = sum_parts(stats_b)
    fine, act_c, edge, stats_c, kept_b, kept_pool, hats_b, total_b = run(
        "stage_c",
        functools.partial(stage_c, members),
        [
            rows_of(-3, 14), rows_of(-1, 6), Field(shape(128, 2 * HALF), 1), stat,
            Saved(flat_rows(0, 8, 256), when=None), Saved(flat_rows(0, 4, 192)),
            Saved(rows_of(-1, 10, BF16)), total,
        ],
        None,
        stats_b, Saved(wsecond, when=1), act_b, Saved(act_a, when=1), Saved(wdown, when=1),
        scratch=[
            ((256, 18 * HALF), BF16), ((16, 128, HALF), F32), pltpu.SemaphoreType.DMA((1,)),
        ],
    )
    got_a, got_b = swap(edge.array, edge.array)
    stats_c = sum_parts(stats_c)
    merged, hats_c, stats_d, kept_c, kept_up, total_c = run(
        "stage_d",
        functools.partial(stage_d, members_c),
        [
            rows_of(-3, 14), Saved(rows_of(-2, 8, BF16)), stat,
            Saved(flat_rows(0, 4, 384), when=None), Saved(flat_rows(0, 4, 384)), total,
        ],
        None,
        stats_c, Saved(wcoarse, when=1), got_a, got_b, act_c, Saved(wup, when=1), fine,
        scratch=[((384, 10 * HALF), BF16), pltpu.SemaphoreType.DMA((1,))],
    )
    stats_d = sum_parts(stats_d)
    edge = Field(shape(128, 3 * HALF, dtype=BF16), 0)
    denoised, back_d, edge_a, edge_b, stats_ed, hats_d, cotangents, kept_d, total_d = run(
        "stage_out",
        functools.partial(stage_out, members),
        [
            Saved(shape(96, 512)), rows_of(0, 8, BF16), edge, edge, stat,
            Saved(rows_of(-3, 14, BF16)),
            Field(shape(10, 32, HALF, dtype=BF16), -1),
            Saved(flat_rows(0, 8, 256), when=None), shape(1, 4, 128),
        ],
        None,
        stats_d, Saved(wout, when=1), merged, Saved(line_a, when=1), Saved(line_b, when=1),
        Saved(target, when=1), Saved(noise, when=1), Saved(wout_t, when=1),
        Saved(figures, when=1),
        scratch=[
            ((160, 512), F32), ((160, 512), F32),
            ((4, 96, 128), F32), ((4, 96, 128), F32), ((4, 96, 128), F32),
            ((256, 12 * HALF), BF16), pltpu.SemaphoreType.DMA((1,)),
        ],
    )
    got_a, got_b = swap(edge_a.array, edge_b.array)
    (grad_out,) = run(
        "grads_out",
        grads_out,
        [Saved(shape(count, 80, 128, dtype=BF16))],
        None,
        cotangents, Saved(kept_d),
        scratch=[((96, 8 * HALF), BF16)],
    )
    stats_ed = sum_parts(stats_ed)
    grad_merged, back_c, grad_coarse, edge_a, edge_b, stats_ec, loss, total_c = run(
        "stage_up",
        functools.partial(stage_up, members, members_c),
        [
            rows_of(-2, 12, BF16), rows_of(0, 4, BF16), rows_of(-1, 6, BF16), edge, edge, stat,
            shape(8, 128), shape(1, 4, 128),
        ],
        None,
        total_d, stats_ed, got_a, got_b, Saved(hats_d, when=1), back_d, Saved(wup_t, when=1),
        Saved(total_c, when=1),
        Saved(hats_c, when=1), Saved(wcoarse_t, when=1), Saved(grad_out, when=None),
    )
    got_a, got_b = swap(edge_a.array, edge_b.array)
    (early,) = run(
        "grads_up",
        grads_up,
        [Saved(group_shape(9 * (fine_o + coarse_o) + 80, count))],
        None,
        grad_merged, grad_coarse, Saved(kept_up), Saved(kept_c), Saved(grad_out),
        scratch=[
            ((384, 8 * HALF), BF16), ((384, 8 * HALF), BF16), ((384, 4 * HALF), BF16)
        ],
    )
    stats_ec = sum_parts(stats_ec)
    if count == 2:
        loss_other = lax.ppermute(loss, "fsdp", [(0, 1), (1, 0)])
    else:
        loss_other = lax.psum(loss, "fsdp") - loss
    grad_fine, back_b, stats_eb, grad_c, total_b = run(
        "stage_down",
        functools.partial(stage_down, members, members_c),
        [
            rows_of(-1, 10, BF16), rows_of(-1, 10, BF16), stat, Saved(rows_of(-1, 6, BF16)),
            shape(1, 4, 128),
        ],
        None,
        total_c, stats_ec, got_a, got_b, Saved(hats_c, when=1), back_c, grad_coarse,
        Saved(wdown_t, when=1), grad_merged, Saved(total_b, when=1), Saved(wsecond_t, when=1),
        Saved(hats_b, 0, 8, when=1), Saved(early, when=None),
    )
    (middle,) = run(
        "grads_down",
        grads_down,
        [Saved(group_shape(5 * (fine_o + coarse_o), count))],
        None,
        grad_fine, Saved(grad_c), Saved(kept_pool), Saved(kept_b),
        scratch=[((384, 8 * HALF), BF16), ((384, 4 * HALF), BF16)],
    )
    stats_eb = sum_parts(stats_eb)
    back_a, stats_ea, grad_b, line, total_a = run(
        "stage_first",
        functools.partial(stage_first, members),
        [
            rows_of(0, 8, BF16), stat, rows_of(-1, 10, BF16), shape(8, 128),
            shape(1, 4, 128),
        ],
        None,
        total_b, stats_eb, Saved(hats_b, when=1), back_b, Saved(wfirst_t, when=1), Saved(total_a, when=1),
        Saved(hats_a, when=1), Saved(middle, when=None),
    )
    (grad_first,) = run(
        "grads_first",
        grads_first,
        [Saved(shape(count, 5 * fine_o + embed_matrix.shape[0], 128, dtype=BF16))],
        None,
        grad_b, line, vector, Saved(kept_a),
        scratch=[((384, 8 * HALF), BF16)],
    )
    stats_ea = sum_parts(stats_ea)
    late = group_shape(8 * fine_o + embed_matrix.shape[0], count)
    starts = [early.shape[1], early.shape[1] + middle.shape[1]]
    total = starts[1] + late.shape[1]
    chunk = -(-total // (16 * bands)) * 16
    chips = bands // 2
    half = shape(count, chunk * chips, 128, dtype=BF16)
    keep, send, loss = run(
        "stage_last",
        functools.partial(stage_last, members, members_all),
        [half, half, shape(1, 1)],
        None,
        total_a, stats_ea, Saved(hats_a), back_a, grad_fine, Saved(kept_in, when=1),
        Saved(early, when=None), Saved(middle, when=None), Saved(grad_first, when=1), loss, loss_other,
        scratch=[
            ((128, 8 * HALF), BF16), ((count, chunk * bands, 128), BF16),
            pltpu.SemaphoreType.DMA((2,)),
        ],
    )
    loss_value = loss.reshape(())
    pairs = [(i, i ^ 1) for i in range(bands)]
    got = lax.ppermute(send, "rows", pairs)
    (both,) = run("join", join, [half], None, keep, got)
    both = both.reshape(count * chips, chunk, 128)
    cores = [[f * bands + r for f in range(count) for r in range(c, bands, 2)] for c in range(2)]
    got = lax.all_to_all(both, ("fsdp", "rows"), 0, 0, axis_index_groups=cores)
    (mine,) = run("add_up", add_up, [shape(chips, chunk, 128, dtype=BF16)], None, got)
    cores = [[r for r in range(c, bands, 2)] for c in range(2)]
    mine = lax.all_to_all(mine, "rows", 0, 0, axis_index_groups=cores)
    mine = mine.reshape(chips * chunk, 128)
    other = lax.ppermute(mine, "rows", pairs)
    first_g, down_g, second_g, coarse_g, up_g, out_g, embed_g, in_g = run(
        "unpack",
        functools.partial(unpack, starts),
        [
            shape(*first_kernel.shape),
            shape(*down_kernel.shape),
            shape(*second_kernel.shape),
            shape(*coarse_kernel.shape),
            shape(*upward_kernel.shape),
            shape(9, 12, output_kernel.shape[2] if count == 2 else 64),
            shape(*embed_matrix.shape),
            shape(*inputs_t.shape),
        ],
        None,
        mine, other,
        scratch=[((chunk * bands, 128), F32)],
    )
    width = output_kernel.shape[2]
    if count != 2:
        out_g = lax.dynamic_slice_in_dim(out_g, lax.axis_index("fsdp") * width, width, axis=2)
    return (
        denoised.reshape(residual_target.shape),
        loss_value,
        jnp.swapaxes(in_g, 1, 2),
        first_g,
        second_g,
        down_g,
        coarse_g,
        up_g,
        out_g,
        embed_g,
    )


def solution(mesh):
    in_specs = (
        P("fsdp", None, "rows", None),
        P("fsdp", None, "rows", None),
        P("fsdp", None, "rows", None),
        P("fsdp"),
        P(None, "fsdp", None),
        P(None, "fsdp", None),
        P(None, "fsdp", None),
        P(None, "fsdp", None),
        P(None, "fsdp", None),
        P(None, "fsdp", None),
        P(None, None, "fsdp"),
        P("fsdp", None),
    )
    out_specs = (
        P("fsdp", None, "rows", None),
        P(),
        P(None, "fsdp", None),
        P(None, "fsdp", None),
        P(None, "fsdp", None),
        P(None, "fsdp", None),
        P(None, "fsdp", None),
        P(None, "fsdp", None),
        P(None, None, "fsdp"),
        P("fsdp", None),
    )
    return jax.shard_map(
        per_device, mesh=mesh, in_specs=in_specs, out_specs=out_specs, check_vma=False
    )
```

```python
import functools

import jax
import jax.numpy as jnp
from jax import lax
from jax.experimental import pallas as pl
from jax.experimental.pallas import tpu as pltpu
from jax.sharding import PartitionSpec as P

GROUPS = 32
STEPS = 64

sigma_low = 0.002
sigma_high = 80.0
sigma_data = 0.5
rho_power = 7.0
eps_norm = 1e-05

F32 = jnp.float32
BF16 = jnp.bfloat16

HALF = 256
ROWS = 8
CROWS = 4
FAR = 7
LIMIT = 24 * 1024 * 1024


def preconditions(level_index):
    ramp_value = level_index.astype(jnp.float32) / (STEPS - 1)
    top_root = sigma_high ** (1.0 / rho_power)
    bottom = sigma_low ** (1.0 / rho_power)
    sigma_level = (top_root + ramp_value * (bottom - top_root)) ** rho_power
    sigma_total = sigma_level * sigma_level + sigma_data * sigma_data
    skip_scale = sigma_data * sigma_data / sigma_total
    out_scale = sigma_level * sigma_data * lax.rsqrt(sigma_total)
    in_scale = lax.rsqrt(sigma_total)
    weight = sigma_total / (sigma_level * sigma_data) ** 2
    return (sigma_level, skip_scale, out_scale, in_scale, weight)


def embedding(sigma_level, features):
    half_count = features // 2
    ramp_steps = jnp.arange(half_count, dtype=jnp.float32) / half_count
    frequency = 64.0 * 0.01**ramp_steps
    phase_angle = 0.25 * jnp.log(sigma_level) * frequency
    return jnp.concatenate([jnp.cos(phase_angle), jnp.sin(phase_angle)]).astype(jnp.bfloat16)


class Source:
    def __init__(self, spot, copies, first):
        self.spot, self.copies, self.first = spot, copies, first
        self.shape = spot.shape
        for _, copy in copies:
            copy.start()

    def wait(self, stage):
        for when, copy in self.copies:
            if when == stage:
                copy.wait()


class Sink:
    def __init__(self, spot, copies, first):
        self.spot, self.copies, self.first = spot, copies, first
        self.shape = spot.shape
        self.started = []

    def done(self, index):
        for last, copy in self.copies:
            if last == index:
                copy.start()
                self.started.append(copy)

    def send(self, source, sem):
        copy = pltpu.make_async_copy(source, self.spot, sem)
        copy.start()
        self.started.append(copy)

    def finish(self):
        for _, copy in self.copies:
            if not any(copy is other for other in self.started):
                copy.start()
                self.started.append(copy)


def spot(ref, index):
    if len(ref.shape) == 3:
        return (index - getattr(ref, "first", 0),)
    start = index - getattr(ref, "first", 0)
    return (slice(None), slice(start * HALF, (start + 1) * HALF))


def row(ref, index):
    return getattr(ref, "spot", ref)[spot(ref, index)]


def put(ref, index, value):
    getattr(ref, "spot", ref)[spot(ref, index)] = value
    if isinstance(ref, Sink):
        ref.done(index)


def whole(ref):
    return ref.spot[...]


def give(ref, value):
    ref.spot[...] = value
    ref.finish()


def lane(shape):
    return lax.broadcasted_iota(jnp.int32, shape, 1)


def from_left(value):
    moved = pltpu.roll(value, 1, 1)
    return jnp.where(lane(value.shape) == 0, 0.0, moved)


def from_right(value):
    moved = pltpu.roll(value, value.shape[1] - 1, 1)
    return jnp.where(lane(value.shape) == value.shape[1] - 1, 0.0, moved)


def mm(left, right):
    return jnp.dot(left, right, preferred_element_type=F32)


def mm_nt(left, right):
    return lax.dot_general(left, right, (((1,), (1,)), ((), ())), preferred_element_type=F32)


def fine_taps(value):
    half = value.shape[0] // 2
    even, odd = value[:half], value[half:]
    return jnp.concatenate([from_left(odd), value, from_right(even)], axis=0).astype(BF16)


def coarse_taps(value):
    return jnp.concatenate([from_left(value), value, from_right(value)], axis=0).astype(BF16)


def fine_untap(taps):
    size = taps.shape[0] // 4
    even = taps[size : 2 * size] + from_left(taps[3 * size :])
    odd = taps[2 * size : 3 * size] + from_right(taps[:size])
    return jnp.concatenate([even, odd], axis=0)


def coarse_untap(taps):
    size = taps.shape[0] // 3
    return taps[size : 2 * size] + from_right(taps[:size]) + from_left(taps[2 * size :])


def spread(parts, first, last):
    out = {}
    for i in range(first, last + 1):
        size = parts[i - 1].shape[0] // 3
        out[i] = parts[i - 1][:size] + parts[i][size : 2 * size] + parts[i + 1][2 * size :]
    return out


def stack_rows(g, r):
    return jnp.concatenate([g[r + 1], g[r], g[r - 1]], axis=0)


def same_group(size, fine):
    left = lax.broadcasted_iota(jnp.int32, (size, size), 0)
    right = lax.broadcasted_iota(jnp.int32, (size, size), 1)
    if fine:
        half = size // 2
        left, right = left % half, right % half
        per = half // GROUPS
    else:
        per = size // GROUPS
    return left // per == right // per


def total_stats(stats):
    total = stats.spot[0]
    for index in range(1, stats.shape[0]):
        total = total + stats.spot[index]
    return total


def group_sums(stats, fine):
    total = total_stats(stats)
    member = same_group(128, fine)
    first = jnp.sum(jnp.where(member, total[0:1, :], 0.0), axis=1, keepdims=True)
    second = jnp.sum(jnp.where(member, total[1:2, :], 0.0), axis=1, keepdims=True)
    return first, second


def norm_columns(stats_ref, fine, members):
    first, second = group_sums(stats_ref, fine)
    mean = first / members
    inverse = lax.rsqrt(second / members - mean * mean + eps_norm)
    return mean, inverse


def back_columns(stats_ref, fine, members):
    first, second = group_sums(stats_ref, fine)
    return first / members, second / members


def to_row(column):
    size = column.shape[0]
    diagonal = lax.broadcasted_iota(jnp.int32, (size, size), 0) == lax.broadcasted_iota(
        jnp.int32, (size, size), 1
    )
    return jnp.sum(jnp.where(diagonal, column, 0.0), axis=0, keepdims=True)


def put_stats(ref, first, second, third=None):
    first = to_row(jnp.sum(first, axis=1, keepdims=True))
    second = to_row(jnp.sum(second, axis=1, keepdims=True))
    if third is None:
        third = jnp.zeros((1, 128), F32)
    block = jnp.concatenate([first, second, third, jnp.zeros((1, 128), F32)], axis=0)
    for index in range(ref.shape[0]):
        ref.spot[index] = block
    ref.finish()


def silu(h):
    t = 0.5 * h
    return t + t * jnp.tanh(t)


def silu_slope(h):
    s = 0.5 + 0.5 * jnp.tanh(0.5 * h)
    return s * (1.0 + h * (1.0 - s))


def masked(value, index, rows, scal):
    if index < 0:
        return value * scal[6]
    if index >= rows:
        return value * scal[7]
    return value


def pick(scal, when_odd, when_even):
    return jnp.where(scal[8] > 0.5, when_odd, when_even)


def spill(ref, value):
    for t in range(4):
        ref[t, : value.shape[0], :] = value[:, 128 * t : 128 * (t + 1)]


def strided(ref, index, size):
    return jnp.concatenate(
        [ref[t, pl.ds(index, size, stride=ROWS), :] for t in range(4)], axis=1
    )


def interleave(transposed):
    left = lax.broadcasted_iota(jnp.int32, (512, 512), 0)
    right = lax.broadcasted_iota(jnp.int32, (512, 512), 1)
    if transposed:
        left, right = right, left
    place = (left & 1) * HALF + (left >> 1)
    return jnp.where(place == right, 1.0, 0.0).astype(BF16)


def fine_grad(blocks, outs, ins):
    parts = []
    for a in range(3):
        even = blocks[(2 * a) * outs : (2 * a + 1) * outs]
        odd = blocks[(2 * a + 1) * outs : (2 * a + 2) * outs]
        parts.append(even[:, : 3 * ins] + odd[:, ins : 4 * ins])
    return parts


def grad_blocks(parts, ins):
    if ins == 128:
        return [part[:, 128 * b : 128 * (b + 1)] for part in parts for b in range(3)]
    if ins == 64:
        blank = jnp.zeros(parts[0][:, :64].shape, F32)
        blocks = [part[:, :128] for part in parts]
        blocks.append(jnp.concatenate([parts[0][:, 128:192], parts[1][:, 128:192]], axis=1))
        blocks.append(jnp.concatenate([parts[2][:, 128:192], blank], axis=1))
        return blocks
    return parts


def put_grad(ref, start, blocks, split=True):
    count = ref.shape[0]
    size = blocks[0].shape[0] // count if split else blocks[0].shape[0]
    for block in blocks:
        for f in range(count):
            piece = block[f * size : (f + 1) * size] if split else block
            ref.spot[f, start : start + size, :] = piece.astype(BF16)
        start += size
    return start


def clear_rest(ref, start):
    count, size, _ = ref.shape
    if start < size:
        for f in range(count):
            ref.spot[f, start:, :] = jnp.zeros((size - start, 128), BF16)


def place(width, target, offset):
    left = lax.broadcasted_iota(jnp.int32, (width, target), 0)
    right = lax.broadcasted_iota(jnp.int32, (width, target), 1)
    return jnp.where(left + offset == right, 1.0, 0.0).astype(BF16)


def flipped(value):
    size = value.shape[1]
    return mm_nt(place(size, size, 0), value).astype(BF16)


def tap_of(pieces, offset, index, size, side=1):
    each = size // len(pieces)
    start = offset + index // side * each
    tap = jnp.concatenate([piece[start : start + each, :] for piece in pieces], axis=0)
    width = 128 // side
    return tap[:, width * (index % side) : width * (index % side + 1)].astype(BF16)


def in_order(scal, pieces):
    if len(pieces) == 2:
        mine, other = whole(pieces[0]), whole(pieces[1])
        low = scal[9] > 0.5
        return [jnp.where(low, mine, other), jnp.where(low, other, mine)]
    return [whole(piece) for piece in pieces]


def fine_matrix(taps, slot):
    rows = []
    for a in range(3):
        total = None
        for b in range(3):
            spread_out = jnp.concatenate(
                [place(slot, 4 * slot, b * slot), place(slot, 4 * slot, (b + 1) * slot)], axis=1
            )
            term = mm(taps[3 * a + b][:, :slot], spread_out)
            total = term if total is None else total + term
        rows += [total[:, : 4 * slot], total[:, 4 * slot :]]
    return jnp.concatenate(rows, axis=0).astype(BF16)


def pack(widths, scal, *refs):
    shards, (out, scratch) = refs[: len(widths)], refs[-2:]
    scratch[...] = jnp.zeros(scratch.shape, F32)
    start = 0
    for shard, (taps, rows, swapped) in zip(shards, widths):
        if taps == 1:
            scratch[start : start + rows, : shard.shape[1]] = whole(shard)
            start += rows
        else:
            for t in range(taps):
                value = shard.spot[t]
                if swapped:
                    value = mm_nt(place(value.shape[1], value.shape[1], 0), value.astype(BF16))
                if value.shape[1] in (24, 64):
                    side = 4 if value.shape[1] == 24 else 2
                    low = t % side * (128 // side)
                    scratch[start : start + value.shape[0], low : low + value.shape[1]] = value
                    start += rows if t % side == side - 1 or t == taps - 1 else 0
                else:
                    scratch[start : start + value.shape[0], : value.shape[1]] = value
                    start += rows
    give(out, scratch[...].astype(BF16))


def prepare_rest(scal, *refs):
    pieces = refs[:-10]
    wsecond, wsecond_t, wdown, wdown_t, wcoarse, wcoarse_t, wup, wup_t, wout, wout_t = refs[-10:]
    count = len(pieces)
    pieces = in_order(scal, pieces)
    start = 0

    def taps_of(size, paired=False):
        nonlocal start
        taps = [tap_of(pieces, start, t, size, 2 if paired else 1) for t in range(9)]
        start += (5 if paired else 9) * (size // count)
        return taps

    def both(value, forward, backward):
        give(forward, value)
        give(backward, flipped(value))

    both(fine_matrix(taps_of(64, True), 64), wsecond, wsecond_t)
    taps = taps_of(128, True)
    rows = []
    for a in range(3):
        total = None
        for b in range(3):
            term = mm(taps[3 * a + b][:, :64], place(64, 256, 64 * b))
            total = term if total is None else total + term
        rows.append(total)
    both(jnp.concatenate(rows, axis=0)[:, :192].astype(BF16), wdown, wdown_t)
    taps = taps_of(128)
    rows = [jnp.concatenate(taps[3 * a : 3 * a + 3], axis=1) for a in range(3)]
    both(jnp.concatenate(rows, axis=0), wcoarse, wcoarse_t)
    taps = taps_of(64)
    rows = []
    blank = jnp.zeros((64, 128), BF16)
    for a in range(3):
        rows.append(jnp.concatenate(taps[3 * a : 3 * a + 3] + [blank], axis=1))
        rows.append(jnp.concatenate([blank] + taps[3 * a : 3 * a + 3], axis=1))
    up = jnp.concatenate(rows, axis=0)
    give(wup, up)
    turned = flipped(up).astype(F32)
    turned = jnp.concatenate([turned[:128], turned[128:256] + turned[256:384], turned[384:]], axis=0)
    a0, a1, a2 = turned[:, :128], turned[:, 128:256], turned[:, 256:]
    give(wup_t, jnp.concatenate([a0, a0 + a1, a1 + a2, a2], axis=1).astype(BF16))
    taps = []
    width = 64 // count
    for t in range(9):
        total = None
        for s in range(count):
            tap = pieces[s][start + 16 * t : start + 16 * (t + 1), :].astype(BF16)
            term = mm(tap[:, :width], place(width, 128, s * width))
            total = term if total is None else total + term
        taps.append(total.astype(BF16))
    both(fine_matrix(taps, 64), wout, wout_t)


def enter(
    widths, scal, target, condition, noise, *refs
):
    *shards, packed, own, edge_a, edge_b, figures, taps, scratch, marks = refs
    for item in shards:
        item.wait(1)
    pack(widths, scal, *shards, packed, taps)
    for item in (target, condition, noise):
        item.wait(2)
    values = [jnp.full((1, 128), scal[k], F32) for k in range(6)]
    give(figures, jnp.concatenate(values + [jnp.zeros((2, 128), F32)], axis=0))
    sigma, skip, in_scale = scal[0], scal[1], scal[3]
    goal = whole(target)
    noisy = goal + sigma * whole(noise)
    q = skip * noisy - goal
    natural = jnp.concatenate([in_scale * noisy, whole(condition)], axis=0).astype(BF16)
    spill(scratch, mm(natural, interleave(False)))
    blank = jnp.zeros((8, 512), F32)
    for i in range(ROWS):
        value = strided(scratch, i, 24)
        own.spot[:, i * 512 : (i + 1) * 512] = jnp.concatenate([value, blank], axis=0).astype(BF16)
    spill(scratch, q)
    blank = jnp.zeros((4, 512), F32)
    for j, i in enumerate((0, ROWS - 1)):
        rest = jnp.concatenate([strided(scratch, i, 12), blank], axis=0)
        marks[j] = jnp.zeros(marks.shape[1:], BF16)
        for part in range(3):
            piece = rest.astype(BF16)
            rest = rest - piece.astype(F32)
            for k in range(2):
                lanes = slice((2 * part + k) * 512, (2 * part + k + 1) * 512)
                marks[j, 8:, lanes] = piece[8 * k : 8 * k + 8]
    for j, edge in enumerate((edge_a, edge_b)):
        odd = scal[8] > 0.5 if j == 0 else scal[8] < 0.5
        low = (ROWS - FAR) * 512
        edge.spot[:16, :] = jnp.where(odd, own.spot[:16, : FAR * 512], own.spot[:16, low:])
        edge.spot[16:, :] = jnp.where(odd, own.spot[16:, : FAR * 512], own.spot[16:, low:]) + (
            jnp.where(odd, marks[0], marks[1])
        )


def marked(scal, got):
    halves = []
    for k in range(2):
        total = None
        for part in range(3):
            lanes = slice((2 * part + k) * 512, (2 * part + k + 1) * 512)
            piece = got.spot[16:32, lanes].astype(F32)[8:]
            total = piece if total is None else total + piece
        halves.append(total)
    return jnp.concatenate(halves, axis=0)


def stage_a(scal, got_a, got_b, own, done, *refs):
    *pieces, act, stats, kept, line_a, line_b, above, below = refs
    pieces = in_order(scal, pieces)
    weights = fine_matrix([tap_of(pieces, 0, t, 64, 4) for t in range(9)], 32)
    give(line_a, marked(scal, got_a))
    give(line_b, marked(scal, got_b))
    above[...] = pick(scal, whole(got_a), whole(got_b))
    below[...] = pick(scal, whole(got_b), whole(got_a))
    clear = jnp.zeros((16, FAR * 512), BF16)
    keep = lax.broadcasted_iota(jnp.int32, (16, FAR * 512), 0) < 8
    for ref in (above, below):
        ref[16:, :] = jnp.where(keep, ref[16:, :], clear)
    parts = {}
    total = jnp.zeros((128, HALF), F32)
    square = jnp.zeros((128, HALF), F32)
    for r in range(-FAR, ROWS + FAR):
        if r < 0:
            value = above[:, (r + FAR) * 512 : (r + FAR + 1) * 512]
        elif r < ROWS:
            value = own.spot[:, r * 512 : (r + 1) * 512]
        else:
            value = below[:, (r - ROWS) * 512 : (r - ROWS + 1) * 512]
        value = value.astype(F32)
        z = fine_taps(jnp.concatenate([value[:, :HALF], value[:, HALF:]], axis=0))
        if -1 <= r <= ROWS:
            put(kept, r, z)
        parts[r] = mm(weights, z)
        i = r - 1
        if i > -FAR:
            value = spread(parts, i, i)[i]
            put(act, i, value)
            del parts[i - 1]
            if 0 <= i < ROWS:
                total = total + value
                square = square + value * value
    put_stats(stats, total, square)


def slot(ref, index):
    return ref[:, index * HALF : (index + 1) * HALF]


def fill(ref, index, value):
    ref[:, index * HALF : (index + 1) * HALF] = value


def stage_b(members, embed_size, scal, stats_a, act_a, vec, *refs):
    *pieces, act_b, stats, kept, hats, passed, totals, wfirst_t, wfirst, zs, sems = refs
    passed.send(act_a.spot.at[pl.ds(2, 16)], sems.at[0])
    give(totals, total_stats(stats_a)[None])
    count = len(pieces)
    pieces = in_order(scal, pieces)
    start = 3 * (64 // count)
    first = fine_matrix([tap_of(pieces, start, t, 64, 2) for t in range(9)], 64)
    start += 5 * (64 // count)
    wfirst[...] = first
    give(wfirst_t, flipped(first))
    line = mm(whole(vec), tap_of(pieces, start, 0, embed_size))[0:1, :64]
    both = jnp.concatenate([line, line], axis=1)
    lift = jnp.sum(place(128, 128, 0).astype(F32) * both, axis=1, keepdims=True)
    mean, inverse = norm_columns(stats_a, True, members)
    for r in range(-6, ROWS + 6):
        hat = (row(act_a, r) - mean) * inverse
        fill(zs, r + 6, fine_taps(masked(silu(hat), r, ROWS, scal)))
        if 0 <= r < ROWS:
            hats.spot[r] = hat.astype(BF16)
    hats.finish()
    kept.send(zs.at[:, pl.ds(6 * HALF, 8 * HALF)], sems.at[1])
    parts = {}
    total = jnp.zeros((128, HALF), F32)
    square = jnp.zeros((128, HALF), F32)
    for r in range(-6, ROWS + 6):
        parts[r] = mm(wfirst[...], slot(zs, r + 6))
        i = r - 1
        if i > -6:
            value = spread(parts, i, i)[i] + lift
            put(act_b, i, value)
            del parts[i - 1]
            if 0 <= i < ROWS:
                total = total + value
                square = square + value * value
    put_stats(stats, total, square)


def stage_c(
    members, scal, stats_b, wsecond, act_b, act_a, wdown,
    fine, act_c, edge, stats, kept, kept_pool, hats, totals, zs, convolved, sems,
):
    give(totals, total_stats(stats_b)[None])
    mean, inverse = norm_columns(stats_b, True, members)
    for r in range(-5, ROWS + 5):
        hat = (row(act_b, r) - mean) * inverse
        fill(zs, r + 5, fine_taps(masked(silu(hat), r, ROWS, scal)))
        if -1 <= r <= ROWS:
            hats.spot[r + 1] = hat.astype(BF16)
    hats.finish()
    kept.send(zs.at[:, pl.ds(5 * HALF, 8 * HALF)], sems.at[0])
    wsecond.wait(1)
    parts = {}
    for r in range(-5, ROWS + 5):
        parts[r] = mm(whole(wsecond), slot(zs, r + 5))
        i = r - 1
        if i > -5:
            convolved[i + 4] = spread(parts, i, i)[i]
            del parts[i - 1]
    act_a.wait(1)
    wdown.wait(1)
    pooled = {}
    half = {}
    for i in range(-4, ROWS + 4):
        value = convolved[i + 4] + row(act_a, i)
        if -3 <= i < ROWS + 3:
            put(fine, i, value)
        half[i] = value[:64] + value[64:]
        if i % 2:
            value = 0.25 * (half.pop(i - 1) + half.pop(i))
            value = masked(value, i // 2, CROWS, scal)
            pooled[i // 2] = value.astype(BF16).astype(F32)
    weights = whole(wdown)
    parts = {}
    total = jnp.zeros((128, HALF), F32)
    square = jnp.zeros((128, HALF), F32)
    for r in range(-2, CROWS + 2):
        z = coarse_taps(pooled[r])
        if 0 <= r < CROWS:
            put(kept_pool, r, z)
        parts[r] = mm(weights, z)
        i = r - 1
        if i > -2:
            value = spread(parts, i, i)[i]
            put(act_c, i, value)
            del parts[i - 1]
            if 0 <= i < CROWS:
                total = total + value
                square = square + value * value
            if i in (1, 2):
                put(edge, i, value)
    put_stats(stats, total, square)


def stage_d(
    members, scal, stats_c, wcoarse, got_a, got_b, act_c, wup, fine,
    merged, hats, stats, kept_c, kept_up, totals, zs, sems,
):
    give(totals, total_stats(stats_c)[None])
    mean, inverse = norm_columns(stats_c, False, members)
    ring = {}
    for j in range(2):
        ring[j - 3] = pick(scal, row(got_a, j), row(got_b, j))
        ring[CROWS + 1 + j] = pick(scal, row(got_b, j), row(got_a, j))
    for j in range(-1, CROWS + 1):
        ring[j] = row(act_c, j)
    for r in range(-3, CROWS + 3):
        hat = (ring[r] - mean) * inverse
        fill(zs, r + 3, coarse_taps(masked(silu(hat), r, CROWS, scal)))
        if -2 <= r < CROWS + 2:
            hats.spot[r + 2] = hat.astype(BF16)
    hats.finish()
    kept_c.send(zs.at[:, pl.ds(3 * HALF, 4 * HALF)], sems.at[0])
    wcoarse.wait(1)
    wup.wait(1)
    parts = {}
    lifted = {}
    for r in range(-3, CROWS + 3):
        parts[r] = mm(whole(wcoarse), slot(zs, r + 3))
        i = r - 1
        if i > -3:
            value = spread(parts, i, i)[i] + ring[i]
            del parts[i - 1]
            lifted[i] = masked(value, i, CROWS, scal).astype(BF16).astype(F32)
    weights = whole(wup)
    parts = {}
    total = jnp.zeros((128, HALF), F32)
    square = jnp.zeros((128, HALF), F32)
    for r in range(-2, CROWS + 2):
        z = coarse_taps(lifted[r])
        if 0 <= r < CROWS:
            put(kept_up, r, z)
        four = jnp.concatenate([z[:128], z[128:256], z[128:256], z[256:]], axis=0)
        parts[2 * r] = parts[2 * r + 1] = mm(weights, four)
        for i in (2 * r - 1, 2 * r):
            if i >= -3:
                value = spread(parts, i, i)[i] + row(fine, i)
                put(merged, i, value)
                parts.pop(i - 1)
                if 0 <= i < ROWS:
                    total = total + value
                    square = square + value * value
    put_stats(stats, total, square)


def stage_out(
    members, scal, stats_d, wout, merged, line_a, line_b, target, noise, wout_t, figures,
    denoised, back, edge_a, edge_b, stats, hats, cotangents, kept, totals, pairs, cells,
    goals, noisies, found, zs, sems,
):
    give(totals, total_stats(stats_d)[None])
    mean, inverse = norm_columns(stats_d, True, members)
    for r in range(-3, ROWS + 3):
        hat = (row(merged, r) - mean) * inverse
        hats.spot[r + 3] = hat.astype(BF16)
        if -3 < r < ROWS + 2:
            fill(zs, r + 2, fine_taps(masked(silu(hat), r, ROWS, scal)))
    hats.finish()
    kept.send(zs.at[:, pl.ds(2 * HALF, 8 * HALF)], sems.at[0])
    for item in (wout, line_a, line_b, target, noise, wout_t, figures):
        item.wait(1)
    parts = {}
    for r in range(-2, ROWS + 2):
        parts[r] = mm(whole(wout), slot(zs, r + 2))
        i = r - 1
        if i > -2:
            value = spread(parts, i, i)[i]
            del parts[i - 1]
            pairs[16 * (i + 1) : 16 * (i + 2), :] = jnp.concatenate(
                [value[:16], value[16:]], axis=1
            )
    value = pairs[...]
    high = value.astype(BF16)
    low = (value - high.astype(F32)).astype(BF16)
    sigma, skip, out_scale, weight, coef = [
        figures.spot[k : k + 1, 0:1] for k in (0, 1, 2, 4, 5)
    ]
    back_order = interleave(True)
    pairs[...] = mm(high, back_order) + mm(low, back_order)
    blank = jnp.zeros((4, 512), F32)
    loss_sum = jnp.zeros((12, 512), F32)
    top = pick(scal, whole(line_a), whole(line_b)) + out_scale * pairs[0:16, :]
    cells[0:16, :] = coef * scal[6] * top
    low = pick(scal, whole(line_b), whole(line_a)) + out_scale * pairs[16 * (ROWS + 1) :, :]
    cells[16 * (ROWS + 1) :, :] = coef * scal[7] * low
    spill(goals, whole(target))
    spill(noisies, whole(target) + sigma * whole(noise))
    for i in range(ROWS):
        goal = strided(goals, i, 12)
        noisy = strided(noisies, i, 12)
        estimate = skip * noisy + out_scale * pairs[16 * (i + 1) : 16 * (i + 1) + 12, :]
        for t in range(4):
            found[t, pl.ds(i, 12, stride=ROWS), :] = estimate[:, 128 * t : 128 * (t + 1)]
        mismatch = estimate - goal
        loss_sum = loss_sum + weight * mismatch * mismatch
        cells[16 * (i + 1) : 16 * (i + 2), :] = jnp.concatenate([coef * mismatch, blank], axis=0)
    give(denoised, jnp.concatenate([found[t] for t in range(4)], axis=1))
    loss_sum = jnp.broadcast_to(
        jnp.sum(jnp.sum(loss_sum, axis=1, keepdims=True), axis=0, keepdims=True), (1, 128)
    )
    pairs[...] = mm(cells[...].astype(BF16), interleave(False))
    g = {}
    for i in range(-1, ROWS + 1):
        value = pairs[16 * (i + 1) : 16 * (i + 2), :]
        g[i] = jnp.concatenate([value[:, :HALF], value[:, HALF:]], axis=0).astype(BF16)
        put(cotangents, i, g[i])
    weights = whole(wout_t)
    total = jnp.zeros((128, HALF), F32)
    cross = jnp.zeros((128, HALF), F32)
    for r in range(ROWS):
        value = fine_untap(mm(weights, stack_rows(g, r)))
        put(back, r, value.astype(BF16))
        hat = row(hats, r).astype(F32)
        e = value * silu_slope(hat)
        total = total + e
        cross = cross + e * hat
    for j in range(3):
        top, low = row(back, j), row(back, ROWS - 3 + j)
        put(edge_a, j, pick(scal, top, low))
        put(edge_b, j, pick(scal, low, top))
    put_stats(stats, total, cross, loss_sum)


def grads_out(scal, cotangents, zs, grad, gs):
    g = {r: row(cotangents, r) for r in range(-1, ROWS + 1)}
    for r in range(ROWS):
        put(gs, r, stack_rows(g, r))
    parts = fine_grad(mm_nt(gs[...], whole(zs)), 16, 64)
    put_grad(grad, 0, grad_blocks(parts, 64), split=False)


def grads_up(scal, grad_merged, grad_coarse, kept_up, kept_c, grad_out, grads, gs, zs, gc):
    g = {r: row(grad_merged, r) for r in range(-1, ROWS + 1)}
    for r in range(ROWS):
        put(gs, r, stack_rows(g, r))
        put(zs, r, row(kept_up, r // 2))
    g = {r: row(grad_coarse, r) for r in range(-1, CROWS + 1)}
    for r in range(CROWS):
        put(gc, r, stack_rows(g, r))
    blocks = mm_nt(gs[...], zs[...])
    parts = []
    for a in range(3):
        even = blocks[128 * a : 128 * a + 64]
        odd = blocks[128 * a + 64 : 128 * a + 128]
        parts.append(
            jnp.concatenate(
                [
                    even[:, :128] + odd[:, 128:256],
                    even[:, 128:256] + odd[:, 128:256],
                    even[:, 128:256] + odd[:, 256:],
                ],
                axis=1,
            )
        )
    start = put_grad(grads, 0, grad_blocks(parts, 128))
    blocks = mm_nt(gc[...], whole(kept_c))
    parts = [blocks[128 * a : 128 * (a + 1)] for a in range(3)]
    start = put_grad(grads, start, grad_blocks(parts, 128))
    for f in range(grads.shape[0]):
        grads.spot[f, start : start + 80, :] = grad_out.spot[f]
    clear_rest(grads, start + 80)


def grads_down(scal, grad_fine, grad_c, kept_pool, kept_b, grads, gs, gc):
    g = {r: row(grad_fine, r) for r in range(-1, ROWS + 1)}
    for r in range(ROWS):
        put(gs, r, stack_rows(g, r))
    g = {r: row(grad_c, r) for r in range(-1, CROWS + 1)}
    for r in range(CROWS):
        put(gc, r, stack_rows(g, r))
    blocks = mm_nt(gc[...], whole(kept_pool))
    parts = [blocks[128 * a : 128 * (a + 1)] for a in range(3)]
    start = put_grad(grads, 0, grad_blocks(parts, 64))
    parts = fine_grad(mm_nt(gs[...], whole(kept_b)), 64, 64)
    clear_rest(grads, put_grad(grads, start, grad_blocks(parts, 64)))


def grads_first(scal, grad_b, line, vec, kept_a, grads, gs):
    g = {r: row(grad_b, r) for r in range(-1, ROWS + 1)}
    for r in range(ROWS):
        put(gs, r, stack_rows(g, r))
    parts = fine_grad(mm_nt(gs[...], whole(kept_a)), 64, 64)
    start = put_grad(grads, 0, grad_blocks(parts, 64))
    line = line.spot[0:1, :]
    line = line + pltpu.roll(line, 64, 1)
    column = jnp.sum(
        place(128, 128, 0).astype(F32) * vec.spot[0:1, :].astype(F32), axis=1, keepdims=True
    )
    outer = (column * line).astype(BF16)
    size = 128 // grads.shape[0]
    for f in range(grads.shape[0]):
        grads.spot[f, start : start + size, :] = outer[f * size : (f + 1) * size]


def stage_up(
    members, members_c, scal, stats_d, stats_ed, got_a, got_b, hats, back, wup_t, stats_c, hats_c,
    wcoarse_t, done,
    grad_merged, back_c, grad_coarse, edge_a, edge_b, stats, loss, total_next,
):
    give(loss, jnp.broadcast_to(total_stats(stats_ed)[2:3, :], (8, 128)))
    mean, inverse = norm_columns(stats_d, True, members)
    shift, slope = back_columns(stats_ed, True, members)
    hats.wait(1)
    g = {}
    for r in range(-3, ROWS + 3):
        hat = row(hats, r).astype(F32)
        if r < 0:
            u = pick(scal, row(got_a, r + 3), row(got_b, r + 3)).astype(F32)
        elif r < ROWS:
            u = row(back, r).astype(F32)
        else:
            u = pick(scal, row(got_b, r - ROWS), row(got_a, r - ROWS)).astype(F32)
        value = inverse * (u * silu_slope(hat) - shift - hat * slope)
        g[r] = masked(value, r, ROWS, scal).astype(BF16)
        if -2 <= r < ROWS + 2:
            put(grad_merged, r, g[r])
    wup_t.wait(1)
    weights = whole(wup_t)
    gk = {}
    for r in range(-1, CROWS + 1):
        rows = jnp.concatenate([g[2 * r + 2], g[2 * r + 1], g[2 * r], g[2 * r - 1]], axis=0)
        value = coarse_untap(mm(weights, rows))
        gk[r] = masked(value, r, CROWS, scal).astype(BF16)
        put(grad_coarse, r, gk[r])
    wcoarse_t.wait(1)
    hats_c.wait(1)
    stats_c.wait(1)
    weights = whole(wcoarse_t)
    mean, inverse = norm_columns(stats_c, False, members_c)
    total = jnp.zeros((128, HALF), F32)
    cross = jnp.zeros((128, HALF), F32)
    for r in range(CROWS):
        value = coarse_untap(mm(weights, stack_rows(gk, r)))
        put(back_c, r, value.astype(BF16))
        hat = row(hats_c, r).astype(F32)
        e = value * silu_slope(hat)
        total = total + e
        cross = cross + e * hat
    top = [row(back_c, 0), row(back_c, 1), gk[1]]
    low = [row(back_c, 2), row(back_c, 3), gk[2]]
    for j in range(3):
        put(edge_a, j, pick(scal, top[j], low[j]))
        put(edge_b, j, pick(scal, low[j], top[j]))
    put_stats(stats, total, cross)
    give(total_next, whole(stats_c))


def stage_down(
    members, members_c, scal, stats_c, stats_ec, got_a, got_b, hats_c, back_c, grad_coarse,
    wdown_t, grad_merged, stats_b, wsecond_t, hats, done,
    grad_fine, back_b, stats, grad_c, total_next,
):
    mean, inverse = norm_columns(stats_c, False, members_c)
    shift, slope = back_columns(stats_ec, False, members_c)
    hats_c.wait(1)
    g = {}
    for r in range(-2, CROWS + 2):
        hat = row(hats_c, r).astype(F32)
        if r < 0:
            u = pick(scal, row(got_a, r + 2), row(got_b, r + 2)).astype(F32)
        elif r < CROWS:
            u = row(back_c, r).astype(F32)
        else:
            u = pick(scal, row(got_b, r - CROWS), row(got_a, r - CROWS)).astype(F32)
        if r == -2:
            through = pick(scal, row(got_a, 2), row(got_b, 2)).astype(F32)
        elif r == CROWS + 1:
            through = pick(scal, row(got_b, 2), row(got_a, 2)).astype(F32)
        else:
            through = row(grad_coarse, r).astype(F32)
        value = through + inverse * (u * silu_slope(hat) - shift - hat * slope)
        g[r] = masked(value, r, CROWS, scal).astype(BF16)
        if -1 <= r <= CROWS:
            put(grad_c, r, g[r])
    wdown_t.wait(1)
    weights = whole(wdown_t)
    fine = {}
    for r in range(-1, CROWS + 1):
        value = 0.25 * coarse_untap(mm(weights, stack_rows(g, r)))
        both = jnp.concatenate([value, value], axis=0)
        for i in (2 * r, 2 * r + 1):
            value = masked(row(grad_merged, i).astype(F32) + both, i, ROWS, scal)
            fine[i] = value.astype(BF16)
            if -1 <= i <= ROWS:
                put(grad_fine, i, fine[i])
    wsecond_t.wait(1)
    hats.wait(1)
    stats_b.wait(1)
    weights = whole(wsecond_t)
    mean, inverse = norm_columns(stats_b, True, members)
    total = jnp.zeros((128, HALF), F32)
    cross = jnp.zeros((128, HALF), F32)
    for r in range(-1, ROWS + 1):
        value = fine_untap(mm(weights, stack_rows(fine, r)))
        put(back_b, r, value.astype(BF16))
        if 0 <= r < ROWS:
            hat = row(hats, r).astype(F32)
            e = value * silu_slope(hat)
            total = total + e
            cross = cross + e * hat
    put_stats(stats, total, cross)
    give(total_next, whole(stats_b))


def stage_first(
    members, scal, stats_b, stats_eb, hats_b, back_b, wfirst_t, stats_a, hats, done,
    back_a, stats, grad_b, line, total_next,
):
    mean, inverse = norm_columns(stats_b, True, members)
    shift, slope = back_columns(stats_eb, True, members)
    hats_b.wait(1)
    g = {}
    sums = jnp.zeros((128, HALF), F32)
    for r in range(-1, ROWS + 1):
        hat = row(hats_b, r).astype(F32)
        u = row(back_b, r).astype(F32)
        value = inverse * (u * silu_slope(hat) - shift - hat * slope)
        if 0 <= r < ROWS:
            sums = sums + value
        g[r] = masked(value, r, ROWS, scal).astype(BF16)
        put(grad_b, r, g[r])
    wfirst_t.wait(1)
    hats.wait(1)
    stats_a.wait(1)
    weights = whole(wfirst_t)
    total = jnp.zeros((128, HALF), F32)
    cross = jnp.zeros((128, HALF), F32)
    for r in range(ROWS):
        value = fine_untap(mm(weights, stack_rows(g, r)))
        put(back_a, r, value.astype(BF16))
        hat = row(hats, r).astype(F32)
        e = value * silu_slope(hat)
        total = total + e
        cross = cross + e * hat
    put_stats(stats, total, cross)
    sums = to_row(jnp.sum(sums, axis=1, keepdims=True))
    give(line, jnp.broadcast_to(sums, (8, 128)))
    give(total_next, whole(stats_a))


def stage_last(
    members, members_all, scal, stats_a, stats_ea, hats, back_a, grad_fine, kept_in, early, middle, first,
    loss, loss_other, keep, send, loss_sum, gs, held, sems,
):
    grads = Source(held, [], 0)
    copies, start = [], 0
    for index, ref in enumerate((early, middle)):
        rows = pl.ds(start, ref.shape[1])
        copies.append(
            pltpu.make_async_copy(ref.spot, grads.spot.at[:, rows, :], sems.at[index])
        )
        copies[index].start()
        start += ref.shape[1]
    give(loss_sum, (loss.spot[0:1, 0:1] + loss_other.spot[0:1, 0:1]) * (1.0 / members_all))
    mean, inverse = norm_columns(stats_a, True, members)
    shift, slope = back_columns(stats_ea, True, members)
    for r in range(ROWS):
        hat = row(hats, r).astype(F32)
        u = row(back_a, r).astype(F32)
        value = row(grad_fine, r).astype(F32) + inverse * (
            u * silu_slope(hat) - shift - hat * slope
        )
        put(gs, r, value.astype(BF16))
    kept_in.wait(1)
    first.wait(1)
    parts = []
    for a in range(3):
        blocks = mm_nt(gs[...], kept_in.spot[:, a * HALF : (a + ROWS) * HALF])
        parts.append(
            jnp.concatenate(
                [blocks[:64, :96] + blocks[64:, 32:128], jnp.zeros((64, 32), F32)], axis=1
            )
        )
    size = first.shape[1]
    for f in range(grads.shape[0]):
        grads.spot[f, start : start + size, :] = first.spot[f]
    clear_rest(grads, put_grad(grads, start + size, parts))
    for copy in copies:
        copy.wait()
    half = keep.shape[1]
    odd = scal[8] > 0.5
    for f in range(keep.shape[0]):
        low, high = held[f, :half, :], held[f, half:, :]
        keep.spot[f] = jnp.where(odd, high, low)
        send.spot[f] = jnp.where(odd, low, high)


def join(scal, kept, got, out):
    give(out, (whole(kept).astype(F32) + whole(got).astype(F32)).astype(BF16))


def add_up(scal, got, out):
    total = got.spot[0].astype(F32)
    for index in range(1, got.shape[0]):
        total = total + got.spot[index].astype(F32)
    total = total.astype(BF16)
    for index in range(out.shape[0]):
        out.spot[index] = total


def unpack(starts, scal, mine, other, *refs):
    first, down, second, coarse, up, out, embed, inputs, flat = refs
    half = mine.shape[0]
    odd = scal[8] > 0.5
    flat[:half, :] = jnp.where(odd, whole(other), whole(mine)).astype(F32)
    flat[half:, :] = jnp.where(odd, whole(mine), whole(other)).astype(F32)

    def take(ref, start, out, size, ins, trim=False):
        for t in range(9):
            a, b = t // 3, t % 3
            if ins == 128:
                at, lanes = t, 0
            elif ins == 64:
                at, lanes = (a, b) if b < 2 else (3 + a // 2, a % 2)
            else:
                at, lanes = a, b
            value = ref[start + at * size : start + (at + 1) * size, :]
            if ins == 24:
                out.spot[t] = mm_nt(place(24, 128, 32 * lanes), value.astype(BF16))
                continue
            value = value[:, lanes * ins : (lanes + 1) * ins]
            if trim:
                value = value[:12]
                if out.shape[2] == 32:
                    value = jnp.where(scal[9] > 0.5, value[:, :32], value[:, 32:])
            out.spot[t] = value
        return start + (9 if ins == 128 else 5 if ins == 64 else 3) * size

    start = take(flat, 0, up, up.shape[1], 128)
    start = take(flat, start, coarse, coarse.shape[1], 128)
    take(flat, start, out, 16, 64, trim=True)
    start = take(flat, starts[0], down, down.shape[1], 64)
    take(flat, start, second, second.shape[1], 64)
    start = take(flat, starts[1], first, first.shape[1], 64)
    size = embed.shape[0]
    give(embed, flat[start : start + size, :64])
    take(flat, start + size, inputs, inputs.shape[2], 24)


class Field:
    def __init__(self, array, first):
        self.array, self.first = array, first


class Saved:
    def __init__(self, item, low=None, high=None, when=0):
        self.item, self.low, self.high, self.when = item, low, high, when


def shape(*dims, dtype=F32):
    return jax.ShapeDtypeStruct(dims, dtype)


def rows_of(first, number, dtype=F32):
    return Field(shape(number, 128, HALF, dtype=dtype), first)


def flat_rows(first, number, channels):
    return Field(shape(channels, number * HALF, dtype=BF16), first)


def opened(item):
    saved = item if isinstance(item, Saved) else None
    item = saved.item if saved else item
    if isinstance(item, Field):
        return saved, item.array, item.first
    return saved, item, 0


def position():
    me, bands = lax.axis_index("rows"), lax.axis_size("rows")
    return {
        6: jnp.where(me > 0, 1.0, 0.0),
        7: jnp.where(me < bands - 1, 1.0, 0.0),
        8: jnp.where(me % 2 == 1, 1.0, 0.0),
        9: jnp.where(lax.axis_index("fsdp") == 0, 1.0, 0.0),
    }


def run(name, kernel, outs, scal, *operands, scratch=()):
    vmem, hbm = pl.BlockSpec(memory_space=pltpu.VMEM), pl.BlockSpec(memory_space=pltpu.HBM)
    in_specs, arrays, plans, spots = [], [], [], []
    if scal is not None:
        in_specs, arrays = [pl.BlockSpec(memory_space=pltpu.SMEM)], [scal]
    for item in operands:
        saved, item, first = opened(item)
        if saved is None:
            in_specs.append(vmem)
            arrays.append(item)
            plans.append((first, None, None))
            continue
        part = None
        dims = item.shape
        if saved.low is not None:
            part = pl.ds(saved.low - first, saved.high - saved.low)
            dims = (saved.high - saved.low,) + dims[1:]
            first = saved.low
        in_specs.append(hbm)
        arrays.append(pltpu.with_memory_space_constraint(item, pltpu.HBM))
        if saved.when is None:
            plans.append((first, None, None))
            continue
        plans.append((first, (saved.when, part), len(spots)))
        spots.append(pltpu.VMEM(dims, item.dtype))
    ins = len(operands)
    out_specs, out_shapes = [], []
    for item in outs:
        saved, item, first = opened(item)
        if saved is None:
            out_specs.append(vmem)
            out_shapes.append(item)
            plans.append((first, None, None))
            continue
        out_specs.append(hbm)
        out_shapes.append(pltpu.HBM(item.shape, item.dtype))
        last = None
        if isinstance(saved.item, Field):
            count = item.shape[0] if len(item.shape) == 3 else item.shape[1] // HALF
            last = first + count - 1
        if saved.when is None:
            plans.append((first, None, None))
            continue
        plans.append((first, (last, None), len(spots)))
        spots.append(pltpu.VMEM(item.shape, item.dtype))

    def body(*refs):
        numbers = position()
        if scal is not None:
            numbers.update({index: refs[0][index] for index in range(6)})
            refs = refs[1:]
        given, refs = refs[: len(plans)], refs[len(plans) :]
        held, refs = refs[: len(spots)], refs[len(spots) :]
        sems, extra = refs[0], refs[1:]
        wrapped = []
        for index, (ref, (first, plan, place_at)) in enumerate(zip(given, plans)):
            copies = []
            if plan is not None:
                where = held[place_at]
                when, part = plan
                if index < ins:
                    source = ref if part is None else ref.at[part]
                    copies.append((when, pltpu.make_async_copy(source, where, sems.at[place_at])))
                else:
                    copies.append((when, pltpu.make_async_copy(where, ref, sems.at[place_at])))
                ref = where
            wrapped.append((Source if index < ins else Sink)(ref, copies, first))
        for item in wrapped[:ins]:
            item.wait(0)
        kernel(numbers, *wrapped, *extra)
        for item in wrapped[ins:]:
            item.finish()
        for item in wrapped[ins:]:
            for copy in item.started:
                copy.wait()

    made = pl.pallas_call(
        body,
        out_shape=tuple(out_shapes),
        in_specs=in_specs,
        out_specs=tuple(out_specs),
        scratch_shapes=spots
        + [pltpu.SemaphoreType.DMA((max(len(spots), 1),))]
        + [pltpu.VMEM(*item) if isinstance(item, tuple) else item for item in scratch],
        compiler_params=pltpu.CompilerParams(vmem_limit_bytes=LIMIT),
        name=name,
    )(*arrays)
    results = []
    for array, item in zip(made, outs):
        item = item.item if isinstance(item, Saved) else item
        results.append(Field(array, item.first) if isinstance(item, Field) else array)
    return results


def sum_parts(stats):
    return lax.all_to_all(stats, "rows", 0, 0)


def swap(value_a, value_b):
    count = lax.axis_size("rows")
    pairs = [(i, i ^ 1) for i in range(count)]
    across = []
    for i in range(1, count - 1, 2):
        across += [(i, i + 1), (i + 1, i)]
    return lax.ppermute(value_a, "rows", pairs), lax.ppermute(value_b, "rows", across)


def gather_packed(packed):
    if lax.axis_size("fsdp") == 2:
        return [packed, lax.ppermute(packed, "fsdp", [(0, 1), (1, 0)])]
    whole = lax.all_gather(packed, "fsdp").astype(F32)
    return [whole[i] for i in range(whole.shape[0])]


def group_shape(rows, count):
    return shape(count, -(-rows // 16) * 16, 128, dtype=BF16)


def per_device(
    residual_target,
    conditioning,
    noise_sample,
    noise_level,
    input_kernel,
    first_kernel,
    second_kernel,
    down_kernel,
    coarse_kernel,
    upward_kernel,
    output_kernel,
    embed_matrix,
):
    bands, count = lax.axis_size("rows"), lax.axis_size("fsdp")
    members = 2 * ROWS * 2 * HALF * bands
    members_c = 4 * CROWS * HALF * bands
    members_all = count * residual_target.size * bands
    sigma_level, skip_scale, out_scale, in_scale, weight = preconditions(noise_level[0])
    coef = 2.0 * weight * out_scale / members_all
    scal = jnp.stack([sigma_level, skip_scale, out_scale, in_scale, weight, coef])
    embedded = embedding(sigma_level, embed_matrix.shape[0] * count)
    target = residual_target.reshape(12 * ROWS, 512)
    condition = conditioning.reshape(12 * ROWS, 512)
    noise = noise_sample.reshape(12 * ROWS, 512)

    def widths_of(shards, rows):
        widths = tuple(
            (9 if item.ndim == 3 else 1, size, item.ndim == 3 and item.shape[1] == 24)
            for item, size in zip(shards, rows)
        )
        total = 0
        for item, (taps, size, swapped) in zip(shards, widths):
            paired = taps == 9 and item.shape[2] == 64
            total += (3 if swapped else 5 if paired else taps) * size
        return widths, total

    fine_o, coarse_o = input_kernel.shape[1], down_kernel.shape[1]
    inputs_t = jnp.swapaxes(input_kernel, 1, 2)
    shards = [inputs_t, first_kernel, embed_matrix]
    widths, packed_rows = widths_of(shards, [fine_o, fine_o, embed_matrix.shape[0]])
    far = shape(32, FAR * 512, dtype=BF16)
    early, own, edge_a, edge_b, figures = run(
        "enter",
        functools.partial(enter, widths),
        [
            shape(packed_rows, 128, dtype=BF16), shape(32, ROWS * 512, dtype=BF16), far, far,
            Saved(shape(8, 128)),
        ],
        scal,
        Saved(target, when=2),
        Saved(condition, when=2),
        Saved(noise, when=2),
        *[Saved(item, when=1) for item in shards],
        scratch=[
            ((packed_rows, 128), F32), ((4, 192, 128), F32), ((2, 16, FAR * 512), BF16)
        ],
    )
    got_a, got_b = swap(edge_a, edge_b)
    early = gather_packed(early)
    shards = [second_kernel, down_kernel, coarse_kernel, upward_kernel, output_kernel]
    widths, packed_rows = widths_of(shards, [fine_o, coarse_o, coarse_o, fine_o, 16])
    (rest,) = run(
        "pack_rest",
        functools.partial(pack, widths),
        [shape(packed_rows, 128, dtype=BF16)],
        None,
        *[Saved(item) for item in shards],
        own,
        scratch=[((packed_rows, 128), F32)],
    )
    vector = jnp.broadcast_to(embedded[None, :], (16, embedded.shape[0]))
    stat = shape(bands, 4, 128)
    total = Saved(shape(1, 4, 128))
    act_a, stats_a, kept_in, line_a, line_b = run(
        "stage_a",
        stage_a,
        [
            rows_of(-6, 20), stat, Saved(flat_rows(-1, 10, 128)),
            Saved(shape(16, 512)), Saved(shape(16, 512)),
        ],
        None,
        got_a, got_b, own, rest, *early,
        scratch=[((32, FAR * 512), BF16), ((32, FAR * 512), BF16)],
    )
    stats_a = sum_parts(stats_a)
    rest, stats_a = lax.optimization_barrier((rest, stats_a))
    (
        wsecond, wsecond_t, wdown, wdown_t, wcoarse, wcoarse_t, wup, wup_t, wout, wout_t
    ) = run(
        "prepare_rest",
        prepare_rest,
        [
            Saved(shape(384, 256, dtype=BF16)), Saved(shape(256, 384, dtype=BF16)),
            Saved(shape(384, 192, dtype=BF16)), Saved(shape(192, 384, dtype=BF16)),
            Saved(shape(384, 384, dtype=BF16)), Saved(shape(384, 384, dtype=BF16)),
            Saved(shape(384, 512, dtype=BF16)), Saved(shape(384, 512, dtype=BF16)),
            Saved(shape(96, 256, dtype=BF16)), Saved(shape(256, 96, dtype=BF16)),
        ],
        None,
        *gather_packed(rest),
    )

    act_b, stats_b, kept_a, hats_a, act_a, total_a, wfirst_t = run(
        "stage_b",
        functools.partial(stage_b, members, embedded.shape[0]),
        [
            rows_of(-5, 18), stat, Saved(flat_rows(0, 8, 256), when=None),
            Saved(rows_of(0, 8, BF16)),
            Saved(rows_of(-4, 16), when=None), total, Saved(shape(256, 384, dtype=BF16)),
        ],
        None,
        stats_a, act_a, vector, *early,
        scratch=[((384, 256), BF16), ((256, 20 * HALF), BF16), pltpu.SemaphoreType.DMA((2,))],
    )
    stats_b = sum_parts(stats_b)
    fine, act_c, edge, stats_c, kept_b, kept_pool, hats_b, total_b = run(
        "stage_c",
        functools.partial(stage_c, members),
        [
            rows_of(-3, 14), rows_of(-1, 6), Field(shape(128, 2 * HALF), 1), stat,
            Saved(flat_rows(0, 8, 256), when=None), Saved(flat_rows(0, 4, 192)),
            Saved(rows_of(-1, 10, BF16)), total,
        ],
        None,
        stats_b, Saved(wsecond, when=1), act_b, Saved(act_a, when=1), Saved(wdown, when=1),
        scratch=[
            ((256, 18 * HALF), BF16), ((16, 128, HALF), F32), pltpu.SemaphoreType.DMA((1,)),
        ],
    )
    got_a, got_b = swap(edge.array, edge.array)
    stats_c = sum_parts(stats_c)
    merged, hats_c, stats_d, kept_c, kept_up, total_c = run(
        "stage_d",
        functools.partial(stage_d, members_c),
        [
            rows_of(-3, 14), Saved(rows_of(-2, 8, BF16)), stat,
            Saved(flat_rows(0, 4, 384), when=None), Saved(flat_rows(0, 4, 384)), total,
        ],
        None,
        stats_c, Saved(wcoarse, when=1), got_a, got_b, act_c, Saved(wup, when=1), fine,
        scratch=[((384, 10 * HALF), BF16), pltpu.SemaphoreType.DMA((1,))],
    )
    stats_d = sum_parts(stats_d)
    edge = Field(shape(128, 3 * HALF, dtype=BF16), 0)
    denoised, back_d, edge_a, edge_b, stats_ed, hats_d, cotangents, kept_d, total_d = run(
        "stage_out",
        functools.partial(stage_out, members),
        [
            Saved(shape(96, 512)), rows_of(0, 8, BF16), edge, edge, stat,
            Saved(rows_of(-3, 14, BF16)),
            Field(shape(10, 32, HALF, dtype=BF16), -1),
            Saved(flat_rows(0, 8, 256), when=None), shape(1, 4, 128),
        ],
        None,
        stats_d, Saved(wout, when=1), merged, Saved(line_a, when=1), Saved(line_b, when=1),
        Saved(target, when=1), Saved(noise, when=1), Saved(wout_t, when=1),
        Saved(figures, when=1),
        scratch=[
            ((160, 512), F32), ((160, 512), F32),
            ((4, 96, 128), F32), ((4, 96, 128), F32), ((4, 96, 128), F32),
            ((256, 12 * HALF), BF16), pltpu.SemaphoreType.DMA((1,)),
        ],
    )
    got_a, got_b = swap(edge_a.array, edge_b.array)
    (grad_out,) = run(
        "grads_out",
        grads_out,
        [Saved(shape(count, 80, 128, dtype=BF16))],
        None,
        cotangents, Saved(kept_d),
        scratch=[((96, 8 * HALF), BF16)],
    )
    stats_ed = sum_parts(stats_ed)
    grad_merged, back_c, grad_coarse, edge_a, edge_b, stats_ec, loss, total_c = run(
        "stage_up",
        functools.partial(stage_up, members, members_c),
        [
            rows_of(-2, 12, BF16), rows_of(0, 4, BF16), rows_of(-1, 6, BF16), edge, edge, stat,
            shape(8, 128), shape(1, 4, 128),
        ],
        None,
        total_d, stats_ed, got_a, got_b, Saved(hats_d, when=1), back_d, Saved(wup_t, when=1),
        Saved(total_c, when=1),
        Saved(hats_c, when=1), Saved(wcoarse_t, when=1), Saved(grad_out, when=None),
    )
    got_a, got_b = swap(edge_a.array, edge_b.array)
    (early,) = run(
        "grads_up",
        grads_up,
        [Saved(group_shape(9 * (fine_o + coarse_o) + 80, count))],
        None,
        grad_merged, grad_coarse, Saved(kept_up), Saved(kept_c), Saved(grad_out),
        scratch=[
            ((384, 8 * HALF), BF16), ((384, 8 * HALF), BF16), ((384, 4 * HALF), BF16)
        ],
    )
    stats_ec = sum_parts(stats_ec)
    if count == 2:
        loss_other = lax.ppermute(loss, "fsdp", [(0, 1), (1, 0)])
    else:
        loss_other = lax.psum(loss, "fsdp") - loss
    grad_fine, back_b, stats_eb, grad_c, total_b = run(
        "stage_down",
        functools.partial(stage_down, members, members_c),
        [
            rows_of(-1, 10, BF16), rows_of(-1, 10, BF16), stat, Saved(rows_of(-1, 6, BF16)),
            shape(1, 4, 128),
        ],
        None,
        total_c, stats_ec, got_a, got_b, Saved(hats_c, when=1), back_c, grad_coarse,
        Saved(wdown_t, when=1), grad_merged, Saved(total_b, when=1), Saved(wsecond_t, when=1),
        Saved(hats_b, 0, 8, when=1), Saved(early, when=None),
    )
    (middle,) = run(
        "grads_down",
        grads_down,
        [Saved(group_shape(5 * (fine_o + coarse_o), count))],
        None,
        grad_fine, Saved(grad_c), Saved(kept_pool), Saved(kept_b),
        scratch=[((384, 8 * HALF), BF16), ((384, 4 * HALF), BF16)],
    )
    stats_eb = sum_parts(stats_eb)
    back_a, stats_ea, grad_b, line, total_a = run(
        "stage_first",
        functools.partial(stage_first, members),
        [
            rows_of(0, 8, BF16), stat, rows_of(-1, 10, BF16), shape(8, 128),
            shape(1, 4, 128),
        ],
        None,
        total_b, stats_eb, Saved(hats_b, when=1), back_b, Saved(wfirst_t, when=1), Saved(total_a, when=1),
        Saved(hats_a, when=1), Saved(middle, when=None),
    )
    (grad_first,) = run(
        "grads_first",
        grads_first,
        [Saved(shape(count, 5 * fine_o + embed_matrix.shape[0], 128, dtype=BF16))],
        None,
        grad_b, line, vector, Saved(kept_a),
        scratch=[((384, 8 * HALF), BF16)],
    )
    stats_ea = sum_parts(stats_ea)
    late = group_shape(8 * fine_o + embed_matrix.shape[0], count)
    starts = [early.shape[1], early.shape[1] + middle.shape[1]]
    total = starts[1] + late.shape[1]
    chunk = -(-total // (16 * bands)) * 16
    chips = bands // 2
    half = shape(count, chunk * chips, 128, dtype=BF16)
    keep, send, loss = run(
        "stage_last",
        functools.partial(stage_last, members, members_all),
        [half, half, shape(1, 1)],
        None,
        total_a, stats_ea, Saved(hats_a), back_a, grad_fine, Saved(kept_in, when=1),
        Saved(early, when=None), Saved(middle, when=None), Saved(grad_first, when=1), loss, loss_other,
        scratch=[
            ((128, 8 * HALF), BF16), ((count, chunk * bands, 128), BF16),
            pltpu.SemaphoreType.DMA((2,)),
        ],
    )
    loss_value = loss.reshape(())
    pairs = [(i, i ^ 1) for i in range(bands)]
    got = lax.ppermute(send, "rows", pairs)
    (both,) = run("join", join, [half], None, keep, got)
    both = both.reshape(count * chips, chunk, 128)
    cores = [[f * bands + r for f in range(count) for r in range(c, bands, 2)] for c in range(2)]
    got = lax.all_to_all(both, ("fsdp", "rows"), 0, 0, axis_index_groups=cores)
    (mine,) = run("add_up", add_up, [shape(chips, chunk, 128, dtype=BF16)], None, got)
    cores = [[r for r in range(c, bands, 2)] for c in range(2)]
    mine = lax.all_to_all(mine, "rows", 0, 0, axis_index_groups=cores)
    mine = mine.reshape(chips * chunk, 128)
    other = lax.ppermute(mine, "rows", pairs)
    first_g, down_g, second_g, coarse_g, up_g, out_g, embed_g, in_g = run(
        "unpack",
        functools.partial(unpack, starts),
        [
            shape(*first_kernel.shape),
            shape(*down_kernel.shape),
            shape(*second_kernel.shape),
            shape(*coarse_kernel.shape),
            shape(*upward_kernel.shape),
            shape(9, 12, output_kernel.shape[2] if count == 2 else 64),
            shape(*embed_matrix.shape),
            shape(*inputs_t.shape),
        ],
        None,
        mine, other,
        scratch=[((chunk * bands, 128), F32)],
    )
    width = output_kernel.shape[2]
    if count != 2:
        out_g = lax.dynamic_slice_in_dim(out_g, lax.axis_index("fsdp") * width, width, axis=2)
    return (
        denoised.reshape(residual_target.shape),
        loss_value,
        jnp.swapaxes(in_g, 1, 2),
        first_g,
        second_g,
        down_g,
        coarse_g,
        up_g,
        out_g,
        embed_g,
    )


def solution(mesh):
    in_specs = (
        P("fsdp", None, "rows", None),
        P("fsdp", None, "rows", None),
        P("fsdp", None, "rows", None),
        P("fsdp"),
        P(None, "fsdp", None),
        P(None, "fsdp", None),
        P(None, "fsdp", None),
        P(None, "fsdp", None),
        P(None, "fsdp", None),
        P(None, "fsdp", None),
        P(None, None, "fsdp"),
        P("fsdp", None),
    )
    out_specs = (
        P("fsdp", None, "rows", None),
        P(),
        P(None, "fsdp", None),
        P(None, "fsdp", None),
        P(None, "fsdp", None),
        P(None, "fsdp", None),
        P(None, "fsdp", None),
        P(None, "fsdp", None),
        P(None, None, "fsdp"),
        P("fsdp", None),
    )
    return jax.shard_map(
        per_device, mesh=mesh, in_specs=in_specs, out_specs=out_specs, check_vma=False
    )
```

```python
import functools

import jax
import jax.numpy as jnp
from jax import lax
from jax.experimental import pallas as pl
from jax.experimental.pallas import tpu as pltpu
from jax.sharding import PartitionSpec as P

GROUPS = 32
STEPS = 64

sigma_low = 0.002
sigma_high = 80.0
sigma_data = 0.5
rho_power = 7.0
eps_norm = 1e-05

F32 = jnp.float32
BF16 = jnp.bfloat16

HALF = 256
ROWS = 8
CROWS = 4
FAR = 7
LIMIT = 24 * 1024 * 1024


def preconditions(level_index):
    ramp_value = level_index.astype(jnp.float32) / (STEPS - 1)
    top_root = sigma_high ** (1.0 / rho_power)
    bottom = sigma_low ** (1.0 / rho_power)
    sigma_level = (top_root + ramp_value * (bottom - top_root)) ** rho_power
    sigma_total = sigma_level * sigma_level + sigma_data * sigma_data
    skip_scale = sigma_data * sigma_data / sigma_total
    out_scale = sigma_level * sigma_data * lax.rsqrt(sigma_total)
    in_scale = lax.rsqrt(sigma_total)
    weight = sigma_total / (sigma_level * sigma_data) ** 2
    return (sigma_level, skip_scale, out_scale, in_scale, weight)


def embedding(sigma_level, features):
    half_count = features // 2
    ramp_steps = jnp.arange(half_count, dtype=jnp.float32) / half_count
    frequency = 64.0 * 0.01**ramp_steps
    phase_angle = 0.25 * jnp.log(sigma_level) * frequency
    return jnp.concatenate([jnp.cos(phase_angle), jnp.sin(phase_angle)]).astype(jnp.bfloat16)


class Source:
    def __init__(self, spot, copies, first):
        self.spot, self.copies, self.first = spot, copies, first
        self.shape = spot.shape
        for _, copy in copies:
            copy.start()

    def wait(self, stage):
        for when, copy in self.copies:
            if when == stage:
                copy.wait()


class Sink:
    def __init__(self, spot, copies, first):
        self.spot, self.copies, self.first = spot, copies, first
        self.shape = spot.shape
        self.started = []

    def done(self, index):
        for last, copy in self.copies:
            if last == index:
                copy.start()
                self.started.append(copy)

    def send(self, source, sem):
        copy = pltpu.make_async_copy(source, self.spot, sem)
        copy.start()
        self.started.append(copy)

    def finish(self):
        for _, copy in self.copies:
            if not any(copy is other for other in self.started):
                copy.start()
                self.started.append(copy)


def spot(ref, index):
    if len(ref.shape) == 3:
        return (index - getattr(ref, "first", 0),)
    start = index - getattr(ref, "first", 0)
    return (slice(None), slice(start * HALF, (start + 1) * HALF))


def row(ref, index):
    return getattr(ref, "spot", ref)[spot(ref, index)]


def put(ref, index, value):
    getattr(ref, "spot", ref)[spot(ref, index)] = value
    if isinstance(ref, Sink):
        ref.done(index)


def whole(ref):
    return ref.spot[...]


def give(ref, value):
    ref.spot[...] = value
    ref.finish()


def lane(shape):
    return lax.broadcasted_iota(jnp.int32, shape, 1)


def from_left(value):
    moved = pltpu.roll(value, 1, 1)
    return jnp.where(lane(value.shape) == 0, jnp.zeros_like(moved), moved)


def from_right(value):
    moved = pltpu.roll(value, value.shape[1] - 1, 1)
    return jnp.where(lane(value.shape) == value.shape[1] - 1, jnp.zeros_like(moved), moved)


def mm(left, right):
    return jnp.dot(left, right, preferred_element_type=F32)


def mm_nt(left, right):
    return lax.dot_general(left, right, (((1,), (1,)), ((), ())), preferred_element_type=F32)


def fine_taps(value):
    half = value.shape[0] // 2
    value = value.astype(BF16)
    even, odd = value[:half], value[half:]
    return jnp.concatenate([from_left(odd), value, from_right(even)], axis=0)


def coarse_taps(value):
    value = value.astype(BF16)
    return jnp.concatenate([from_left(value), value, from_right(value)], axis=0)


def fine_untap(taps):
    size = taps.shape[0] // 4
    even = taps[size : 2 * size] + from_left(taps[3 * size :])
    odd = taps[2 * size : 3 * size] + from_right(taps[:size])
    return jnp.concatenate([even, odd], axis=0)


def coarse_untap(taps):
    size = taps.shape[0] // 3
    return taps[size : 2 * size] + from_right(taps[:size]) + from_left(taps[2 * size :])


def spread(parts, first, last):
    out = {}
    for i in range(first, last + 1):
        size = parts[i - 1].shape[0] // 3
        out[i] = parts[i - 1][:size] + parts[i][size : 2 * size] + parts[i + 1][2 * size :]
    return out


def stack_rows(g, r):
    return jnp.concatenate([g[r + 1], g[r], g[r - 1]], axis=0)


def same_group(size, fine):
    left = lax.broadcasted_iota(jnp.int32, (size, size), 0)
    right = lax.broadcasted_iota(jnp.int32, (size, size), 1)
    if fine:
        half = size // 2
        left, right = left % half, right % half
        per = half // GROUPS
    else:
        per = size // GROUPS
    return left // per == right // per


def total_stats(stats):
    total = stats.spot[0]
    for index in range(1, stats.shape[0]):
        total = total + stats.spot[index]
    return total


def group_sums(stats, fine):
    total = total_stats(stats)
    member = same_group(128, fine)
    first = jnp.sum(jnp.where(member, total[0:1, :], 0.0), axis=1, keepdims=True)
    second = jnp.sum(jnp.where(member, total[1:2, :], 0.0), axis=1, keepdims=True)
    return first, second


def norm_columns(stats_ref, fine, members):
    first, second = group_sums(stats_ref, fine)
    mean = first / members
    inverse = lax.rsqrt(second / members - mean * mean + eps_norm)
    return mean, inverse


def back_columns(stats_ref, fine, members):
    first, second = group_sums(stats_ref, fine)
    return first / members, second / members


def to_row(column):
    size = column.shape[0]
    diagonal = lax.broadcasted_iota(jnp.int32, (size, size), 0) == lax.broadcasted_iota(
        jnp.int32, (size, size), 1
    )
    return jnp.sum(jnp.where(diagonal, column, 0.0), axis=0, keepdims=True)


def put_stats(ref, first, second, third=None):
    first = to_row(jnp.sum(first, axis=1, keepdims=True))
    second = to_row(jnp.sum(second, axis=1, keepdims=True))
    if third is None:
        third = jnp.zeros((1, 128), F32)
    block = jnp.concatenate([first, second, third, jnp.zeros((1, 128), F32)], axis=0)
    block = block[: ref.shape[1]]
    for index in range(ref.shape[0]):
        ref.spot[index] = block
    ref.finish()


def silu(h):
    t = 0.5 * h
    return t + t * jnp.tanh(t)


def silu_slope(h):
    s = 0.5 + 0.5 * jnp.tanh(0.5 * h)
    return s * (1.0 + h * (1.0 - s))


def masked(value, index, rows, scal):
    if index < 0:
        return value * scal[6]
    if index >= rows:
        return value * scal[7]
    return value


def pick(scal, when_odd, when_even):
    return jnp.where(scal[8] > 0.5, when_odd, when_even)


def spill(ref, value):
    for t in range(4):
        ref[t, : value.shape[0], :] = value[:, 128 * t : 128 * (t + 1)]


def strided(ref, index, size):
    return jnp.concatenate(
        [ref[t, pl.ds(index, size, stride=ROWS), :] for t in range(4)], axis=1
    )


def interleave(transposed):
    left = lax.broadcasted_iota(jnp.int32, (512, 512), 0)
    right = lax.broadcasted_iota(jnp.int32, (512, 512), 1)
    if transposed:
        left, right = right, left
    place = (left & 1) * HALF + (left >> 1)
    return jnp.where(place == right, 1.0, 0.0).astype(BF16)


def fine_grad(blocks, outs, ins):
    parts = []
    for a in range(3):
        even = blocks[(2 * a) * outs : (2 * a + 1) * outs]
        odd = blocks[(2 * a + 1) * outs : (2 * a + 2) * outs]
        parts.append(even[:, : 3 * ins] + odd[:, ins : 4 * ins])
    return parts


def grad_blocks(parts, ins):
    if ins == 128:
        return [part[:, 128 * b : 128 * (b + 1)] for part in parts for b in range(3)]
    if ins == 64:
        blank = jnp.zeros(parts[0][:, :64].shape, F32)
        blocks = [part[:, :128] for part in parts]
        blocks.append(jnp.concatenate([parts[0][:, 128:192], parts[1][:, 128:192]], axis=1))
        blocks.append(jnp.concatenate([parts[2][:, 128:192], blank], axis=1))
        return blocks
    return parts


def put_grad(ref, start, blocks, split=True):
    count = ref.shape[0]
    size = blocks[0].shape[0] // count if split else blocks[0].shape[0]
    for block in blocks:
        for f in range(count):
            piece = block[f * size : (f + 1) * size] if split else block
            ref.spot[f, start : start + size, :] = piece.astype(BF16)
        start += size
    return start


def clear_rest(ref, start):
    count, size, _ = ref.shape
    if start < size:
        for f in range(count):
            ref.spot[f, start:, :] = jnp.zeros((size - start, 128), BF16)


def place(width, target, offset):
    left = lax.broadcasted_iota(jnp.int32, (width, target), 0)
    right = lax.broadcasted_iota(jnp.int32, (width, target), 1)
    return jnp.where(left + offset == right, 1.0, 0.0).astype(BF16)


def flipped(value):
    size = value.shape[1]
    return mm_nt(place(size, size, 0), value).astype(BF16)


def tap_of(pieces, offset, index, size, side=1):
    each = size // len(pieces)
    start = offset + index // side * each
    tap = jnp.concatenate([piece[start : start + each, :] for piece in pieces], axis=0)
    width = 128 // side
    return tap[:, width * (index % side) : width * (index % side + 1)].astype(BF16)


def in_order(scal, pieces):
    if len(pieces) == 2:
        mine, other = whole(pieces[0]), whole(pieces[1])
        low = scal[9] > 0.5
        return [jnp.where(low, mine, other), jnp.where(low, other, mine)]
    return [whole(piece) for piece in pieces]


def fine_matrix(taps, slot):
    rows = []
    for a in range(3):
        total = None
        for b in range(3):
            spread_out = jnp.concatenate(
                [place(slot, 4 * slot, b * slot), place(slot, 4 * slot, (b + 1) * slot)], axis=1
            )
            term = mm(taps[3 * a + b][:, :slot], spread_out)
            total = term if total is None else total + term
        rows += [total[:, : 4 * slot], total[:, 4 * slot :]]
    return jnp.concatenate(rows, axis=0).astype(BF16)


def pack(widths, scal, *refs):
    shards, (out, scratch) = refs[: len(widths)], refs[-2:]
    scratch[...] = jnp.zeros(scratch.shape, F32)
    start = 0
    for shard, (taps, rows, swapped) in zip(shards, widths):
        if taps == 1:
            scratch[start : start + rows, : shard.shape[1]] = whole(shard)
            start += rows
        else:
            for t in range(taps):
                value = shard.spot[t]
                if swapped:
                    value = mm_nt(place(value.shape[1], value.shape[1], 0), value.astype(BF16))
                if value.shape[1] in (24, 64):
                    side = 4 if value.shape[1] == 24 else 2
                    low = t % side * (128 // side)
                    scratch[start : start + value.shape[0], low : low + value.shape[1]] = value
                    start += rows if t % side == side - 1 or t == taps - 1 else 0
                else:
                    scratch[start : start + value.shape[0], : value.shape[1]] = value
                    start += rows
    give(out, scratch[...].astype(BF16))


def prepare_rest(scal, *refs):
    pieces = refs[:-10]
    wsecond, wsecond_t, wdown, wdown_t, wcoarse, wcoarse_t, wup, wup_t, wout, wout_t = refs[-10:]
    count = len(pieces)
    pieces = in_order(scal, pieces)
    start = 0

    def taps_of(size, paired=False):
        nonlocal start
        taps = [tap_of(pieces, start, t, size, 2 if paired else 1) for t in range(9)]
        start += (5 if paired else 9) * (size // count)
        return taps

    def both(value, forward, backward):
        give(forward, value)
        give(backward, flipped(value))

    both(fine_matrix(taps_of(64, True), 64), wsecond, wsecond_t)
    taps = taps_of(128, True)
    rows = []
    for a in range(3):
        total = None
        for b in range(3):
            term = mm(taps[3 * a + b][:, :64], place(64, 256, 64 * b))
            total = term if total is None else total + term
        rows.append(total)
    both(jnp.concatenate(rows, axis=0)[:, :192].astype(BF16), wdown, wdown_t)
    taps = taps_of(128)
    rows = [jnp.concatenate(taps[3 * a : 3 * a + 3], axis=1) for a in range(3)]
    both(jnp.concatenate(rows, axis=0), wcoarse, wcoarse_t)
    taps = taps_of(64)
    rows = []
    blank = jnp.zeros((64, 128), BF16)
    for a in range(3):
        rows.append(jnp.concatenate(taps[3 * a : 3 * a + 3] + [blank], axis=1))
        rows.append(jnp.concatenate([blank] + taps[3 * a : 3 * a + 3], axis=1))
    up = jnp.concatenate(rows, axis=0)
    give(wup, up)
    turned = flipped(up).astype(F32)
    turned = jnp.concatenate([turned[:128], turned[128:256] + turned[256:384], turned[384:]], axis=0)
    a0, a1, a2 = turned[:, :128], turned[:, 128:256], turned[:, 256:]
    give(wup_t, jnp.concatenate([a0, a0 + a1, a1 + a2, a2], axis=1).astype(BF16))
    taps = []
    width = 64 // count
    for t in range(9):
        total = None
        for s in range(count):
            tap = pieces[s][start + 16 * t : start + 16 * (t + 1), :].astype(BF16)
            term = mm(tap[:, :width], place(width, 128, s * width))
            total = term if total is None else total + term
        taps.append(total.astype(BF16))
    both(fine_matrix(taps, 64), wout, wout_t)


def enter(
    widths, scal, target, condition, noise, *refs
):
    *shards, packed, own, edge_a, edge_b, figures, taps, scratch, marks = refs
    for item in shards:
        item.wait(1)
    pack(widths, scal, *shards, packed, taps)
    for item in (target, condition, noise):
        item.wait(2)
    values = [jnp.full((1, 128), scal[k], F32) for k in range(6)]
    give(figures, jnp.concatenate(values + [jnp.zeros((2, 128), F32)], axis=0))
    sigma, skip, in_scale = scal[0], scal[1], scal[3]
    goal = whole(target)
    noisy = goal + sigma * whole(noise)
    q = skip * noisy - goal
    natural = jnp.concatenate([in_scale * noisy, whole(condition)], axis=0).astype(BF16)
    spill(scratch, mm(natural, interleave(False)))
    blank = jnp.zeros((8, 512), F32)
    for i in range(ROWS):
        value = strided(scratch, i, 24)
        own.spot[:, i * 512 : (i + 1) * 512] = jnp.concatenate([value, blank], axis=0).astype(BF16)
    spill(scratch, q)
    blank = jnp.zeros((4, 512), F32)
    for j, i in enumerate((0, ROWS - 1)):
        rest = jnp.concatenate([strided(scratch, i, 12), blank], axis=0)
        marks[j] = jnp.zeros(marks.shape[1:], BF16)
        for part in range(3):
            piece = rest.astype(BF16)
            rest = rest - piece.astype(F32)
            for k in range(2):
                lanes = slice((2 * part + k) * 512, (2 * part + k + 1) * 512)
                marks[j, 8:, lanes] = piece[8 * k : 8 * k + 8]
    for j, edge in enumerate((edge_a, edge_b)):
        odd = scal[8] > 0.5 if j == 0 else scal[8] < 0.5
        low = (ROWS - FAR) * 512
        edge.spot[:16, :] = jnp.where(odd, own.spot[:16, : FAR * 512], own.spot[:16, low:])
        edge.spot[16:, :] = jnp.where(odd, own.spot[16:, : FAR * 512], own.spot[16:, low:]) + (
            jnp.where(odd, marks[0], marks[1])
        )


def marked(scal, got):
    halves = []
    for k in range(2):
        total = None
        for part in range(3):
            lanes = slice((2 * part + k) * 512, (2 * part + k + 1) * 512)
            piece = got.spot[16:32, lanes].astype(F32)[8:]
            total = piece if total is None else total + piece
        halves.append(total)
    return jnp.concatenate(halves, axis=0)


def stage_a(scal, got_a, got_b, own, done, *refs):
    *pieces, act, stats, kept, line_a, line_b, above, below = refs
    pieces = in_order(scal, pieces)
    weights = fine_matrix([tap_of(pieces, 0, t, 64, 4) for t in range(9)], 32)
    give(line_a, marked(scal, got_a))
    give(line_b, marked(scal, got_b))
    above[...] = pick(scal, whole(got_a), whole(got_b))
    below[...] = pick(scal, whole(got_b), whole(got_a))
    clear = jnp.zeros((16, FAR * 512), BF16)
    keep = lax.broadcasted_iota(jnp.int32, (16, FAR * 512), 0) < 8
    for ref in (above, below):
        ref[16:, :] = jnp.where(keep, ref[16:, :], clear)
    parts = {}
    total = jnp.zeros((128, HALF), F32)
    square = jnp.zeros((128, HALF), F32)
    for r in range(-FAR, ROWS + FAR):
        if r < 0:
            value = above[:, (r + FAR) * 512 : (r + FAR + 1) * 512]
        elif r < ROWS:
            value = own.spot[:, r * 512 : (r + 1) * 512]
        else:
            value = below[:, (r - ROWS) * 512 : (r - ROWS + 1) * 512]
        z = fine_taps(jnp.concatenate([value[:, :HALF], value[:, HALF:]], axis=0))
        if -1 <= r <= ROWS:
            put(kept, r, z)
        parts[r] = mm(weights, z)
        i = r - 1
        if i > -FAR:
            value = spread(parts, i, i)[i]
            put(act, i, value)
            del parts[i - 1]
            if 0 <= i < ROWS:
                total = total + value
                square = square + value * value
    put_stats(stats, total, square)


def slot(ref, index):
    return ref[:, index * HALF : (index + 1) * HALF]


def fill(ref, index, value):
    ref[:, index * HALF : (index + 1) * HALF] = value


def stage_b(members, embed_size, scal, stats_a, act_a, vec, *refs):
    *pieces, act_b, stats, kept, hats, passed, totals, wfirst_t, wfirst, zs, sems = refs
    passed.send(act_a.spot.at[pl.ds(2, 16)], sems.at[0])
    give(totals, total_stats(stats_a)[None])
    count = len(pieces)
    pieces = in_order(scal, pieces)
    start = 3 * (64 // count)
    first = fine_matrix([tap_of(pieces, start, t, 64, 2) for t in range(9)], 64)
    start += 5 * (64 // count)
    wfirst[...] = first
    give(wfirst_t, flipped(first))
    line = mm(whole(vec), tap_of(pieces, start, 0, embed_size))[0:1, :64]
    both = jnp.concatenate([line, line], axis=1)
    lift = jnp.sum(place(128, 128, 0).astype(F32) * both, axis=1, keepdims=True)
    mean, inverse = norm_columns(stats_a, True, members)
    for r in range(-6, ROWS + 6):
        hat = (row(act_a, r) - mean) * inverse
        fill(zs, r + 6, fine_taps(masked(silu(hat), r, ROWS, scal)))
        if 0 <= r < ROWS:
            hats.spot[r] = hat.astype(BF16)
    hats.finish()
    kept.send(zs.at[:, pl.ds(6 * HALF, 8 * HALF)], sems.at[1])
    parts = {}
    total = jnp.zeros((128, HALF), F32)
    square = jnp.zeros((128, HALF), F32)
    for r in range(-6, ROWS + 6):
        parts[r] = mm(wfirst[...], slot(zs, r + 6))
        i = r - 1
        if i > -6:
            value = spread(parts, i, i)[i] + lift
            put(act_b, i, value)
            del parts[i - 1]
            if 0 <= i < ROWS:
                total = total + value
                square = square + value * value
    put_stats(stats, total, square)


def stage_c(
    members, scal, stats_b, wsecond, act_b, act_a, wdown,
    fine, act_c, edge, stats, kept, kept_pool, hats, totals, zs, convolved, sems,
):
    give(totals, total_stats(stats_b)[None])
    mean, inverse = norm_columns(stats_b, True, members)
    for r in range(-5, ROWS + 5):
        hat = (row(act_b, r) - mean) * inverse
        fill(zs, r + 5, fine_taps(masked(silu(hat), r, ROWS, scal)))
        if -1 <= r <= ROWS:
            hats.spot[r + 1] = hat.astype(BF16)
    hats.finish()
    kept.send(zs.at[:, pl.ds(5 * HALF, 8 * HALF)], sems.at[0])
    wsecond.wait(1)
    parts = {}
    for r in range(-5, ROWS + 5):
        parts[r] = mm(whole(wsecond), slot(zs, r + 5))
        i = r - 1
        if i > -5:
            convolved[i + 4] = spread(parts, i, i)[i]
            del parts[i - 1]
    act_a.wait(1)
    wdown.wait(1)
    pooled = {}
    half = {}
    for i in range(-4, ROWS + 4):
        value = convolved[i + 4] + row(act_a, i)
        if -3 <= i < ROWS + 3:
            put(fine, i, value)
        half[i] = value[:64] + value[64:]
        if i % 2:
            value = 0.25 * (half.pop(i - 1) + half.pop(i))
            value = masked(value, i // 2, CROWS, scal)
            pooled[i // 2] = value
    weights = whole(wdown)
    parts = {}
    total = jnp.zeros((128, HALF), F32)
    square = jnp.zeros((128, HALF), F32)
    for r in range(-2, CROWS + 2):
        z = coarse_taps(pooled[r])
        if 0 <= r < CROWS:
            put(kept_pool, r, z)
        parts[r] = mm(weights, z)
        i = r - 1
        if i > -2:
            value = spread(parts, i, i)[i]
            put(act_c, i, value)
            del parts[i - 1]
            if 0 <= i < CROWS:
                total = total + value
                square = square + value * value
            if i in (1, 2):
                put(edge, i, value)
    put_stats(stats, total, square)


def stage_d(
    members, scal, stats_c, wcoarse, got_a, got_b, act_c, wup, fine,
    merged, hats, stats, kept_c, kept_up, totals, zs, sems,
):
    give(totals, total_stats(stats_c)[None])
    mean, inverse = norm_columns(stats_c, False, members)
    ring = {}
    for j in range(2):
        ring[j - 3] = pick(scal, row(got_a, j), row(got_b, j))
        ring[CROWS + 1 + j] = pick(scal, row(got_b, j), row(got_a, j))
    for j in range(-1, CROWS + 1):
        ring[j] = row(act_c, j)
    for r in range(-3, CROWS + 3):
        hat = (ring[r] - mean) * inverse
        fill(zs, r + 3, coarse_taps(masked(silu(hat), r, CROWS, scal)))
        if -2 <= r < CROWS + 2:
            hats.spot[r + 2] = hat.astype(BF16)
    hats.finish()
    kept_c.send(zs.at[:, pl.ds(3 * HALF, 4 * HALF)], sems.at[0])
    wcoarse.wait(1)
    wup.wait(1)
    parts = {}
    lifted = {}
    for r in range(-3, CROWS + 3):
        parts[r] = mm(whole(wcoarse), slot(zs, r + 3))
        i = r - 1
        if i > -3:
            value = spread(parts, i, i)[i] + ring[i]
            del parts[i - 1]
            lifted[i] = masked(value, i, CROWS, scal)
    weights = whole(wup)
    parts = {}
    total = jnp.zeros((128, HALF), F32)
    square = jnp.zeros((128, HALF), F32)
    for r in range(-2, CROWS + 2):
        z = coarse_taps(lifted[r])
        if 0 <= r < CROWS:
            put(kept_up, r, z)
        four = jnp.concatenate([z[:128], z[128:256], z[128:256], z[256:]], axis=0)
        parts[2 * r] = parts[2 * r + 1] = mm(weights, four)
        for i in (2 * r - 1, 2 * r):
            if i >= -3:
                value = spread(parts, i, i)[i] + row(fine, i)
                put(merged, i, value)
                parts.pop(i - 1)
                if 0 <= i < ROWS:
                    total = total + value
                    square = square + value * value
    put_stats(stats, total, square)


def stage_out(
    members, scal, stats_d, wout, merged, line_a, line_b, target, noise, wout_t, figures,
    denoised, back, edge_a, edge_b, stats, hats, cotangents, kept, totals, pairs, cells,
    goals, noisies, found, zs, sems,
):
    give(totals, total_stats(stats_d)[None])
    mean, inverse = norm_columns(stats_d, True, members)
    for r in range(-3, ROWS + 3):
        hat = (row(merged, r) - mean) * inverse
        hats.spot[r + 3] = hat.astype(BF16)
        if -3 < r < ROWS + 2:
            fill(zs, r + 2, fine_taps(masked(silu(hat), r, ROWS, scal)))
    hats.finish()
    kept.send(zs.at[:, pl.ds(2 * HALF, 8 * HALF)], sems.at[0])
    for item in (wout, line_a, line_b, target, noise, wout_t, figures):
        item.wait(1)
    parts = {}
    for r in range(-2, ROWS + 2):
        parts[r] = mm(whole(wout), slot(zs, r + 2))
        i = r - 1
        if i > -2:
            value = spread(parts, i, i)[i]
            del parts[i - 1]
            pairs[16 * (i + 1) : 16 * (i + 2), :] = jnp.concatenate(
                [value[:16], value[16:]], axis=1
            )
    value = pairs[...]
    high = value.astype(BF16)
    low = (value - high.astype(F32)).astype(BF16)
    sigma, skip, out_scale, weight, coef = [
        figures.spot[k : k + 1, 0:1] for k in (0, 1, 2, 4, 5)
    ]
    back_order = interleave(True)
    pairs[...] = mm(high, back_order) + mm(low, back_order)
    blank = jnp.zeros((4, 512), F32)
    loss_sum = jnp.zeros((12, 512), F32)
    top = pick(scal, whole(line_a), whole(line_b)) + out_scale * pairs[0:16, :]
    cells[0:16, :] = coef * scal[6] * top
    low = pick(scal, whole(line_b), whole(line_a)) + out_scale * pairs[16 * (ROWS + 1) :, :]
    cells[16 * (ROWS + 1) :, :] = coef * scal[7] * low
    spill(goals, whole(target))
    spill(noisies, whole(target) + sigma * whole(noise))
    for i in range(ROWS):
        goal = strided(goals, i, 12)
        noisy = strided(noisies, i, 12)
        estimate = skip * noisy + out_scale * pairs[16 * (i + 1) : 16 * (i + 1) + 12, :]
        for t in range(4):
            found[t, pl.ds(i, 12, stride=ROWS), :] = estimate[:, 128 * t : 128 * (t + 1)]
        mismatch = estimate - goal
        loss_sum = loss_sum + weight * mismatch * mismatch
        cells[16 * (i + 1) : 16 * (i + 2), :] = jnp.concatenate([coef * mismatch, blank], axis=0)
    give(denoised, jnp.concatenate([found[t] for t in range(4)], axis=1))
    loss_sum = jnp.broadcast_to(
        jnp.sum(jnp.sum(loss_sum, axis=1, keepdims=True), axis=0, keepdims=True), (1, 128)
    )
    pairs[...] = mm(cells[...].astype(BF16), interleave(False))
    g = {}
    for i in range(-1, ROWS + 1):
        value = pairs[16 * (i + 1) : 16 * (i + 2), :]
        g[i] = jnp.concatenate([value[:, :HALF], value[:, HALF:]], axis=0).astype(BF16)
        put(cotangents, i, g[i])
    weights = whole(wout_t)
    total = jnp.zeros((128, HALF), F32)
    cross = jnp.zeros((128, HALF), F32)
    for r in range(ROWS):
        value = fine_untap(mm(weights, stack_rows(g, r)))
        put(back, r, value.astype(BF16))
        hat = row(hats, r).astype(F32)
        e = value * silu_slope(hat)
        total = total + e
        cross = cross + e * hat
    for j in range(3):
        top, low = row(back, j), row(back, ROWS - 3 + j)
        put(edge_a, j, pick(scal, top, low))
        put(edge_b, j, pick(scal, low, top))
    put_stats(stats, total, cross, loss_sum)


def grads_out(scal, cotangents, zs, grad, gs):
    g = {r: row(cotangents, r) for r in range(-1, ROWS + 1)}
    for r in range(ROWS):
        put(gs, r, stack_rows(g, r))
    parts = fine_grad(mm_nt(gs[...], whole(zs)), 16, 64)
    put_grad(grad, 0, grad_blocks(parts, 64), split=False)


def grads_up(scal, grad_merged, grad_coarse, kept_up, kept_c, grad_out, grads, gs, zs, gc):
    g = {r: row(grad_merged, r) for r in range(-1, ROWS + 1)}
    for r in range(ROWS):
        put(gs, r, stack_rows(g, r))
        put(zs, r, row(kept_up, r // 2))
    g = {r: row(grad_coarse, r) for r in range(-1, CROWS + 1)}
    for r in range(CROWS):
        put(gc, r, stack_rows(g, r))
    blocks = mm_nt(gs[...], zs[...])
    parts = []
    for a in range(3):
        even = blocks[128 * a : 128 * a + 64]
        odd = blocks[128 * a + 64 : 128 * a + 128]
        parts.append(
            jnp.concatenate(
                [
                    even[:, :128] + odd[:, 128:256],
                    even[:, 128:256] + odd[:, 128:256],
                    even[:, 128:256] + odd[:, 256:],
                ],
                axis=1,
            )
        )
    start = put_grad(grads, 0, grad_blocks(parts, 128))
    blocks = mm_nt(gc[...], whole(kept_c))
    parts = [blocks[128 * a : 128 * (a + 1)] for a in range(3)]
    start = put_grad(grads, start, grad_blocks(parts, 128))
    for f in range(grads.shape[0]):
        grads.spot[f, start : start + 80, :] = grad_out.spot[f]
    clear_rest(grads, start + 80)


def grads_down(scal, grad_fine, grad_c, kept_pool, kept_b, grads, gs, gc):
    g = {r: row(grad_fine, r) for r in range(-1, ROWS + 1)}
    for r in range(ROWS):
        put(gs, r, stack_rows(g, r))
    g = {r: row(grad_c, r) for r in range(-1, CROWS + 1)}
    for r in range(CROWS):
        put(gc, r, stack_rows(g, r))
    blocks = mm_nt(gc[...], whole(kept_pool))
    parts = [blocks[128 * a : 128 * (a + 1)] for a in range(3)]
    start = put_grad(grads, 0, grad_blocks(parts, 64))
    parts = fine_grad(mm_nt(gs[...], whole(kept_b)), 64, 64)
    clear_rest(grads, put_grad(grads, start, grad_blocks(parts, 64)))


def grads_first(scal, grad_b, line, vec, kept_a, grads, gs):
    g = {r: row(grad_b, r) for r in range(-1, ROWS + 1)}
    for r in range(ROWS):
        put(gs, r, stack_rows(g, r))
    parts = fine_grad(mm_nt(gs[...], whole(kept_a)), 64, 64)
    start = put_grad(grads, 0, grad_blocks(parts, 64))
    line = line.spot[0:1, :]
    line = line + pltpu.roll(line, 64, 1)
    column = jnp.sum(
        place(128, 128, 0).astype(F32) * vec.spot[0:1, :].astype(F32), axis=1, keepdims=True
    )
    outer = (column * line).astype(BF16)
    size = 128 // grads.shape[0]
    for f in range(grads.shape[0]):
        grads.spot[f, start : start + size, :] = outer[f * size : (f + 1) * size]


def stage_up(
    members, members_c, scal, stats_d, stats_ed, got_a, got_b, hats, back, wup_t, stats_c, hats_c,
    wcoarse_t, done,
    grad_merged, back_c, grad_coarse, edge_a, edge_b, stats, loss, total_next,
):
    give(loss, jnp.broadcast_to(total_stats(stats_ed)[2:3, :], (8, 128)))
    mean, inverse = norm_columns(stats_d, True, members)
    shift, slope = back_columns(stats_ed, True, members)
    hats.wait(1)
    g = {}
    for r in range(-3, ROWS + 3):
        hat = row(hats, r).astype(F32)
        if r < 0:
            u = pick(scal, row(got_a, r + 3), row(got_b, r + 3)).astype(F32)
        elif r < ROWS:
            u = row(back, r).astype(F32)
        else:
            u = pick(scal, row(got_b, r - ROWS), row(got_a, r - ROWS)).astype(F32)
        value = inverse * (u * silu_slope(hat) - shift - hat * slope)
        g[r] = masked(value, r, ROWS, scal).astype(BF16)
        if -2 <= r < ROWS + 2:
            put(grad_merged, r, g[r])
    wup_t.wait(1)
    weights = whole(wup_t)
    gk = {}
    for r in range(-1, CROWS + 1):
        rows = jnp.concatenate([g[2 * r + 2], g[2 * r + 1], g[2 * r], g[2 * r - 1]], axis=0)
        value = coarse_untap(mm(weights, rows))
        gk[r] = masked(value, r, CROWS, scal).astype(BF16)
        put(grad_coarse, r, gk[r])
    wcoarse_t.wait(1)
    hats_c.wait(1)
    stats_c.wait(1)
    weights = whole(wcoarse_t)
    mean, inverse = norm_columns(stats_c, False, members_c)
    total = jnp.zeros((128, HALF), F32)
    cross = jnp.zeros((128, HALF), F32)
    for r in range(CROWS):
        value = coarse_untap(mm(weights, stack_rows(gk, r)))
        put(back_c, r, value.astype(BF16))
        hat = row(hats_c, r).astype(F32)
        e = value * silu_slope(hat)
        total = total + e
        cross = cross + e * hat
    top = [row(back_c, 0), row(back_c, 1), gk[1]]
    low = [row(back_c, 2), row(back_c, 3), gk[2]]
    for j in range(3):
        put(edge_a, j, pick(scal, top[j], low[j]))
        put(edge_b, j, pick(scal, low[j], top[j]))
    put_stats(stats, total, cross)
    give(total_next, whole(stats_c))


def stage_down(
    members, members_c, scal, stats_c, stats_ec, got_a, got_b, hats_c, back_c, grad_coarse,
    wdown_t, grad_merged, stats_b, wsecond_t, hats, done,
    grad_fine, back_b, stats, grad_c, total_next,
):
    mean, inverse = norm_columns(stats_c, False, members_c)
    shift, slope = back_columns(stats_ec, False, members_c)
    hats_c.wait(1)
    g = {}
    for r in range(-2, CROWS + 2):
        hat = row(hats_c, r).astype(F32)
        if r < 0:
            u = pick(scal, row(got_a, r + 2), row(got_b, r + 2)).astype(F32)
        elif r < CROWS:
            u = row(back_c, r).astype(F32)
        else:
            u = pick(scal, row(got_b, r - CROWS), row(got_a, r - CROWS)).astype(F32)
        if r == -2:
            through = pick(scal, row(got_a, 2), row(got_b, 2)).astype(F32)
        elif r == CROWS + 1:
            through = pick(scal, row(got_b, 2), row(got_a, 2)).astype(F32)
        else:
            through = row(grad_coarse, r).astype(F32)
        value = through + inverse * (u * silu_slope(hat) - shift - hat * slope)
        g[r] = masked(value, r, CROWS, scal).astype(BF16)
        if -1 <= r <= CROWS:
            put(grad_c, r, g[r])
    wdown_t.wait(1)
    weights = whole(wdown_t)
    fine = {}
    for r in range(-1, CROWS + 1):
        value = 0.25 * coarse_untap(mm(weights, stack_rows(g, r)))
        both = jnp.concatenate([value, value], axis=0)
        for i in (2 * r, 2 * r + 1):
            value = masked(row(grad_merged, i).astype(F32) + both, i, ROWS, scal)
            fine[i] = value.astype(BF16)
            if -1 <= i <= ROWS:
                put(grad_fine, i, fine[i])
    wsecond_t.wait(1)
    hats.wait(1)
    stats_b.wait(1)
    weights = whole(wsecond_t)
    mean, inverse = norm_columns(stats_b, True, members)
    total = jnp.zeros((128, HALF), F32)
    cross = jnp.zeros((128, HALF), F32)
    for r in range(-1, ROWS + 1):
        value = fine_untap(mm(weights, stack_rows(fine, r)))
        put(back_b, r, value.astype(BF16))
        if 0 <= r < ROWS:
            hat = row(hats, r).astype(F32)
            e = value * silu_slope(hat)
            total = total + e
            cross = cross + e * hat
    put_stats(stats, total, cross)
    give(total_next, whole(stats_b))


def stage_first(
    members, scal, stats_b, stats_eb, hats_b, back_b, wfirst_t, stats_a, hats, done,
    back_a, stats, grad_b, line, total_next,
):
    mean, inverse = norm_columns(stats_b, True, members)
    shift, slope = back_columns(stats_eb, True, members)
    hats_b.wait(1)
    g = {}
    sums = jnp.zeros((128, HALF), F32)
    for r in range(-1, ROWS + 1):
        hat = row(hats_b, r).astype(F32)
        u = row(back_b, r).astype(F32)
        value = inverse * (u * silu_slope(hat) - shift - hat * slope)
        if 0 <= r < ROWS:
            sums = sums + value
        g[r] = masked(value, r, ROWS, scal).astype(BF16)
        put(grad_b, r, g[r])
    wfirst_t.wait(1)
    hats.wait(1)
    stats_a.wait(1)
    weights = whole(wfirst_t)
    total = jnp.zeros((128, HALF), F32)
    cross = jnp.zeros((128, HALF), F32)
    for r in range(ROWS):
        value = fine_untap(mm(weights, stack_rows(g, r)))
        put(back_a, r, value.astype(BF16))
        hat = row(hats, r).astype(F32)
        e = value * silu_slope(hat)
        total = total + e
        cross = cross + e * hat
    put_stats(stats, total, cross)
    sums = to_row(jnp.sum(sums, axis=1, keepdims=True))
    give(line, jnp.broadcast_to(sums, (8, 128)))
    give(total_next, whole(stats_a))


def stage_last(
    members, members_all, scal, stats_a, stats_ea, hats, back_a, grad_fine, kept_in, early, middle, first,
    loss, loss_other, keep, send, loss_sum, gs, held, sems,
):
    grads = Source(held, [], 0)
    copies, start = [], 0
    for index, ref in enumerate((early, middle)):
        rows = pl.ds(start, ref.shape[1])
        copies.append(
            pltpu.make_async_copy(ref.spot, grads.spot.at[:, rows, :], sems.at[index])
        )
        copies[index].start()
        start += ref.shape[1]
    give(loss_sum, (loss.spot[0:1, 0:1] + loss_other.spot[0:1, 0:1]) * (1.0 / members_all))
    mean, inverse = norm_columns(stats_a, True, members)
    shift, slope = back_columns(stats_ea, True, members)
    for r in range(ROWS):
        hat = row(hats, r).astype(F32)
        u = row(back_a, r).astype(F32)
        value = row(grad_fine, r).astype(F32) + inverse * (
            u * silu_slope(hat) - shift - hat * slope
        )
        put(gs, r, value.astype(BF16))
    kept_in.wait(1)
    first.wait(1)
    parts = []
    for a in range(3):
        blocks = mm_nt(gs[...], kept_in.spot[:, a * HALF : (a + ROWS) * HALF])
        parts.append(
            jnp.concatenate(
                [blocks[:64, :96] + blocks[64:, 32:128], jnp.zeros((64, 32), F32)], axis=1
            )
        )
    size = first.shape[1]
    for f in range(grads.shape[0]):
        grads.spot[f, start : start + size, :] = first.spot[f]
    clear_rest(grads, put_grad(grads, start + size, parts))
    for copy in copies:
        copy.wait()
    half = keep.shape[1]
    odd = scal[8] > 0.5
    for f in range(keep.shape[0]):
        low, high = held[f, :half, :], held[f, half:, :]
        keep.spot[f] = jnp.where(odd, high, low)
        send.spot[f] = jnp.where(odd, low, high)


def join(scal, kept, got, out):
    give(out, (whole(kept).astype(F32) + whole(got).astype(F32)).astype(BF16))


def add_up(scal, got, out):
    total = got.spot[0].astype(F32)
    for index in range(1, got.shape[0]):
        total = total + got.spot[index].astype(F32)
    total = total.astype(BF16)
    for index in range(out.shape[0]):
        out.spot[index] = total


def unpack(starts, scal, mine, other, *refs):
    first, down, second, coarse, up, out, embed, inputs, flat = refs
    half = mine.shape[0]
    odd = scal[8] > 0.5
    flat[:half, :] = jnp.where(odd, whole(other), whole(mine)).astype(F32)
    flat[half:, :] = jnp.where(odd, whole(mine), whole(other)).astype(F32)

    def take(ref, start, out, size, ins, trim=False):
        for t in range(9):
            a, b = t // 3, t % 3
            if ins == 128:
                at, lanes = t, 0
            elif ins == 64:
                at, lanes = (a, b) if b < 2 else (3 + a // 2, a % 2)
            else:
                at, lanes = a, b
            value = ref[start + at * size : start + (at + 1) * size, :]
            if ins == 24:
                out.spot[t] = mm_nt(place(24, 128, 32 * lanes), value.astype(BF16))
                continue
            value = value[:, lanes * ins : (lanes + 1) * ins]
            if trim:
                value = value[:12]
                if out.shape[2] == 32:
                    value = jnp.where(scal[9] > 0.5, value[:, :32], value[:, 32:])
            out.spot[t] = value
        return start + (9 if ins == 128 else 5 if ins == 64 else 3) * size

    start = take(flat, 0, up, up.shape[1], 128)
    start = take(flat, start, coarse, coarse.shape[1], 128)
    take(flat, start, out, 16, 64, trim=True)
    start = take(flat, starts[0], down, down.shape[1], 64)
    take(flat, start, second, second.shape[1], 64)
    start = take(flat, starts[1], first, first.shape[1], 64)
    size = embed.shape[0]
    give(embed, flat[start : start + size, :64])
    take(flat, start + size, inputs, inputs.shape[2], 24)


class Field:
    def __init__(self, array, first):
        self.array, self.first = array, first


class Saved:
    def __init__(self, item, low=None, high=None, when=0):
        self.item, self.low, self.high, self.when = item, low, high, when


def shape(*dims, dtype=F32):
    return jax.ShapeDtypeStruct(dims, dtype)


def rows_of(first, number, dtype=F32):
    return Field(shape(number, 128, HALF, dtype=dtype), first)


def flat_rows(first, number, channels):
    return Field(shape(channels, number * HALF, dtype=BF16), first)


def opened(item):
    saved = item if isinstance(item, Saved) else None
    item = saved.item if saved else item
    if isinstance(item, Field):
        return saved, item.array, item.first
    return saved, item, 0


def position():
    me, bands = lax.axis_index("rows"), lax.axis_size("rows")
    return {
        6: jnp.where(me > 0, 1.0, 0.0),
        7: jnp.where(me < bands - 1, 1.0, 0.0),
        8: jnp.where(me % 2 == 1, 1.0, 0.0),
        9: jnp.where(lax.axis_index("fsdp") == 0, 1.0, 0.0),
    }


def run(name, kernel, outs, scal, *operands, scratch=()):
    vmem, hbm = pl.BlockSpec(memory_space=pltpu.VMEM), pl.BlockSpec(memory_space=pltpu.HBM)
    in_specs, arrays, plans, spots = [], [], [], []
    if scal is not None:
        in_specs, arrays = [pl.BlockSpec(memory_space=pltpu.SMEM)], [scal]
    for item in operands:
        saved, item, first = opened(item)
        if saved is None:
            in_specs.append(vmem)
            arrays.append(item)
            plans.append((first, None, None))
            continue
        part = None
        dims = item.shape
        if saved.low is not None:
            part = pl.ds(saved.low - first, saved.high - saved.low)
            dims = (saved.high - saved.low,) + dims[1:]
            first = saved.low
        in_specs.append(hbm)
        arrays.append(pltpu.with_memory_space_constraint(item, pltpu.HBM))
        if saved.when is None:
            plans.append((first, None, None))
            continue
        plans.append((first, (saved.when, part), len(spots)))
        spots.append(pltpu.VMEM(dims, item.dtype))
    ins = len(operands)
    out_specs, out_shapes = [], []
    for item in outs:
        saved, item, first = opened(item)
        if saved is None:
            out_specs.append(vmem)
            out_shapes.append(item)
            plans.append((first, None, None))
            continue
        out_specs.append(hbm)
        out_shapes.append(pltpu.HBM(item.shape, item.dtype))
        last = None
        if isinstance(saved.item, Field):
            count = item.shape[0] if len(item.shape) == 3 else item.shape[1] // HALF
            last = first + count - 1
        if saved.when is None:
            plans.append((first, None, None))
            continue
        plans.append((first, (last, None), len(spots)))
        spots.append(pltpu.VMEM(item.shape, item.dtype))

    def body(*refs):
        numbers = position()
        if scal is not None:
            numbers.update({index: refs[0][index] for index in range(6)})
            refs = refs[1:]
        given, refs = refs[: len(plans)], refs[len(plans) :]
        held, refs = refs[: len(spots)], refs[len(spots) :]
        sems, extra = refs[0], refs[1:]
        wrapped = []
        for index, (ref, (first, plan, place_at)) in enumerate(zip(given, plans)):
            copies = []
            if plan is not None:
                where = held[place_at]
                when, part = plan
                if index < ins:
                    source = ref if part is None else ref.at[part]
                    copies.append((when, pltpu.make_async_copy(source, where, sems.at[place_at])))
                else:
                    copies.append((when, pltpu.make_async_copy(where, ref, sems.at[place_at])))
                ref = where
            wrapped.append((Source if index < ins else Sink)(ref, copies, first))
        for item in wrapped[:ins]:
            item.wait(0)
        kernel(numbers, *wrapped, *extra)
        for item in wrapped[ins:]:
            item.finish()
        for item in wrapped[ins:]:
            for copy in item.started:
                copy.wait()

    made = pl.pallas_call(
        body,
        out_shape=tuple(out_shapes),
        in_specs=in_specs,
        out_specs=tuple(out_specs),
        scratch_shapes=spots
        + [pltpu.SemaphoreType.DMA((max(len(spots), 1),))]
        + [pltpu.VMEM(*item) if isinstance(item, tuple) else item for item in scratch],
        compiler_params=pltpu.CompilerParams(vmem_limit_bytes=LIMIT),
        name=name,
    )(*arrays)
    results = []
    for array, item in zip(made, outs):
        item = item.item if isinstance(item, Saved) else item
        results.append(Field(array, item.first) if isinstance(item, Field) else array)
    return results


def sum_parts(stats):
    return lax.all_to_all(stats, "rows", 0, 0)


def swap(value_a, value_b):
    count = lax.axis_size("rows")
    pairs = [(i, i ^ 1) for i in range(count)]
    across = []
    for i in range(1, count - 1, 2):
        across += [(i, i + 1), (i + 1, i)]
    return lax.ppermute(value_a, "rows", pairs), lax.ppermute(value_b, "rows", across)


def gather_packed(packed):
    if lax.axis_size("fsdp") == 2:
        return [packed, lax.ppermute(packed, "fsdp", [(0, 1), (1, 0)])]
    whole = lax.all_gather(packed, "fsdp").astype(F32)
    return [whole[i] for i in range(whole.shape[0])]


def group_shape(rows, count):
    return shape(count, -(-rows // 16) * 16, 128, dtype=BF16)


def per_device(
    residual_target,
    conditioning,
    noise_sample,
    noise_level,
    input_kernel,
    first_kernel,
    second_kernel,
    down_kernel,
    coarse_kernel,
    upward_kernel,
    output_kernel,
    embed_matrix,
):
    bands, count = lax.axis_size("rows"), lax.axis_size("fsdp")
    members = 2 * ROWS * 2 * HALF * bands
    members_c = 4 * CROWS * HALF * bands
    members_all = count * residual_target.size * bands
    sigma_level, skip_scale, out_scale, in_scale, weight = preconditions(noise_level[0])
    coef = 2.0 * weight * out_scale / members_all
    scal = jnp.stack([sigma_level, skip_scale, out_scale, in_scale, weight, coef])
    embedded = embedding(sigma_level, embed_matrix.shape[0] * count)
    target = residual_target.reshape(12 * ROWS, 512)
    condition = conditioning.reshape(12 * ROWS, 512)
    noise = noise_sample.reshape(12 * ROWS, 512)

    def widths_of(shards, rows):
        widths = tuple(
            (9 if item.ndim == 3 else 1, size, item.ndim == 3 and item.shape[1] == 24)
            for item, size in zip(shards, rows)
        )
        total = 0
        for item, (taps, size, swapped) in zip(shards, widths):
            paired = taps == 9 and item.shape[2] == 64
            total += (3 if swapped else 5 if paired else taps) * size
        return widths, total

    fine_o, coarse_o = input_kernel.shape[1], down_kernel.shape[1]
    inputs_t = jnp.swapaxes(input_kernel, 1, 2)
    shards = [inputs_t, first_kernel, embed_matrix]
    widths, packed_rows = widths_of(shards, [fine_o, fine_o, embed_matrix.shape[0]])
    far = shape(32, FAR * 512, dtype=BF16)
    early, own, edge_a, edge_b, figures = run(
        "enter",
        functools.partial(enter, widths),
        [
            shape(packed_rows, 128, dtype=BF16), shape(32, ROWS * 512, dtype=BF16), far, far,
            Saved(shape(8, 128)),
        ],
        scal,
        Saved(target, when=2),
        Saved(condition, when=2),
        Saved(noise, when=2),
        *[Saved(item, when=1) for item in shards],
        scratch=[
            ((packed_rows, 128), F32), ((4, 192, 128), F32), ((2, 16, FAR * 512), BF16)
        ],
    )
    got_a, got_b = swap(edge_a, edge_b)
    early = gather_packed(early)
    shards = [second_kernel, down_kernel, coarse_kernel, upward_kernel, output_kernel]
    widths, packed_rows = widths_of(shards, [fine_o, coarse_o, coarse_o, fine_o, 16])
    (rest,) = run(
        "pack_rest",
        functools.partial(pack, widths),
        [shape(packed_rows, 128, dtype=BF16)],
        None,
        *[Saved(item) for item in shards],
        own,
        scratch=[((packed_rows, 128), F32)],
    )
    vector = jnp.broadcast_to(embedded[None, :], (16, embedded.shape[0]))
    stat = shape(bands, 2, 128)
    total = Saved(shape(1, 2, 128))
    act_a, stats_a, kept_in, line_a, line_b = run(
        "stage_a",
        stage_a,
        [
            rows_of(-6, 20), stat, Saved(flat_rows(-1, 10, 128)),
            Saved(shape(16, 512)), Saved(shape(16, 512)),
        ],
        None,
        got_a, got_b, own, rest, *early,
        scratch=[((32, FAR * 512), BF16), ((32, FAR * 512), BF16)],
    )
    stats_a = sum_parts(stats_a)
    rest, stats_a = lax.optimization_barrier((rest, stats_a))
    (
        wsecond, wsecond_t, wdown, wdown_t, wcoarse, wcoarse_t, wup, wup_t, wout, wout_t
    ) = run(
        "prepare_rest",
        prepare_rest,
        [
            Saved(shape(384, 256, dtype=BF16)), Saved(shape(256, 384, dtype=BF16)),
            Saved(shape(384, 192, dtype=BF16)), Saved(shape(192, 384, dtype=BF16)),
            Saved(shape(384, 384, dtype=BF16)), Saved(shape(384, 384, dtype=BF16)),
            Saved(shape(384, 512, dtype=BF16)), Saved(shape(384, 512, dtype=BF16)),
            Saved(shape(96, 256, dtype=BF16)), Saved(shape(256, 96, dtype=BF16)),
        ],
        None,
        *gather_packed(rest),
    )

    act_b, stats_b, kept_a, hats_a, act_a, total_a, wfirst_t = run(
        "stage_b",
        functools.partial(stage_b, members, embedded.shape[0]),
        [
            rows_of(-5, 18), stat, Saved(flat_rows(0, 8, 256), when=None),
            Saved(rows_of(0, 8, BF16)),
            Saved(rows_of(-4, 16), when=None), total, Saved(shape(256, 384, dtype=BF16)),
        ],
        None,
        stats_a, act_a, vector, *early,
        scratch=[((384, 256), BF16), ((256, 20 * HALF), BF16), pltpu.SemaphoreType.DMA((2,))],
    )
    stats_b = sum_parts(stats_b)
    fine, act_c, edge, stats_c, kept_b, kept_pool, hats_b, total_b = run(
        "stage_c",
        functools.partial(stage_c, members),
        [
            rows_of(-3, 14), rows_of(-1, 6), Field(shape(128, 2 * HALF), 1), stat,
            Saved(flat_rows(0, 8, 256), when=None), Saved(flat_rows(0, 4, 192)),
            Saved(rows_of(-1, 10, BF16)), total,
        ],
        None,
        stats_b, Saved(wsecond, when=1), act_b, Saved(act_a, when=1), Saved(wdown, when=1),
        scratch=[
            ((256, 18 * HALF), BF16), ((16, 128, HALF), F32), pltpu.SemaphoreType.DMA((1,)),
        ],
    )
    got_a, got_b = swap(edge.array, edge.array)
    stats_c = sum_parts(stats_c)
    merged, hats_c, stats_d, kept_c, kept_up, total_c = run(
        "stage_d",
        functools.partial(stage_d, members_c),
        [
            rows_of(-3, 14), Saved(rows_of(-2, 8, BF16)), stat,
            Saved(flat_rows(0, 4, 384), when=None), Saved(flat_rows(0, 4, 384)), total,
        ],
        None,
        stats_c, Saved(wcoarse, when=1), got_a, got_b, act_c, Saved(wup, when=1), fine,
        scratch=[((384, 10 * HALF), BF16), pltpu.SemaphoreType.DMA((1,))],
    )
    stats_d = sum_parts(stats_d)
    edge = Field(shape(128, 3 * HALF, dtype=BF16), 0)
    denoised, back_d, edge_a, edge_b, stats_ed, hats_d, cotangents, kept_d, total_d = run(
        "stage_out",
        functools.partial(stage_out, members),
        [
            Saved(shape(96, 512)), rows_of(0, 8, BF16), edge, edge, shape(bands, 4, 128),
            Saved(rows_of(-3, 14, BF16)),
            Field(shape(10, 32, HALF, dtype=BF16), -1),
            Saved(flat_rows(0, 8, 256), when=None), shape(1, 2, 128),
        ],
        None,
        stats_d, Saved(wout, when=1), merged, Saved(line_a, when=1), Saved(line_b, when=1),
        Saved(target, when=1), Saved(noise, when=1), Saved(wout_t, when=1),
        Saved(figures, when=1),
        scratch=[
            ((160, 512), F32), ((160, 512), F32),
            ((4, 96, 128), F32), ((4, 96, 128), F32), ((4, 96, 128), F32),
            ((256, 12 * HALF), BF16), pltpu.SemaphoreType.DMA((1,)),
        ],
    )
    got_a, got_b = swap(edge_a.array, edge_b.array)
    (grad_out,) = run(
        "grads_out",
        grads_out,
        [Saved(shape(count, 80, 128, dtype=BF16))],
        None,
        cotangents, Saved(kept_d),
        scratch=[((96, 8 * HALF), BF16)],
    )
    stats_ed = sum_parts(stats_ed)
    grad_merged, back_c, grad_coarse, edge_a, edge_b, stats_ec, loss, total_c = run(
        "stage_up",
        functools.partial(stage_up, members, members_c),
        [
            rows_of(-2, 12, BF16), rows_of(0, 4, BF16), rows_of(-1, 6, BF16), edge, edge, stat,
            shape(8, 128), shape(1, 2, 128),
        ],
        None,
        total_d, stats_ed, got_a, got_b, Saved(hats_d, when=1), back_d, Saved(wup_t, when=1),
        Saved(total_c, when=1),
        Saved(hats_c, when=1), Saved(wcoarse_t, when=1), Saved(grad_out, when=None),
    )
    got_a, got_b = swap(edge_a.array, edge_b.array)
    (early,) = run(
        "grads_up",
        grads_up,
        [Saved(group_shape(9 * (fine_o + coarse_o) + 80, count))],
        None,
        grad_merged, grad_coarse, Saved(kept_up), Saved(kept_c), Saved(grad_out),
        scratch=[
            ((384, 8 * HALF), BF16), ((384, 8 * HALF), BF16), ((384, 4 * HALF), BF16)
        ],
    )
    stats_ec = sum_parts(stats_ec)
    if count == 2:
        loss_other = lax.ppermute(loss, "fsdp", [(0, 1), (1, 0)])
    else:
        loss_other = lax.psum(loss, "fsdp") - loss
    grad_fine, back_b, stats_eb, grad_c, total_b = run(
        "stage_down",
        functools.partial(stage_down, members, members_c),
        [
            rows_of(-1, 10, BF16), rows_of(-1, 10, BF16), stat, Saved(rows_of(-1, 6, BF16)),
            shape(1, 2, 128),
        ],
        None,
        total_c, stats_ec, got_a, got_b, Saved(hats_c, when=1), back_c, grad_coarse,
        Saved(wdown_t, when=1), grad_merged, Saved(total_b, when=1), Saved(wsecond_t, when=1),
        Saved(hats_b, 0, 8, when=1), Saved(early, when=None),
    )
    (middle,) = run(
        "grads_down",
        grads_down,
        [Saved(group_shape(5 * (fine_o + coarse_o), count))],
        None,
        grad_fine, Saved(grad_c), Saved(kept_pool), Saved(kept_b),
        scratch=[((384, 8 * HALF), BF16), ((384, 4 * HALF), BF16)],
    )
    stats_eb = sum_parts(stats_eb)
    back_a, stats_ea, grad_b, line, total_a = run(
        "stage_first",
        functools.partial(stage_first, members),
        [
            rows_of(0, 8, BF16), stat, rows_of(-1, 10, BF16), shape(8, 128),
            shape(1, 2, 128),
        ],
        None,
        total_b, stats_eb, Saved(hats_b, when=1), back_b, Saved(wfirst_t, when=1), Saved(total_a, when=1),
        Saved(hats_a, when=1), Saved(middle, when=None),
    )
    (grad_first,) = run(
        "grads_first",
        grads_first,
        [Saved(shape(count, 5 * fine_o + embed_matrix.shape[0], 128, dtype=BF16))],
        None,
        grad_b, line, vector, Saved(kept_a),
        scratch=[((384, 8 * HALF), BF16)],
    )
    stats_ea = sum_parts(stats_ea)
    late = group_shape(8 * fine_o + embed_matrix.shape[0], count)
    starts = [early.shape[1], early.shape[1] + middle.shape[1]]
    total = starts[1] + late.shape[1]
    chunk = -(-total // (16 * bands)) * 16
    chips = bands // 2
    half = shape(count, chunk * chips, 128, dtype=BF16)
    keep, send, loss = run(
        "stage_last",
        functools.partial(stage_last, members, members_all),
        [half, half, shape(1, 1)],
        None,
        total_a, stats_ea, Saved(hats_a), back_a, grad_fine, Saved(kept_in, when=1),
        Saved(early, when=None), Saved(middle, when=None), Saved(grad_first, when=1), loss, loss_other,
        scratch=[
            ((128, 8 * HALF), BF16), ((count, chunk * bands, 128), BF16),
            pltpu.SemaphoreType.DMA((2,)),
        ],
    )
    loss_value = loss.reshape(())
    pairs = [(i, i ^ 1) for i in range(bands)]
    got = lax.ppermute(send, "rows", pairs)
    (both,) = run("join", join, [half], None, keep, got)
    both = both.reshape(count * chips, chunk, 128)
    cores = [[f * bands + r for f in range(count) for r in range(c, bands, 2)] for c in range(2)]
    got = lax.all_to_all(both, ("fsdp", "rows"), 0, 0, axis_index_groups=cores)
    (mine,) = run("add_up", add_up, [shape(chips, chunk, 128, dtype=BF16)], None, got)
    cores = [[r for r in range(c, bands, 2)] for c in range(2)]
    mine = lax.all_to_all(mine, "rows", 0, 0, axis_index_groups=cores)
    mine = mine.reshape(chips * chunk, 128)
    other = lax.ppermute(mine, "rows", pairs)
    first_g, down_g, second_g, coarse_g, up_g, out_g, embed_g, in_g = run(
        "unpack",
        functools.partial(unpack, starts),
        [
            shape(*first_kernel.shape),
            shape(*down_kernel.shape),
            shape(*second_kernel.shape),
            shape(*coarse_kernel.shape),
            shape(*upward_kernel.shape),
            shape(9, 12, output_kernel.shape[2] if count == 2 else 64),
            shape(*embed_matrix.shape),
            shape(*inputs_t.shape),
        ],
        None,
        mine, other,
        scratch=[((chunk * bands, 128), F32)],
    )
    width = output_kernel.shape[2]
    if count != 2:
        out_g = lax.dynamic_slice_in_dim(out_g, lax.axis_index("fsdp") * width, width, axis=2)
    return (
        denoised.reshape(residual_target.shape),
        loss_value,
        jnp.swapaxes(in_g, 1, 2),
        first_g,
        second_g,
        down_g,
        coarse_g,
        up_g,
        out_g,
        embed_g,
    )


def solution(mesh):
    in_specs = (
        P("fsdp", None, "rows", None),
        P("fsdp", None, "rows", None),
        P("fsdp", None, "rows", None),
        P("fsdp"),
        P(None, "fsdp", None),
        P(None, "fsdp", None),
        P(None, "fsdp", None),
        P(None, "fsdp", None),
        P(None, "fsdp", None),
        P(None, "fsdp", None),
        P(None, None, "fsdp"),
        P("fsdp", None),
    )
    out_specs = (
        P("fsdp", None, "rows", None),
        P(),
        P(None, "fsdp", None),
        P(None, "fsdp", None),
        P(None, "fsdp", None),
        P(None, "fsdp", None),
        P(None, "fsdp", None),
        P(None, "fsdp", None),
        P(None, None, "fsdp"),
        P("fsdp", None),
    )
    return jax.shard_map(
        per_device, mesh=mesh, in_specs=in_specs, out_specs=out_specs, check_vma=False
    )
```

```python
import functools

import jax
import jax.numpy as jnp
from jax import lax
from jax.experimental import pallas as pl
from jax.experimental.pallas import tpu as pltpu
from jax.sharding import PartitionSpec as P

GROUPS = 32
STEPS = 64

sigma_low = 0.002
sigma_high = 80.0
sigma_data = 0.5
rho_power = 7.0
eps_norm = 1e-05

F32 = jnp.float32
BF16 = jnp.bfloat16

HALF = 256
ROWS = 8
CROWS = 4
FAR = 7
LIMIT = 24 * 1024 * 1024


def preconditions(level_index):
    ramp_value = level_index.astype(jnp.float32) / (STEPS - 1)
    top_root = sigma_high ** (1.0 / rho_power)
    bottom = sigma_low ** (1.0 / rho_power)
    sigma_level = (top_root + ramp_value * (bottom - top_root)) ** rho_power
    sigma_total = sigma_level * sigma_level + sigma_data * sigma_data
    skip_scale = sigma_data * sigma_data / sigma_total
    out_scale = sigma_level * sigma_data * lax.rsqrt(sigma_total)
    in_scale = lax.rsqrt(sigma_total)
    weight = sigma_total / (sigma_level * sigma_data) ** 2
    return (sigma_level, skip_scale, out_scale, in_scale, weight)


def embedding(sigma_level, features):
    half_count = features // 2
    ramp_steps = jnp.arange(half_count, dtype=jnp.float32) / half_count
    frequency = 64.0 * 0.01**ramp_steps
    phase_angle = 0.25 * jnp.log(sigma_level) * frequency
    return jnp.concatenate([jnp.cos(phase_angle), jnp.sin(phase_angle)]).astype(jnp.bfloat16)


class Source:
    def __init__(self, spot, copies, first):
        self.spot, self.copies, self.first = spot, copies, first
        self.shape = spot.shape
        for _, copy in copies:
            copy.start()

    def wait(self, stage):
        for when, copy in self.copies:
            if when == stage:
                copy.wait()


class Sink:
    def __init__(self, spot, copies, first):
        self.spot, self.copies, self.first = spot, copies, first
        self.shape = spot.shape
        self.started = []

    def done(self, index):
        for last, copy in self.copies:
            if last == index:
                copy.start()
                self.started.append(copy)

    def send(self, source, sem):
        copy = pltpu.make_async_copy(source, self.spot, sem)
        copy.start()
        self.started.append(copy)

    def finish(self):
        for _, copy in self.copies:
            if not any(copy is other for other in self.started):
                copy.start()
                self.started.append(copy)


def spot(ref, index):
    if len(ref.shape) == 3:
        return (index - getattr(ref, "first", 0),)
    start = index - getattr(ref, "first", 0)
    return (slice(None), slice(start * HALF, (start + 1) * HALF))


def row(ref, index):
    return getattr(ref, "spot", ref)[spot(ref, index)]


def put(ref, index, value):
    getattr(ref, "spot", ref)[spot(ref, index)] = value
    if isinstance(ref, Sink):
        ref.done(index)


def whole(ref):
    return ref.spot[...]


def give(ref, value):
    ref.spot[...] = value
    ref.finish()


def lane(shape):
    return lax.broadcasted_iota(jnp.int32, shape, 1)


def from_left(value):
    moved = pltpu.roll(value, 1, 1)
    return jnp.where(lane(value.shape) == 0, jnp.zeros_like(moved), moved)


def from_right(value):
    moved = pltpu.roll(value, value.shape[1] - 1, 1)
    return jnp.where(lane(value.shape) == value.shape[1] - 1, jnp.zeros_like(moved), moved)


def mm(left, right):
    return jnp.dot(left, right, preferred_element_type=F32)


def mm_nt(left, right):
    return lax.dot_general(left, right, (((1,), (1,)), ((), ())), preferred_element_type=F32)


def fine_taps(value):
    half = value.shape[0] // 2
    value = value.astype(BF16)
    even, odd = value[:half], value[half:]
    return jnp.concatenate([from_left(odd), value, from_right(even)], axis=0)


def coarse_taps(value):
    value = value.astype(BF16)
    return jnp.concatenate([from_left(value), value, from_right(value)], axis=0)


def fine_untap(taps):
    size = taps.shape[0] // 4
    even = taps[size : 2 * size] + from_left(taps[3 * size :])
    odd = taps[2 * size : 3 * size] + from_right(taps[:size])
    return jnp.concatenate([even, odd], axis=0)


def coarse_untap(taps):
    size = taps.shape[0] // 3
    return taps[size : 2 * size] + from_right(taps[:size]) + from_left(taps[2 * size :])


def spread(parts, first, last):
    out = {}
    for i in range(first, last + 1):
        size = parts[i - 1].shape[0] // 3
        out[i] = parts[i - 1][:size] + parts[i][size : 2 * size] + parts[i + 1][2 * size :]
    return out


def stack_rows(g, r):
    return jnp.concatenate([g[r + 1], g[r], g[r - 1]], axis=0)


def same_group(size, fine):
    left = lax.broadcasted_iota(jnp.int32, (size, size), 0)
    right = lax.broadcasted_iota(jnp.int32, (size, size), 1)
    if fine:
        half = size // 2
        left, right = left % half, right % half
        per = half // GROUPS
    else:
        per = size // GROUPS
    return left // per == right // per


def total_stats(stats):
    total = stats.spot[0]
    for index in range(1, stats.shape[0]):
        total = total + stats.spot[index]
    return total


def group_sums(stats, fine):
    total = total_stats(stats)
    member = same_group(128, fine)
    first = jnp.sum(jnp.where(member, total[0:1, :], 0.0), axis=1, keepdims=True)
    second = jnp.sum(jnp.where(member, total[1:2, :], 0.0), axis=1, keepdims=True)
    return first, second


def norm_columns(stats_ref, fine, members):
    first, second = group_sums(stats_ref, fine)
    mean = first / members
    inverse = lax.rsqrt(second / members - mean * mean + eps_norm)
    return mean, inverse


def back_columns(stats_ref, fine, members):
    first, second = group_sums(stats_ref, fine)
    return first / members, second / members


def to_row(column):
    size = column.shape[0]
    diagonal = lax.broadcasted_iota(jnp.int32, (size, size), 0) == lax.broadcasted_iota(
        jnp.int32, (size, size), 1
    )
    return jnp.sum(jnp.where(diagonal, column, 0.0), axis=0, keepdims=True)


def put_stats(ref, first, second, third=None):
    first = to_row(jnp.sum(first, axis=1, keepdims=True))
    second = to_row(jnp.sum(second, axis=1, keepdims=True))
    if third is None:
        third = jnp.zeros((1, 128), F32)
    block = jnp.concatenate([first, second, third, jnp.zeros((1, 128), F32)], axis=0)
    block = block[: ref.shape[1]]
    for index in range(ref.shape[0]):
        ref.spot[index] = block
    ref.finish()


def silu(h):
    t = 0.5 * h
    return t + t * jnp.tanh(t)


def silu_slope(h):
    s = 0.5 + 0.5 * jnp.tanh(0.5 * h)
    return s * (1.0 + h * (1.0 - s))


def masked(value, index, rows, scal):
    if index < 0:
        return value * scal[6]
    if index >= rows:
        return value * scal[7]
    return value


def pick(scal, when_odd, when_even):
    return jnp.where(scal[8] > 0.5, when_odd, when_even)


def spill(ref, value):
    for t in range(4):
        ref[t, : value.shape[0], :] = value[:, 128 * t : 128 * (t + 1)]


def strided(ref, index, size):
    return jnp.concatenate(
        [ref[t, pl.ds(index, size, stride=ROWS), :] for t in range(4)], axis=1
    )


def interleave(transposed):
    left = lax.broadcasted_iota(jnp.int32, (512, 512), 0)
    right = lax.broadcasted_iota(jnp.int32, (512, 512), 1)
    if transposed:
        left, right = right, left
    place = (left & 1) * HALF + (left >> 1)
    return jnp.where(place == right, 1.0, 0.0).astype(BF16)


def fine_grad(blocks, outs, ins):
    parts = []
    for a in range(3):
        even = blocks[(2 * a) * outs : (2 * a + 1) * outs]
        odd = blocks[(2 * a + 1) * outs : (2 * a + 2) * outs]
        parts.append(even[:, : 3 * ins] + odd[:, ins : 4 * ins])
    return parts


def grad_blocks(parts, ins):
    if ins == 128:
        return [part[:, 128 * b : 128 * (b + 1)] for part in parts for b in range(3)]
    if ins == 64:
        blank = jnp.zeros(parts[0][:, :64].shape, F32)
        blocks = [part[:, :128] for part in parts]
        blocks.append(jnp.concatenate([parts[0][:, 128:192], parts[1][:, 128:192]], axis=1))
        blocks.append(jnp.concatenate([parts[2][:, 128:192], blank], axis=1))
        return blocks
    return parts


def put_grad(ref, start, blocks, split=True):
    count = ref.shape[0]
    size = blocks[0].shape[0] // count if split else blocks[0].shape[0]
    for block in blocks:
        for f in range(count):
            piece = block[f * size : (f + 1) * size] if split else block
            ref.spot[f, start : start + size, :] = piece.astype(BF16)
        start += size
    return start


def clear_rest(ref, start):
    count, size, _ = ref.shape
    if start < size:
        for f in range(count):
            ref.spot[f, start:, :] = jnp.zeros((size - start, 128), BF16)


def place(width, target, offset):
    left = lax.broadcasted_iota(jnp.int32, (width, target), 0)
    right = lax.broadcasted_iota(jnp.int32, (width, target), 1)
    return jnp.where(left + offset == right, 1.0, 0.0).astype(BF16)


def flipped(value):
    size = value.shape[1]
    return mm_nt(place(size, size, 0), value).astype(BF16)


def tap_of(pieces, offset, index, size, side=1):
    each = size // len(pieces)
    start = offset + index // side * each
    tap = jnp.concatenate([piece[start : start + each, :] for piece in pieces], axis=0)
    width = 128 // side
    return tap[:, width * (index % side) : width * (index % side + 1)].astype(BF16)


def in_order(scal, pieces):
    if len(pieces) == 2:
        mine, other = whole(pieces[0]), whole(pieces[1])
        low = scal[9] > 0.5
        return [jnp.where(low, mine, other), jnp.where(low, other, mine)]
    return [whole(piece) for piece in pieces]


def fine_matrix(taps, slot):
    rows = []
    for a in range(3):
        total = None
        for b in range(3):
            spread_out = jnp.concatenate(
                [place(slot, 4 * slot, b * slot), place(slot, 4 * slot, (b + 1) * slot)], axis=1
            )
            term = mm(taps[3 * a + b][:, :slot], spread_out)
            total = term if total is None else total + term
        rows += [total[:, : 4 * slot], total[:, 4 * slot :]]
    return jnp.concatenate(rows, axis=0).astype(BF16)


def pack(widths, scal, *refs):
    shards, (out, scratch) = refs[: len(widths)], refs[-2:]
    scratch[...] = jnp.zeros(scratch.shape, F32)
    start = 0
    for shard, (taps, rows, swapped) in zip(shards, widths):
        if taps == 1:
            scratch[start : start + rows, : shard.shape[1]] = whole(shard)
            start += rows
        else:
            for t in range(taps):
                value = shard.spot[t]
                if swapped:
                    value = mm_nt(place(value.shape[1], value.shape[1], 0), value.astype(BF16))
                if value.shape[1] in (24, 64):
                    side = 4 if value.shape[1] == 24 else 2
                    low = t % side * (128 // side)
                    scratch[start : start + value.shape[0], low : low + value.shape[1]] = value
                    start += rows if t % side == side - 1 or t == taps - 1 else 0
                else:
                    scratch[start : start + value.shape[0], : value.shape[1]] = value
                    start += rows
    give(out, scratch[...].astype(BF16))


def prepare_rest(scal, *refs):
    pieces = refs[:-10]
    wsecond, wsecond_t, wdown, wdown_t, wcoarse, wcoarse_t, wup, wup_t, wout, wout_t = refs[-10:]
    count = len(pieces)
    pieces = in_order(scal, pieces)
    start = 0

    def taps_of(size, paired=False):
        nonlocal start
        taps = [tap_of(pieces, start, t, size, 2 if paired else 1) for t in range(9)]
        start += (5 if paired else 9) * (size // count)
        return taps

    def both(value, forward, backward):
        give(forward, value)
        give(backward, flipped(value))

    both(fine_matrix(taps_of(64, True), 64), wsecond, wsecond_t)
    taps = taps_of(128, True)
    rows = []
    for a in range(3):
        total = None
        for b in range(3):
            term = mm(taps[3 * a + b][:, :64], place(64, 256, 64 * b))
            total = term if total is None else total + term
        rows.append(total)
    both(jnp.concatenate(rows, axis=0)[:, :192].astype(BF16), wdown, wdown_t)
    taps = taps_of(128)
    rows = [jnp.concatenate(taps[3 * a : 3 * a + 3], axis=1) for a in range(3)]
    both(jnp.concatenate(rows, axis=0), wcoarse, wcoarse_t)
    taps = taps_of(64)
    rows = []
    blank = jnp.zeros((64, 128), BF16)
    for a in range(3):
        rows.append(jnp.concatenate(taps[3 * a : 3 * a + 3] + [blank], axis=1))
        rows.append(jnp.concatenate([blank] + taps[3 * a : 3 * a + 3], axis=1))
    up = jnp.concatenate(rows, axis=0)
    give(wup, up)
    turned = flipped(up).astype(F32)
    turned = jnp.concatenate([turned[:128], turned[128:256] + turned[256:384], turned[384:]], axis=0)
    a0, a1, a2 = turned[:, :128], turned[:, 128:256], turned[:, 256:]
    give(wup_t, jnp.concatenate([a0, a0 + a1, a1 + a2, a2], axis=1).astype(BF16))
    taps = []
    width = 64 // count
    for t in range(9):
        total = None
        for s in range(count):
            tap = pieces[s][start + 16 * t : start + 16 * (t + 1), :].astype(BF16)
            term = mm(tap[:, :width], place(width, 128, s * width))
            total = term if total is None else total + term
        taps.append(total.astype(BF16))
    both(fine_matrix(taps, 64), wout, wout_t)


def enter(
    widths, scal, target, condition, noise, *refs
):
    *shards, packed, own, edge_a, edge_b, figures, taps, scratch, marks = refs
    for item in shards:
        item.wait(1)
    pack(widths, scal, *shards, packed, taps)
    for item in (target, condition, noise):
        item.wait(2)
    values = [jnp.full((1, 128), scal[k], F32) for k in range(6)]
    give(figures, jnp.concatenate(values + [jnp.zeros((2, 128), F32)], axis=0))
    sigma, skip, in_scale = scal[0], scal[1], scal[3]
    goal = whole(target)
    noisy = goal + sigma * whole(noise)
    q = skip * noisy - goal
    natural = jnp.concatenate([in_scale * noisy, whole(condition)], axis=0).astype(BF16)
    spill(scratch, mm(natural, interleave(False)))
    blank = jnp.zeros((8, 512), F32)
    for i in range(ROWS):
        value = strided(scratch, i, 24)
        own.spot[:, i * 512 : (i + 1) * 512] = jnp.concatenate([value, blank], axis=0).astype(BF16)
    spill(scratch, q)
    blank = jnp.zeros((4, 512), F32)
    for j, i in enumerate((0, ROWS - 1)):
        rest = jnp.concatenate([strided(scratch, i, 12), blank], axis=0)
        marks[j] = jnp.zeros(marks.shape[1:], BF16)
        for part in range(3):
            piece = rest.astype(BF16)
            rest = rest - piece.astype(F32)
            for k in range(2):
                lanes = slice((2 * part + k) * 512, (2 * part + k + 1) * 512)
                marks[j, 8:, lanes] = piece[8 * k : 8 * k + 8]
    for j, edge in enumerate((edge_a, edge_b)):
        odd = scal[8] > 0.5 if j == 0 else scal[8] < 0.5
        low = (ROWS - FAR) * 512
        edge.spot[:16, :] = jnp.where(odd, own.spot[:16, : FAR * 512], own.spot[:16, low:])
        edge.spot[16:, :] = jnp.where(odd, own.spot[16:, : FAR * 512], own.spot[16:, low:]) + (
            jnp.where(odd, marks[0], marks[1])
        )


def marked(scal, got):
    halves = []
    for k in range(2):
        total = None
        for part in range(3):
            lanes = slice((2 * part + k) * 512, (2 * part + k + 1) * 512)
            piece = got.spot[16:32, lanes].astype(F32)[8:]
            total = piece if total is None else total + piece
        halves.append(total)
    return jnp.concatenate(halves, axis=0)


def stage_a(scal, got_a, got_b, own, done, *refs):
    *pieces, act, stats, kept, line_a, line_b, above, below = refs
    pieces = in_order(scal, pieces)
    weights = fine_matrix([tap_of(pieces, 0, t, 64, 4) for t in range(9)], 32)
    give(line_a, marked(scal, got_a))
    give(line_b, marked(scal, got_b))
    above[...] = pick(scal, whole(got_a), whole(got_b))
    below[...] = pick(scal, whole(got_b), whole(got_a))
    clear = jnp.zeros((16, FAR * 512), BF16)
    keep = lax.broadcasted_iota(jnp.int32, (16, FAR * 512), 0) < 8
    for ref in (above, below):
        ref[16:, :] = jnp.where(keep, ref[16:, :], clear)
    parts = {}
    total = jnp.zeros((128, HALF), F32)
    square = jnp.zeros((128, HALF), F32)
    for r in range(-FAR, ROWS + FAR):
        if r < 0:
            value = above[:, (r + FAR) * 512 : (r + FAR + 1) * 512]
        elif r < ROWS:
            value = own.spot[:, r * 512 : (r + 1) * 512]
        else:
            value = below[:, (r - ROWS) * 512 : (r - ROWS + 1) * 512]
        z = fine_taps(jnp.concatenate([value[:, :HALF], value[:, HALF:]], axis=0))
        if -1 <= r <= ROWS:
            put(kept, r, z)
        parts[r] = mm(weights, z)
        i = r - 1
        if i > -FAR:
            value = spread(parts, i, i)[i]
            put(act, i, value)
            del parts[i - 1]
            if 0 <= i < ROWS:
                total = total + value
                square = square + value * value
    put_stats(stats, total, square)


def slot(ref, index):
    return ref[:, index * HALF : (index + 1) * HALF]


def fill(ref, index, value):
    ref[:, index * HALF : (index + 1) * HALF] = value


def stage_b(members, embed_size, scal, stats_a, act_a, vec, *refs):
    *pieces, act_b, stats, kept, hats, passed, totals, wfirst_t, wfirst, zs, sems = refs
    passed.send(act_a.spot.at[pl.ds(2, 16)], sems.at[0])
    give(totals, total_stats(stats_a)[None])
    count = len(pieces)
    pieces = in_order(scal, pieces)
    start = 3 * (64 // count)
    first = fine_matrix([tap_of(pieces, start, t, 64, 2) for t in range(9)], 64)
    start += 5 * (64 // count)
    wfirst[...] = first
    give(wfirst_t, flipped(first))
    line = mm(whole(vec), tap_of(pieces, start, 0, embed_size))[0:1, :64]
    both = jnp.concatenate([line, line], axis=1)
    lift = jnp.sum(place(128, 128, 0).astype(F32) * both, axis=1, keepdims=True)
    mean, inverse = norm_columns(stats_a, True, members)
    for r in range(-6, ROWS + 6):
        hat = (row(act_a, r) - mean) * inverse
        fill(zs, r + 6, fine_taps(masked(silu(hat), r, ROWS, scal)))
        if 0 <= r < ROWS:
            hats.spot[r] = hat.astype(BF16)
    hats.finish()
    kept.send(zs.at[:, pl.ds(6 * HALF, 8 * HALF)], sems.at[1])
    parts = {}
    total = jnp.zeros((128, HALF), F32)
    square = jnp.zeros((128, HALF), F32)
    for r in range(-6, ROWS + 6):
        parts[r] = mm(wfirst[...], slot(zs, r + 6))
        i = r - 1
        if i > -6:
            value = spread(parts, i, i)[i] + lift
            put(act_b, i, value)
            del parts[i - 1]
            if 0 <= i < ROWS:
                total = total + value
                square = square + value * value
    put_stats(stats, total, square)


def stage_c(
    members, scal, stats_b, wsecond, act_b, act_a, wdown,
    fine, act_c, edge, stats, kept, kept_pool, hats, totals, zs, convolved, sems,
):
    give(totals, total_stats(stats_b)[None])
    mean, inverse = norm_columns(stats_b, True, members)
    for r in range(-5, ROWS + 5):
        hat = (row(act_b, r) - mean) * inverse
        fill(zs, r + 5, fine_taps(masked(silu(hat), r, ROWS, scal)))
        if -1 <= r <= ROWS:
            hats.spot[r + 1] = hat.astype(BF16)
    hats.finish()
    kept.send(zs.at[:, pl.ds(5 * HALF, 8 * HALF)], sems.at[0])
    wsecond.wait(1)
    parts = {}
    for r in range(-5, ROWS + 5):
        parts[r] = mm(whole(wsecond), slot(zs, r + 5))
        i = r - 1
        if i > -5:
            convolved[i + 4] = spread(parts, i, i)[i]
            del parts[i - 1]
    act_a.wait(1)
    wdown.wait(1)
    pooled = {}
    half = {}
    for i in range(-4, ROWS + 4):
        value = convolved[i + 4] + row(act_a, i)
        if -3 <= i < ROWS + 3:
            put(fine, i, value)
        half[i] = value[:64] + value[64:]
        if i % 2:
            value = 0.25 * (half.pop(i - 1) + half.pop(i))
            value = masked(value, i // 2, CROWS, scal)
            pooled[i // 2] = value
    weights = whole(wdown)
    parts = {}
    total = jnp.zeros((128, HALF), F32)
    square = jnp.zeros((128, HALF), F32)
    for r in range(-2, CROWS + 2):
        z = coarse_taps(pooled[r])
        if 0 <= r < CROWS:
            put(kept_pool, r, z)
        parts[r] = mm(weights, z)
        i = r - 1
        if i > -2:
            value = spread(parts, i, i)[i]
            put(act_c, i, value)
            del parts[i - 1]
            if 0 <= i < CROWS:
                total = total + value
                square = square + value * value
            if i in (1, 2):
                put(edge, i, value)
    put_stats(stats, total, square)


def stage_d(
    members, scal, stats_c, wcoarse, got_a, got_b, act_c, wup, fine,
    merged, hats, stats, kept_c, kept_up, totals, zs, sems,
):
    give(totals, total_stats(stats_c)[None])
    mean, inverse = norm_columns(stats_c, False, members)
    ring = {}
    for j in range(2):
        ring[j - 3] = pick(scal, row(got_a, j), row(got_b, j))
        ring[CROWS + 1 + j] = pick(scal, row(got_b, j), row(got_a, j))
    for j in range(-1, CROWS + 1):
        ring[j] = row(act_c, j)
    for r in range(-3, CROWS + 3):
        hat = (ring[r] - mean) * inverse
        fill(zs, r + 3, coarse_taps(masked(silu(hat), r, CROWS, scal)))
        if -2 <= r < CROWS + 2:
            hats.spot[r + 2] = hat.astype(BF16)
    hats.finish()
    kept_c.send(zs.at[:, pl.ds(3 * HALF, 4 * HALF)], sems.at[0])
    wcoarse.wait(1)
    wup.wait(1)
    parts = {}
    lifted = {}
    for r in range(-3, CROWS + 3):
        parts[r] = mm(whole(wcoarse), slot(zs, r + 3))
        i = r - 1
        if i > -3:
            value = spread(parts, i, i)[i] + ring[i]
            del parts[i - 1]
            lifted[i] = masked(value, i, CROWS, scal)
    weights = whole(wup)
    parts = {}
    total = jnp.zeros((128, HALF), F32)
    square = jnp.zeros((128, HALF), F32)
    for r in range(-2, CROWS + 2):
        z = coarse_taps(lifted[r])
        if 0 <= r < CROWS:
            put(kept_up, r, z)
        four = jnp.concatenate([z[:128], z[128:256], z[128:256], z[256:]], axis=0)
        parts[2 * r] = parts[2 * r + 1] = mm(weights, four)
        for i in (2 * r - 1, 2 * r):
            if i >= -3:
                value = spread(parts, i, i)[i] + row(fine, i)
                put(merged, i, value)
                parts.pop(i - 1)
                if 0 <= i < ROWS:
                    total = total + value
                    square = square + value * value
    put_stats(stats, total, square)


def stage_out(
    members, scal, stats_d, wout, merged, line_a, line_b, target, noise, wout_t, figures,
    denoised, back, edge_a, edge_b, stats, hats, cotangents, kept, totals, pairs, cells,
    goals, noisies, found, zs, sems,
):
    give(totals, total_stats(stats_d)[None])
    mean, inverse = norm_columns(stats_d, True, members)
    for r in range(-3, ROWS + 3):
        hat = (row(merged, r) - mean) * inverse
        hats.spot[r + 3] = hat.astype(BF16)
        if -3 < r < ROWS + 2:
            fill(zs, r + 2, fine_taps(masked(silu(hat), r, ROWS, scal)))
    hats.finish()
    kept.send(zs.at[:, pl.ds(2 * HALF, 8 * HALF)], sems.at[0])
    for item in (wout, line_a, line_b, target, noise, wout_t, figures):
        item.wait(1)
    parts = {}
    for r in range(-2, ROWS + 2):
        parts[r] = mm(whole(wout), slot(zs, r + 2))
        i = r - 1
        if i > -2:
            value = spread(parts, i, i)[i]
            del parts[i - 1]
            pairs[16 * (i + 1) : 16 * (i + 2), :] = jnp.concatenate(
                [value[:16], value[16:]], axis=1
            )
    value = pairs[...]
    high = value.astype(BF16)
    low = (value - high.astype(F32)).astype(BF16)
    sigma, skip, out_scale, weight, coef = [
        figures.spot[k : k + 1, 0:1] for k in (0, 1, 2, 4, 5)
    ]
    back_order = interleave(True)
    pairs[...] = mm(high, back_order) + mm(low, back_order)
    blank = jnp.zeros((4, 512), F32)
    loss_sum = jnp.zeros((12, 512), F32)
    top = pick(scal, whole(line_a), whole(line_b)) + out_scale * pairs[0:16, :]
    cells[0:16, :] = coef * scal[6] * top
    low = pick(scal, whole(line_b), whole(line_a)) + out_scale * pairs[16 * (ROWS + 1) :, :]
    cells[16 * (ROWS + 1) :, :] = coef * scal[7] * low
    spill(goals, whole(target))
    spill(noisies, whole(target) + sigma * whole(noise))
    for i in range(ROWS):
        goal = strided(goals, i, 12)
        noisy = strided(noisies, i, 12)
        estimate = skip * noisy + out_scale * pairs[16 * (i + 1) : 16 * (i + 1) + 12, :]
        for t in range(4):
            found[t, pl.ds(i, 12, stride=ROWS), :] = estimate[:, 128 * t : 128 * (t + 1)]
        mismatch = estimate - goal
        loss_sum = loss_sum + weight * mismatch * mismatch
        cells[16 * (i + 1) : 16 * (i + 2), :] = jnp.concatenate([coef * mismatch, blank], axis=0)
    give(denoised, jnp.concatenate([found[t, :96, :] for t in range(4)], axis=1))
    loss_sum = jnp.broadcast_to(
        jnp.sum(jnp.sum(loss_sum, axis=1, keepdims=True), axis=0, keepdims=True), (1, 128)
    )
    pairs[...] = mm(cells[...].astype(BF16), interleave(False))
    g = {}
    for i in range(-1, ROWS + 1):
        value = pairs[16 * (i + 1) : 16 * (i + 2), :]
        g[i] = jnp.concatenate([value[:, :HALF], value[:, HALF:]], axis=0).astype(BF16)
        put(cotangents, i, g[i])
    weights = whole(wout_t)
    total = jnp.zeros((128, HALF), F32)
    cross = jnp.zeros((128, HALF), F32)
    for r in range(ROWS):
        value = fine_untap(mm(weights, stack_rows(g, r)))
        put(back, r, value.astype(BF16))
        hat = row(hats, r).astype(F32)
        e = value * silu_slope(hat)
        total = total + e
        cross = cross + e * hat
    for j in range(3):
        top, low = row(back, j), row(back, ROWS - 3 + j)
        put(edge_a, j, pick(scal, top, low))
        put(edge_b, j, pick(scal, low, top))
    put_stats(stats, total, cross, loss_sum)


def grads_out(scal, cotangents, zs, grad, gs):
    g = {r: row(cotangents, r) for r in range(-1, ROWS + 1)}
    for r in range(ROWS):
        put(gs, r, stack_rows(g, r))
    parts = fine_grad(mm_nt(gs[...], whole(zs)), 16, 64)
    put_grad(grad, 0, grad_blocks(parts, 64), split=False)


def grads_up(scal, grad_merged, grad_coarse, kept_up, kept_c, grad_out, grads, gs, zs, gc):
    g = {r: row(grad_merged, r) for r in range(-1, ROWS + 1)}
    for r in range(ROWS):
        put(gs, r, stack_rows(g, r))
        put(zs, r, row(kept_up, r // 2))
    g = {r: row(grad_coarse, r) for r in range(-1, CROWS + 1)}
    for r in range(CROWS):
        put(gc, r, stack_rows(g, r))
    blocks = mm_nt(gs[...], zs[...])
    parts = []
    for a in range(3):
        even = blocks[128 * a : 128 * a + 64]
        odd = blocks[128 * a + 64 : 128 * a + 128]
        parts.append(
            jnp.concatenate(
                [
                    even[:, :128] + odd[:, 128:256],
                    even[:, 128:256] + odd[:, 128:256],
                    even[:, 128:256] + odd[:, 256:],
                ],
                axis=1,
            )
        )
    start = put_grad(grads, 0, grad_blocks(parts, 128))
    blocks = mm_nt(gc[...], whole(kept_c))
    parts = [blocks[128 * a : 128 * (a + 1)] for a in range(3)]
    start = put_grad(grads, start, grad_blocks(parts, 128))
    for f in range(grads.shape[0]):
        grads.spot[f, start : start + 80, :] = grad_out.spot[f]
    clear_rest(grads, start + 80)


def grads_down(scal, grad_fine, grad_c, kept_pool, kept_b, grads, gs, gc):
    g = {r: row(grad_fine, r) for r in range(-1, ROWS + 1)}
    for r in range(ROWS):
        put(gs, r, stack_rows(g, r))
    g = {r: row(grad_c, r) for r in range(-1, CROWS + 1)}
    for r in range(CROWS):
        put(gc, r, stack_rows(g, r))
    blocks = mm_nt(gc[...], whole(kept_pool))
    parts = [blocks[128 * a : 128 * (a + 1)] for a in range(3)]
    start = put_grad(grads, 0, grad_blocks(parts, 64))
    parts = fine_grad(mm_nt(gs[...], whole(kept_b)), 64, 64)
    clear_rest(grads, put_grad(grads, start, grad_blocks(parts, 64)))


def grads_first(scal, grad_b, line, vec, kept_a, grads, gs):
    g = {r: row(grad_b, r) for r in range(-1, ROWS + 1)}
    for r in range(ROWS):
        put(gs, r, stack_rows(g, r))
    parts = fine_grad(mm_nt(gs[...], whole(kept_a)), 64, 64)
    start = put_grad(grads, 0, grad_blocks(parts, 64))
    line = line.spot[0:1, :]
    line = line + pltpu.roll(line, 64, 1)
    column = jnp.sum(
        place(128, 128, 0).astype(F32) * vec.spot[0:1, :].astype(F32), axis=1, keepdims=True
    )
    outer = (column * line).astype(BF16)
    size = 128 // grads.shape[0]
    for f in range(grads.shape[0]):
        grads.spot[f, start : start + size, :] = outer[f * size : (f + 1) * size]


def stage_up(
    members, members_c, scal, stats_d, stats_ed, got_a, got_b, hats, back, wup_t, stats_c, hats_c,
    wcoarse_t, done,
    grad_merged, back_c, grad_coarse, edge_a, edge_b, stats, loss, total_next,
):
    give(loss, jnp.broadcast_to(total_stats(stats_ed)[2:3, :], (8, 128)))
    mean, inverse = norm_columns(stats_d, True, members)
    shift, slope = back_columns(stats_ed, True, members)
    hats.wait(1)
    g = {}
    for r in range(-3, ROWS + 3):
        hat = row(hats, r).astype(F32)
        if r < 0:
            u = pick(scal, row(got_a, r + 3), row(got_b, r + 3)).astype(F32)
        elif r < ROWS:
            u = row(back, r).astype(F32)
        else:
            u = pick(scal, row(got_b, r - ROWS), row(got_a, r - ROWS)).astype(F32)
        value = inverse * (u * silu_slope(hat) - shift - hat * slope)
        g[r] = masked(value, r, ROWS, scal).astype(BF16)
        if -2 <= r < ROWS + 2:
            put(grad_merged, r, g[r])
    wup_t.wait(1)
    weights = whole(wup_t)
    gk = {}
    for r in range(-1, CROWS + 1):
        rows = jnp.concatenate([g[2 * r + 2], g[2 * r + 1], g[2 * r], g[2 * r - 1]], axis=0)
        value = coarse_untap(mm(weights, rows))
        gk[r] = masked(value, r, CROWS, scal).astype(BF16)
        put(grad_coarse, r, gk[r])
    wcoarse_t.wait(1)
    hats_c.wait(1)
    stats_c.wait(1)
    weights = whole(wcoarse_t)
    mean, inverse = norm_columns(stats_c, False, members_c)
    total = jnp.zeros((128, HALF), F32)
    cross = jnp.zeros((128, HALF), F32)
    for r in range(CROWS):
        value = coarse_untap(mm(weights, stack_rows(gk, r)))
        put(back_c, r, value.astype(BF16))
        hat = row(hats_c, r).astype(F32)
        e = value * silu_slope(hat)
        total = total + e
        cross = cross + e * hat
    top = [row(back_c, 0), row(back_c, 1), gk[1]]
    low = [row(back_c, 2), row(back_c, 3), gk[2]]
    for j in range(3):
        put(edge_a, j, pick(scal, top[j], low[j]))
        put(edge_b, j, pick(scal, low[j], top[j]))
    put_stats(stats, total, cross)
    give(total_next, whole(stats_c))


def stage_down(
    members, members_c, scal, stats_c, stats_ec, got_a, got_b, hats_c, back_c, grad_coarse,
    wdown_t, grad_merged, stats_b, wsecond_t, hats, done,
    grad_fine, back_b, stats, grad_c, total_next,
):
    mean, inverse = norm_columns(stats_c, False, members_c)
    shift, slope = back_columns(stats_ec, False, members_c)
    hats_c.wait(1)
    g = {}
    for r in range(-2, CROWS + 2):
        hat = row(hats_c, r).astype(F32)
        if r < 0:
            u = pick(scal, row(got_a, r + 2), row(got_b, r + 2)).astype(F32)
        elif r < CROWS:
            u = row(back_c, r).astype(F32)
        else:
            u = pick(scal, row(got_b, r - CROWS), row(got_a, r - CROWS)).astype(F32)
        if r == -2:
            through = pick(scal, row(got_a, 2), row(got_b, 2)).astype(F32)
        elif r == CROWS + 1:
            through = pick(scal, row(got_b, 2), row(got_a, 2)).astype(F32)
        else:
            through = row(grad_coarse, r).astype(F32)
        value = through + inverse * (u * silu_slope(hat) - shift - hat * slope)
        g[r] = masked(value, r, CROWS, scal).astype(BF16)
        if -1 <= r <= CROWS:
            put(grad_c, r, g[r])
    wdown_t.wait(1)
    weights = whole(wdown_t)
    fine = {}
    for r in range(-1, CROWS + 1):
        value = 0.25 * coarse_untap(mm(weights, stack_rows(g, r)))
        both = jnp.concatenate([value, value], axis=0)
        for i in (2 * r, 2 * r + 1):
            value = masked(row(grad_merged, i).astype(F32) + both, i, ROWS, scal)
            fine[i] = value.astype(BF16)
            if -1 <= i <= ROWS:
                put(grad_fine, i, fine[i])
    wsecond_t.wait(1)
    hats.wait(1)
    stats_b.wait(1)
    weights = whole(wsecond_t)
    mean, inverse = norm_columns(stats_b, True, members)
    total = jnp.zeros((128, HALF), F32)
    cross = jnp.zeros((128, HALF), F32)
    for r in range(-1, ROWS + 1):
        value = fine_untap(mm(weights, stack_rows(fine, r)))
        put(back_b, r, value.astype(BF16))
        if 0 <= r < ROWS:
            hat = row(hats, r).astype(F32)
            e = value * silu_slope(hat)
            total = total + e
            cross = cross + e * hat
    put_stats(stats, total, cross)
    give(total_next, whole(stats_b))


def stage_first(
    members, scal, stats_b, stats_eb, hats_b, back_b, wfirst_t, stats_a, hats, done,
    back_a, stats, grad_b, line, total_next,
):
    mean, inverse = norm_columns(stats_b, True, members)
    shift, slope = back_columns(stats_eb, True, members)
    hats_b.wait(1)
    g = {}
    sums = jnp.zeros((128, HALF), F32)
    for r in range(-1, ROWS + 1):
        hat = row(hats_b, r).astype(F32)
        u = row(back_b, r).astype(F32)
        value = inverse * (u * silu_slope(hat) - shift - hat * slope)
        if 0 <= r < ROWS:
            sums = sums + value
        g[r] = masked(value, r, ROWS, scal).astype(BF16)
        put(grad_b, r, g[r])
    wfirst_t.wait(1)
    hats.wait(1)
    stats_a.wait(1)
    weights = whole(wfirst_t)
    total = jnp.zeros((128, HALF), F32)
    cross = jnp.zeros((128, HALF), F32)
    for r in range(ROWS):
        value = fine_untap(mm(weights, stack_rows(g, r)))
        put(back_a, r, value.astype(BF16))
        hat = row(hats, r).astype(F32)
        e = value * silu_slope(hat)
        total = total + e
        cross = cross + e * hat
    put_stats(stats, total, cross)
    sums = to_row(jnp.sum(sums, axis=1, keepdims=True))
    give(line, jnp.broadcast_to(sums, (8, 128)))
    give(total_next, whole(stats_a))


def stage_last(
    members, members_all, scal, stats_a, stats_ea, hats, back_a, grad_fine, kept_in, early, middle, first,
    loss, loss_other, keep, send, loss_sum, gs, held, sems,
):
    grads = Source(held, [], 0)
    copies, start = [], 0
    for index, ref in enumerate((early, middle)):
        rows = pl.ds(start, ref.shape[1])
        copies.append(
            pltpu.make_async_copy(ref.spot, grads.spot.at[:, rows, :], sems.at[index])
        )
        copies[index].start()
        start += ref.shape[1]
    give(loss_sum, (loss.spot[0:1, 0:1] + loss_other.spot[0:1, 0:1]) * (1.0 / members_all))
    mean, inverse = norm_columns(stats_a, True, members)
    shift, slope = back_columns(stats_ea, True, members)
    for r in range(ROWS):
        hat = row(hats, r).astype(F32)
        u = row(back_a, r).astype(F32)
        value = row(grad_fine, r).astype(F32) + inverse * (
            u * silu_slope(hat) - shift - hat * slope
        )
        put(gs, r, value.astype(BF16))
    kept_in.wait(1)
    first.wait(1)
    parts = []
    for a in range(3):
        blocks = mm_nt(gs[...], kept_in.spot[:, a * HALF : (a + ROWS) * HALF])
        parts.append(
            jnp.concatenate(
                [blocks[:64, :96] + blocks[64:, 32:128], jnp.zeros((64, 32), F32)], axis=1
            )
        )
    size = first.shape[1]
    for f in range(grads.shape[0]):
        grads.spot[f, start : start + size, :] = first.spot[f]
    clear_rest(grads, put_grad(grads, start + size, parts))
    for copy in copies:
        copy.wait()
    half = keep.shape[1]
    odd = scal[8] > 0.5
    for f in range(keep.shape[0]):
        low, high = held[f, :half, :], held[f, half:, :]
        keep.spot[f] = jnp.where(odd, high, low)
        send.spot[f] = jnp.where(odd, low, high)


def join(scal, kept, got, out):
    give(out, (whole(kept).astype(F32) + whole(got).astype(F32)).astype(BF16))


def add_up(scal, got, out):
    total = got.spot[0].astype(F32)
    for index in range(1, got.shape[0]):
        total = total + got.spot[index].astype(F32)
    total = total.astype(BF16)
    for index in range(out.shape[0]):
        out.spot[index] = total


def unpack(starts, scal, mine, other, *refs):
    first, down, second, coarse, up, out, embed, inputs, flat = refs
    half = mine.shape[0]
    odd = scal[8] > 0.5
    flat[:half, :] = jnp.where(odd, whole(other), whole(mine)).astype(F32)
    flat[half:, :] = jnp.where(odd, whole(mine), whole(other)).astype(F32)

    def take(ref, start, out, size, ins, trim=False):
        for t in range(9):
            a, b = t // 3, t % 3
            if ins == 128:
                at, lanes = t, 0
            elif ins == 64:
                at, lanes = (a, b) if b < 2 else (3 + a // 2, a % 2)
            else:
                at, lanes = a, b
            value = ref[start + at * size : start + (at + 1) * size, :]
            if ins == 24:
                out.spot[t] = mm_nt(place(24, 128, 32 * lanes), value.astype(BF16))
                continue
            value = value[:, lanes * ins : (lanes + 1) * ins]
            if trim:
                value = value[:12]
                if out.shape[2] == 32:
                    value = jnp.where(scal[9] > 0.5, value[:, :32], value[:, 32:])
            out.spot[t] = value
        return start + (9 if ins == 128 else 5 if ins == 64 else 3) * size

    start = take(flat, 0, up, up.shape[1], 128)
    start = take(flat, start, coarse, coarse.shape[1], 128)
    take(flat, start, out, 16, 64, trim=True)
    start = take(flat, starts[0], down, down.shape[1], 64)
    take(flat, start, second, second.shape[1], 64)
    start = take(flat, starts[1], first, first.shape[1], 64)
    size = embed.shape[0]
    give(embed, flat[start : start + size, :64])
    take(flat, start + size, inputs, inputs.shape[2], 24)


class Field:
    def __init__(self, array, first):
        self.array, self.first = array, first


class Saved:
    def __init__(self, item, low=None, high=None, when=0):
        self.item, self.low, self.high, self.when = item, low, high, when


def shape(*dims, dtype=F32):
    return jax.ShapeDtypeStruct(dims, dtype)


def rows_of(first, number, dtype=F32):
    return Field(shape(number, 128, HALF, dtype=dtype), first)


def flat_rows(first, number, channels):
    return Field(shape(channels, number * HALF, dtype=BF16), first)


def opened(item):
    saved = item if isinstance(item, Saved) else None
    item = saved.item if saved else item
    if isinstance(item, Field):
        return saved, item.array, item.first
    return saved, item, 0


def position():
    me, bands = lax.axis_index("rows"), lax.axis_size("rows")
    return {
        6: jnp.where(me > 0, 1.0, 0.0),
        7: jnp.where(me < bands - 1, 1.0, 0.0),
        8: jnp.where(me % 2 == 1, 1.0, 0.0),
        9: jnp.where(lax.axis_index("fsdp") == 0, 1.0, 0.0),
    }


def run(name, kernel, outs, scal, *operands, scratch=()):
    vmem, hbm = pl.BlockSpec(memory_space=pltpu.VMEM), pl.BlockSpec(memory_space=pltpu.HBM)
    in_specs, arrays, plans, spots = [], [], [], []
    if scal is not None:
        in_specs, arrays = [pl.BlockSpec(memory_space=pltpu.SMEM)], [scal]
    for item in operands:
        saved, item, first = opened(item)
        if saved is None:
            in_specs.append(vmem)
            arrays.append(item)
            plans.append((first, None, None))
            continue
        part = None
        dims = item.shape
        if saved.low is not None:
            part = pl.ds(saved.low - first, saved.high - saved.low)
            dims = (saved.high - saved.low,) + dims[1:]
            first = saved.low
        in_specs.append(hbm)
        arrays.append(pltpu.with_memory_space_constraint(item, pltpu.HBM))
        if saved.when is None:
            plans.append((first, None, None))
            continue
        plans.append((first, (saved.when, part), len(spots)))
        spots.append(pltpu.VMEM(dims, item.dtype))
    ins = len(operands)
    out_specs, out_shapes = [], []
    for item in outs:
        saved, item, first = opened(item)
        if saved is None:
            out_specs.append(vmem)
            out_shapes.append(item)
            plans.append((first, None, None))
            continue
        out_specs.append(hbm)
        out_shapes.append(pltpu.HBM(item.shape, item.dtype))
        last = None
        if isinstance(saved.item, Field):
            count = item.shape[0] if len(item.shape) == 3 else item.shape[1] // HALF
            last = first + count - 1
        if saved.when is None:
            plans.append((first, None, None))
            continue
        plans.append((first, (last, None), len(spots)))
        spots.append(pltpu.VMEM(item.shape, item.dtype))

    def body(*refs):
        numbers = position()
        if scal is not None:
            numbers.update({index: refs[0][index] for index in range(6)})
            refs = refs[1:]
        given, refs = refs[: len(plans)], refs[len(plans) :]
        held, refs = refs[: len(spots)], refs[len(spots) :]
        sems, extra = refs[0], refs[1:]
        wrapped = []
        for index, (ref, (first, plan, place_at)) in enumerate(zip(given, plans)):
            copies = []
            if plan is not None:
                where = held[place_at]
                when, part = plan
                if index < ins:
                    source = ref if part is None else ref.at[part]
                    copies.append((when, pltpu.make_async_copy(source, where, sems.at[place_at])))
                else:
                    copies.append((when, pltpu.make_async_copy(where, ref, sems.at[place_at])))
                ref = where
            wrapped.append((Source if index < ins else Sink)(ref, copies, first))
        for item in wrapped[:ins]:
            item.wait(0)
        kernel(numbers, *wrapped, *extra)
        for item in wrapped[ins:]:
            item.finish()
        for item in wrapped[ins:]:
            for copy in item.started:
                copy.wait()

    made = pl.pallas_call(
        body,
        out_shape=tuple(out_shapes),
        in_specs=in_specs,
        out_specs=tuple(out_specs),
        scratch_shapes=spots
        + [pltpu.SemaphoreType.DMA((max(len(spots), 1),))]
        + [pltpu.VMEM(*item) if isinstance(item, tuple) else item for item in scratch],
        compiler_params=pltpu.CompilerParams(vmem_limit_bytes=LIMIT),
        name=name,
    )(*arrays)
    results = []
    for array, item in zip(made, outs):
        item = item.item if isinstance(item, Saved) else item
        results.append(Field(array, item.first) if isinstance(item, Field) else array)
    return results


def sum_parts(stats):
    return lax.all_to_all(stats, "rows", 0, 0)


def swap(value_a, value_b):
    count = lax.axis_size("rows")
    pairs = [(i, i ^ 1) for i in range(count)]
    across = []
    for i in range(1, count - 1, 2):
        across += [(i, i + 1), (i + 1, i)]
    return lax.ppermute(value_a, "rows", pairs), lax.ppermute(value_b, "rows", across)


def gather_packed(packed):
    if lax.axis_size("fsdp") == 2:
        return [packed, lax.ppermute(packed, "fsdp", [(0, 1), (1, 0)])]
    whole = lax.all_gather(packed, "fsdp").astype(F32)
    return [whole[i] for i in range(whole.shape[0])]


def group_shape(rows, count):
    return shape(count, -(-rows // 16) * 16, 128, dtype=BF16)


def per_device(
    residual_target,
    conditioning,
    noise_sample,
    noise_level,
    input_kernel,
    first_kernel,
    second_kernel,
    down_kernel,
    coarse_kernel,
    upward_kernel,
    output_kernel,
    embed_matrix,
):
    bands, count = lax.axis_size("rows"), lax.axis_size("fsdp")
    members = 2 * ROWS * 2 * HALF * bands
    members_c = 4 * CROWS * HALF * bands
    members_all = count * residual_target.size * bands
    sigma_level, skip_scale, out_scale, in_scale, weight = preconditions(noise_level[0])
    coef = 2.0 * weight * out_scale / members_all
    scal = jnp.stack([sigma_level, skip_scale, out_scale, in_scale, weight, coef])
    embedded = embedding(sigma_level, embed_matrix.shape[0] * count)
    target = residual_target.reshape(12 * ROWS, 512)
    condition = conditioning.reshape(12 * ROWS, 512)
    noise = noise_sample.reshape(12 * ROWS, 512)

    def widths_of(shards, rows):
        widths = tuple(
            (9 if item.ndim == 3 else 1, size, item.ndim == 3 and item.shape[1] == 24)
            for item, size in zip(shards, rows)
        )
        total = 0
        for item, (taps, size, swapped) in zip(shards, widths):
            paired = taps == 9 and item.shape[2] == 64
            total += (3 if swapped else 5 if paired else taps) * size
        return widths, total

    fine_o, coarse_o = input_kernel.shape[1], down_kernel.shape[1]
    inputs_t = jnp.swapaxes(input_kernel, 1, 2)
    shards = [inputs_t, first_kernel, embed_matrix]
    widths, packed_rows = widths_of(shards, [fine_o, fine_o, embed_matrix.shape[0]])
    far = shape(32, FAR * 512, dtype=BF16)
    early, own, edge_a, edge_b, figures = run(
        "enter",
        functools.partial(enter, widths),
        [
            shape(packed_rows, 128, dtype=BF16), shape(32, ROWS * 512, dtype=BF16), far, far,
            Saved(shape(8, 128)),
        ],
        scal,
        Saved(target, when=2),
        Saved(condition, when=2),
        Saved(noise, when=2),
        *[Saved(item, when=1) for item in shards],
        scratch=[
            ((packed_rows, 128), F32), ((4, 192, 128), F32), ((2, 16, FAR * 512), BF16)
        ],
    )
    got_a, got_b = swap(edge_a, edge_b)
    early = gather_packed(early)
    shards = [second_kernel, down_kernel, coarse_kernel, upward_kernel, output_kernel]
    widths, packed_rows = widths_of(shards, [fine_o, coarse_o, coarse_o, fine_o, 16])
    (rest,) = run(
        "pack_rest",
        functools.partial(pack, widths),
        [shape(packed_rows, 128, dtype=BF16)],
        None,
        *[Saved(item) for item in shards],
        own,
        scratch=[((packed_rows, 128), F32)],
    )
    vector = jnp.broadcast_to(embedded[None, :], (16, embedded.shape[0]))
    stat = shape(bands, 2, 128)
    total = Saved(shape(1, 2, 128))
    act_a, stats_a, kept_in, line_a, line_b = run(
        "stage_a",
        stage_a,
        [
            rows_of(-6, 20), stat, Saved(flat_rows(-1, 10, 128)),
            Saved(shape(16, 512)), Saved(shape(16, 512)),
        ],
        None,
        got_a, got_b, own, rest, *early,
        scratch=[((32, FAR * 512), BF16), ((32, FAR * 512), BF16)],
    )
    stats_a = sum_parts(stats_a)
    rest, stats_a = lax.optimization_barrier((rest, stats_a))
    (
        wsecond, wsecond_t, wdown, wdown_t, wcoarse, wcoarse_t, wup, wup_t, wout, wout_t
    ) = run(
        "prepare_rest",
        prepare_rest,
        [
            Saved(shape(384, 256, dtype=BF16)), Saved(shape(256, 384, dtype=BF16)),
            Saved(shape(384, 192, dtype=BF16)), Saved(shape(192, 384, dtype=BF16)),
            Saved(shape(384, 384, dtype=BF16)), Saved(shape(384, 384, dtype=BF16)),
            Saved(shape(384, 512, dtype=BF16)), Saved(shape(384, 512, dtype=BF16)),
            Saved(shape(96, 256, dtype=BF16)), Saved(shape(256, 96, dtype=BF16)),
        ],
        None,
        *gather_packed(rest),
    )

    act_b, stats_b, kept_a, hats_a, act_a, total_a, wfirst_t = run(
        "stage_b",
        functools.partial(stage_b, members, embedded.shape[0]),
        [
            rows_of(-5, 18), stat, Saved(flat_rows(0, 8, 256), when=None),
            Saved(rows_of(0, 8, BF16)),
            Saved(rows_of(-4, 16), when=None), total, Saved(shape(256, 384, dtype=BF16)),
        ],
        None,
        stats_a, act_a, vector, *early,
        scratch=[((384, 256), BF16), ((256, 20 * HALF), BF16), pltpu.SemaphoreType.DMA((2,))],
    )
    stats_b = sum_parts(stats_b)
    fine, act_c, edge, stats_c, kept_b, kept_pool, hats_b, total_b = run(
        "stage_c",
        functools.partial(stage_c, members),
        [
            rows_of(-3, 14), rows_of(-1, 6), Field(shape(128, 2 * HALF), 1), stat,
            Saved(flat_rows(0, 8, 256), when=None), Saved(flat_rows(0, 4, 192)),
            Saved(rows_of(-1, 10, BF16)), total,
        ],
        None,
        stats_b, Saved(wsecond, when=1), act_b, Saved(act_a, when=1), Saved(wdown, when=1),
        scratch=[
            ((256, 18 * HALF), BF16), ((16, 128, HALF), F32), pltpu.SemaphoreType.DMA((1,)),
        ],
    )
    got_a, got_b = swap(edge.array, edge.array)
    stats_c = sum_parts(stats_c)
    merged, hats_c, stats_d, kept_c, kept_up, total_c = run(
        "stage_d",
        functools.partial(stage_d, members_c),
        [
            rows_of(-3, 14), Saved(rows_of(-2, 8, BF16)), stat,
            Saved(flat_rows(0, 4, 384), when=None), Saved(flat_rows(0, 4, 384)), total,
        ],
        None,
        stats_c, Saved(wcoarse, when=1), got_a, got_b, act_c, Saved(wup, when=1), fine,
        scratch=[((384, 10 * HALF), BF16), pltpu.SemaphoreType.DMA((1,))],
    )
    stats_d = sum_parts(stats_d)
    edge = Field(shape(128, 3 * HALF, dtype=BF16), 0)
    denoised, back_d, edge_a, edge_b, stats_ed, hats_d, cotangents, kept_d, total_d = run(
        "stage_out",
        functools.partial(stage_out, members),
        [
            Saved(shape(96, 512)), rows_of(0, 8, BF16), edge, edge, shape(bands, 4, 128),
            Saved(rows_of(-3, 14, BF16)),
            Field(shape(10, 32, HALF, dtype=BF16), -1),
            Saved(flat_rows(0, 8, 256), when=None), shape(1, 2, 128),
        ],
        None,
        stats_d, Saved(wout, when=1), merged, Saved(line_a, when=1), Saved(line_b, when=1),
        Saved(target, when=1), Saved(noise, when=1), Saved(wout_t, when=1),
        Saved(figures, when=1),
        scratch=[
            ((160, 512), F32), ((160, 512), F32),
            ((4, 128, 128), F32), ((4, 128, 128), F32), ((4, 128, 128), F32),
            ((256, 12 * HALF), BF16), pltpu.SemaphoreType.DMA((1,)),
        ],
    )
    got_a, got_b = swap(edge_a.array, edge_b.array)
    (grad_out,) = run(
        "grads_out",
        grads_out,
        [Saved(shape(count, 80, 128, dtype=BF16))],
        None,
        cotangents, Saved(kept_d),
        scratch=[((96, 8 * HALF), BF16)],
    )
    stats_ed = sum_parts(stats_ed)
    grad_merged, back_c, grad_coarse, edge_a, edge_b, stats_ec, loss, total_c = run(
        "stage_up",
        functools.partial(stage_up, members, members_c),
        [
            rows_of(-2, 12, BF16), rows_of(0, 4, BF16), rows_of(-1, 6, BF16), edge, edge, stat,
            shape(8, 128), shape(1, 2, 128),
        ],
        None,
        total_d, stats_ed, got_a, got_b, Saved(hats_d, when=1), back_d, Saved(wup_t, when=1),
        Saved(total_c, when=1),
        Saved(hats_c, when=1), Saved(wcoarse_t, when=1), Saved(grad_out, when=None),
    )
    got_a, got_b = swap(edge_a.array, edge_b.array)
    (early,) = run(
        "grads_up",
        grads_up,
        [Saved(group_shape(9 * (fine_o + coarse_o) + 80, count))],
        None,
        grad_merged, grad_coarse, Saved(kept_up), Saved(kept_c), Saved(grad_out),
        scratch=[
            ((384, 8 * HALF), BF16), ((384, 8 * HALF), BF16), ((384, 4 * HALF), BF16)
        ],
    )
    stats_ec = sum_parts(stats_ec)
    if count == 2:
        loss_other = lax.ppermute(loss, "fsdp", [(0, 1), (1, 0)])
    else:
        loss_other = lax.psum(loss, "fsdp") - loss
    grad_fine, back_b, stats_eb, grad_c, total_b = run(
        "stage_down",
        functools.partial(stage_down, members, members_c),
        [
            rows_of(-1, 10, BF16), rows_of(-1, 10, BF16), stat, Saved(rows_of(-1, 6, BF16)),
            shape(1, 2, 128),
        ],
        None,
        total_c, stats_ec, got_a, got_b, Saved(hats_c, when=1), back_c, grad_coarse,
        Saved(wdown_t, when=1), grad_merged, Saved(total_b, when=1), Saved(wsecond_t, when=1),
        Saved(hats_b, 0, 8, when=1), Saved(early, when=None),
    )
    (middle,) = run(
        "grads_down",
        grads_down,
        [Saved(group_shape(5 * (fine_o + coarse_o), count))],
        None,
        grad_fine, Saved(grad_c), Saved(kept_pool), Saved(kept_b),
        scratch=[((384, 8 * HALF), BF16), ((384, 4 * HALF), BF16)],
    )
    stats_eb = sum_parts(stats_eb)
    back_a, stats_ea, grad_b, line, total_a = run(
        "stage_first",
        functools.partial(stage_first, members),
        [
            rows_of(0, 8, BF16), stat, rows_of(-1, 10, BF16), shape(8, 128),
            shape(1, 2, 128),
        ],
        None,
        total_b, stats_eb, Saved(hats_b, when=1), back_b, Saved(wfirst_t, when=1), Saved(total_a, when=1),
        Saved(hats_a, when=1), Saved(middle, when=None),
    )
    (grad_first,) = run(
        "grads_first",
        grads_first,
        [Saved(shape(count, 5 * fine_o + embed_matrix.shape[0], 128, dtype=BF16))],
        None,
        grad_b, line, vector, Saved(kept_a),
        scratch=[((384, 8 * HALF), BF16)],
    )
    stats_ea = sum_parts(stats_ea)
    late = group_shape(8 * fine_o + embed_matrix.shape[0], count)
    starts = [early.shape[1], early.shape[1] + middle.shape[1]]
    total = starts[1] + late.shape[1]
    chunk = -(-total // (16 * bands)) * 16
    chips = bands // 2
    half = shape(count, chunk * chips, 128, dtype=BF16)
    keep, send, loss = run(
        "stage_last",
        functools.partial(stage_last, members, members_all),
        [half, half, shape(1, 1)],
        None,
        total_a, stats_ea, Saved(hats_a), back_a, grad_fine, Saved(kept_in, when=1),
        Saved(early, when=None), Saved(middle, when=None), Saved(grad_first, when=1), loss, loss_other,
        scratch=[
            ((128, 8 * HALF), BF16), ((count, chunk * bands, 128), BF16),
            pltpu.SemaphoreType.DMA((2,)),
        ],
    )
    loss_value = loss.reshape(())
    pairs = [(i, i ^ 1) for i in range(bands)]
    got = lax.ppermute(send, "rows", pairs)
    (both,) = run("join", join, [half], None, keep, got)
    both = both.reshape(count * chips, chunk, 128)
    cores = [[f * bands + r for f in range(count) for r in range(c, bands, 2)] for c in range(2)]
    got = lax.all_to_all(both, ("fsdp", "rows"), 0, 0, axis_index_groups=cores)
    (mine,) = run("add_up", add_up, [shape(chips, chunk, 128, dtype=BF16)], None, got)
    cores = [[r for r in range(c, bands, 2)] for c in range(2)]
    mine = lax.all_to_all(mine, "rows", 0, 0, axis_index_groups=cores)
    mine = mine.reshape(chips * chunk, 128)
    other = lax.ppermute(mine, "rows", pairs)
    first_g, down_g, second_g, coarse_g, up_g, out_g, embed_g, in_g = run(
        "unpack",
        functools.partial(unpack, starts),
        [
            shape(*first_kernel.shape),
            shape(*down_kernel.shape),
            shape(*second_kernel.shape),
            shape(*coarse_kernel.shape),
            shape(*upward_kernel.shape),
            shape(9, 12, output_kernel.shape[2] if count == 2 else 64),
            shape(*embed_matrix.shape),
            shape(*inputs_t.shape),
        ],
        None,
        mine, other,
        scratch=[((chunk * bands, 128), F32)],
    )
    width = output_kernel.shape[2]
    if count != 2:
        out_g = lax.dynamic_slice_in_dim(out_g, lax.axis_index("fsdp") * width, width, axis=2)
    return (
        denoised.reshape(residual_target.shape),
        loss_value,
        jnp.swapaxes(in_g, 1, 2),
        first_g,
        second_g,
        down_g,
        coarse_g,
        up_g,
        out_g,
        embed_g,
    )


def solution(mesh):
    in_specs = (
        P("fsdp", None, "rows", None),
        P("fsdp", None, "rows", None),
        P("fsdp", None, "rows", None),
        P("fsdp"),
        P(None, "fsdp", None),
        P(None, "fsdp", None),
        P(None, "fsdp", None),
        P(None, "fsdp", None),
        P(None, "fsdp", None),
        P(None, "fsdp", None),
        P(None, None, "fsdp"),
        P("fsdp", None),
    )
    out_specs = (
        P("fsdp", None, "rows", None),
        P(),
        P(None, "fsdp", None),
        P(None, "fsdp", None),
        P(None, "fsdp", None),
        P(None, "fsdp", None),
        P(None, "fsdp", None),
        P(None, "fsdp", None),
        P(None, None, "fsdp"),
        P("fsdp", None),
    )
    return jax.shard_map(
        per_device, mesh=mesh, in_specs=in_specs, out_specs=out_specs, check_vma=False
    )
```
